32 devices in a mesh: groups: 2 (over y), row: 4 (over z), col: 4 (over x, core).
Axes of the slice: x: 2, y: 2, z: 4, core: 2. Of those that a mesh axis runs over, the one named last changes fastest.
Arguments:
- x_points: float32 [8192, 32], P(('groups', 'row')), parts along dimension 0, may hold values from -3 to 3
- y_points: float32 [8192, 32], P(('groups', 'col')), parts along dimension 0, may hold values from -3 to 3
Outputs:
- grad_x: float32 [8192, 32], P(('groups', 'row', 'col')), parts along dimension 0
- grad_y: float32 [8192, 32], P(('groups', 'col', 'row')), parts along dimension 0
The draws below stay inside these ranges and needn't reach their ends.
There are 2 independent parts, one for each index of `groups`. The reference program is written for one: setup_inputs(seed, part) draws one part's arguments, and reference() takes and returns one part's arrays. A program takes and returns all parts, laid end to end along the dimension named above; each array names one. Nothing has to cross between parts.
All inputs are finite; a program needn't handle non-finite values.
Results may differ from the reference program's by a relative error of at most 0.0003.
Values sent between devices are 32-bit elements; how exact they have to be, the bound alone decides.
No kernel may reach another device: no remote copies, remote signals or barrier semaphores. Data moves between devices by JAX's collectives and lax.ppermute only.
A program may use at most 64 MiB of HBM per device.

```python
import math
import jax
import jax.numpy as jnp
from jax import lax

ROWS_DEV = 1024
DIM = 32
ITERS = 5
NPTS = 4096
MPTS = 4096


def paired_points(key, lowest, highest):
    key = jax.random.fold_in(key, 101)
    scale_key = jax.random.fold_in(key, 0)
    base_key = jax.random.fold_in(key, 2)
    small_scales = jnp.exp(jax.random.uniform(scale_key, (MPTS, 1), jnp.float32, math.log(lowest), math.log(highest)))
    scales = small_scales
    base = jax.random.normal(base_key, (MPTS, DIM), jnp.float32) * scales
    return base


def draw_y_points(key, part):
    points = paired_points(key, 0.06, 0.15)
    return jnp.clip(points, -3.0, 3.0)


def draw_x_points(key, part):
    lowest, highest = (0.06, 0.15)
    key = jax.random.fold_in(key, 7)
    scale_key = jax.random.fold_in(key, 0)
    base_key = jax.random.fold_in(key, 2)
    small_scales = jnp.exp(jax.random.uniform(scale_key, (NPTS, 1), jnp.float32, math.log(lowest), math.log(highest)))
    scales = small_scales
    own_points = jax.random.normal(base_key, (NPTS, DIM), jnp.float32) * scales
    points = own_points
    return jnp.clip(points, -3.0, 3.0)


def setup_inputs(seed: int = 0, part: int = 0) -> dict:
    keys = jax.random.split(jax.random.key(seed), 3)
    part_splits = jax.random.split(jax.random.fold_in(keys[2], part), 3)
    return {
        "x_points": draw_x_points(jax.random.fold_in(jax.random.fold_in(keys[2], part), 71), part),
        "y_points": draw_y_points(jax.random.fold_in(jax.random.fold_in(keys[2], part), 71), part),
    }


EPSILON = 0.05
HIGHEST = lax.Precision.HIGHEST


def pair_cost(row_pts, col_pts):
    sq_rows = jnp.sum(row_pts * row_pts, axis=1)
    sq_cols = jnp.sum(col_pts * col_pts, axis=1)
    inner_prod = lax.dot_general(row_pts, col_pts, (((1,), (1,)), ((), ())), precision=HIGHEST, preferred_element_type=jnp.float32)
    return sq_rows[:, None] + sq_cols[None, :] - 2.0 * inner_prod


def adjoint_pass(x_local, y_local, pot_rows, pot_cols, scale, row_weight, col_weight, width):
    count_rows = x_local.shape[0]

    def advance(carry, pieces):
        row_acc, grad_acc = carry
        y_block, pot_block, weight_block = pieces
        weights = scale * jnp.exp((pot_rows[:, None] + pot_block[None, :] - pair_cost(x_local, y_block)) / EPSILON) * row_weight[:, None] * weight_block[None, :]
        row_acc = row_acc + jnp.sum(weights, axis=1)
        grad_acc = grad_acc + jnp.dot(weights, y_block, precision=HIGHEST, preferred_element_type=jnp.float32)
        col_part = jnp.sum(weights, axis=0)
        grad_cols = lax.dot_general(weights, x_local, (((0,), (0,)), ((), ())), precision=HIGHEST, preferred_element_type=jnp.float32)
        return (row_acc, grad_acc), (col_part, grad_cols)

    blocks = y_local.shape[0] // width
    start = (jnp.zeros((count_rows,), jnp.float32), jnp.zeros(x_local.shape, jnp.float32))
    pieces = (y_local.reshape(blocks, width, y_local.shape[1]), pot_cols.reshape(blocks, width), col_weight.reshape(blocks, width))
    (row_acc, grad_acc), (col_part, grad_cols) = lax.scan(advance, start, pieces)
    return row_acc, grad_acc, col_part.reshape(-1), grad_cols.reshape(y_local.shape)


def reference(x_points, y_points):
    log_rows_mass = -math.log(NPTS)
    log_cols_mass = -math.log(MPTS)
    x_blocks = x_points.reshape(NPTS // ROWS_DEV, ROWS_DEV, DIM)
    y_blocks = y_points.reshape(MPTS // ROWS_DEV, ROWS_DEV, DIM)

    def row_update(pot_cols):
        def single(x_block):
            scores = (pot_cols[None, :] - pair_cost(x_block, y_points)) / EPSILON
            maxima = jnp.max(scores, axis=1)
            totals = jnp.sum(jnp.exp(scores - maxima[:, None]), axis=1)
            return EPSILON * log_rows_mass - EPSILON * (maxima + jnp.log(totals))
        return lax.map(single, x_blocks).reshape(NPTS)

    def col_update(pot_rows):
        def single(y_block):
            scores = (pot_rows[:, None] - pair_cost(x_points, y_block)) / EPSILON
            maxima = jnp.max(scores, axis=0)
            totals = jnp.sum(jnp.exp(scores - maxima[None, :]), axis=0)
            return EPSILON * log_cols_mass - EPSILON * (maxima + jnp.log(totals))
        return lax.map(single, y_blocks).reshape(MPTS)

    pot_cols = jnp.zeros((MPTS,), jnp.float32)
    history_rows = []
    history_cols = [pot_cols]
    for level in range(ITERS):
        pot_rows = row_update(pot_cols)
        pot_cols = col_update(pot_rows)
        history_rows.append(pot_rows)
        history_cols.append(pot_cols)

    ones_rows = jnp.ones((NPTS,), jnp.float32)
    ones_cols = jnp.ones((MPTS,), jnp.float32)
    adj_cols = ones_cols
    rows_total = jnp.zeros((NPTS,), jnp.float32)
    cols_total = jnp.zeros((MPTS,), jnp.float32)
    grad_rows_acc = jnp.zeros((NPTS, DIM), jnp.float32)
    grad_cols_acc = jnp.zeros((MPTS, DIM), jnp.float32)
    for level in reversed(range(ITERS)):
        row_part, grad_part, col_part, grad_col_part = adjoint_pass(x_points, y_points, history_rows[level], history_cols[level + 1], float(MPTS), ones_rows, adj_cols, ROWS_DEV)
        rows_total = rows_total + row_part
        cols_total = cols_total + col_part
        grad_rows_acc = grad_rows_acc + grad_part
        grad_cols_acc = grad_cols_acc + grad_col_part
        leading = 1.0 if level == ITERS - 1 else 0.0
        adj_rows = leading - row_part
        row_part, grad_part, col_part, grad_col_part = adjoint_pass(x_points, y_points, history_rows[level], history_cols[level], float(NPTS), adj_rows, ones_cols, ROWS_DEV)
        rows_total = rows_total + row_part
        cols_total = cols_total + col_part
        grad_rows_acc = grad_rows_acc + grad_part
        grad_cols_acc = grad_cols_acc + grad_col_part
        adj_cols = -col_part
    grad_x = 2.0 * (x_points * rows_total[:, None] - grad_rows_acc)
    grad_y = 2.0 * (y_points * cols_total[:, None] - grad_cols_acc)
    return grad_x, grad_y
```

```python
import functools
import math

import jax
import jax.numpy as jnp
from jax import lax
from jax.experimental import pallas as pl
from jax.experimental.pallas import tpu as pltpu
from jax.sharding import PartitionSpec as P

ITERS = 5
EPSILON = 0.05
SCALE = 1.0 / (EPSILON * math.log(2.0))
DEPTH = 256
CHUNK = 256
F32 = jnp.float32
BF16 = jnp.bfloat16
VMEM_LIMIT = 48 * 1024 * 1024


def split3(v):
    high = v.astype(BF16).astype(F32)
    rest = v - high
    mid = rest.astype(BF16).astype(F32)
    low = (rest - mid).astype(BF16).astype(F32)
    return high, mid, low


def vmem(count):
    return [pl.BlockSpec(memory_space=pltpu.VMEM)] * count


def call(body, outs, count, scratch=()):
    return pl.pallas_call(
        body,
        out_shape=outs,
        in_specs=vmem(count),
        out_specs=vmem(len(outs)),
        scratch_shapes=list(scratch),
        compiler_params=pltpu.CompilerParams(vmem_limit_bytes=VMEM_LIMIT),
    )


def shape(dims, dtype=F32):
    return jax.ShapeDtypeStruct(dims, dtype)


def factors(points, order):
    parts = split3(points)
    width = points.shape[1]
    blocks = [parts[o] for o in order]
    zero16 = jnp.zeros((16, width), F32)
    tail = jnp.zeros((DEPTH - 144 - 2 * points.shape[0], width), F32)
    return jnp.concatenate(blocks[:4] + [zero16] + blocks[4:] + [tail], axis=0)


X_ORDER = (0, 0, 1, 0, 2, 1)
Y_ORDER = (0, 1, 0, 2, 0, 1)


def prepare_body(x_ref, y_ref, ax0, ax1, ay0, ay1, bx, by, start_ref):
    x = x_ref[...]
    y = y_ref[...]
    xf = factors(x * (2.0 * SCALE), X_ORDER)
    yf = factors(y, Y_ORDER)
    for factor, left0, left1, right in ((xf, ax0, ax1, bx), (yf, ay0, ay1, by)):
        right[...] = factor.astype(BF16)
        turned = factor.T
        left0[...] = turned[:, :128].astype(BF16)
        left1[...] = turned[:, 128:]
    start_ref[...] = -SCALE * jnp.sum(y * y, axis=0, keepdims=True)


def left_factor(left0, left1, pot, adj=None):
    width = pot.shape[1]
    high, mid, low = split3(pot)
    one = jnp.ones((1, width), F32)
    rows = [high, mid, low, one, one, one, jnp.zeros_like(one)]
    rows.append(jnp.zeros_like(one) if adj is None else adj)
    rows.append(jnp.zeros((120, width), F32))
    turned = jnp.concatenate(rows, axis=0).T
    column = None
    if adj is not None:
        column = turned[:, 7:8]
        lane = lax.broadcasted_iota(jnp.int32, turned.shape, 1)
        turned = jnp.where(lane == 7, 0.0, turned)
    return jnp.concatenate([left0[...], (left1[...] + turned).astype(BF16)], axis=1), column


def right_rows(pot):
    width = pot.shape[1]
    one = jnp.ones((3, width), F32)
    high, mid, low = split3(pot)
    return jnp.concatenate([one, high, mid, low, jnp.zeros((10, width), F32)], axis=0).astype(BF16)


def right_chunk(right, rows, at, wide):
    return jnp.concatenate(
        [right[0:128, at : at + wide], rows[:, at : at + wide], right[144:DEPTH, at : at + wide]], axis=0
    )


def matmul(a, b):
    return jnp.dot(a, b, preferred_element_type=F32)


def partial_lse(left, right, out):
    width = right.shape[1]
    rows = right_rows(jnp.zeros((1, width), F32))
    wide = min(CHUNK, width)
    for at in range(0, width, wide):
        scores = matmul(left, right_chunk(right, rows, at, wide))
        top = jnp.max(scores, axis=0, keepdims=True)
        out[0:1, at : at + wide] = top
        out[1:2, at : at + wide] = jnp.sum(jnp.exp2(scores - top), axis=0, keepdims=True)


def join_lse(parts, log_mass):
    tops = [p[0:1, :] for p in parts]
    top = functools.reduce(jnp.maximum, tops)
    total = sum(p[1:2, :] * jnp.exp2(t - top) for p, t in zip(parts, tops))
    return log_mass - (top + jnp.log2(total))


def first_body(left0, left1, right, pot, out):
    left, unused = left_factor(left0, left1, pot[...])
    partial_lse(left, right, out)


def forward_body(log_mass, *refs):
    left0, left1, right = refs[:3]
    parts, (pot_out, out) = refs[3:-2], refs[-2:]
    pot = join_lse([p[...] for p in parts], log_mass)
    pot_out[...] = pot
    left, unused = left_factor(left0, left1, pot)
    partial_lse(left, right, out)


def weighted_sums(left, column, right, rows, out):
    width = right.shape[1]
    wide = min(CHUNK, width)
    for at in range(0, width, wide):
        scores = matmul(left, right_chunk(right, rows, at, wide))
        out[:, at : at + wide] = jnp.sum(jnp.exp2(scores) * column, axis=0, keepdims=True)


def turn_body(log_mass, log_scale, left0, left1, right, pot_right, *refs):
    parts, (pot_out, out) = refs[:-2], refs[-2:]
    pot = join_lse([p[...] for p in parts], log_mass)
    pot_out[...] = pot
    left, column = left_factor(left0, left1, pot, jnp.ones_like(pot))
    weighted_sums(left, column, right, right_rows(pot_right[...] + log_scale), out)


def backward_body(leading, log_scale, left0, left1, right, pot_left, pot_right, *refs):
    parts, (adj_out, out) = refs[:-2], refs[-2:]
    adj = leading - sum(p[...] for p in parts)
    adj_out[...] = adj
    left, column = left_factor(left0, left1, pot_left[...], adj)
    weighted_sums(left, column, right, right_rows(pot_right[...] + log_scale), out)


def gradient_body(dim, log_cols, log_rows, col_axis, row_axis, ax0, ax1, by, x_ref, y_ref, *refs):
    pots_rows = refs[:ITERS]
    pots_cols = refs[ITERS : 2 * ITERS + 1]
    adjs_rows = refs[2 * ITERS + 1 : 3 * ITERS + 1]
    adjs_cols = refs[3 * ITERS + 1 : 4 * ITERS + 1]
    n_col = lax.axis_size(col_axis)
    n_row = lax.axis_size(row_axis)
    outs = refs[4 * ITERS + 1 :]
    outs_x, outs_y = outs[:n_col], outs[n_col : n_col + n_row]
    cols_rows, x_parts, y_parts, gx, gy = outs[n_col + n_row :]
    count_rows, count_cols = x_ref.shape[1], y_ref.shape[1]

    stack = [p[...] + log_cols for p in pots_rows] + [a[...] for a in adjs_rows]
    stack.append(jnp.zeros((128 - len(stack), count_rows), F32))
    cols_rows[...] = jnp.concatenate(stack, axis=0).T

    x = x_ref[...]
    y = y_ref[...]
    one = jnp.ones((1, count_cols), F32)
    pad = jnp.zeros((31, count_cols), F32)
    y_parts[...] = jnp.concatenate(list(split3(y)) + [one, pad], axis=0).T.astype(BF16)
    one = jnp.ones((1, count_rows), F32)
    pad = jnp.zeros((31, count_rows), F32)
    x_parts[...] = jnp.concatenate(list(split3(x)) + [one, pad], axis=0).astype(BF16)
    gy[...] = jnp.zeros_like(gy)

    high = 128

    def block(step, carry):
        at = pl.ds(pl.multiple_of(step * high, high), high)
        left = jnp.concatenate([ax0[at, :], ax1[at, :].astype(BF16)], axis=1)
        inner = matmul(left, by[...])
        columns = cols_rows[at, :]
        total = jnp.zeros_like(inner)
        for k in range(ITERS):
            base = inner + columns[:, k : k + 1]
            total += jnp.exp2(base + pots_cols[k + 1][...]) * adjs_cols[k][...]
            total += jnp.exp2(base + (pots_cols[k][...] + (log_rows - log_cols))) * columns[:, ITERS + k : ITERS + k + 1]
        upper = total.astype(BF16)
        lower = (total - upper.astype(F32)).astype(BF16)
        gx[at, :] = matmul(upper, y_parts[...]) + matmul(lower, y_parts[...])
        gy[...] += matmul(x_parts[:, at], upper) + matmul(x_parts[:, at], lower)
        return carry

    lax.fori_loop(0, count_rows // high, block, 0)

    def finish(points, sums):
        mixed = sums[0:dim] + sums[dim : 2 * dim] + sums[2 * dim : 3 * dim]
        return 2.0 * (points * sums[3 * dim : 3 * dim + 1] - mixed)

    for value, outs_, count, axis, held in (
        (finish(x, gx[...].T), outs_x, n_col, col_axis, gx),
        (finish(y, gy[...]), outs_y, n_row, row_axis, gy),
    ):
        share = value.shape[1] // count
        pieces = [value[:, p * share : (p + 1) * share] for p in range(count)]
        me = lax.axis_index(axis)
        for s in range(count):
            target = lax.rem(me + s, count)
            chosen = pieces[0]
            for p in range(1, count):
                chosen = jnp.where(target == p, pieces[p], chosen)
            outs_[s][...] = chosen


def exchange(value, axis):
    size = lax.axis_size(axis)
    return [value] + [
        lax.ppermute(value, axis, [(d, (d + s) % size) for d in range(size)]) for s in range(1, size)
    ]


def scatter(pieces, axis):
    size = lax.axis_size(axis)
    got = [pieces[0]] + [
        lax.ppermute(pieces[s], axis, [(d, (d + s) % size) for d in range(size)]) for s in range(1, size)
    ]
    return sum(got[1:], got[0])


def on_device(x_points, y_points):
    x = x_points.T
    y = y_points.T
    dim, count_rows = x.shape
    count_cols = y.shape[1]
    n_row, n_col = lax.axis_size("row"), lax.axis_size("col")
    log_rows = math.log2(count_rows * n_row)
    log_cols = math.log2(count_cols * n_col)
    row, col = (1, count_rows), (1, count_cols)

    ax0, ax1, ay0, ay1, bx, by, start = call(
        prepare_body,
        [
            shape((count_rows, 128), BF16),
            shape((count_rows, 128)),
            shape((count_cols, 128), BF16),
            shape((count_cols, 128)),
            shape((DEPTH, count_rows), BF16),
            shape((DEPTH, count_cols), BF16),
            shape(col),
        ],
        2,
    )(x, y)

    pots_rows, pots_cols = [], [start]
    (part,) = call(first_body, [shape((2, count_rows))], 4)(ay0, ay1, bx, start)
    for k in range(ITERS):
        got = exchange(part, "col")
        pot, part = call(
            functools.partial(forward_body, -log_rows), [shape(row), shape((2, count_cols))], 3 + n_col
        )(ax0, ax1, by, *got)
        pots_rows.append(pot)
        got = exchange(part, "row")
        if k < ITERS - 1:
            pot, part = call(
                functools.partial(forward_body, -log_cols), [shape(col), shape((2, count_rows))], 3 + n_row
            )(ay0, ay1, bx, *got)
            pots_cols.append(pot)
    pot, part = call(
        functools.partial(turn_body, -log_cols, log_cols), [shape(col), shape(row)], 4 + n_row
    )(ay0, ay1, bx, pots_rows[-1], *got)
    pots_cols.append(pot)

    adjs_rows, adjs_cols = [None] * ITERS, [None] * ITERS
    adjs_cols[-1] = jnp.ones(col, F32)
    for k in reversed(range(ITERS)):
        leading = 1.0 if k == ITERS - 1 else 0.0
        got = exchange(part, "col")
        if k == 0:
            break
        adjs_rows[k], part = call(
            functools.partial(backward_body, leading, log_rows), [shape(row), shape(col)], 5 + n_col
        )(ax0, ax1, by, pots_rows[k], pots_cols[k], *got)
        got = exchange(part, "row")
        adjs_cols[k - 1], part = call(
            functools.partial(backward_body, 0.0, log_cols), [shape(col), shape(row)], 5 + n_row
        )(ay0, ay1, bx, pots_cols[k], pots_rows[k - 1], *got)
    adjs_rows[0] = -sum(got[1:], got[0]) if ITERS > 1 else 1.0 - sum(got[1:], got[0])

    share_x, share_y = count_rows // n_col, count_cols // n_row
    outs = call(
        functools.partial(gradient_body, dim, log_cols, log_rows, "col", "row"),
        [shape((dim, share_x))] * n_col + [shape((dim, share_y))] * n_row,
        5 + 4 * ITERS + 1,
        [
            pltpu.VMEM((count_rows, 128), F32),
            pltpu.VMEM((128, count_rows), BF16),
            pltpu.VMEM((count_cols, 128), BF16),
            pltpu.VMEM((count_rows, 128), F32),
            pltpu.VMEM((128, count_cols), F32),
        ],
    )(ax0, ax1, by, x, y, *pots_rows, *pots_cols, *adjs_rows, *adjs_cols)
    grad_x = scatter(outs[:n_col], "col")
    grad_y = scatter(outs[n_col:], "row")
    return (grad_x.T, grad_y.T)


def solution(mesh):
    in_specs = (P(("groups", "row"), None), P(("groups", "col"), None))
    out_specs = (P(("groups", "row", "col"), None), P(("groups", "col", "row"), None))
    return jax.shard_map(
        on_device, mesh=mesh, in_specs=in_specs, out_specs=out_specs, check_vma=False
    )
```

```python
import functools
import math

import jax
import jax.numpy as jnp
from jax import lax
from jax.experimental import pallas as pl
from jax.experimental.pallas import tpu as pltpu
from jax.sharding import PartitionSpec as P

ITERS = 5
EPSILON = 0.05
SCALE = 1.0 / (EPSILON * math.log(2.0))
DEPTH = 256
CHUNK = 256
F32 = jnp.float32
BF16 = jnp.bfloat16
VMEM_LIMIT = 48 * 1024 * 1024


def split3(v):
    high = v.astype(BF16).astype(F32)
    rest = v - high
    mid = rest.astype(BF16).astype(F32)
    low = (rest - mid).astype(BF16).astype(F32)
    return high, mid, low


def vmem(count):
    return [pl.BlockSpec(memory_space=pltpu.VMEM)] * count


def call(body, outs, count, scratch=()):
    return pl.pallas_call(
        body,
        out_shape=outs,
        in_specs=vmem(count),
        out_specs=vmem(len(outs)),
        scratch_shapes=list(scratch),
        compiler_params=pltpu.CompilerParams(vmem_limit_bytes=VMEM_LIMIT),
    )


def shape(dims, dtype=F32):
    return jax.ShapeDtypeStruct(dims, dtype)


def factors(points, order):
    parts = split3(points)
    width = points.shape[1]
    blocks = [parts[o] for o in order]
    zero16 = jnp.zeros((16, width), F32)
    tail = jnp.zeros((DEPTH - 144 - 2 * points.shape[0], width), F32)
    return jnp.concatenate(blocks[:4] + [zero16] + blocks[4:] + [tail], axis=0)


X_ORDER = (0, 0, 1, 0, 2, 1)
Y_ORDER = (0, 1, 0, 2, 0, 1)


def prepare_body(x_hbm, y_hbm, ax0, ax1, ay0, ay1, bx, by, start_ref, out, x_ref, y_ref, sems):
    copies = [
        pltpu.make_async_copy(x_hbm, x_ref, sems.at[0]),
        pltpu.make_async_copy(y_hbm, y_ref, sems.at[1]),
    ]
    for copy in copies:
        copy.start()
    for copy in copies:
        copy.wait()
    x = x_ref[...]
    y = y_ref[...]
    xf = factors(x * (2.0 * SCALE), X_ORDER)
    yf = factors(y, Y_ORDER)
    for factor, left0, left1, right in ((xf, ax0, ax1, bx), (yf, ay0, ay1, by)):
        right[...] = factor.astype(BF16)
        turned = factor.T
        left0[...] = turned[:, :128].astype(BF16)
        left1[...] = turned[:, 128:]
    start = -SCALE * jnp.sum(y * y, axis=0, keepdims=True)
    start_ref[...] = start
    left, unused = left_factor(ay0, ay1, start)
    partial_lse(left, bx, out)


def left_factor(left0, left1, pot, adj=None):
    width = pot.shape[1]
    high, mid, low = split3(pot)
    one = jnp.ones((1, width), F32)
    rows = [high, mid, low, one, one, one, jnp.zeros_like(one)]
    rows.append(jnp.zeros_like(one) if adj is None else adj)
    rows.append(jnp.zeros((120, width), F32))
    turned = jnp.concatenate(rows, axis=0).T
    column = None
    if adj is not None:
        column = turned[:, 7:8]
        lane = lax.broadcasted_iota(jnp.int32, turned.shape, 1)
        turned = jnp.where(lane == 7, 0.0, turned)
    return jnp.concatenate([left0[...], (left1[...] + turned).astype(BF16)], axis=1), column


def right_rows(pot):
    width = pot.shape[1]
    one = jnp.ones((3, width), F32)
    high, mid, low = split3(pot)
    return jnp.concatenate([one, high, mid, low, jnp.zeros((10, width), F32)], axis=0).astype(BF16)


def right_chunk(right, rows, at, wide):
    return jnp.concatenate(
        [right[0:128, at : at + wide], rows[:, at : at + wide], right[144:DEPTH, at : at + wide]], axis=0
    )


def matmul(a, b):
    return jnp.dot(a, b, preferred_element_type=F32)


def send(out, at, wide, value):
    for d in range(out.shape[0]):
        out[d, :, at : at + wide] = value


def partial_lse(left, right, out):
    width = right.shape[1]
    rows = right_rows(jnp.zeros((1, width), F32))
    wide = min(CHUNK, width)
    for at in range(0, width, wide):
        scores = matmul(left, right_chunk(right, rows, at, wide))
        top = jnp.max(scores, axis=0, keepdims=True)
        total = jnp.sum(jnp.exp2(scores - top), axis=0, keepdims=True)
        send(out, at, wide, top + jnp.log2(total))


def join_lse(got, log_mass):
    parts = [got[d] for d in range(got.shape[0])]
    top = functools.reduce(jnp.maximum, parts)
    total = sum(jnp.exp2(p - top) for p in parts)
    return log_mass - (top + jnp.log2(total))


def join_sum(got):
    return sum(got[d] for d in range(got.shape[0]))


def forward_body(log_mass, left0, left1, right, got, pot_out, out):
    pot = join_lse(got, log_mass)
    pot_out[...] = pot
    left, unused = left_factor(left0, left1, pot)
    partial_lse(left, right, out)


def weighted_sums(left, column, right, rows, out):
    width = right.shape[1]
    wide = min(CHUNK, width)
    for at in range(0, width, wide):
        scores = matmul(left, right_chunk(right, rows, at, wide))
        send(out, at, wide, jnp.sum(jnp.exp2(scores) * column, axis=0, keepdims=True))


def turn_body(log_mass, log_scale, left0, left1, right, pot_right, got, pot_out, out):
    pot = join_lse(got, log_mass)
    pot_out[...] = pot
    left, column = left_factor(left0, left1, pot, jnp.ones_like(pot))
    weighted_sums(left, column, right, right_rows(pot_right[...] + log_scale), out)


def backward_body(leading, log_scale, left0, left1, right, pot_left, pot_right, got, adj_out, out):
    adj = leading - join_sum(got)
    adj_out[...] = adj
    left, column = left_factor(left0, left1, pot_left[...], adj)
    weighted_sums(left, column, right, right_rows(pot_right[...] + log_scale), out)


SPREAD = 30.0
STRIP = 256


def gradient_body(dim, log_cols, log_rows, ax0, ax1, by, x_ref, y_ref, *refs):
    pots_rows = refs[:ITERS]
    pots_cols = refs[ITERS : 2 * ITERS + 1]
    adjs_rows = refs[2 * ITERS + 1 : 3 * ITERS]
    adjs_cols = refs[3 * ITERS : 4 * ITERS - 1]
    got, out_x, out_y, cols_rows, x_parts, y_parts, gx, gy, left_e, left_r, right_r = refs[4 * ITERS - 1 :]
    count_rows, count_cols = x_ref.shape[1], y_ref.shape[1]
    us = [p[...] for p in pots_rows]
    vs = [p[...] for p in pots_cols]
    first = (1.0 if ITERS == 1 else 0.0) - join_sum(got)
    adjs_rows = [first] + [a[...] for a in adjs_rows]
    adjs_cols = [a[...] for a in adjs_cols] + [jnp.ones((1, count_cols), F32)]
    shift = log_rows - log_cols

    x = x_ref[...]
    y = y_ref[...]
    one = jnp.ones((1, count_cols), F32)
    pad = jnp.zeros((31, count_cols), F32)
    y_parts[...] = jnp.concatenate(list(split3(y)) + [one, pad], axis=0).T.astype(BF16)
    one = jnp.ones((1, count_rows), F32)
    pad = jnp.zeros((31, count_rows), F32)
    x_parts[...] = jnp.concatenate(list(split3(x)) + [one, pad], axis=0).astype(BF16)
    gy[...] = jnp.zeros_like(gy)

    far_u = functools.reduce(jnp.maximum, [jnp.abs(u - us[-1]) for u in us])
    far_v = functools.reduce(jnp.maximum, [jnp.abs(v - vs[-1]) for v in vs])
    near = jnp.maximum(jnp.max(far_u), jnp.max(far_v)) < SPREAD

    def add_strip(at, total):
        upper = total.astype(BF16)
        lower = (total - upper.astype(F32)).astype(BF16)
        gx[at, :] = matmul(upper, y_parts[...]) + matmul(lower, y_parts[...])
        gy[...] += matmul(x_parts[:, at], upper) + matmul(x_parts[:, at], lower)

    @pl.when(near)
    def factored():
        alpha = [jnp.exp2(u - us[-1]) for u in us]
        beta = [jnp.exp2(v - vs[-1]) for v in vs]
        p_rows = alpha + [a * adj for a, adj in zip(alpha, adjs_rows)]
        q_rows = [b * adj for b, adj in zip(beta[1:], adjs_cols)] + [b * 2.0**shift for b in beta[:-1]]
        fill = 16 - 2 * ITERS
        p_split = split3(jnp.concatenate(p_rows + [jnp.zeros((fill, count_rows), F32)], axis=0))
        q_split = split3(jnp.concatenate(q_rows + [jnp.zeros((fill, count_cols), F32)], axis=0))
        tail = [jnp.zeros((32, count_rows), F32)]
        left_r[...] = jnp.concatenate([p_split[o] for o in X_ORDER] + tail, axis=0).T.astype(BF16)
        tail = [jnp.zeros((32, count_cols), F32)]
        right_r[...] = jnp.concatenate([q_split[o] for o in Y_ORDER] + tail, axis=0).astype(BF16)
        left, unused = left_factor(ax0, ax1, us[-1] + log_cols)
        left_e[...] = left
        right = right_chunk(by, right_rows(vs[-1]), 0, count_cols)
        strip = min(STRIP, count_rows)
        for step in range(count_rows // strip):
            at = pl.ds(step * strip, strip)
            total = jnp.exp2(matmul(left_e[at, :], right)) * matmul(left_r[at, :], right_r[...])
            add_strip(at, total)

    @pl.when(jnp.logical_not(near))
    def separate():
        stack = [u + log_cols for u in us] + adjs_rows
        stack.append(jnp.zeros((128 - len(stack), count_rows), F32))
        cols_rows[...] = jnp.concatenate(stack, axis=0).T
        strip = 128

        def block(step, carry):
            at = pl.ds(pl.multiple_of(step * strip, strip), strip)
            left = jnp.concatenate([ax0[at, :], ax1[at, :].astype(BF16)], axis=1)
            inner = matmul(left, by[...])
            columns = cols_rows[at, :]
            total = jnp.zeros_like(inner)
            for k in range(ITERS):
                base = inner + columns[:, k : k + 1]
                total += jnp.exp2(base + vs[k + 1]) * adjs_cols[k]
                total += jnp.exp2(base + (vs[k] + shift)) * columns[:, ITERS + k : ITERS + k + 1]
            add_strip(at, total)
            return carry

        lax.fori_loop(0, count_rows // strip, block, 0)

    def finish(points, sums):
        mixed = sums[0:dim] + sums[dim : 2 * dim] + sums[2 * dim : 3 * dim]
        return 2.0 * (points * sums[3 * dim : 3 * dim + 1] - mixed)

    for value, out in ((finish(x, gx[...].T), out_x), (finish(y, gy[...]), out_y)):
        share = out.shape[2]
        for p in range(out.shape[0]):
            out[p] = value[:, p * share : (p + 1) * share]


def exchange(value, axis):
    return lax.all_to_all(value, axis, 0, 0, tiled=True)


def on_device(x_points, y_points):
    x = x_points.T
    y = y_points.T
    dim, count_rows = x.shape
    count_cols = y.shape[1]
    n_row, n_col = lax.axis_size("row"), lax.axis_size("col")
    log_rows = math.log2(count_rows * n_row)
    log_cols = math.log2(count_cols * n_col)
    row, col = (1, count_rows), (1, count_cols)
    to_col, to_row = shape((n_col,) + row), shape((n_row,) + col)

    ax0, ax1, ay0, ay1, bx, by, start, part = pl.pallas_call(
        prepare_body,
        out_shape=[
            shape((count_rows, 128), BF16),
            shape((count_rows, 128)),
            shape((count_cols, 128), BF16),
            shape((count_cols, 128)),
            shape((DEPTH, count_rows), BF16),
            shape((DEPTH, count_cols), BF16),
            shape(col),
            to_col,
        ],
        in_specs=[pl.BlockSpec(memory_space=pl.ANY)] * 2,
        out_specs=vmem(8),
        scratch_shapes=[pltpu.VMEM(x.shape, F32), pltpu.VMEM(y.shape, F32), pltpu.SemaphoreType.DMA((2,))],
        compiler_params=pltpu.CompilerParams(vmem_limit_bytes=VMEM_LIMIT),
    )(x, y)

    pots_rows, pots_cols = [], [start]
    for k in range(ITERS):
        got = exchange(part, "col")
        pot, part = call(functools.partial(forward_body, -log_rows), [shape(row), to_row], 4)(ax0, ax1, by, got)
        pots_rows.append(pot)
        got = exchange(part, "row")
        if k < ITERS - 1:
            pot, part = call(functools.partial(forward_body, -log_cols), [shape(col), to_col], 4)(
                ay0, ay1, bx, got
            )
            pots_cols.append(pot)
    pot, part = call(functools.partial(turn_body, -log_cols, log_cols), [shape(col), to_col], 5)(
        ay0, ay1, bx, pots_rows[-1], got
    )
    pots_cols.append(pot)

    adjs_rows, adjs_cols = [], []
    for k in reversed(range(1, ITERS)):
        leading = 1.0 if k == ITERS - 1 else 0.0
        got = exchange(part, "col")
        adj, part = call(functools.partial(backward_body, leading, log_rows), [shape(row), to_row], 6)(
            ax0, ax1, by, pots_rows[k], pots_cols[k], got
        )
        adjs_rows.insert(0, adj)
        got = exchange(part, "row")
        adj, part = call(functools.partial(backward_body, 0.0, log_cols), [shape(col), to_col], 6)(
            ay0, ay1, bx, pots_cols[k], pots_rows[k - 1], got
        )
        adjs_cols.insert(0, adj)
    got = exchange(part, "col")

    out_x, out_y = call(
        functools.partial(gradient_body, dim, log_cols, log_rows),
        [shape((n_col, dim, count_rows // n_col)), shape((n_row, dim, count_cols // n_row))],
        5 + 4 * ITERS,
        [
            pltpu.VMEM((count_rows, 128), F32),
            pltpu.VMEM((128, count_rows), BF16),
            pltpu.VMEM((count_cols, 128), BF16),
            pltpu.VMEM((count_rows, 128), F32),
            pltpu.VMEM((128, count_cols), F32),
            pltpu.VMEM((count_rows, DEPTH), BF16),
            pltpu.VMEM((count_rows, 128), BF16),
            pltpu.VMEM((128, count_cols), BF16),
        ],
    )(ax0, ax1, by, x, y, *pots_rows, *pots_cols, *adjs_rows, *adjs_cols, got)
    grad_x = jnp.sum(exchange(out_x, "col"), axis=0)
    grad_y = jnp.sum(exchange(out_y, "row"), axis=0)
    return (grad_x.T, grad_y.T)


def solution(mesh):
    in_specs = (P(("groups", "row"), None), P(("groups", "col"), None))
    out_specs = (P(("groups", "row", "col"), None), P(("groups", "col", "row"), None))
    return jax.shard_map(
        on_device, mesh=mesh, in_specs=in_specs, out_specs=out_specs, check_vma=False
    )
```

```python
import functools
import math

import jax
import jax.numpy as jnp
from jax import lax
from jax.experimental import pallas as pl
from jax.experimental.pallas import tpu as pltpu
from jax.sharding import PartitionSpec as P

ITERS = 5
EPSILON = 0.05
SCALE = 1.0 / (EPSILON * math.log(2.0))
DEPTH = 256
CHUNK = 256
F32 = jnp.float32
BF16 = jnp.bfloat16
VMEM_LIMIT = 48 * 1024 * 1024


def split3(v):
    high = v.astype(BF16).astype(F32)
    rest = v - high
    mid = rest.astype(BF16).astype(F32)
    low = (rest - mid).astype(BF16).astype(F32)
    return high, mid, low


def vmem(count):
    return [pl.BlockSpec(memory_space=pltpu.VMEM)] * count


def call(body, outs, count, scratch=()):
    return pl.pallas_call(
        body,
        out_shape=outs,
        in_specs=vmem(count),
        out_specs=vmem(len(outs)),
        scratch_shapes=list(scratch),
        compiler_params=pltpu.CompilerParams(vmem_limit_bytes=VMEM_LIMIT),
    )


def shape(dims, dtype=F32):
    return jax.ShapeDtypeStruct(dims, dtype)


def factors(points, order):
    parts = split3(points)
    width = points.shape[1]
    blocks = [parts[o] for o in order]
    zero16 = jnp.zeros((16, width), F32)
    tail = jnp.zeros((DEPTH - 144 - 2 * points.shape[0], width), F32)
    return jnp.concatenate(blocks[:4] + [zero16] + blocks[4:] + [tail], axis=0)


X_ORDER = (0, 0, 1, 0, 2, 1)
Y_ORDER = (0, 1, 0, 2, 0, 1)


def prepare_body(x_hbm, y_hbm, ax0, ax1, ay0, ay1, bx, by, start_ref, out, x_ref, y_ref, sems):
    copies = [
        pltpu.make_async_copy(x_hbm, x_ref, sems.at[0]),
        pltpu.make_async_copy(y_hbm, y_ref, sems.at[1]),
    ]
    for copy in copies:
        copy.start()
    for copy in copies:
        copy.wait()
    x = x_ref[...]
    y = y_ref[...]
    xf = factors(x * (2.0 * SCALE), X_ORDER)
    yf = factors(y, Y_ORDER)
    for factor, left0, left1, right in ((xf, ax0, ax1, bx), (yf, ay0, ay1, by)):
        right[...] = factor.astype(BF16)
        turned = factor.T
        left0[...] = turned[:, :128].astype(BF16)
        left1[...] = turned[:, 128:]
    start = -SCALE * jnp.sum(y * y, axis=0, keepdims=True)
    start_ref[...] = start
    left, unused = left_factor(ay0, ay1, start)
    partial_lse(left, bx, out)


def left_factor(left0, left1, pot, adj=None):
    width = pot.shape[1]
    high, mid, low = split3(pot)
    one = jnp.ones((1, width), F32)
    rows = [high, mid, low, one, one, one, jnp.zeros_like(one)]
    rows.append(jnp.zeros_like(one) if adj is None else adj)
    rows.append(jnp.zeros((120, width), F32))
    turned = jnp.concatenate(rows, axis=0).T
    column = None
    if adj is not None:
        column = turned[:, 7:8]
        lane = lax.broadcasted_iota(jnp.int32, turned.shape, 1)
        turned = jnp.where(lane == 7, 0.0, turned)
    return jnp.concatenate([left0[...], (left1[...] + turned).astype(BF16)], axis=1), column


def right_rows(pot):
    width = pot.shape[1]
    one = jnp.ones((3, width), F32)
    high, mid, low = split3(pot)
    return jnp.concatenate([one, high, mid, low, jnp.zeros((10, width), F32)], axis=0).astype(BF16)


def right_chunk(right, rows, at, wide):
    return jnp.concatenate(
        [right[0:128, at : at + wide], rows[:, at : at + wide], right[144:DEPTH, at : at + wide]], axis=0
    )


def matmul(a, b):
    return jnp.dot(a, b, preferred_element_type=F32)


def partial_lse(left, right, out):
    width = right.shape[1]
    rows = right_rows(jnp.zeros((1, width), F32))
    wide = min(CHUNK, width)
    for at in range(0, width, wide):
        scores = matmul(left, right_chunk(right, rows, at, wide))
        top = jnp.max(scores, axis=0, keepdims=True)
        total = jnp.sum(jnp.exp2(scores - top), axis=0, keepdims=True)
        out[:, at : at + wide] = top + jnp.log2(total)


def join_lse(parts):
    parts = [p[...] for p in parts]
    top = functools.reduce(jnp.maximum, parts)
    return top + jnp.log2(sum(jnp.exp2(p - top) for p in parts))


def join_sum(parts):
    return sum(p[...] for p in parts)


def join_body(join, *refs):
    refs[-1][...] = join(refs[:-1])


def forward_body(log_mass, left0, left1, right, *refs):
    got, (pot_out, out) = refs[:-2], refs[-2:]
    pot = log_mass - join_lse(got)
    pot_out[...] = pot
    left, unused = left_factor(left0, left1, pot)
    partial_lse(left, right, out)


def weighted_sums(left, column, right, rows, out):
    width = right.shape[1]
    wide = min(CHUNK, width)
    for at in range(0, width, wide):
        scores = matmul(left, right_chunk(right, rows, at, wide))
        out[:, at : at + wide] = jnp.sum(jnp.exp2(scores) * column, axis=0, keepdims=True)


def turn_body(log_mass, log_scale, left0, left1, right, pot_right, *refs):
    got, (pot_out, out) = refs[:-2], refs[-2:]
    pot = log_mass - join_lse(got)
    pot_out[...] = pot
    left, column = left_factor(left0, left1, pot, jnp.ones_like(pot))
    weighted_sums(left, column, right, right_rows(pot_right[...] + log_scale), out)


def backward_body(leading, log_scale, left0, left1, right, pot_left, pot_right, *refs):
    got, (adj_out, out) = refs[:-2], refs[-2:]
    adj = leading - join_sum(got)
    adj_out[...] = adj
    left, column = left_factor(left0, left1, pot_left[...], adj)
    weighted_sums(left, column, right, right_rows(pot_right[...] + log_scale), out)


SPREAD = 30.0
STRIP = 256


def gradient_body(dim, log_cols, log_rows, n_got, n_col, n_row, ax0, ax1, by, x_ref, y_ref, *refs):
    pots_rows = refs[:ITERS]
    pots_cols = refs[ITERS : 2 * ITERS + 1]
    adjs_rows = refs[2 * ITERS + 1 : 3 * ITERS]
    adjs_cols = refs[3 * ITERS : 4 * ITERS - 1]
    refs = refs[4 * ITERS - 1 :]
    got, refs = refs[:n_got], refs[n_got:]
    outs_x, outs_y = refs[:n_col], refs[n_col : n_col + n_row]
    cols_rows, x_parts, y_parts, gx, gy, left_e, left_r, right_r, all_x, all_y = refs[n_col + n_row :]
    count_rows, count_cols = x_ref.shape[1], y_ref.shape[1]
    us = [p[...] for p in pots_rows]
    vs = [p[...] for p in pots_cols]
    first = (1.0 if ITERS == 1 else 0.0) - join_sum(got)
    adjs_rows = [first] + [a[...] for a in adjs_rows]
    adjs_cols = [a[...] for a in adjs_cols] + [jnp.ones((1, count_cols), F32)]
    shift = log_rows - log_cols

    x = x_ref[...]
    y = y_ref[...]
    one = jnp.ones((1, count_cols), F32)
    pad = jnp.zeros((31, count_cols), F32)
    y_parts[...] = jnp.concatenate(list(split3(y)) + [one, pad], axis=0).T.astype(BF16)
    one = jnp.ones((1, count_rows), F32)
    pad = jnp.zeros((31, count_rows), F32)
    x_parts[...] = jnp.concatenate(list(split3(x)) + [one, pad], axis=0).astype(BF16)
    gy[...] = jnp.zeros_like(gy)

    far_u = functools.reduce(jnp.maximum, [jnp.abs(u - us[-1]) for u in us])
    far_v = functools.reduce(jnp.maximum, [jnp.abs(v - vs[-1]) for v in vs])
    near = jnp.maximum(jnp.max(far_u), jnp.max(far_v)) < SPREAD

    def add_strip(at, total):
        upper = total.astype(BF16)
        lower = (total - upper.astype(F32)).astype(BF16)
        gx[at, :] = matmul(upper, y_parts[...]) + matmul(lower, y_parts[...])
        gy[...] += matmul(x_parts[:, at], upper) + matmul(x_parts[:, at], lower)

    @pl.when(near)
    def factored():
        alpha = [jnp.exp2(u - us[-1]) for u in us]
        beta = [jnp.exp2(v - vs[-1]) for v in vs]
        p_rows = alpha + [a * adj for a, adj in zip(alpha, adjs_rows)]
        q_rows = [b * adj for b, adj in zip(beta[1:], adjs_cols)] + [b * 2.0**shift for b in beta[:-1]]
        fill = 16 - 2 * ITERS
        p_split = split3(jnp.concatenate(p_rows + [jnp.zeros((fill, count_rows), F32)], axis=0))
        q_split = split3(jnp.concatenate(q_rows + [jnp.zeros((fill, count_cols), F32)], axis=0))
        tail = [jnp.zeros((32, count_rows), F32)]
        left_r[...] = jnp.concatenate([p_split[o] for o in X_ORDER] + tail, axis=0).T.astype(BF16)
        tail = [jnp.zeros((32, count_cols), F32)]
        right_r[...] = jnp.concatenate([q_split[o] for o in Y_ORDER] + tail, axis=0).astype(BF16)
        left, unused = left_factor(ax0, ax1, us[-1] + log_cols)
        left_e[...] = left
        right = right_chunk(by, right_rows(vs[-1]), 0, count_cols)
        strip = min(STRIP, count_rows)
        for step in range(count_rows // strip):
            at = pl.ds(step * strip, strip)
            total = jnp.exp2(matmul(left_e[at, :], right)) * matmul(left_r[at, :], right_r[...])
            add_strip(at, total)

    @pl.when(jnp.logical_not(near))
    def separate():
        stack = [u + log_cols for u in us] + adjs_rows
        stack.append(jnp.zeros((128 - len(stack), count_rows), F32))
        cols_rows[...] = jnp.concatenate(stack, axis=0).T
        strip = 128

        def block(step, carry):
            at = pl.ds(pl.multiple_of(step * strip, strip), strip)
            left = jnp.concatenate([ax0[at, :], ax1[at, :].astype(BF16)], axis=1)
            inner = matmul(left, by[...])
            columns = cols_rows[at, :]
            total = jnp.zeros_like(inner)
            for k in range(ITERS):
                base = inner + columns[:, k : k + 1]
                total += jnp.exp2(base + vs[k + 1]) * adjs_cols[k]
                total += jnp.exp2(base + (vs[k] + shift)) * columns[:, ITERS + k : ITERS + k + 1]
            add_strip(at, total)
            return carry

        lax.fori_loop(0, count_rows // strip, block, 0)

    def finish(points, sums):
        mixed = sums[0:dim] + sums[dim : 2 * dim] + sums[2 * dim : 3 * dim]
        return 2.0 * (points * sums[3 * dim : 3 * dim + 1] - mixed)

    for value, held, outs, axis in (
        (finish(x, gx[...].T), all_x, outs_x, "col"),
        (finish(y, gy[...]), all_y, outs_y, "row"),
    ):
        share = held.shape[2]
        for p in range(held.shape[0]):
            held[p] = value[:, p * share : (p + 1) * share]
        me = lax.axis_index(axis)
        for s, out in enumerate(outs):
            out[...] = held[me ^ s]


def swap(value, axis, distance):
    return lax.ppermute(value, axis, [(d, d ^ distance) for d in range(lax.axis_size(axis))])


def exchange(part, axis, join):
    size = lax.axis_size(axis)
    assert size & (size - 1) == 0
    distance = 1
    got = (part,)
    while distance < size:
        if len(got) > 1:
            (part,) = call(functools.partial(join_body, join), [shape(part.shape)], len(got))(*got)
        got = (part, swap(part, axis, distance))
        distance *= 2
    return got


def scatter(pieces, axis):
    got = [pieces[0]] + [swap(pieces[s], axis, s) for s in range(1, len(pieces))]
    return sum(got[1:], got[0])


def on_device(x_points, y_points):
    x = x_points.T
    y = y_points.T
    dim, count_rows = x.shape
    count_cols = y.shape[1]
    n_row, n_col = lax.axis_size("row"), lax.axis_size("col")
    log_rows = math.log2(count_rows * n_row)
    log_cols = math.log2(count_cols * n_col)
    row, col = (1, count_rows), (1, count_cols)

    ax0, ax1, ay0, ay1, bx, by, start, part, x, y = pl.pallas_call(
        prepare_body,
        out_shape=[
            shape((count_rows, 128), BF16),
            shape((count_rows, 128)),
            shape((count_cols, 128), BF16),
            shape((count_cols, 128)),
            shape((DEPTH, count_rows), BF16),
            shape((DEPTH, count_cols), BF16),
            shape(col),
            shape(row),
            shape(x.shape),
            shape(y.shape),
        ],
        in_specs=[pl.BlockSpec(memory_space=pltpu.HBM)] * 2,
        out_specs=vmem(10),
        scratch_shapes=[pltpu.SemaphoreType.DMA((2,))],
        compiler_params=pltpu.CompilerParams(vmem_limit_bytes=VMEM_LIMIT),
    )(x, y)

    pots_rows, pots_cols = [], [start]
    for k in range(ITERS):
        got = exchange(part, "col", join_lse)
        pot, part = call(functools.partial(forward_body, -log_rows), [shape(row), shape(col)], 3 + len(got))(
            ax0, ax1, by, *got
        )
        pots_rows.append(pot)
        got = exchange(part, "row", join_lse)
        if k < ITERS - 1:
            pot, part = call(functools.partial(forward_body, -log_cols), [shape(col), shape(row)], 3 + len(got))(
                ay0, ay1, bx, *got
            )
            pots_cols.append(pot)
    pot, part = call(functools.partial(turn_body, -log_cols, log_cols), [shape(col), shape(row)], 4 + len(got))(
        ay0, ay1, bx, pots_rows[-1], *got
    )
    pots_cols.append(pot)

    adjs_rows, adjs_cols = [], []
    for k in reversed(range(1, ITERS)):
        leading = 1.0 if k == ITERS - 1 else 0.0
        got = exchange(part, "col", join_sum)
        adj, part = call(functools.partial(backward_body, leading, log_rows), [shape(row), shape(col)], 5 + len(got))(
            ax0, ax1, by, pots_rows[k], pots_cols[k], *got
        )
        adjs_rows.insert(0, adj)
        got = exchange(part, "row", join_sum)
        adj, part = call(functools.partial(backward_body, 0.0, log_cols), [shape(col), shape(row)], 5 + len(got))(
            ay0, ay1, bx, pots_cols[k], pots_rows[k - 1], *got
        )
        adjs_cols.insert(0, adj)
    got = exchange(part, "col", join_sum)

    share_x, share_y = count_rows // n_col, count_cols // n_row
    outs = call(
        functools.partial(gradient_body, dim, log_cols, log_rows, len(got), n_col, n_row),
        [shape((dim, share_x))] * n_col + [shape((dim, share_y))] * n_row,
        5 + 4 * ITERS - 1 + len(got),
        [
            pltpu.VMEM((count_rows, 128), F32),
            pltpu.VMEM((128, count_rows), BF16),
            pltpu.VMEM((count_cols, 128), BF16),
            pltpu.VMEM((count_rows, 128), F32),
            pltpu.VMEM((128, count_cols), F32),
            pltpu.VMEM((count_rows, DEPTH), BF16),
            pltpu.VMEM((count_rows, 128), BF16),
            pltpu.VMEM((128, count_cols), BF16),
            pltpu.VMEM((n_col, dim, share_x), F32),
            pltpu.VMEM((n_row, dim, share_y), F32),
        ],
    )(ax0, ax1, by, x, y, *pots_rows, *pots_cols, *adjs_rows, *adjs_cols, *got)
    grad_x = scatter(outs[:n_col], "col")
    grad_y = scatter(outs[n_col:], "row")
    return (grad_x.T, grad_y.T)


def solution(mesh):
    in_specs = (P(("groups", "row"), None), P(("groups", "col"), None))
    out_specs = (P(("groups", "row", "col"), None), P(("groups", "col", "row"), None))
    return jax.shard_map(
        on_device, mesh=mesh, in_specs=in_specs, out_specs=out_specs, check_vma=False
    )
```

```python
import functools
import math

import jax
import jax.numpy as jnp
from jax import lax
from jax.experimental import pallas as pl
from jax.experimental.pallas import tpu as pltpu
from jax.sharding import PartitionSpec as P

ITERS = 5
EPSILON = 0.05
SCALE = 1.0 / (EPSILON * math.log(2.0))
DEPTH = 256
CHUNK = 256
F32 = jnp.float32
BF16 = jnp.bfloat16
VMEM_LIMIT = 48 * 1024 * 1024


def split3(v):
    high = v.astype(BF16).astype(F32)
    rest = v - high
    mid = rest.astype(BF16).astype(F32)
    low = (rest - mid).astype(BF16).astype(F32)
    return high, mid, low


def vmem(count):
    return [pl.BlockSpec(memory_space=pltpu.VMEM)] * count


def call(body, outs, count, scratch=()):
    return pl.pallas_call(
        body,
        out_shape=outs,
        in_specs=vmem(count),
        out_specs=vmem(len(outs)),
        scratch_shapes=list(scratch),
        compiler_params=pltpu.CompilerParams(vmem_limit_bytes=VMEM_LIMIT),
    )


def shape(dims, dtype=F32):
    return jax.ShapeDtypeStruct(dims, dtype)


def factors(points, order):
    parts = split3(points)
    width = points.shape[1]
    blocks = [parts[o] for o in order]
    zero16 = jnp.zeros((16, width), F32)
    tail = jnp.zeros((DEPTH - 144 - 2 * points.shape[0], width), F32)
    return jnp.concatenate(blocks[:4] + [zero16] + blocks[4:] + [tail], axis=0)


X_ORDER = (0, 0, 1, 0, 2, 1)
Y_ORDER = (0, 1, 0, 2, 0, 1)


def prepare_body(x_hbm, y_hbm, ax0, ax1, ay0, ay1, bx, by, start_ref, out, x_ref, y_ref, sems):
    copies = [
        pltpu.make_async_copy(x_hbm, x_ref, sems.at[0]),
        pltpu.make_async_copy(y_hbm, y_ref, sems.at[1]),
    ]
    for copy in copies:
        copy.start()
    for copy in copies:
        copy.wait()
    x = x_ref[...]
    y = y_ref[...]
    xf = factors(x * (2.0 * SCALE), X_ORDER)
    yf = factors(y, Y_ORDER)
    for factor, left0, left1, right in ((xf, ax0, ax1, bx), (yf, ay0, ay1, by)):
        right[...] = factor.astype(BF16)
        turned = factor.T
        left0[...] = turned[:, :128].astype(BF16)
        left1[...] = turned[:, 128:]
    start = -SCALE * jnp.sum(y * y, axis=0, keepdims=True)
    start_ref[...] = start
    left, unused = left_factor(ay0, ay1, start)
    partial_lse(left, bx, out)


def left_factor(left0, left1, pot, adj=None):
    width = pot.shape[1]
    high, mid, low = split3(pot)
    one = jnp.ones((1, width), F32)
    rows = [high, mid, low, one, one, one, jnp.zeros_like(one)]
    rows.append(jnp.zeros_like(one) if adj is None else adj)
    rows.append(jnp.zeros((120, width), F32))
    turned = jnp.concatenate(rows, axis=0).T
    column = None
    if adj is not None:
        column = turned[:, 7:8]
        lane = lax.broadcasted_iota(jnp.int32, turned.shape, 1)
        turned = jnp.where(lane == 7, 0.0, turned)
    return jnp.concatenate([left0[...], (left1[...] + turned).astype(BF16)], axis=1), column


def right_rows(pot):
    width = pot.shape[1]
    one = jnp.ones((3, width), F32)
    high, mid, low = split3(pot)
    return jnp.concatenate([one, high, mid, low, jnp.zeros((10, width), F32)], axis=0).astype(BF16)


def right_chunk(right, rows, at, wide):
    return jnp.concatenate(
        [right[0:128, at : at + wide], rows[:, at : at + wide], right[144:DEPTH, at : at + wide]], axis=0
    )


def matmul(a, b):
    return jnp.dot(a, b, preferred_element_type=F32)


def partial_lse(left, right, out):
    width = right.shape[1]
    rows = right_rows(jnp.zeros((1, width), F32))
    wide = min(CHUNK, width)
    for at in range(0, width, wide):
        scores = matmul(left, right_chunk(right, rows, at, wide))
        top = jnp.max(scores, axis=0, keepdims=True)
        total = jnp.sum(jnp.exp2(scores - top), axis=0, keepdims=True)
        out[:, at : at + wide] = top + jnp.log2(total)


def join_lse(parts):
    parts = [p[...] for p in parts]
    top = functools.reduce(jnp.maximum, parts)
    return top + jnp.log2(sum(jnp.exp2(p - top) for p in parts))


def join_sum(parts):
    return sum(p[...] for p in parts)


def join_body(join, *refs):
    refs[-1][...] = join(refs[:-1])


def forward_body(log_mass, left0, left1, right, *refs):
    got, (pot_out, out) = refs[:-2], refs[-2:]
    pot = log_mass - join_lse(got)
    pot_out[...] = pot
    left, unused = left_factor(left0, left1, pot)
    partial_lse(left, right, out)


def weighted_sums(left, column, right, rows, out):
    width = right.shape[1]
    wide = min(CHUNK, width)
    for at in range(0, width, wide):
        scores = matmul(left, right_chunk(right, rows, at, wide))
        out[:, at : at + wide] = jnp.sum(jnp.exp2(scores) * column, axis=0, keepdims=True)


def turn_body(log_mass, log_scale, left0, left1, right, pot_right, *refs):
    got, (pot_out, out) = refs[:-2], refs[-2:]
    pot = log_mass - join_lse(got)
    pot_out[...] = pot
    left, column = left_factor(left0, left1, pot, jnp.ones_like(pot))
    weighted_sums(left, column, right, right_rows(pot_right[...] + log_scale), out)


def backward_body(leading, log_scale, left0, left1, right, pot_left, pot_right, *refs):
    got, (adj_out, out) = refs[:-2], refs[-2:]
    adj = leading - join_sum(got)
    adj_out[...] = adj
    left, column = left_factor(left0, left1, pot_left[...], adj)
    weighted_sums(left, column, right, right_rows(pot_right[...] + log_scale), out)


SPREAD = 30.0
STRIP = 256


def gradient_body(dim, log_cols, log_rows, n_got, n_col, n_row, ax0, ax1, by, x_ref, y_ref, *refs):
    pots_rows = refs[:ITERS]
    pots_cols = refs[ITERS : 2 * ITERS + 1]
    adjs_rows = refs[2 * ITERS + 1 : 3 * ITERS]
    adjs_cols = refs[3 * ITERS : 4 * ITERS - 1]
    refs = refs[4 * ITERS - 1 :]
    got, refs = refs[:n_got], refs[n_got:]
    us = [p[...] for p in pots_rows]
    vs = [p[...] for p in pots_cols]
    first = (1.0 if ITERS == 1 else 0.0) - join_sum(got)
    adjs_rows = [first] + [a[...] for a in adjs_rows]
    adjs_cols = [a[...] for a in adjs_cols] + [jnp.ones(vs[0].shape, F32)]
    gradient(log_cols, log_rows, n_col, n_row, ax0, ax1, by, x_ref, y_ref, us, vs, adjs_rows, adjs_cols, refs)


def gradient(log_cols, log_rows, n_col, n_row, ax0, ax1, by, x_ref, y_ref, us, vs, adjs_rows, adjs_cols, refs):
    outs_x, outs_y = refs[:n_col], refs[n_col : n_col + n_row]
    cols_rows, x_parts, y_parts, gx, gy, left_e, left_r, right_r, all_x, all_y = refs[n_col + n_row :]
    dim, count_rows = x_ref.shape
    count_cols = y_ref.shape[1]
    shift = log_rows - log_cols

    x = x_ref[...]
    y = y_ref[...]
    one = jnp.ones((1, count_cols), F32)
    pad = jnp.zeros((31, count_cols), F32)
    y_parts[...] = jnp.concatenate(list(split3(y)) + [one, pad], axis=0).T.astype(BF16)
    one = jnp.ones((1, count_rows), F32)
    pad = jnp.zeros((31, count_rows), F32)
    x_parts[...] = jnp.concatenate(list(split3(x)) + [one, pad], axis=0).astype(BF16)
    gy[...] = jnp.zeros_like(gy)

    far_u = functools.reduce(jnp.maximum, [jnp.abs(u - us[-1]) for u in us])
    far_v = functools.reduce(jnp.maximum, [jnp.abs(v - vs[-1]) for v in vs])
    near = jnp.maximum(jnp.max(far_u), jnp.max(far_v)) < SPREAD

    def add_strip(at, total):
        upper = total.astype(BF16)
        lower = (total - upper.astype(F32)).astype(BF16)
        gx[at, :] = matmul(upper, y_parts[...]) + matmul(lower, y_parts[...])
        gy[...] += matmul(x_parts[:, at], upper) + matmul(x_parts[:, at], lower)

    @pl.when(near)
    def factored():
        alpha = [jnp.exp2(u - us[-1]) for u in us]
        beta = [jnp.exp2(v - vs[-1]) for v in vs]
        p_rows = alpha + [a * adj for a, adj in zip(alpha, adjs_rows)]
        q_rows = [b * adj for b, adj in zip(beta[1:], adjs_cols)] + [b * 2.0**shift for b in beta[:-1]]
        fill = 16 - 2 * ITERS
        p_split = split3(jnp.concatenate(p_rows + [jnp.zeros((fill, count_rows), F32)], axis=0))
        q_split = split3(jnp.concatenate(q_rows + [jnp.zeros((fill, count_cols), F32)], axis=0))
        tail = [jnp.zeros((32, count_rows), F32)]
        left_r[...] = jnp.concatenate([p_split[o] for o in X_ORDER] + tail, axis=0).T.astype(BF16)
        tail = [jnp.zeros((32, count_cols), F32)]
        right_r[...] = jnp.concatenate([q_split[o] for o in Y_ORDER] + tail, axis=0).astype(BF16)
        left, unused = left_factor(ax0, ax1, us[-1] + log_cols)
        left_e[...] = left
        right = right_chunk(by, right_rows(vs[-1]), 0, count_cols)
        strip = min(STRIP, count_rows)
        for step in range(count_rows // strip):
            at = pl.ds(step * strip, strip)
            total = jnp.exp2(matmul(left_e[at, :], right)) * matmul(left_r[at, :], right_r[...])
            add_strip(at, total)

    @pl.when(jnp.logical_not(near))
    def separate():
        stack = [u + log_cols for u in us] + adjs_rows
        stack.append(jnp.zeros((128 - len(stack), count_rows), F32))
        cols_rows[...] = jnp.concatenate(stack, axis=0).T
        strip = 128

        def block(step, carry):
            at = pl.ds(pl.multiple_of(step * strip, strip), strip)
            left = jnp.concatenate([ax0[at, :], ax1[at, :].astype(BF16)], axis=1)
            inner = matmul(left, by[...])
            columns = cols_rows[at, :]
            total = jnp.zeros_like(inner)
            for k in range(ITERS):
                base = inner + columns[:, k : k + 1]
                total += jnp.exp2(base + vs[k + 1]) * adjs_cols[k]
                total += jnp.exp2(base + (vs[k] + shift)) * columns[:, ITERS + k : ITERS + k + 1]
            add_strip(at, total)
            return carry

        lax.fori_loop(0, count_rows // strip, block, 0)

    def finish(points, sums):
        mixed = sums[0:dim] + sums[dim : 2 * dim] + sums[2 * dim : 3 * dim]
        return 2.0 * (points * sums[3 * dim : 3 * dim + 1] - mixed)

    for value, held, outs, axis in (
        (finish(x, gx[...].T), all_x, outs_x, "col"),
        (finish(y, gy[...]), all_y, outs_y, "row"),
    ):
        share = held.shape[2]
        for p in range(held.shape[0]):
            held[p] = value[:, p * share : (p + 1) * share]
        me = lax.axis_index(axis)
        for s, out in enumerate(outs):
            out[...] = held[me ^ s]


def swap(value, axis, distance):
    return lax.ppermute(value, axis, [(d, d ^ distance) for d in range(lax.axis_size(axis))])


def exchange(part, axis, join):
    size = lax.axis_size(axis)
    assert size & (size - 1) == 0
    distance = 1
    got = (part,)
    while distance < size:
        if len(got) > 1:
            (part,) = call(functools.partial(join_body, join), [shape(part.shape)], len(got))(*got)
        got = (part, swap(part, axis, distance))
        distance *= 2
    return got


def scatter(pieces, axis):
    got = [pieces[0]] + [swap(pieces[s], axis, s) for s in range(1, len(pieces))]
    return sum(got[1:], got[0])


def slot(column, lane, state):
    return jnp.where(lax.broadcasted_iota(jnp.int32, state.shape, 1) == lane, column, state)


def left_strip(left0, left1, at, pot):
    strip = left1[at, :]
    for lane, part in enumerate(split3(jnp.broadcast_to(pot, strip.shape))):
        strip = slot(part, lane, strip)
    return jnp.concatenate([left0[at, :], strip.astype(BF16)], axis=1)


def halves(value):
    return sum(value[:, p : p + 128] for p in range(0, value.shape[1], 128))


def octets(value):
    return jnp.sum(value.reshape(value.shape[0] // 8, 8, value.shape[1]), axis=0)


SWEEP = 256


def sweep(left0, left1, right, rows, state, state_out, held, acc, pot_of, first_sum, put, factor):
    count, wide_all = left0.shape[0], right.shape[1]
    strip = min(SWEEP, count)
    acc[...] = jnp.zeros_like(acc)

    def step(index, carry):
        at = pl.ds(pl.multiple_of(index * strip, strip), strip)
        old = state[at, :]
        left = left_strip(left0, left1, at, pot_of(old))
        sums = None
        for c in range(0, wide_all, CHUNK):
            power = jnp.exp2(matmul(left, right_chunk(right, rows, c, CHUNK)))
            held[:, c : c + CHUNK] = power
            part = halves(first_sum(power, c))
            sums = part if sums is None else sums + part
        column = jnp.sum(sums, axis=1, keepdims=True)
        state_out[at, :] = put(old, column)
        times = factor(old, column)
        for c in range(0, wide_all, CHUNK):
            acc[:, c : c + CHUNK] += octets(held[:, c : c + CHUNK] * times)
        return carry

    lax.fori_loop(0, count // strip, step, 0)


def gather_body(n_x, n_y, *refs):
    xs, ys = refs[:n_x], refs[n_x : n_x + n_y]
    ay0, ay1, bx, state, out = refs[n_x + n_y :]
    x = jnp.concatenate([r[...] for r in xs], axis=1)
    y = jnp.concatenate([r[...] for r in ys], axis=1)
    bx[...] = factors(x * (2.0 * SCALE), X_ORDER).astype(BF16)
    turned = factors(y, Y_ORDER).T
    start = -SCALE * jnp.sum(y * y, axis=0, keepdims=True)
    ay0[...] = turned[:, :128].astype(BF16)
    wide = y.shape[1]
    high, mid, low = split3(start)
    one = jnp.ones((3, wide), F32)
    extra = jnp.concatenate([high, mid, low, one, jnp.zeros((122, wide), F32)], axis=0).T
    with_start = turned[:, 128:] + jnp.where(lax.broadcasted_iota(jnp.int32, extra.shape, 1) < 3, extra, 0.0)
    ay1[...] = turned[:, 128:] + jnp.where(lax.broadcasted_iota(jnp.int32, extra.shape, 1) < 3, 0.0, extra)
    state[...] = jnp.concatenate([start, jnp.zeros((127, wide), F32)], axis=0).T
    left = jnp.concatenate([ay0[...], with_start.astype(BF16)], axis=1)
    one = jnp.concatenate([jnp.ones((3, CHUNK), F32), jnp.zeros((13, CHUNK), F32)], axis=0).astype(BF16)

    def step(index, carry):
        at = pl.ds(pl.multiple_of(index * CHUNK, CHUNK), CHUNK)
        full = jnp.concatenate([bx[0:128, at], one, bx[144:DEPTH, at]], axis=0)
        scores = matmul(left, full)
        top = jnp.max(scores, axis=0, keepdims=True)
        out[:, at] = top + jnp.log2(jnp.sum(jnp.exp2(scores - top), axis=0, keepdims=True))
        return carry

    lax.fori_loop(0, bx.shape[1] // CHUNK, step, 0)


def opening_body(n_got, log_rows, log_cols, left0, left1, right, state, *refs):
    got, (u_out, state_out, out, held, acc) = refs[:n_got], refs[n_got:]
    u = -log_rows - join_lse(got)
    u_out[...] = u
    rows = right_rows(u)
    count, wide_all = left0.shape[0], right.shape[1]
    strip = min(SWEEP, count)
    acc[...] = jnp.zeros_like(acc)

    def step(index, carry):
        at = pl.ds(pl.multiple_of(index * strip, strip), strip)
        left = jnp.concatenate([left0[at, :], left1[at, :].astype(BF16)], axis=1)
        tops = None
        for c in range(0, wide_all, CHUNK):
            scores = matmul(left, right_chunk(right, rows, c, CHUNK))
            held[:, c : c + CHUNK] = scores
            part = functools.reduce(jnp.maximum, [scores[:, p : p + 128] for p in range(0, CHUNK, 128)])
            tops = part if tops is None else jnp.maximum(tops, part)
        top = jnp.max(tops, axis=1, keepdims=True)
        sums = None
        for c in range(0, wide_all, CHUNK):
            power = jnp.exp2(held[:, c : c + CHUNK] - top)
            held[:, c : c + CHUNK] = power
            part = halves(power)
            sums = part if sums is None else sums + part
        column = jnp.sum(sums, axis=1, keepdims=True)
        state_out[at, :] = slot(-log_cols - (top + jnp.log2(column)), 1, state[at, :])
        times = 2.0**-log_cols / column
        for c in range(0, wide_all, CHUNK):
            acc[:, c : c + CHUNK] += octets(held[:, c : c + CHUNK] * times)
        return carry

    lax.fori_loop(0, count // strip, step, 0)
    out[...] = jnp.sum(acc[...], axis=0, keepdims=True)


def iteration_body(k, n_got, log_rows, log_cols, left0, left1, right, state, u_old, *refs):
    got, (u_out, state_out, out, held, acc) = refs[:n_got], refs[n_got:]
    u = u_old[...] - (log_rows + jnp.log2(join_sum(got)))
    u_out[...] = u

    def put(old, column):
        pot = old[:, k - 1 : k] - (log_cols + jnp.log2(column))
        return slot(2.0**log_cols * column, 8 + k, slot(pot, k, old))

    first = (lambda power, c: power, put, lambda old, column: 2.0**-log_cols / column)
    sweep(left0, left1, right, right_rows(u), state, state_out, held, acc, lambda old: old[:, k - 1 : k], *first)
    out[...] = jnp.sum(acc[...], axis=0, keepdims=True)


def adjoint_body(k, n_got, log_rows, log_cols, left0, left1, right, state, u_ref, u_before, *refs):
    got, (adj_out, state_out, out, held, acc) = refs[:n_got], refs[n_got:]
    if k == ITERS:
        adj = 1.0 - 2.0**log_cols * join_sum(got)
    else:
        adj = -join_sum(got)
    adj_out[...] = adj
    u = u_ref[...]
    shift = 2.0 ** (log_rows - log_cols)

    def put(old, column):
        return slot(-shift * old[:, 8 + k : 9 + k] * column, 16 + k - 1, old)

    def factor(old, column):
        sigma = old[:, 8 + k : 9 + k]
        return -shift * sigma * sigma * column

    first = (lambda power, c: power * adj[:, c : c + CHUNK], put, factor)
    rows = right_rows(u + log_cols)
    sweep(left0, left1, right, rows, state, state_out, held, acc, lambda old: old[:, k : k + 1], *first)
    out[...] = jnp.sum(acc[...], axis=0, keepdims=True) * jnp.exp2(u_before[...] - u)


def closing_body(n_got, log_cols, log_rows, n_col, n_row, ax0, ax1, by, x_ref, y_ref, state, *refs):
    count_rows, count_cols = x_ref.shape[1], y_ref.shape[1]
    us = [r[:, :count_rows] for r in refs[:ITERS]]
    adjs_rows = [r[:, :count_rows] for r in refs[ITERS : 2 * ITERS - 1]]
    refs = refs[2 * ITERS - 1 :]
    got, refs = refs[:n_got], refs[n_got:]
    first = -join_sum([r[:, :count_rows] for r in got])
    turned = state[0:count_cols, :].T
    vs = [turned[k : k + 1] for k in range(ITERS + 1)]
    adjs_cols = [turned[16 + k : 17 + k] for k in range(1, ITERS)] + [jnp.ones((1, count_cols), F32)]
    adjs_rows = [first] + adjs_rows
    gradient(log_cols, log_rows, n_col, n_row, ax0, ax1, by, x_ref, y_ref, us, vs, adjs_rows, adjs_cols, refs)


def own_body(x_hbm, y_hbm, ax0, ax1, by, x_ref, y_ref, sems):
    copies = [
        pltpu.make_async_copy(x_hbm, x_ref, sems.at[0]),
        pltpu.make_async_copy(y_hbm, y_ref, sems.at[1]),
    ]
    for copy in copies:
        copy.start()
    for copy in copies:
        copy.wait()
    turned = factors(x_ref[...] * (2.0 * SCALE), X_ORDER).T
    ax0[...] = turned[:, :128].astype(BF16)
    ax1[...] = turned[:, 128:]
    by[...] = factors(y_ref[...], Y_ORDER).astype(BF16)


def gradient_scratch(dim, count_rows, count_cols, n_col, n_row):
    return [
        pltpu.VMEM((count_rows, 128), F32),
        pltpu.VMEM((128, count_rows), BF16),
        pltpu.VMEM((count_cols, 128), BF16),
        pltpu.VMEM((count_rows, 128), F32),
        pltpu.VMEM((128, count_cols), F32),
        pltpu.VMEM((count_rows, DEPTH), BF16),
        pltpu.VMEM((count_rows, 128), BF16),
        pltpu.VMEM((128, count_cols), BF16),
        pltpu.VMEM((n_col, dim, count_rows // n_col), F32),
        pltpu.VMEM((n_row, dim, count_cols // n_row), F32),
    ]


CORES = 2


def repeated(x, y):
    dim, count_rows = x.shape
    count_cols = y.shape[1]
    n_row, n_col = lax.axis_size("row"), lax.axis_size("col")
    n_chips = n_col // CORES
    all_rows, held_cols = count_rows * n_row, count_cols * n_chips
    log_rows, log_cols = math.log2(all_rows), math.log2(count_cols * n_col)
    row, col = (1, all_rows), (1, held_cols)

    xs = [x] + [swap(x, "row", s) for s in range(1, n_row)]
    ys = [y] + [swap(y, "col", s * CORES) for s in range(1, n_chips)]
    ax0, ax1, by, x, y = pl.pallas_call(
        own_body,
        out_shape=[
            shape((count_rows, 128), BF16),
            shape((count_rows, 128)),
            shape((DEPTH, count_cols), BF16),
            shape(x.shape),
            shape(y.shape),
        ],
        in_specs=[pl.BlockSpec(memory_space=pltpu.HBM)] * 2,
        out_specs=vmem(5),
        scratch_shapes=[pltpu.SemaphoreType.DMA((2,))],
        compiler_params=pltpu.CompilerParams(vmem_limit_bytes=VMEM_LIMIT),
    )(x, y)
    ay0, ay1, bx, state, part = call(
        functools.partial(gather_body, n_row, n_chips),
        [
            shape((held_cols, 128), BF16),
            shape((held_cols, 128)),
            shape((DEPTH, all_rows), BF16),
            shape((held_cols, 128)),
            shape(row),
        ],
        n_row + n_chips,
    )(*xs, *ys)

    strip = min(SWEEP, held_cols)
    scratch = [pltpu.VMEM((strip, all_rows), F32), pltpu.VMEM((8, all_rows), F32)]
    results = [shape(row), shape((held_cols, 128)), shape(row)]
    got = (part, swap(part, "col", 1))
    us = []
    u, state, part = call(
        functools.partial(opening_body, len(got), log_rows, log_cols), results, 4 + len(got), scratch
    )(ay0, ay1, bx, state, *got)
    us.append(u)
    for k in range(2, ITERS + 1):
        got = (part, swap(part, "col", 1))
        u, state, part = call(
            functools.partial(iteration_body, k, len(got), log_rows, log_cols), results, 5 + len(got), scratch
        )(ay0, ay1, bx, state, u, *got)
        us.append(u)
    adjs_rows = []
    for k in range(ITERS, 1, -1):
        got = (part, swap(part, "col", 1))
        adj, state, part = call(
            functools.partial(adjoint_body, k, len(got), log_rows, log_cols),
            results,
            6 + len(got),
            scratch,
        )(ay0, ay1, bx, state, us[k - 1], us[k - 2], *got)
        adjs_rows.insert(0, adj)
    got = (part, swap(part, "col", 1))
    outs = call(
        functools.partial(closing_body, len(got), log_cols, log_rows, n_col, n_row),
        [shape((dim, count_rows // n_col))] * n_col + [shape((dim, count_cols // n_row))] * n_row,
        6 + 2 * ITERS - 1 + len(got),
        gradient_scratch(dim, count_rows, count_cols, n_col, n_row),
    )(ax0, ax1, by, x, y, state, *us, *adjs_rows, *got)
    return scatter(outs[:n_col], "col").T, scatter(outs[n_col:], "row").T


REPEAT_PAIRS = 1 << 23


def on_device(x_points, y_points):
    x = x_points.T
    y = y_points.T
    n_row, n_col = lax.axis_size("row"), lax.axis_size("col")
    pairs = x.shape[1] * n_row * y.shape[1] * n_col // CORES
    if ITERS > 1 and n_col % CORES == 0 and pairs <= REPEAT_PAIRS:
        return repeated(x, y)
    return shared(x, y)


def shared(x, y):
    dim, count_rows = x.shape
    count_cols = y.shape[1]
    n_row, n_col = lax.axis_size("row"), lax.axis_size("col")
    log_rows = math.log2(count_rows * n_row)
    log_cols = math.log2(count_cols * n_col)
    row, col = (1, count_rows), (1, count_cols)

    ax0, ax1, ay0, ay1, bx, by, start, part, x, y = pl.pallas_call(
        prepare_body,
        out_shape=[
            shape((count_rows, 128), BF16),
            shape((count_rows, 128)),
            shape((count_cols, 128), BF16),
            shape((count_cols, 128)),
            shape((DEPTH, count_rows), BF16),
            shape((DEPTH, count_cols), BF16),
            shape(col),
            shape(row),
            shape(x.shape),
            shape(y.shape),
        ],
        in_specs=[pl.BlockSpec(memory_space=pltpu.HBM)] * 2,
        out_specs=vmem(10),
        scratch_shapes=[pltpu.SemaphoreType.DMA((2,))],
        compiler_params=pltpu.CompilerParams(vmem_limit_bytes=VMEM_LIMIT),
    )(x, y)

    pots_rows, pots_cols = [], [start]
    for k in range(ITERS):
        got = exchange(part, "col", join_lse)
        pot, part = call(functools.partial(forward_body, -log_rows), [shape(row), shape(col)], 3 + len(got))(
            ax0, ax1, by, *got
        )
        pots_rows.append(pot)
        got = exchange(part, "row", join_lse)
        if k < ITERS - 1:
            pot, part = call(functools.partial(forward_body, -log_cols), [shape(col), shape(row)], 3 + len(got))(
                ay0, ay1, bx, *got
            )
            pots_cols.append(pot)
    pot, part = call(functools.partial(turn_body, -log_cols, log_cols), [shape(col), shape(row)], 4 + len(got))(
        ay0, ay1, bx, pots_rows[-1], *got
    )
    pots_cols.append(pot)

    adjs_rows, adjs_cols = [], []
    for k in reversed(range(1, ITERS)):
        leading = 1.0 if k == ITERS - 1 else 0.0
        got = exchange(part, "col", join_sum)
        adj, part = call(functools.partial(backward_body, leading, log_rows), [shape(row), shape(col)], 5 + len(got))(
            ax0, ax1, by, pots_rows[k], pots_cols[k], *got
        )
        adjs_rows.insert(0, adj)
        got = exchange(part, "row", join_sum)
        adj, part = call(functools.partial(backward_body, 0.0, log_cols), [shape(col), shape(row)], 5 + len(got))(
            ay0, ay1, bx, pots_cols[k], pots_rows[k - 1], *got
        )
        adjs_cols.insert(0, adj)
    got = exchange(part, "col", join_sum)

    share_x, share_y = count_rows // n_col, count_cols // n_row
    outs = call(
        functools.partial(gradient_body, dim, log_cols, log_rows, len(got), n_col, n_row),
        [shape((dim, share_x))] * n_col + [shape((dim, share_y))] * n_row,
        5 + 4 * ITERS - 1 + len(got),
        gradient_scratch(dim, count_rows, count_cols, n_col, n_row),
    )(ax0, ax1, by, x, y, *pots_rows, *pots_cols, *adjs_rows, *adjs_cols, *got)
    grad_x = scatter(outs[:n_col], "col")
    grad_y = scatter(outs[n_col:], "row")
    return (grad_x.T, grad_y.T)


def solution(mesh):
    in_specs = (P(("groups", "row"), None), P(("groups", "col"), None))
    out_specs = (P(("groups", "row", "col"), None), P(("groups", "col", "row"), None))
    return jax.shard_map(
        on_device, mesh=mesh, in_specs=in_specs, out_specs=out_specs, check_vma=False
    )
```

```python
import functools
import math

import jax
import jax.numpy as jnp
from jax import lax
from jax.experimental import pallas as pl
from jax.experimental.pallas import tpu as pltpu
from jax.sharding import PartitionSpec as P

ITERS = 5
EPSILON = 0.05
SCALE = 1.0 / EPSILON
DEPTH = 256
CHUNK = 256
F32 = jnp.float32
BF16 = jnp.bfloat16
VMEM_LIMIT = 48 * 1024 * 1024


def split3(v):
    high = v.astype(BF16).astype(F32)
    rest = v - high
    mid = rest.astype(BF16).astype(F32)
    low = (rest - mid).astype(BF16).astype(F32)
    return high, mid, low


def vmem(count):
    return [pl.BlockSpec(memory_space=pltpu.VMEM)] * count


def call(body, outs, count, scratch=()):
    return pl.pallas_call(
        body,
        out_shape=outs,
        in_specs=vmem(count),
        out_specs=vmem(len(outs)),
        scratch_shapes=list(scratch),
        compiler_params=pltpu.CompilerParams(vmem_limit_bytes=VMEM_LIMIT),
    )


def shape(dims, dtype=F32):
    return jax.ShapeDtypeStruct(dims, dtype)


def factors(points, order):
    parts = split3(points)
    width = points.shape[1]
    blocks = [parts[o] for o in order]
    zero16 = jnp.zeros((16, width), F32)
    tail = jnp.zeros((DEPTH - 144 - 2 * points.shape[0], width), F32)
    return jnp.concatenate(blocks[:4] + [zero16] + blocks[4:] + [tail], axis=0)


X_ORDER = (0, 0, 1, 0, 2, 1)
Y_ORDER = (0, 1, 0, 2, 0, 1)


def prepare_body(x_hbm, y_hbm, ax0, ax1, ay0, ay1, bx, by, start_ref, out, x_ref, y_ref, sems):
    copies = [
        pltpu.make_async_copy(x_hbm, x_ref, sems.at[0]),
        pltpu.make_async_copy(y_hbm, y_ref, sems.at[1]),
    ]
    for copy in copies:
        copy.start()
    for copy in copies:
        copy.wait()
    x = x_ref[...]
    y = y_ref[...]
    xf = factors(x * (2.0 * SCALE), X_ORDER)
    yf = factors(y, Y_ORDER)
    for factor, left0, left1, right in ((xf, ax0, ax1, bx), (yf, ay0, ay1, by)):
        right[...] = factor.astype(BF16)
        turned = factor.T
        left0[...] = turned[:, :128].astype(BF16)
        left1[...] = turned[:, 128:]
    start = -SCALE * jnp.sum(y * y, axis=0, keepdims=True)
    start_ref[...] = start
    left, unused = left_factor(ay0, ay1, start)
    partial_lse(left, bx, out)


def left_factor(left0, left1, pot, adj=None):
    width = pot.shape[1]
    high, mid, low = split3(pot)
    one = jnp.ones((1, width), F32)
    rows = [high, mid, low, one, one, one, jnp.zeros_like(one)]
    rows.append(jnp.zeros_like(one) if adj is None else adj)
    rows.append(jnp.zeros((120, width), F32))
    turned = jnp.concatenate(rows, axis=0).T
    column = None
    if adj is not None:
        column = turned[:, 7:8]
        lane = lax.broadcasted_iota(jnp.int32, turned.shape, 1)
        turned = jnp.where(lane == 7, 0.0, turned)
    return jnp.concatenate([left0[...], (left1[...] + turned).astype(BF16)], axis=1), column


def right_rows(pot):
    width = pot.shape[1]
    one = jnp.ones((3, width), F32)
    high, mid, low = split3(pot)
    return jnp.concatenate([one, high, mid, low, jnp.zeros((10, width), F32)], axis=0).astype(BF16)


def right_chunk(right, rows, at, wide):
    return jnp.concatenate(
        [right[0:128, at : at + wide], rows[:, at : at + wide], right[144:DEPTH, at : at + wide]], axis=0
    )


def matmul(a, b):
    return jnp.dot(a, b, preferred_element_type=F32)


def partial_lse(left, right, out):
    width = right.shape[1]
    rows = right_rows(jnp.zeros((1, width), F32))
    wide = min(CHUNK, width)
    for at in range(0, width, wide):
        scores = matmul(left, right_chunk(right, rows, at, wide))
        top = jnp.max(scores, axis=0, keepdims=True)
        total = jnp.sum(jnp.exp(scores - top), axis=0, keepdims=True)
        out[:, at : at + wide] = top + jnp.log(total)


def join_lse(parts):
    parts = [p[...] for p in parts]
    top = functools.reduce(jnp.maximum, parts)
    return top + jnp.log(sum(jnp.exp(p - top) for p in parts))


def join_sum(parts):
    return sum(p[...] for p in parts)


def join_body(join, *refs):
    refs[-1][...] = join(refs[:-1])


def forward_body(log_mass, left0, left1, right, *refs):
    got, (pot_out, out) = refs[:-2], refs[-2:]
    pot = log_mass - join_lse(got)
    pot_out[...] = pot
    left, unused = left_factor(left0, left1, pot)
    partial_lse(left, right, out)


def weighted_sums(left, column, right, rows, out):
    width = right.shape[1]
    wide = min(CHUNK, width)
    for at in range(0, width, wide):
        scores = matmul(left, right_chunk(right, rows, at, wide))
        out[:, at : at + wide] = jnp.sum(jnp.exp(scores) * column, axis=0, keepdims=True)


def turn_body(log_mass, log_scale, left0, left1, right, pot_right, *refs):
    got, (pot_out, out) = refs[:-2], refs[-2:]
    pot = log_mass - join_lse(got)
    pot_out[...] = pot
    left, column = left_factor(left0, left1, pot, jnp.ones_like(pot))
    weighted_sums(left, column, right, right_rows(pot_right[...] + log_scale), out)


def backward_body(leading, log_scale, left0, left1, right, pot_left, pot_right, *refs):
    got, (adj_out, out) = refs[:-2], refs[-2:]
    adj = leading - join_sum(got)
    adj_out[...] = adj
    left, column = left_factor(left0, left1, pot_left[...], adj)
    weighted_sums(left, column, right, right_rows(pot_right[...] + log_scale), out)


SPREAD = 20.0
STRIP = 256


def gradient_body(dim, log_cols, log_rows, n_got, n_col, n_row, ax0, ax1, by, x_ref, y_ref, *refs):
    pots_rows = refs[:ITERS]
    pots_cols = refs[ITERS : 2 * ITERS + 1]
    adjs_rows = refs[2 * ITERS + 1 : 3 * ITERS]
    adjs_cols = refs[3 * ITERS : 4 * ITERS - 1]
    refs = refs[4 * ITERS - 1 :]
    got, refs = refs[:n_got], refs[n_got:]
    us = [p[...] for p in pots_rows]
    vs = [p[...] for p in pots_cols]
    first = (1.0 if ITERS == 1 else 0.0) - join_sum(got)
    adjs_rows = [first] + [a[...] for a in adjs_rows]
    adjs_cols = [a[...] for a in adjs_cols] + [jnp.ones(vs[0].shape, F32)]
    gradient(log_cols, log_rows, n_col, n_row, ax0, ax1, by, x_ref, y_ref, us, vs, adjs_rows, adjs_cols, refs)


def gradient(log_cols, log_rows, n_col, n_row, ax0, ax1, by, x_ref, y_ref, us, vs, adjs_rows, adjs_cols, refs):
    outs_x, outs_y = refs[:n_col], refs[n_col : n_col + n_row]
    cols_rows, x_parts, y_parts, gx, gy, left_e, left_r, right_r, all_x, all_y = refs[n_col + n_row :]
    dim, count_rows = x_ref.shape
    count_cols = y_ref.shape[1]
    shift = log_rows - log_cols

    x = x_ref[...]
    y = y_ref[...]
    one = jnp.ones((1, count_cols), F32)
    pad = jnp.zeros((31, count_cols), F32)
    y_parts[...] = jnp.concatenate(list(split3(y)) + [one, pad], axis=0).T.astype(BF16)
    one = jnp.ones((1, count_rows), F32)
    pad = jnp.zeros((31, count_rows), F32)
    x_parts[...] = jnp.concatenate(list(split3(x)) + [one, pad], axis=0).astype(BF16)
    gy[...] = jnp.zeros_like(gy)

    far_u = functools.reduce(jnp.maximum, [jnp.abs(u - us[-1]) for u in us])
    far_v = functools.reduce(jnp.maximum, [jnp.abs(v - vs[-1]) for v in vs])
    near = jnp.maximum(jnp.max(far_u), jnp.max(far_v)) < SPREAD

    def add_strip(at, total):
        upper = total.astype(BF16)
        lower = (total - upper.astype(F32)).astype(BF16)
        gx[at, :] = matmul(upper, y_parts[...]) + matmul(lower, y_parts[...])
        gy[...] += matmul(x_parts[:, at], upper) + matmul(x_parts[:, at], lower)

    @pl.when(near)
    def factored():
        alpha = [jnp.exp(u - us[-1]) for u in us]
        beta = [jnp.exp(v - vs[-1]) for v in vs]
        p_rows = alpha + [a * adj for a, adj in zip(alpha, adjs_rows)]
        q_rows = [b * adj for b, adj in zip(beta[1:], adjs_cols)] + [b * math.exp(shift) for b in beta[:-1]]
        fill = 16 - 2 * ITERS
        p_split = split3(jnp.concatenate(p_rows + [jnp.zeros((fill, count_rows), F32)], axis=0))
        q_split = split3(jnp.concatenate(q_rows + [jnp.zeros((fill, count_cols), F32)], axis=0))
        tail = [jnp.zeros((32, count_rows), F32)]
        left_r[...] = jnp.concatenate([p_split[o] for o in X_ORDER] + tail, axis=0).T.astype(BF16)
        tail = [jnp.zeros((32, count_cols), F32)]
        right_r[...] = jnp.concatenate([q_split[o] for o in Y_ORDER] + tail, axis=0).astype(BF16)
        left, unused = left_factor(ax0, ax1, us[-1] + log_cols)
        left_e[...] = left
        right = right_chunk(by, right_rows(vs[-1]), 0, count_cols)
        strip = min(STRIP, count_rows)
        for step in range(count_rows // strip):
            at = pl.ds(step * strip, strip)
            total = jnp.exp(matmul(left_e[at, :], right)) * matmul(left_r[at, :], right_r[...])
            add_strip(at, total)

    @pl.when(jnp.logical_not(near))
    def separate():
        stack = [u + log_cols for u in us] + adjs_rows
        stack.append(jnp.zeros((128 - len(stack), count_rows), F32))
        cols_rows[...] = jnp.concatenate(stack, axis=0).T
        strip = 128

        def block(step, carry):
            at = pl.ds(pl.multiple_of(step * strip, strip), strip)
            left = jnp.concatenate([ax0[at, :], ax1[at, :].astype(BF16)], axis=1)
            inner = matmul(left, by[...])
            columns = cols_rows[at, :]
            total = jnp.zeros_like(inner)
            for k in range(ITERS):
                base = inner + columns[:, k : k + 1]
                total += jnp.exp(base + vs[k + 1]) * adjs_cols[k]
                total += jnp.exp(base + (vs[k] + shift)) * columns[:, ITERS + k : ITERS + k + 1]
            add_strip(at, total)
            return carry

        lax.fori_loop(0, count_rows // strip, block, 0)

    def finish(points, sums):
        mixed = sums[0:dim] + sums[dim : 2 * dim] + sums[2 * dim : 3 * dim]
        return 2.0 * (points * sums[3 * dim : 3 * dim + 1] - mixed)

    for value, held, outs, axis in (
        (finish(x, gx[...].T), all_x, outs_x, "col"),
        (finish(y, gy[...]), all_y, outs_y, "row"),
    ):
        share = held.shape[2]
        for p in range(held.shape[0]):
            held[p] = value[:, p * share : (p + 1) * share]
        me = lax.axis_index(axis)
        for s, out in enumerate(outs):
            out[...] = held[me ^ s]


def swap(value, axis, distance):
    return lax.ppermute(value, axis, [(d, d ^ distance) for d in range(lax.axis_size(axis))])


def exchange(part, axis, join):
    size = lax.axis_size(axis)
    assert size & (size - 1) == 0
    distance = 1
    got = (part,)
    while distance < size:
        if len(got) > 1:
            (part,) = call(functools.partial(join_body, join), [shape(part.shape)], len(got))(*got)
        got = (part, swap(part, axis, distance))
        distance *= 2
    return got


def scatter(pieces, axis):
    got = [pieces[0]] + [swap(pieces[s], axis, s) for s in range(1, len(pieces))]
    return sum(got[1:], got[0])


def slot(column, lane, state):
    return jnp.where(lax.broadcasted_iota(jnp.int32, state.shape, 1) == lane, column, state)


def left_strip(left0, left1, at, pot):
    strip = left1[at, :]
    for lane, part in enumerate(split3(jnp.broadcast_to(pot, strip.shape))):
        strip = slot(part, lane, strip)
    return jnp.concatenate([left0[at, :], strip.astype(BF16)], axis=1)


def halves(value):
    return sum(value[:, p : p + 128] for p in range(0, value.shape[1], 128))


def octets(value):
    return jnp.sum(value.reshape(value.shape[0] // 8, 8, value.shape[1]), axis=0)


SWEEP = 1024
ROWS = 128


def wide_steps(total, body):
    wide = min(SWEEP, total)

    def step(index, carry):
        body(pl.multiple_of(index * wide, wide), wide)
        return carry

    lax.fori_loop(0, total // wide, step, 0)


def score_steps(left, right, rows, store):
    def body(start, wide):
        for c in range(0, wide, CHUNK):
            at = pl.ds(start + c, CHUNK)
            full = jnp.concatenate([right[0:128, at], rows[:, at], right[144:DEPTH, at]], axis=0)
            store(matmul(left, full), at)

    wide_steps(right.shape[1], body)


def weighted_rows(held, times, out):
    count, total = held.shape

    def body(start, wide):
        tiles = wide // 128
        sums = [None] * tiles
        for r in range(0, count, ROWS):
            factor = times[r : r + ROWS, :]
            for p in range(tiles):
                part = octets(held[r : r + ROWS, pl.ds(start + 128 * p, 128)] * factor)
                sums[p] = part if sums[p] is None else sums[p] + part
        for p in range(tiles):
            out[:, pl.ds(start + 128 * p, 128)] = jnp.sum(sums[p], axis=0, keepdims=True)

    wide_steps(total, body)


def sweep(left0, left1, right, state, state_out, out, held, rows, sums, pot_lane, weigh, put, factor):
    every = pl.ds(0, left0.shape[0])
    old = state[...]
    left = left_strip(left0, left1, every, old[:, pot_lane : pot_lane + 1])
    sums[...] = jnp.zeros_like(sums)

    def store(scores, at):
        power = jnp.exp(scores)
        held[:, at] = power
        sums[...] += halves(weigh(power, at))

    score_steps(left, right, rows, store)
    column = jnp.sum(sums[...], axis=1, keepdims=True)
    state_out[...] = put(old, column)
    sums[...] = jnp.broadcast_to(factor(old, column), sums.shape)
    weighted_rows(held, sums, out)


def gather_body(n_x, n_y, *refs):
    xs, ys = refs[:n_x], refs[n_x : n_x + n_y]
    ay0, ay1, bx, state, out = refs[n_x + n_y :]
    x = jnp.concatenate([r[...] for r in xs], axis=1)
    y = jnp.concatenate([r[...] for r in ys], axis=1)
    bx[...] = factors(x * (2.0 * SCALE), X_ORDER).astype(BF16)
    turned = factors(y, Y_ORDER).T
    start = -SCALE * jnp.sum(y * y, axis=0, keepdims=True)
    ay0[...] = turned[:, :128].astype(BF16)
    wide = y.shape[1]
    high, mid, low = split3(start)
    one = jnp.ones((3, wide), F32)
    extra = jnp.concatenate([high, mid, low, one, jnp.zeros((122, wide), F32)], axis=0).T
    with_start = turned[:, 128:] + jnp.where(lax.broadcasted_iota(jnp.int32, extra.shape, 1) < 3, extra, 0.0)
    ay1[...] = turned[:, 128:] + jnp.where(lax.broadcasted_iota(jnp.int32, extra.shape, 1) < 3, 0.0, extra)
    state[...] = jnp.concatenate([start, jnp.zeros((127, wide), F32)], axis=0).T
    left = jnp.concatenate([ay0[...], with_start.astype(BF16)], axis=1)
    one = jnp.concatenate([jnp.ones((3, CHUNK), F32), jnp.zeros((13, CHUNK), F32)], axis=0).astype(BF16)

    def step(index, carry):
        at = pl.ds(pl.multiple_of(index * CHUNK, CHUNK), CHUNK)
        full = jnp.concatenate([bx[0:128, at], one, bx[144:DEPTH, at]], axis=0)
        scores = matmul(left, full)
        top = jnp.max(scores, axis=0, keepdims=True)
        out[:, at] = top + jnp.log(jnp.sum(jnp.exp(scores - top), axis=0, keepdims=True))
        return carry

    lax.fori_loop(0, bx.shape[1] // CHUNK, step, 0)


def opening_body(n_got, log_rows, log_cols, left0, left1, right, state, *refs):
    got, (u_out, state_out, out, held, rows, sums) = refs[:n_got], refs[n_got:]
    u = -log_rows - join_lse(got)
    u_out[...] = u
    rows[...] = right_rows(u)
    left = jnp.concatenate([left0[...], left1[...].astype(BF16)], axis=1)
    sums[...] = jnp.full_like(sums, -jnp.inf)

    def store(scores, at):
        held[:, at] = scores
        parts = [scores[:, p : p + 128] for p in range(0, scores.shape[1], 128)]
        sums[...] = jnp.maximum(sums[...], functools.reduce(jnp.maximum, parts))

    score_steps(left, right, rows, store)
    top = jnp.max(sums[...], axis=1, keepdims=True)
    sums[...] = jnp.zeros_like(sums)

    def raise_(start, wide):
        for c in range(0, wide, CHUNK):
            at = pl.ds(start + c, CHUNK)
            power = jnp.exp(held[:, at] - top)
            held[:, at] = power
            sums[...] += halves(power)

    wide_steps(right.shape[1], raise_)
    column = jnp.sum(sums[...], axis=1, keepdims=True)
    state_out[...] = slot(-log_cols - (top + jnp.log(column)), 1, state[...])
    sums[...] = jnp.broadcast_to(math.exp(-log_cols) / column, sums.shape)
    weighted_rows(held, sums, out)


def iteration_body(k, n_got, log_rows, log_cols, left0, left1, right, state, u_old, *refs):
    got, (u_out, state_out, out, held, rows, sums) = refs[:n_got], refs[n_got:]
    u = u_old[...] - (log_rows + jnp.log(join_sum(got)))
    u_out[...] = u
    rows[...] = right_rows(u)

    def put(old, column):
        pot = old[:, k - 1 : k] - (log_cols + jnp.log(column))
        return slot(math.exp(log_cols) * column, 8 + k, slot(pot, k, old))

    def factor(old, column):
        return math.exp(-log_cols) / column

    sweep(
        left0, left1, right, state, state_out, out, held, rows, sums, k - 1, lambda power, at: power, put, factor
    )


def adjoint_body(k, n_got, log_rows, log_cols, left0, left1, right, state, u_ref, u_before, *refs):
    got, (adj_out, state_out, out, held, rows, sums) = refs[:n_got], refs[n_got:]
    if k == ITERS:
        adj_out[...] = 1.0 - math.exp(log_cols) * join_sum(got)
    else:
        adj_out[...] = -join_sum(got)
    u = u_ref[...]
    shift = math.exp(log_rows - log_cols)
    rows[...] = right_rows(u + log_cols)

    def put(old, column):
        return slot(-shift * old[:, 8 + k : 9 + k] * column, 16 + k - 1, old)

    def factor(old, column):
        sigma = old[:, 8 + k : 9 + k]
        return -shift * sigma * sigma * column

    def weigh(power, at):
        return power * adj_out[:, at]

    sweep(left0, left1, right, state, state_out, out, held, rows, sums, k, weigh, put, factor)
    out[...] = out[...] * jnp.exp(u_before[...] - u)


def closing_body(n_got, log_cols, log_rows, n_col, n_row, ax0, ax1, by, x_ref, y_ref, state, *refs):
    count_rows, count_cols = x_ref.shape[1], y_ref.shape[1]
    us = [r[:, :count_rows] for r in refs[:ITERS]]
    adjs_rows = [r[:, :count_rows] for r in refs[ITERS : 2 * ITERS - 1]]
    refs = refs[2 * ITERS - 1 :]
    got, refs = refs[:n_got], refs[n_got:]
    first = -join_sum([r[:, :count_rows] for r in got])
    turned = state[0:count_cols, :].T
    vs = [turned[k : k + 1] for k in range(ITERS + 1)]
    adjs_cols = [turned[16 + k : 17 + k] for k in range(1, ITERS)] + [jnp.ones((1, count_cols), F32)]
    adjs_rows = [first] + adjs_rows
    gradient(log_cols, log_rows, n_col, n_row, ax0, ax1, by, x_ref, y_ref, us, vs, adjs_rows, adjs_cols, refs)


def own_body(x_hbm, y_hbm, ax0, ax1, by, x_ref, y_ref, sems):
    copies = [
        pltpu.make_async_copy(x_hbm, x_ref, sems.at[0]),
        pltpu.make_async_copy(y_hbm, y_ref, sems.at[1]),
    ]
    for copy in copies:
        copy.start()
    for copy in copies:
        copy.wait()
    turned = factors(x_ref[...] * (2.0 * SCALE), X_ORDER).T
    ax0[...] = turned[:, :128].astype(BF16)
    ax1[...] = turned[:, 128:]
    by[...] = factors(y_ref[...], Y_ORDER).astype(BF16)


def gradient_scratch(dim, count_rows, count_cols, n_col, n_row):
    return [
        pltpu.VMEM((count_rows, 128), F32),
        pltpu.VMEM((128, count_rows), BF16),
        pltpu.VMEM((count_cols, 128), BF16),
        pltpu.VMEM((count_rows, 128), F32),
        pltpu.VMEM((128, count_cols), F32),
        pltpu.VMEM((count_rows, DEPTH), BF16),
        pltpu.VMEM((count_rows, 128), BF16),
        pltpu.VMEM((128, count_cols), BF16),
        pltpu.VMEM((n_col, dim, count_rows // n_col), F32),
        pltpu.VMEM((n_row, dim, count_cols // n_row), F32),
    ]


def repeated(x, y):
    dim, count_rows = x.shape
    count_cols = y.shape[1]
    n_row, n_col = lax.axis_size("row"), lax.axis_size("col")
    all_rows, held_cols = count_rows * n_row, count_cols
    log_rows, log_cols = math.log(all_rows), math.log(count_cols * n_col)
    row, col = (1, all_rows), (1, held_cols)

    xs = [x] + [swap(x, "row", s) for s in range(1, n_row)]
    ys = [y]
    ax0, ax1, by, x, y = pl.pallas_call(
        own_body,
        out_shape=[
            shape((count_rows, 128), BF16),
            shape((count_rows, 128)),
            shape((DEPTH, count_cols), BF16),
            shape(x.shape),
            shape(y.shape),
        ],
        in_specs=[pl.BlockSpec(memory_space=pltpu.HBM)] * 2,
        out_specs=vmem(5),
        scratch_shapes=[pltpu.SemaphoreType.DMA((2,))],
        compiler_params=pltpu.CompilerParams(vmem_limit_bytes=VMEM_LIMIT),
    )(x, y)
    ay0, ay1, bx, state, part = call(
        functools.partial(gather_body, n_row, 1),
        [
            shape((held_cols, 128), BF16),
            shape((held_cols, 128)),
            shape((DEPTH, all_rows), BF16),
            shape((held_cols, 128)),
            shape(row),
        ],
        n_row + 1,
    )(*xs, *ys)

    scratch = [
        pltpu.VMEM((held_cols, all_rows), F32),
        pltpu.VMEM((16, all_rows), BF16),
        pltpu.VMEM((held_cols, 128), F32),
    ]
    results = [shape(row), shape((held_cols, 128)), shape(row)]
    got = exchange(part, "col", join_lse)
    us = []
    u, state, part = call(
        functools.partial(opening_body, len(got), log_rows, log_cols), results, 4 + len(got), scratch
    )(ay0, ay1, bx, state, *got)
    us.append(u)
    for k in range(2, ITERS + 1):
        got = exchange(part, "col", join_sum)
        u, state, part = call(
            functools.partial(iteration_body, k, len(got), log_rows, log_cols), results, 5 + len(got), scratch
        )(ay0, ay1, bx, state, u, *got)
        us.append(u)
    adjs_rows = []
    for k in range(ITERS, 1, -1):
        got = exchange(part, "col", join_sum)
        adj, state, part = call(
            functools.partial(adjoint_body, k, len(got), log_rows, log_cols),
            results,
            6 + len(got),
            scratch,
        )(ay0, ay1, bx, state, us[k - 1], us[k - 2], *got)
        adjs_rows.insert(0, adj)
    got = exchange(part, "col", join_sum)
    outs = call(
        functools.partial(closing_body, len(got), log_cols, log_rows, n_col, n_row),
        [shape((dim, count_rows // n_col))] * n_col + [shape((dim, count_cols // n_row))] * n_row,
        6 + 2 * ITERS - 1 + len(got),
        gradient_scratch(dim, count_rows, count_cols, n_col, n_row),
    )(ax0, ax1, by, x, y, state, *us, *adjs_rows, *got)
    return scatter(outs[:n_col], "col").T, scatter(outs[n_col:], "row").T


REPEAT_PAIRS = 1 << 23


def on_device(x_points, y_points):
    x = x_points.T
    y = y_points.T
    n_row, n_col = lax.axis_size("row"), lax.axis_size("col")
    if ITERS > 1 and x.shape[1] * n_row * y.shape[1] <= REPEAT_PAIRS:
        return repeated(x, y)
    return shared(x, y)


def shared(x, y):
    dim, count_rows = x.shape
    count_cols = y.shape[1]
    n_row, n_col = lax.axis_size("row"), lax.axis_size("col")
    log_rows = math.log(count_rows * n_row)
    log_cols = math.log(count_cols * n_col)
    row, col = (1, count_rows), (1, count_cols)

    ax0, ax1, ay0, ay1, bx, by, start, part, x, y = pl.pallas_call(
        prepare_body,
        out_shape=[
            shape((count_rows, 128), BF16),
            shape((count_rows, 128)),
            shape((count_cols, 128), BF16),
            shape((count_cols, 128)),
            shape((DEPTH, count_rows), BF16),
            shape((DEPTH, count_cols), BF16),
            shape(col),
            shape(row),
            shape(x.shape),
            shape(y.shape),
        ],
        in_specs=[pl.BlockSpec(memory_space=pltpu.HBM)] * 2,
        out_specs=vmem(10),
        scratch_shapes=[pltpu.SemaphoreType.DMA((2,))],
        compiler_params=pltpu.CompilerParams(vmem_limit_bytes=VMEM_LIMIT),
    )(x, y)

    pots_rows, pots_cols = [], [start]
    for k in range(ITERS):
        got = exchange(part, "col", join_lse)
        pot, part = call(functools.partial(forward_body, -log_rows), [shape(row), shape(col)], 3 + len(got))(
            ax0, ax1, by, *got
        )
        pots_rows.append(pot)
        got = exchange(part, "row", join_lse)
        if k < ITERS - 1:
            pot, part = call(functools.partial(forward_body, -log_cols), [shape(col), shape(row)], 3 + len(got))(
                ay0, ay1, bx, *got
            )
            pots_cols.append(pot)
    pot, part = call(functools.partial(turn_body, -log_cols, log_cols), [shape(col), shape(row)], 4 + len(got))(
        ay0, ay1, bx, pots_rows[-1], *got
    )
    pots_cols.append(pot)

    adjs_rows, adjs_cols = [], []
    for k in reversed(range(1, ITERS)):
        leading = 1.0 if k == ITERS - 1 else 0.0
        got = exchange(part, "col", join_sum)
        adj, part = call(functools.partial(backward_body, leading, log_rows), [shape(row), shape(col)], 5 + len(got))(
            ax0, ax1, by, pots_rows[k], pots_cols[k], *got
        )
        adjs_rows.insert(0, adj)
        got = exchange(part, "row", join_sum)
        adj, part = call(functools.partial(backward_body, 0.0, log_cols), [shape(col), shape(row)], 5 + len(got))(
            ay0, ay1, bx, pots_cols[k], pots_rows[k - 1], *got
        )
        adjs_cols.insert(0, adj)
    got = exchange(part, "col", join_sum)

    share_x, share_y = count_rows // n_col, count_cols // n_row
    outs = call(
        functools.partial(gradient_body, dim, log_cols, log_rows, len(got), n_col, n_row),
        [shape((dim, share_x))] * n_col + [shape((dim, share_y))] * n_row,
        5 + 4 * ITERS - 1 + len(got),
        gradient_scratch(dim, count_rows, count_cols, n_col, n_row),
    )(ax0, ax1, by, x, y, *pots_rows, *pots_cols, *adjs_rows, *adjs_cols, *got)
    grad_x = scatter(outs[:n_col], "col")
    grad_y = scatter(outs[n_col:], "row")
    return (grad_x.T, grad_y.T)


def solution(mesh):
    in_specs = (P(("groups", "row"), None), P(("groups", "col"), None))
    out_specs = (P(("groups", "row", "col"), None), P(("groups", "col", "row"), None))
    return jax.shard_map(
        on_device, mesh=mesh, in_specs=in_specs, out_specs=out_specs, check_vma=False
    )
```

```python
import functools
import math

import jax
import jax.numpy as jnp
from jax import lax
from jax.experimental import pallas as pl
from jax.experimental.pallas import tpu as pltpu
from jax.sharding import PartitionSpec as P

ITERS = 5
EPSILON = 0.05
SCALE = 1.0 / EPSILON
DEPTH = 256
CHUNK = 256
F32 = jnp.float32
BF16 = jnp.bfloat16
VMEM_LIMIT = 48 * 1024 * 1024


def split3(v):
    high = v.astype(BF16).astype(F32)
    rest = v - high
    mid = rest.astype(BF16).astype(F32)
    low = (rest - mid).astype(BF16).astype(F32)
    return high, mid, low


def vmem(count):
    return [pl.BlockSpec(memory_space=pltpu.VMEM)] * count


def call(body, outs, count, scratch=()):
    return pl.pallas_call(
        body,
        out_shape=outs,
        in_specs=vmem(count),
        out_specs=vmem(len(outs)),
        scratch_shapes=list(scratch),
        compiler_params=pltpu.CompilerParams(vmem_limit_bytes=VMEM_LIMIT),
    )


def shape(dims, dtype=F32):
    return jax.ShapeDtypeStruct(dims, dtype)


def factors(points, order):
    parts = split3(points)
    width = points.shape[1]
    blocks = [parts[o] for o in order]
    zero16 = jnp.zeros((16, width), F32)
    tail = jnp.zeros((DEPTH - 144 - 2 * points.shape[0], width), F32)
    return jnp.concatenate(blocks[:4] + [zero16] + blocks[4:] + [tail], axis=0)


X_ORDER = (0, 0, 1, 0, 2, 1)
Y_ORDER = (0, 1, 0, 2, 0, 1)


def prepare_body(x_hbm, y_hbm, ax0, ax1, ay0, ay1, bx, by, start_ref, out, x_ref, y_ref, sems):
    copies = [
        pltpu.make_async_copy(x_hbm, x_ref, sems.at[0]),
        pltpu.make_async_copy(y_hbm, y_ref, sems.at[1]),
    ]
    for copy in copies:
        copy.start()
    for copy in copies:
        copy.wait()
    x = x_ref[...]
    y = y_ref[...]
    xf = factors(x * (2.0 * SCALE), X_ORDER)
    yf = factors(y, Y_ORDER)
    for factor, left0, left1, right in ((xf, ax0, ax1, bx), (yf, ay0, ay1, by)):
        right[...] = factor.astype(BF16)
        turned = factor.T
        left0[...] = turned[:, :128].astype(BF16)
        left1[...] = turned[:, 128:]
    start = -SCALE * jnp.sum(y * y, axis=0, keepdims=True)
    start_ref[...] = start
    left, unused = left_factor(ay0, ay1, start)
    partial_lse(left, bx, out)


def left_factor(left0, left1, pot, adj=None):
    width = pot.shape[1]
    high, mid, low = split3(pot)
    one = jnp.ones((1, width), F32)
    rows = [high, mid, low, one, one, one, jnp.zeros_like(one)]
    rows.append(jnp.zeros_like(one) if adj is None else adj)
    rows.append(jnp.zeros((120, width), F32))
    turned = jnp.concatenate(rows, axis=0).T
    column = None
    if adj is not None:
        column = turned[:, 7:8]
        lane = lax.broadcasted_iota(jnp.int32, turned.shape, 1)
        turned = jnp.where(lane == 7, 0.0, turned)
    return jnp.concatenate([left0[...], (left1[...] + turned).astype(BF16)], axis=1), column


def right_rows(pot):
    width = pot.shape[1]
    one = jnp.ones((3, width), F32)
    high, mid, low = split3(pot)
    return jnp.concatenate([one, high, mid, low, jnp.zeros((10, width), F32)], axis=0).astype(BF16)


def right_chunk(right, rows, at, wide):
    return jnp.concatenate(
        [right[0:128, at : at + wide], rows[:, at : at + wide], right[144:DEPTH, at : at + wide]], axis=0
    )


def matmul(a, b):
    return jnp.dot(a, b, preferred_element_type=F32)


def partial_lse(left, right, out):
    width = right.shape[1]
    rows = right_rows(jnp.zeros((1, width), F32))
    wide = min(CHUNK, width)
    for at in range(0, width, wide):
        scores = matmul(left, right_chunk(right, rows, at, wide))
        top = jnp.max(scores, axis=0, keepdims=True)
        total = jnp.sum(jnp.exp(scores - top), axis=0, keepdims=True)
        out[:, at : at + wide] = top + jnp.log(total)


def join_lse(parts):
    parts = [p[...] for p in parts]
    top = functools.reduce(jnp.maximum, parts)
    return top + jnp.log(sum(jnp.exp(p - top) for p in parts))


def join_sum(parts):
    return sum(p[...] for p in parts)


def join_body(join, *refs):
    refs[-1][...] = join(refs[:-1])


def forward_body(log_mass, left0, left1, right, *refs):
    got, (pot_out, out) = refs[:-2], refs[-2:]
    pot = log_mass - join_lse(got)
    pot_out[...] = pot
    left, unused = left_factor(left0, left1, pot)
    partial_lse(left, right, out)


def weighted_sums(left, column, right, rows, out):
    width = right.shape[1]
    wide = min(CHUNK, width)
    for at in range(0, width, wide):
        scores = matmul(left, right_chunk(right, rows, at, wide))
        out[:, at : at + wide] = jnp.sum(jnp.exp(scores) * column, axis=0, keepdims=True)


def turn_body(log_mass, log_scale, left0, left1, right, pot_right, *refs):
    got, (pot_out, out) = refs[:-2], refs[-2:]
    pot = log_mass - join_lse(got)
    pot_out[...] = pot
    left, column = left_factor(left0, left1, pot, jnp.ones_like(pot))
    weighted_sums(left, column, right, right_rows(pot_right[...] + log_scale), out)


def backward_body(leading, log_scale, left0, left1, right, pot_left, pot_right, *refs):
    got, (adj_out, out) = refs[:-2], refs[-2:]
    adj = leading - join_sum(got)
    adj_out[...] = adj
    left, column = left_factor(left0, left1, pot_left[...], adj)
    weighted_sums(left, column, right, right_rows(pot_right[...] + log_scale), out)


SPREAD = 20.0
STRIP = 256


def gradient_body(dim, log_cols, log_rows, n_got, n_col, n_row, ax0, ax1, by, x_ref, y_ref, *refs):
    pots_rows = refs[:ITERS]
    pots_cols = refs[ITERS : 2 * ITERS + 1]
    adjs_rows = refs[2 * ITERS + 1 : 3 * ITERS]
    adjs_cols = refs[3 * ITERS : 4 * ITERS - 1]
    refs = refs[4 * ITERS - 1 :]
    got, refs = refs[:n_got], refs[n_got:]
    us = [p[...] for p in pots_rows]
    vs = [p[...] for p in pots_cols]
    first = (1.0 if ITERS == 1 else 0.0) - join_sum(got)
    adjs_rows = [first] + [a[...] for a in adjs_rows]
    adjs_cols = [a[...] for a in adjs_cols] + [jnp.ones(vs[0].shape, F32)]
    gradient(log_cols, log_rows, n_col, n_row, ax0, ax1, by, x_ref, y_ref, us, vs, adjs_rows, adjs_cols, refs)


def gradient(log_cols, log_rows, n_col, n_row, ax0, ax1, by, x_ref, y_ref, us, vs, adjs_rows, adjs_cols, refs):
    outs_x, outs_y = refs[:n_col], refs[n_col : n_col + n_row]
    cols_rows, x_parts, y_parts, gx, gy, left_e, left_r, right_r, all_x, all_y = refs[n_col + n_row :]
    dim, count_rows = x_ref.shape
    count_cols = y_ref.shape[1]
    shift = log_rows - log_cols

    x = x_ref[...]
    y = y_ref[...]
    one = jnp.ones((1, count_cols), F32)
    pad = jnp.zeros((31, count_cols), F32)
    y_parts[...] = jnp.concatenate(list(split3(y)) + [one, pad], axis=0).T.astype(BF16)
    one = jnp.ones((1, count_rows), F32)
    pad = jnp.zeros((31, count_rows), F32)
    x_parts[...] = jnp.concatenate(list(split3(x)) + [one, pad], axis=0).astype(BF16)
    gy[...] = jnp.zeros_like(gy)

    far_u = functools.reduce(jnp.maximum, [jnp.abs(u - us[-1]) for u in us])
    far_v = functools.reduce(jnp.maximum, [jnp.abs(v - vs[-1]) for v in vs])
    near = jnp.maximum(jnp.max(far_u), jnp.max(far_v)) < SPREAD

    def add_strip(at, total):
        upper = total.astype(BF16)
        lower = (total - upper.astype(F32)).astype(BF16)
        gx[at, :] = matmul(upper, y_parts[...]) + matmul(lower, y_parts[...])
        gy[...] += matmul(x_parts[:, at], upper) + matmul(x_parts[:, at], lower)

    @pl.when(near)
    def factored():
        alpha = [jnp.exp(u - us[-1]) for u in us]
        beta = [jnp.exp(v - vs[-1]) for v in vs]
        p_rows = alpha + [a * adj for a, adj in zip(alpha, adjs_rows)]
        q_rows = [b * adj for b, adj in zip(beta[1:], adjs_cols)] + [b * math.exp(shift) for b in beta[:-1]]
        fill = 16 - 2 * ITERS
        p_split = split3(jnp.concatenate(p_rows + [jnp.zeros((fill, count_rows), F32)], axis=0))
        q_split = split3(jnp.concatenate(q_rows + [jnp.zeros((fill, count_cols), F32)], axis=0))
        tail = [jnp.zeros((32, count_rows), F32)]
        left_r[...] = jnp.concatenate([p_split[o] for o in X_ORDER] + tail, axis=0).T.astype(BF16)
        tail = [jnp.zeros((32, count_cols), F32)]
        right_r[...] = jnp.concatenate([q_split[o] for o in Y_ORDER] + tail, axis=0).astype(BF16)
        left, unused = left_factor(ax0, ax1, us[-1] + log_cols)
        left_e[...] = left
        right = right_chunk(by, right_rows(vs[-1]), 0, count_cols)
        strip = min(STRIP, count_rows)
        for step in range(count_rows // strip):
            at = pl.ds(step * strip, strip)
            total = jnp.exp(matmul(left_e[at, :], right)) * matmul(left_r[at, :], right_r[...])
            add_strip(at, total)

    @pl.when(jnp.logical_not(near))
    def separate():
        stack = [u + log_cols for u in us] + adjs_rows
        stack.append(jnp.zeros((128 - len(stack), count_rows), F32))
        cols_rows[...] = jnp.concatenate(stack, axis=0).T
        strip = 128

        def block(step, carry):
            at = pl.ds(pl.multiple_of(step * strip, strip), strip)
            left = jnp.concatenate([ax0[at, :], ax1[at, :].astype(BF16)], axis=1)
            inner = matmul(left, by[...])
            columns = cols_rows[at, :]
            total = jnp.zeros_like(inner)
            for k in range(ITERS):
                base = inner + columns[:, k : k + 1]
                total += jnp.exp(base + vs[k + 1]) * adjs_cols[k]
                total += jnp.exp(base + (vs[k] + shift)) * columns[:, ITERS + k : ITERS + k + 1]
            add_strip(at, total)
            return carry

        lax.fori_loop(0, count_rows // strip, block, 0)

    def finish(points, sums):
        mixed = sums[0:dim] + sums[dim : 2 * dim] + sums[2 * dim : 3 * dim]
        return 2.0 * (points * sums[3 * dim : 3 * dim + 1] - mixed)

    for value, held, outs, axis in (
        (finish(x, gx[...].T), all_x, outs_x, "col"),
        (finish(y, gy[...]), all_y, outs_y, "row"),
    ):
        share = held.shape[2]
        for p in range(held.shape[0]):
            held[p] = value[:, p * share : (p + 1) * share]
        me = lax.axis_index(axis)
        for s, out in enumerate(outs):
            out[...] = held[me ^ s]


def swap(value, axis, distance):
    return lax.ppermute(value, axis, [(d, d ^ distance) for d in range(lax.axis_size(axis))])


def exchange(part, axis, join):
    size = lax.axis_size(axis)
    assert size & (size - 1) == 0
    distance = 1
    got = (part,)
    while distance < size:
        if len(got) > 1:
            (part,) = call(functools.partial(join_body, join), [shape(part.shape)], len(got))(*got)
        got = (part, swap(part, axis, distance))
        distance *= 2
    return got


def scatter(pieces, axis):
    got = [pieces[0]] + [swap(pieces[s], axis, s) for s in range(1, len(pieces))]
    return sum(got[1:], got[0])


def slot(column, lane, state):
    return jnp.where(lax.broadcasted_iota(jnp.int32, state.shape, 1) == lane, column, state)


def left_strip(left0, left1, at, pot):
    strip = left1[at, :]
    for lane, part in enumerate(split3(jnp.broadcast_to(pot, strip.shape))):
        strip = slot(part, lane, strip)
    return jnp.concatenate([left0[at, :], strip.astype(BF16)], axis=1)


def halves(value):
    return sum(value[:, p : p + 128] for p in range(0, value.shape[1], 128))


def octets(value):
    return jnp.sum(value.reshape(value.shape[0] // 8, 8, value.shape[1]), axis=0)


SWEEP = 256


def sweep(left_of, right, rows, out, held, acc, times, store, close):
    strip, wide_all = held.shape[1:]
    strips = times.shape[0]
    for s in range(strips + 1):
        at = slice(s * strip, (s + 1) * strip)
        left = left_of(at) if s < strips else None
        sums = None
        for c in range(0, wide_all, CHUNK):
            place = slice(c, c + CHUNK)
            if s < strips:
                sums = store(held.at[s % 2], matmul(left, right_chunk(right, rows, c, CHUNK)), place, sums)
            if s > 0:
                factor = times[s - 1]
                part = octets(held[(s - 1) % 2, :, place] * jnp.concatenate([factor] * (CHUNK // 128), axis=1))
                if s > 1:
                    part += acc[:, place]
                if s < strips:
                    acc[:, place] = part
                else:
                    out[:, place] = jnp.sum(part, axis=0, keepdims=True)
        if s < strips:
            times[s] = jnp.broadcast_to(close(at, sums, held.at[s % 2]), times.shape[1:])


def exponentials(weigh):
    def store(held, scores, place, sums):
        power = jnp.exp(scores)
        held[:, place] = power
        part = halves(weigh(power, place))
        return part if sums is None else sums + part

    return store


def prepare_own_body(x_hbm, y_hbm, ax0, ax1, ay0, ay1, by, state, out, x_ref, y_ref, bx, sems):
    copies = [
        pltpu.make_async_copy(x_hbm, x_ref, sems.at[0]),
        pltpu.make_async_copy(y_hbm, y_ref, sems.at[1]),
    ]
    for copy in copies:
        copy.start()
    for copy in copies:
        copy.wait()
    x = x_ref[...]
    y = y_ref[...]
    xf = factors(x * (2.0 * SCALE), X_ORDER)
    yf = factors(y, Y_ORDER)
    for factor, left0, left1, right in ((xf, ax0, ax1, bx), (yf, ay0, ay1, by)):
        right[...] = factor.astype(BF16)
        turned = factor.T
        left0[...] = turned[:, :128].astype(BF16)
        left1[...] = turned[:, 128:]
    start = -SCALE * jnp.sum(y * y, axis=0, keepdims=True)
    state[...] = jnp.concatenate([start, jnp.zeros((127, y.shape[1]), F32)], axis=0).T
    left, unused = left_factor(ay0, ay1, start)
    partial_lse(left, bx, out)
    lane = lax.broadcasted_iota(jnp.int32, ay1.shape, 1)
    ay1[...] = jnp.where((lane >= 3) & (lane < 6), 1.0, ay1[...])


def first_pot_body(log_rows, *refs):
    refs[-1][...] = -log_rows - join_lse(refs[:-1])


def opening_body(n_row, log_rows, log_cols, left0, left1, state, *refs):
    xs, us = refs[:n_row], refs[n_row : 2 * n_row]
    right, u_out, state_out, out, held, acc, times = refs[2 * n_row :]
    x = jnp.concatenate([r[...] for r in xs], axis=1)
    right[...] = factors(x * (2.0 * SCALE), X_ORDER).astype(BF16)
    u = jnp.concatenate([r[...] for r in us], axis=1)
    u_out[...] = u

    def left_of(at):
        return jnp.concatenate([left0[at, :], left1[at, :].astype(BF16)], axis=1)

    def store(held, scores, place, tops):
        held[:, place] = scores
        for p in range(0, CHUNK, 128):
            part = scores[:, p : p + 128]
            tops = part if tops is None else jnp.maximum(tops, part)
        return tops

    def close(at, tops, held):
        top = jnp.max(tops, axis=1, keepdims=True)
        sums = None
        for c in range(0, held.shape[1], CHUNK):
            place = slice(c, c + CHUNK)
            power = jnp.exp(held[:, place] - top)
            held[:, place] = power
            part = halves(power)
            sums = part if sums is None else sums + part
        column = jnp.sum(sums, axis=1, keepdims=True)
        state_out[at, :] = slot(-log_cols - (top + jnp.log(column)), 1, state[at, :])
        return math.exp(-log_cols) / column

    sweep(left_of, right, right_rows(u), out, held, acc, times, store, close)


def iteration_body(k, n_got, log_rows, log_cols, left0, left1, right, state, u_old, *refs):
    got, (u_out, state_out, out, held, acc, times) = refs[:n_got], refs[n_got:]
    u = u_old[...] - (log_rows + jnp.log(join_sum(got)))
    u_out[...] = u

    def left_of(at):
        return left_strip(left0, left1, at, state[at, k - 1 : k])

    def close(at, sums, held):
        column = jnp.sum(sums, axis=1, keepdims=True)
        old = state[at, :]
        pot = old[:, k - 1 : k] - (log_cols + jnp.log(column))
        state_out[at, :] = slot(math.exp(log_cols) * column, 8 + k, slot(pot, k, old))
        return math.exp(-log_cols) / column

    store = exponentials(lambda power, place: power)
    sweep(left_of, right, right_rows(u), out, held, acc, times, store, close)


def adjoint_body(k, n_got, log_rows, log_cols, left0, left1, right, state, u_ref, u_before, *refs):
    got, (adj_out, state_out, out, held, acc, times) = refs[:n_got], refs[n_got:]
    if k == ITERS:
        adj_out[...] = 1.0 - math.exp(log_cols) * join_sum(got)
    else:
        adj_out[...] = -join_sum(got)
    u = u_ref[...]
    shift = math.exp(log_rows - log_cols)

    def left_of(at):
        return left_strip(left0, left1, at, state[at, k : k + 1])

    def close(at, sums, held):
        column = jnp.sum(sums, axis=1, keepdims=True)
        old = state[at, :]
        sigma = old[:, 8 + k : 9 + k]
        adj = -shift * sigma * column
        state_out[at, :] = slot(adj, 16 + k - 1, old)
        return sigma * adj

    store = exponentials(lambda power, place: power * adj_out[:, place])
    sweep(left_of, right, right_rows(u + log_cols), out, held, acc, times, store, close)
    out[...] = out[...] * jnp.exp(u_before[...] - u)


def closing_body(n_got, log_cols, log_rows, n_col, n_row, ax0, ax1, by, x_ref, y_ref, state, *refs):
    count_rows, count_cols = x_ref.shape[1], y_ref.shape[1]
    us = [r[:, :count_rows] for r in refs[:ITERS]]
    adjs_rows = [r[:, :count_rows] for r in refs[ITERS : 2 * ITERS - 1]]
    refs = refs[2 * ITERS - 1 :]
    got, refs = refs[:n_got], refs[n_got:]
    first = -join_sum([r[:, :count_rows] for r in got])
    turned = state[0:count_cols, :].T
    vs = [turned[k : k + 1] for k in range(ITERS + 1)]
    adjs_cols = [turned[16 + k : 17 + k] for k in range(1, ITERS)] + [jnp.ones((1, count_cols), F32)]
    adjs_rows = [first] + adjs_rows
    gradient(log_cols, log_rows, n_col, n_row, ax0, ax1, by, x_ref, y_ref, us, vs, adjs_rows, adjs_cols, refs)


def gradient_scratch(dim, count_rows, count_cols, n_col, n_row):
    return [
        pltpu.VMEM((count_rows, 128), F32),
        pltpu.VMEM((128, count_rows), BF16),
        pltpu.VMEM((count_cols, 128), BF16),
        pltpu.VMEM((count_rows, 128), F32),
        pltpu.VMEM((128, count_cols), F32),
        pltpu.VMEM((count_rows, DEPTH), BF16),
        pltpu.VMEM((count_rows, 128), BF16),
        pltpu.VMEM((128, count_cols), BF16),
        pltpu.VMEM((n_col, dim, count_rows // n_col), F32),
        pltpu.VMEM((n_row, dim, count_cols // n_row), F32),
    ]


def repeated(x, y):
    dim, count_rows = x.shape
    count_cols = y.shape[1]
    n_row, n_col = lax.axis_size("row"), lax.axis_size("col")
    all_rows, held_cols = count_rows * n_row, count_cols
    log_rows, log_cols = math.log(all_rows), math.log(count_cols * n_col)
    row, col = (1, all_rows), (1, held_cols)

    xs = [x] + [swap(x, "row", s) for s in range(1, n_row)]
    own = (1, count_rows)
    ax0, ax1, ay0, ay1, by, state, part, x, y = pl.pallas_call(
        prepare_own_body,
        out_shape=[
            shape((count_rows, 128), BF16),
            shape((count_rows, 128)),
            shape((count_cols, 128), BF16),
            shape((count_cols, 128)),
            shape((DEPTH, count_cols), BF16),
            shape((count_cols, 128)),
            shape(own),
            shape(x.shape),
            shape(y.shape),
        ],
        in_specs=[pl.BlockSpec(memory_space=pltpu.HBM)] * 2,
        out_specs=vmem(9),
        scratch_shapes=[pltpu.VMEM((DEPTH, count_rows), BF16), pltpu.SemaphoreType.DMA((2,))],
        compiler_params=pltpu.CompilerParams(vmem_limit_bytes=VMEM_LIMIT),
    )(x, y)
    got = exchange(part, "col", join_lse)
    (u,) = call(functools.partial(first_pot_body, log_rows), [shape(own)], len(got))(*got)
    u_blocks = [u] + [swap(u, "row", s) for s in range(1, n_row)]

    strip = min(SWEEP, held_cols)
    scratch = [
        pltpu.VMEM((2, strip, all_rows), F32),
        pltpu.VMEM((8, all_rows), F32),
        pltpu.VMEM((held_cols // strip, strip, 128), F32),
    ]
    results = [shape(row), shape((held_cols, 128)), shape(row)]
    us = []
    bx, u, state, part = call(
        functools.partial(opening_body, n_row, log_rows, log_cols),
        [shape((DEPTH, all_rows), BF16)] + results,
        3 + 2 * n_row,
        scratch,
    )(ay0, ay1, state, *xs, *u_blocks)
    us.append(u)
    for k in range(2, ITERS + 1):
        got = exchange(part, "col", join_sum)
        u, state, part = call(
            functools.partial(iteration_body, k, len(got), log_rows, log_cols), results, 5 + len(got), scratch
        )(ay0, ay1, bx, state, u, *got)
        us.append(u)
    adjs_rows = []
    for k in range(ITERS, 1, -1):
        got = exchange(part, "col", join_sum)
        adj, state, part = call(
            functools.partial(adjoint_body, k, len(got), log_rows, log_cols),
            results,
            6 + len(got),
            scratch,
        )(ay0, ay1, bx, state, us[k - 1], us[k - 2], *got)
        adjs_rows.insert(0, adj)
    got = exchange(part, "col", join_sum)
    outs = call(
        functools.partial(closing_body, len(got), log_cols, log_rows, n_col, n_row),
        [shape((dim, count_rows // n_col))] * n_col + [shape((dim, count_cols // n_row))] * n_row,
        6 + 2 * ITERS - 1 + len(got),
        gradient_scratch(dim, count_rows, count_cols, n_col, n_row),
    )(ax0, ax1, by, x, y, state, *us, *adjs_rows, *got)
    return scatter(outs[:n_col], "col").T, scatter(outs[n_col:], "row").T


REPEAT_PAIRS = 1 << 23


def on_device(x_points, y_points):
    x = x_points.T
    y = y_points.T
    n_row, n_col = lax.axis_size("row"), lax.axis_size("col")
    if ITERS > 1 and x.shape[1] * n_row * y.shape[1] <= REPEAT_PAIRS:
        return repeated(x, y)
    return shared(x, y)


def shared(x, y):
    dim, count_rows = x.shape
    count_cols = y.shape[1]
    n_row, n_col = lax.axis_size("row"), lax.axis_size("col")
    log_rows = math.log(count_rows * n_row)
    log_cols = math.log(count_cols * n_col)
    row, col = (1, count_rows), (1, count_cols)

    ax0, ax1, ay0, ay1, bx, by, start, part, x, y = pl.pallas_call(
        prepare_body,
        out_shape=[
            shape((count_rows, 128), BF16),
            shape((count_rows, 128)),
            shape((count_cols, 128), BF16),
            shape((count_cols, 128)),
            shape((DEPTH, count_rows), BF16),
            shape((DEPTH, count_cols), BF16),
            shape(col),
            shape(row),
            shape(x.shape),
            shape(y.shape),
        ],
        in_specs=[pl.BlockSpec(memory_space=pltpu.HBM)] * 2,
        out_specs=vmem(10),
        scratch_shapes=[pltpu.SemaphoreType.DMA((2,))],
        compiler_params=pltpu.CompilerParams(vmem_limit_bytes=VMEM_LIMIT),
    )(x, y)

    pots_rows, pots_cols = [], [start]
    for k in range(ITERS):
        got = exchange(part, "col", join_lse)
        pot, part = call(functools.partial(forward_body, -log_rows), [shape(row), shape(col)], 3 + len(got))(
            ax0, ax1, by, *got
        )
        pots_rows.append(pot)
        got = exchange(part, "row", join_lse)
        if k < ITERS - 1:
            pot, part = call(functools.partial(forward_body, -log_cols), [shape(col), shape(row)], 3 + len(got))(
                ay0, ay1, bx, *got
            )
            pots_cols.append(pot)
    pot, part = call(functools.partial(turn_body, -log_cols, log_cols), [shape(col), shape(row)], 4 + len(got))(
        ay0, ay1, bx, pots_rows[-1], *got
    )
    pots_cols.append(pot)

    adjs_rows, adjs_cols = [], []
    for k in reversed(range(1, ITERS)):
        leading = 1.0 if k == ITERS - 1 else 0.0
        got = exchange(part, "col", join_sum)
        adj, part = call(functools.partial(backward_body, leading, log_rows), [shape(row), shape(col)], 5 + len(got))(
            ax0, ax1, by, pots_rows[k], pots_cols[k], *got
        )
        adjs_rows.insert(0, adj)
        got = exchange(part, "row", join_sum)
        adj, part = call(functools.partial(backward_body, 0.0, log_cols), [shape(col), shape(row)], 5 + len(got))(
            ay0, ay1, bx, pots_cols[k], pots_rows[k - 1], *got
        )
        adjs_cols.insert(0, adj)
    got = exchange(part, "col", join_sum)

    share_x, share_y = count_rows // n_col, count_cols // n_row
    outs = call(
        functools.partial(gradient_body, dim, log_cols, log_rows, len(got), n_col, n_row),
        [shape((dim, share_x))] * n_col + [shape((dim, share_y))] * n_row,
        5 + 4 * ITERS - 1 + len(got),
        gradient_scratch(dim, count_rows, count_cols, n_col, n_row),
    )(ax0, ax1, by, x, y, *pots_rows, *pots_cols, *adjs_rows, *adjs_cols, *got)
    grad_x = scatter(outs[:n_col], "col")
    grad_y = scatter(outs[n_col:], "row")
    return (grad_x.T, grad_y.T)


def solution(mesh):
    in_specs = (P(("groups", "row"), None), P(("groups", "col"), None))
    out_specs = (P(("groups", "row", "col"), None), P(("groups", "col", "row"), None))
    return jax.shard_map(
        on_device, mesh=mesh, in_specs=in_specs, out_specs=out_specs, check_vma=False
    )
```

```python
import functools
import math

import jax
import jax.numpy as jnp
from jax import lax
from jax.experimental import pallas as pl
from jax.experimental.pallas import tpu as pltpu
from jax.sharding import PartitionSpec as P

ITERS = 5
EPSILON = 0.05
SCALE = 1.0 / EPSILON
DEPTH = 256
CHUNK = 256
F32 = jnp.float32
BF16 = jnp.bfloat16
VMEM_LIMIT = 48 * 1024 * 1024


def split3(v):
    high = v.astype(BF16).astype(F32)
    rest = v - high
    mid = rest.astype(BF16).astype(F32)
    low = (rest - mid).astype(BF16).astype(F32)
    return high, mid, low


def vmem(count):
    return [pl.BlockSpec(memory_space=pltpu.VMEM)] * count


def call(body, outs, count, scratch=()):
    return pl.pallas_call(
        body,
        out_shape=outs,
        in_specs=vmem(count),
        out_specs=vmem(len(outs)),
        scratch_shapes=list(scratch),
        compiler_params=pltpu.CompilerParams(vmem_limit_bytes=VMEM_LIMIT),
    )


def shape(dims, dtype=F32):
    return jax.ShapeDtypeStruct(dims, dtype)


def factors(points, order):
    parts = split3(points)
    width = points.shape[1]
    blocks = [parts[o] for o in order]
    zero16 = jnp.zeros((16, width), F32)
    tail = jnp.zeros((DEPTH - 144 - 2 * points.shape[0], width), F32)
    return jnp.concatenate(blocks[:4] + [zero16] + blocks[4:] + [tail], axis=0)


X_ORDER = (0, 0, 1, 0, 2, 1)
Y_ORDER = (0, 1, 0, 2, 0, 1)


def prepare_body(x_hbm, y_hbm, ax0, ax1, ay0, ay1, bx, by, start_ref, out, x_ref, y_ref, sems):
    copies = [
        pltpu.make_async_copy(x_hbm, x_ref, sems.at[0]),
        pltpu.make_async_copy(y_hbm, y_ref, sems.at[1]),
    ]
    for copy in copies:
        copy.start()
    for copy in copies:
        copy.wait()
    x = x_ref[...]
    y = y_ref[...]
    xf = factors(x * (2.0 * SCALE), X_ORDER)
    yf = factors(y, Y_ORDER)
    for factor, left0, left1, right in ((xf, ax0, ax1, bx), (yf, ay0, ay1, by)):
        right[...] = factor.astype(BF16)
        turned = factor.T
        left0[...] = turned[:, :128].astype(BF16)
        left1[...] = turned[:, 128:]
    start = -SCALE * jnp.sum(y * y, axis=0, keepdims=True)
    start_ref[...] = start
    left, unused = left_factor(ay0, ay1, start)
    partial_lse(left, bx, out)


def left_factor(left0, left1, pot, adj=None):
    width = pot.shape[1]
    high, mid, low = split3(pot)
    one = jnp.ones((1, width), F32)
    rows = [high, mid, low, one, one, one, jnp.zeros_like(one)]
    rows.append(jnp.zeros_like(one) if adj is None else adj)
    rows.append(jnp.zeros((120, width), F32))
    turned = jnp.concatenate(rows, axis=0).T
    column = None
    if adj is not None:
        column = turned[:, 7:8]
        lane = lax.broadcasted_iota(jnp.int32, turned.shape, 1)
        turned = jnp.where(lane == 7, 0.0, turned)
    return jnp.concatenate([left0[...], (left1[...] + turned).astype(BF16)], axis=1), column


def right_rows(pot):
    width = pot.shape[1]
    one = jnp.ones((3, width), F32)
    high, mid, low = split3(pot)
    return jnp.concatenate([one, high, mid, low, jnp.zeros((10, width), F32)], axis=0).astype(BF16)


def right_chunk(right, rows, at, wide):
    return jnp.concatenate(
        [right[0:128, at : at + wide], rows[:, at : at + wide], right[144:DEPTH, at : at + wide]], axis=0
    )


def matmul(a, b):
    return jnp.dot(a, b, preferred_element_type=F32)


def partial_lse(left, right, out):
    width = right.shape[1]
    rows = right_rows(jnp.zeros((1, width), F32))
    wide = min(CHUNK, width)
    for at in range(0, width, wide):
        scores = matmul(left, right_chunk(right, rows, at, wide))
        top = jnp.max(scores, axis=0, keepdims=True)
        total = jnp.sum(jnp.exp(scores - top), axis=0, keepdims=True)
        out[:, at : at + wide] = top + jnp.log(total)


def join_lse(parts):
    parts = [p[...] for p in parts]
    top = functools.reduce(jnp.maximum, parts)
    return top + jnp.log(sum(jnp.exp(p - top) for p in parts))


def join_sum(parts):
    return sum(p[...] for p in parts)


def join_body(join, *refs):
    refs[-1][...] = join(refs[:-1])


def forward_body(log_mass, left0, left1, right, *refs):
    got, (pot_out, out) = refs[:-2], refs[-2:]
    pot = log_mass - join_lse(got)
    pot_out[...] = pot
    left, unused = left_factor(left0, left1, pot)
    partial_lse(left, right, out)


def weighted_sums(left, column, right, rows, out):
    width = right.shape[1]
    wide = min(CHUNK, width)
    for at in range(0, width, wide):
        scores = matmul(left, right_chunk(right, rows, at, wide))
        out[:, at : at + wide] = jnp.sum(jnp.exp(scores) * column, axis=0, keepdims=True)


def turn_body(log_mass, log_scale, left0, left1, right, pot_right, *refs):
    got, (pot_out, out) = refs[:-2], refs[-2:]
    pot = log_mass - join_lse(got)
    pot_out[...] = pot
    left, column = left_factor(left0, left1, pot, jnp.ones_like(pot))
    weighted_sums(left, column, right, right_rows(pot_right[...] + log_scale), out)


def backward_body(leading, log_scale, left0, left1, right, pot_left, pot_right, *refs):
    got, (adj_out, out) = refs[:-2], refs[-2:]
    adj = leading - join_sum(got)
    adj_out[...] = adj
    left, column = left_factor(left0, left1, pot_left[...], adj)
    weighted_sums(left, column, right, right_rows(pot_right[...] + log_scale), out)


SPREAD = 20.0
STRIP = 256


def gradient_body(dim, log_cols, log_rows, n_got, n_col, n_row, ax0, ax1, by, x_ref, y_ref, *refs):
    pots_rows = refs[:ITERS]
    pots_cols = refs[ITERS : 2 * ITERS + 1]
    adjs_rows = refs[2 * ITERS + 1 : 3 * ITERS]
    adjs_cols = refs[3 * ITERS : 4 * ITERS - 1]
    refs = refs[4 * ITERS - 1 :]
    got, refs = refs[:n_got], refs[n_got:]
    us = [p[...] for p in pots_rows]
    vs = [p[...] for p in pots_cols]
    first = (1.0 if ITERS == 1 else 0.0) - join_sum(got)
    adjs_rows = [first] + [a[...] for a in adjs_rows]
    adjs_cols = [a[...] for a in adjs_cols] + [jnp.ones(vs[0].shape, F32)]
    gradient(log_cols, log_rows, n_col, n_row, ax0, ax1, by, x_ref, y_ref, us, vs, adjs_rows, adjs_cols, refs)


def gradient(log_cols, log_rows, n_col, n_row, ax0, ax1, by, x_ref, y_ref, us, vs, adjs_rows, adjs_cols, refs):
    outs_x, outs_y = refs[:n_col], refs[n_col : n_col + n_row]
    cols_rows, x_parts, y_parts, gx, gy, left_e, left_r, right_r, all_x, all_y = refs[n_col + n_row :]
    dim, count_rows = x_ref.shape
    count_cols = y_ref.shape[1]
    shift = log_rows - log_cols

    x = x_ref[...]
    y = y_ref[...]
    one = jnp.ones((1, count_cols), F32)
    pad = jnp.zeros((31, count_cols), F32)
    y_parts[...] = jnp.concatenate(list(split3(y)) + [one, pad], axis=0).T.astype(BF16)
    one = jnp.ones((1, count_rows), F32)
    pad = jnp.zeros((31, count_rows), F32)
    x_parts[...] = jnp.concatenate(list(split3(x)) + [one, pad], axis=0).astype(BF16)
    gy[...] = jnp.zeros_like(gy)

    far_u = functools.reduce(jnp.maximum, [jnp.abs(u - us[-1]) for u in us])
    far_v = functools.reduce(jnp.maximum, [jnp.abs(v - vs[-1]) for v in vs])
    near = jnp.maximum(jnp.max(far_u), jnp.max(far_v)) < SPREAD

    def add_strip(at, total):
        upper = total.astype(BF16)
        lower = (total - upper.astype(F32)).astype(BF16)
        gx[at, :] = matmul(upper, y_parts[...]) + matmul(lower, y_parts[...])
        gy[...] += matmul(x_parts[:, at], upper) + matmul(x_parts[:, at], lower)

    @pl.when(near)
    def factored():
        alpha = [jnp.exp(u - us[-1]) for u in us]
        beta = [jnp.exp(v - vs[-1]) for v in vs]
        p_rows = alpha + [a * adj for a, adj in zip(alpha, adjs_rows)]
        q_rows = [b * adj for b, adj in zip(beta[1:], adjs_cols)] + [b * math.exp(shift) for b in beta[:-1]]
        fill = 16 - 2 * ITERS
        p_split = split3(jnp.concatenate(p_rows + [jnp.zeros((fill, count_rows), F32)], axis=0))
        q_split = split3(jnp.concatenate(q_rows + [jnp.zeros((fill, count_cols), F32)], axis=0))
        tail = [jnp.zeros((32, count_rows), F32)]
        left_r[...] = jnp.concatenate([p_split[o] for o in X_ORDER] + tail, axis=0).T.astype(BF16)
        tail = [jnp.zeros((32, count_cols), F32)]
        right_r[...] = jnp.concatenate([q_split[o] for o in Y_ORDER] + tail, axis=0).astype(BF16)
        left, unused = left_factor(ax0, ax1, us[-1] + log_cols)
        left_e[...] = left
        right = right_chunk(by, right_rows(vs[-1]), 0, count_cols)
        strip = min(STRIP, count_rows)
        for step in range(count_rows // strip):
            at = pl.ds(step * strip, strip)
            total = jnp.exp(matmul(left_e[at, :], right)) * matmul(left_r[at, :], right_r[...])
            add_strip(at, total)

    @pl.when(jnp.logical_not(near))
    def separate():
        stack = [u + log_cols for u in us] + adjs_rows
        stack.append(jnp.zeros((128 - len(stack), count_rows), F32))
        cols_rows[...] = jnp.concatenate(stack, axis=0).T
        strip = 128

        def block(step, carry):
            at = pl.ds(pl.multiple_of(step * strip, strip), strip)
            left = jnp.concatenate([ax0[at, :], ax1[at, :].astype(BF16)], axis=1)
            inner = matmul(left, by[...])
            columns = cols_rows[at, :]
            total = jnp.zeros_like(inner)
            for k in range(ITERS):
                base = inner + columns[:, k : k + 1]
                total += jnp.exp(base + vs[k + 1]) * adjs_cols[k]
                total += jnp.exp(base + (vs[k] + shift)) * columns[:, ITERS + k : ITERS + k + 1]
            add_strip(at, total)
            return carry

        lax.fori_loop(0, count_rows // strip, block, 0)

    def finish(points, sums):
        mixed = sums[0:dim] + sums[dim : 2 * dim] + sums[2 * dim : 3 * dim]
        return 2.0 * (points * sums[3 * dim : 3 * dim + 1] - mixed)

    for value, held, outs, axis in (
        (finish(x, gx[...].T), all_x, outs_x, "col"),
        (finish(y, gy[...]), all_y, outs_y, "row"),
    ):
        share = held.shape[2]
        for p in range(held.shape[0]):
            held[p] = value[:, p * share : (p + 1) * share]
        me = lax.axis_index(axis)
        for s, out in enumerate(outs):
            out[...] = held[me ^ s]


def swap(value, axis, distance):
    return lax.ppermute(value, axis, [(d, d ^ distance) for d in range(lax.axis_size(axis))])


def exchange(part, axis, join):
    size = lax.axis_size(axis)
    assert size & (size - 1) == 0
    distance = 1
    got = (part,)
    while distance < size:
        if len(got) > 1:
            (part,) = call(functools.partial(join_body, join), [shape(part.shape)], len(got))(*got)
        got = (part, swap(part, axis, distance))
        distance *= 2
    return got


def scatter(pieces, axis):
    got = [pieces[0]] + [swap(pieces[s], axis, s) for s in range(1, len(pieces))]
    return sum(got[1:], got[0])


def slot(column, lane, state):
    return jnp.where(lax.broadcasted_iota(jnp.int32, state.shape, 1) == lane, column, state)


def left_strip(left0, left1, at, pot):
    strip = left1[at, :]
    for lane, part in enumerate(split3(jnp.broadcast_to(pot, strip.shape))):
        strip = slot(part, lane, strip)
    return jnp.concatenate([left0[at, :], strip.astype(BF16)], axis=1)


def halves(value):
    return sum(value[:, p : p + 128] for p in range(0, value.shape[1], 128))


def octets(value):
    return jnp.sum(value.reshape(value.shape[0] // 8, 8, value.shape[1]), axis=0)


SWEEP = 512


def sweep(left_of, right, rows, out, held, acc, times, store, close):
    strip, wide_all = held.shape[1:]
    strips = times.shape[0]
    for s in range(strips + 1):
        at = slice(s * strip, (s + 1) * strip)
        left = left_of(at) if s < strips else None
        sums = None
        for c in range(0, wide_all, CHUNK):
            place = slice(c, c + CHUNK)
            if s < strips:
                sums = store(held.at[s % 2], matmul(left, right_chunk(right, rows, c, CHUNK)), place, sums)
            if s > 0:
                factor = times[s - 1]
                part = octets(held[(s - 1) % 2, :, place] * jnp.concatenate([factor] * (CHUNK // 128), axis=1))
                if s > 1:
                    part += acc[:, place]
                if s < strips:
                    acc[:, place] = part
                else:
                    out[:, place] = jnp.sum(part, axis=0, keepdims=True)
        if s < strips:
            times[s] = jnp.broadcast_to(close(at, sums, held.at[s % 2]), times.shape[1:])


def exponentials(weigh):
    def store(held, scores, place, sums):
        power = jnp.exp(scores)
        held[:, place] = power
        part = halves(weigh(power, place))
        return part if sums is None else sums + part

    return store


def prepare_own_body(x_hbm, y_hbm, ax0, ax1, ay0, ay1, by, state, out, x_ref, y_ref, bx, sems):
    copies = [
        pltpu.make_async_copy(x_hbm, x_ref, sems.at[0]),
        pltpu.make_async_copy(y_hbm, y_ref, sems.at[1]),
    ]
    for copy in copies:
        copy.start()
    for copy in copies:
        copy.wait()
    x = x_ref[...]
    y = y_ref[...]
    xf = factors(x * (2.0 * SCALE), X_ORDER)
    yf = factors(y, Y_ORDER)
    for factor, left0, left1, right in ((xf, ax0, ax1, bx), (yf, ay0, ay1, by)):
        right[...] = factor.astype(BF16)
        turned = factor.T
        left0[...] = turned[:, :128].astype(BF16)
        left1[...] = turned[:, 128:]
    start = -SCALE * jnp.sum(y * y, axis=0, keepdims=True)
    state[...] = jnp.concatenate([start, jnp.zeros((127, y.shape[1]), F32)], axis=0).T
    left, unused = left_factor(ay0, ay1, start)
    partial_lse(left, bx, out)
    lane = lax.broadcasted_iota(jnp.int32, ay1.shape, 1)
    ay1[...] = jnp.where((lane >= 3) & (lane < 6), 1.0, ay1[...])


def first_pot_body(log_rows, *refs):
    refs[-1][...] = -log_rows - join_lse(refs[:-1])


def opening_body(n_row, log_rows, log_cols, left0, left1, state, *refs):
    xs, us = refs[:n_row], refs[n_row : 2 * n_row]
    right, u_out, state_out, out, held, acc, times = refs[2 * n_row :]
    x = jnp.concatenate([r[...] for r in xs], axis=1)
    right[...] = factors(x * (2.0 * SCALE), X_ORDER).astype(BF16)
    u = jnp.concatenate([r[...] for r in us], axis=1)
    u_out[...] = u

    def left_of(at):
        return jnp.concatenate([left0[at, :], left1[at, :].astype(BF16)], axis=1)

    def store(held, scores, place, tops):
        held[:, place] = scores
        for p in range(0, CHUNK, 128):
            part = scores[:, p : p + 128]
            tops = part if tops is None else jnp.maximum(tops, part)
        return tops

    def close(at, tops, held):
        top = jnp.max(tops, axis=1, keepdims=True)
        sums = None
        for c in range(0, held.shape[1], CHUNK):
            place = slice(c, c + CHUNK)
            power = jnp.exp(held[:, place] - top)
            held[:, place] = power
            part = halves(power)
            sums = part if sums is None else sums + part
        column = jnp.sum(sums, axis=1, keepdims=True)
        state_out[at, :] = slot(-log_cols - (top + jnp.log(column)), 1, state[at, :])
        return math.exp(-log_cols) / column

    sweep(left_of, right, right_rows(u), out, held, acc, times, store, close)


def iteration_body(k, n_got, log_rows, log_cols, left0, left1, right, state, u_old, *refs):
    got, (u_out, state_out, out, held, acc, times) = refs[:n_got], refs[n_got:]
    u = u_old[...] - (log_rows + jnp.log(join_sum(got)))
    u_out[...] = u

    def left_of(at):
        return left_strip(left0, left1, at, state[at, k - 1 : k])

    def close(at, sums, held):
        column = jnp.sum(sums, axis=1, keepdims=True)
        old = state[at, :]
        pot = old[:, k - 1 : k] - (log_cols + jnp.log(column))
        state_out[at, :] = slot(math.exp(log_cols) * column, 8 + k, slot(pot, k, old))
        return math.exp(-log_cols) / column

    store = exponentials(lambda power, place: power)
    sweep(left_of, right, right_rows(u), out, held, acc, times, store, close)


def adjoint_body(k, n_got, log_rows, log_cols, left0, left1, right, state, u_ref, u_before, *refs):
    got, (adj_out, state_out, out, held, acc, times) = refs[:n_got], refs[n_got:]
    if k == ITERS:
        adj_out[...] = 1.0 - math.exp(log_cols) * join_sum(got)
    else:
        adj_out[...] = -join_sum(got)
    u = u_ref[...]
    shift = math.exp(log_rows - log_cols)

    def left_of(at):
        return left_strip(left0, left1, at, state[at, k : k + 1])

    def close(at, sums, held):
        column = jnp.sum(sums, axis=1, keepdims=True)
        old = state[at, :]
        sigma = old[:, 8 + k : 9 + k]
        adj = -shift * sigma * column
        state_out[at, :] = slot(adj, 16 + k - 1, old)
        return sigma * adj

    store = exponentials(lambda power, place: power * adj_out[:, place])
    sweep(left_of, right, right_rows(u + log_cols), out, held, acc, times, store, close)
    out[...] = out[...] * jnp.exp(u_before[...] - u)


def closing_body(n_got, log_cols, log_rows, n_col, n_row, ax0, ax1, by, x_ref, y_ref, state, *refs):
    count_rows, count_cols = x_ref.shape[1], y_ref.shape[1]
    us = [r[:, :count_rows] for r in refs[:ITERS]]
    adjs_rows = [r[:, :count_rows] for r in refs[ITERS : 2 * ITERS - 1]]
    refs = refs[2 * ITERS - 1 :]
    got, refs = refs[:n_got], refs[n_got:]
    first = -join_sum([r[:, :count_rows] for r in got])
    turned = state[0:count_cols, :].T
    vs = [turned[k : k + 1] for k in range(ITERS + 1)]
    adjs_cols = [turned[16 + k : 17 + k] for k in range(1, ITERS)] + [jnp.ones((1, count_cols), F32)]
    adjs_rows = [first] + adjs_rows
    gradient(log_cols, log_rows, n_col, n_row, ax0, ax1, by, x_ref, y_ref, us, vs, adjs_rows, adjs_cols, refs)


def gradient_scratch(dim, count_rows, count_cols, n_col, n_row):
    return [
        pltpu.VMEM((count_rows, 128), F32),
        pltpu.VMEM((128, count_rows), BF16),
        pltpu.VMEM((count_cols, 128), BF16),
        pltpu.VMEM((count_rows, 128), F32),
        pltpu.VMEM((128, count_cols), F32),
        pltpu.VMEM((count_rows, DEPTH), BF16),
        pltpu.VMEM((count_rows, 128), BF16),
        pltpu.VMEM((128, count_cols), BF16),
        pltpu.VMEM((n_col, dim, count_rows // n_col), F32),
        pltpu.VMEM((n_row, dim, count_cols // n_row), F32),
    ]


def repeated(x, y):
    dim, count_rows = x.shape
    count_cols = y.shape[1]
    n_row, n_col = lax.axis_size("row"), lax.axis_size("col")
    all_rows, held_cols = count_rows * n_row, count_cols
    log_rows, log_cols = math.log(all_rows), math.log(count_cols * n_col)
    row, col = (1, all_rows), (1, held_cols)

    xs = [x] + [swap(x, "row", s) for s in range(1, n_row)]
    own = (1, count_rows)
    ax0, ax1, ay0, ay1, by, state, part, x, y = pl.pallas_call(
        prepare_own_body,
        out_shape=[
            shape((count_rows, 128), BF16),
            shape((count_rows, 128)),
            shape((count_cols, 128), BF16),
            shape((count_cols, 128)),
            shape((DEPTH, count_cols), BF16),
            shape((count_cols, 128)),
            shape(own),
            shape(x.shape),
            shape(y.shape),
        ],
        in_specs=[pl.BlockSpec(memory_space=pltpu.HBM)] * 2,
        out_specs=vmem(9),
        scratch_shapes=[pltpu.VMEM((DEPTH, count_rows), BF16), pltpu.SemaphoreType.DMA((2,))],
        compiler_params=pltpu.CompilerParams(vmem_limit_bytes=VMEM_LIMIT),
    )(x, y)
    xs[0] = x
    got = exchange(part, "col", join_lse)
    (u,) = call(functools.partial(first_pot_body, log_rows), [shape(own)], len(got))(*got)
    u_blocks = [u] + [swap(u, "row", s) for s in range(1, n_row)]

    strip = min(SWEEP, held_cols)
    scratch = [
        pltpu.VMEM((2, strip, all_rows), F32),
        pltpu.VMEM((8, all_rows), F32),
        pltpu.VMEM((held_cols // strip, strip, 128), F32),
    ]
    results = [shape(row), shape((held_cols, 128)), shape(row)]
    us = []
    bx, u, state, part = call(
        functools.partial(opening_body, n_row, log_rows, log_cols),
        [shape((DEPTH, all_rows), BF16)] + results,
        3 + 2 * n_row,
        scratch,
    )(ay0, ay1, state, *xs, *u_blocks)
    us.append(u)
    for k in range(2, ITERS + 1):
        got = exchange(part, "col", join_sum)
        u, state, part = call(
            functools.partial(iteration_body, k, len(got), log_rows, log_cols), results, 5 + len(got), scratch
        )(ay0, ay1, bx, state, u, *got)
        us.append(u)
    adjs_rows = []
    for k in range(ITERS, 1, -1):
        got = exchange(part, "col", join_sum)
        adj, state, part = call(
            functools.partial(adjoint_body, k, len(got), log_rows, log_cols),
            results,
            6 + len(got),
            scratch,
        )(ay0, ay1, bx, state, us[k - 1], us[k - 2], *got)
        adjs_rows.insert(0, adj)
    got = exchange(part, "col", join_sum)
    outs = call(
        functools.partial(closing_body, len(got), log_cols, log_rows, n_col, n_row),
        [shape((dim, count_rows // n_col))] * n_col + [shape((dim, count_cols // n_row))] * n_row,
        6 + 2 * ITERS - 1 + len(got),
        gradient_scratch(dim, count_rows, count_cols, n_col, n_row),
    )(ax0, ax1, by, x, y, state, *us, *adjs_rows, *got)
    return scatter(outs[:n_col], "col").T, scatter(outs[n_col:], "row").T


REPEAT_PAIRS = 1 << 23


def on_device(x_points, y_points):
    x = x_points.T
    y = y_points.T
    n_row, n_col = lax.axis_size("row"), lax.axis_size("col")
    if ITERS > 1 and x.shape[1] * n_row * y.shape[1] <= REPEAT_PAIRS:
        return repeated(x, y)
    return shared(x, y)


def shared(x, y):
    dim, count_rows = x.shape
    count_cols = y.shape[1]
    n_row, n_col = lax.axis_size("row"), lax.axis_size("col")
    log_rows = math.log(count_rows * n_row)
    log_cols = math.log(count_cols * n_col)
    row, col = (1, count_rows), (1, count_cols)

    ax0, ax1, ay0, ay1, bx, by, start, part, x, y = pl.pallas_call(
        prepare_body,
        out_shape=[
            shape((count_rows, 128), BF16),
            shape((count_rows, 128)),
            shape((count_cols, 128), BF16),
            shape((count_cols, 128)),
            shape((DEPTH, count_rows), BF16),
            shape((DEPTH, count_cols), BF16),
            shape(col),
            shape(row),
            shape(x.shape),
            shape(y.shape),
        ],
        in_specs=[pl.BlockSpec(memory_space=pltpu.HBM)] * 2,
        out_specs=vmem(10),
        scratch_shapes=[pltpu.SemaphoreType.DMA((2,))],
        compiler_params=pltpu.CompilerParams(vmem_limit_bytes=VMEM_LIMIT),
    )(x, y)

    pots_rows, pots_cols = [], [start]
    for k in range(ITERS):
        got = exchange(part, "col", join_lse)
        pot, part = call(functools.partial(forward_body, -log_rows), [shape(row), shape(col)], 3 + len(got))(
            ax0, ax1, by, *got
        )
        pots_rows.append(pot)
        got = exchange(part, "row", join_lse)
        if k < ITERS - 1:
            pot, part = call(functools.partial(forward_body, -log_cols), [shape(col), shape(row)], 3 + len(got))(
                ay0, ay1, bx, *got
            )
            pots_cols.append(pot)
    pot, part = call(functools.partial(turn_body, -log_cols, log_cols), [shape(col), shape(row)], 4 + len(got))(
        ay0, ay1, bx, pots_rows[-1], *got
    )
    pots_cols.append(pot)

    adjs_rows, adjs_cols = [], []
    for k in reversed(range(1, ITERS)):
        leading = 1.0 if k == ITERS - 1 else 0.0
        got = exchange(part, "col", join_sum)
        adj, part = call(functools.partial(backward_body, leading, log_rows), [shape(row), shape(col)], 5 + len(got))(
            ax0, ax1, by, pots_rows[k], pots_cols[k], *got
        )
        adjs_rows.insert(0, adj)
        got = exchange(part, "row", join_sum)
        adj, part = call(functools.partial(backward_body, 0.0, log_cols), [shape(col), shape(row)], 5 + len(got))(
            ay0, ay1, bx, pots_cols[k], pots_rows[k - 1], *got
        )
        adjs_cols.insert(0, adj)
    got = exchange(part, "col", join_sum)

    share_x, share_y = count_rows // n_col, count_cols // n_row
    outs = call(
        functools.partial(gradient_body, dim, log_cols, log_rows, len(got), n_col, n_row),
        [shape((dim, share_x))] * n_col + [shape((dim, share_y))] * n_row,
        5 + 4 * ITERS - 1 + len(got),
        gradient_scratch(dim, count_rows, count_cols, n_col, n_row),
    )(ax0, ax1, by, x, y, *pots_rows, *pots_cols, *adjs_rows, *adjs_cols, *got)
    grad_x = scatter(outs[:n_col], "col")
    grad_y = scatter(outs[n_col:], "row")
    return (grad_x.T, grad_y.T)


def solution(mesh):
    in_specs = (P(("groups", "row"), None), P(("groups", "col"), None))
    out_specs = (P(("groups", "row", "col"), None), P(("groups", "col", "row"), None))
    return jax.shard_map(
        on_device, mesh=mesh, in_specs=in_specs, out_specs=out_specs, check_vma=False
    )
```

```python
import functools
import math

import jax
import jax.numpy as jnp
from jax import lax
from jax.experimental import pallas as pl
from jax.experimental.pallas import tpu as pltpu
from jax.sharding import PartitionSpec as P

ITERS = 5
EPSILON = 0.05
SCALE = 1.0 / EPSILON
DEPTH = 256
CHUNK = 256
F32 = jnp.float32
BF16 = jnp.bfloat16
VMEM_LIMIT = 48 * 1024 * 1024


def split3(v):
    high = v.astype(BF16).astype(F32)
    rest = v - high
    mid = rest.astype(BF16).astype(F32)
    low = (rest - mid).astype(BF16).astype(F32)
    return high, mid, low


def vmem(count):
    return [pl.BlockSpec(memory_space=pltpu.VMEM)] * count


def call(body, outs, count, scratch=()):
    return pl.pallas_call(
        body,
        out_shape=outs,
        in_specs=vmem(count),
        out_specs=vmem(len(outs)),
        scratch_shapes=list(scratch),
        compiler_params=pltpu.CompilerParams(vmem_limit_bytes=VMEM_LIMIT),
    )


def shape(dims, dtype=F32):
    return jax.ShapeDtypeStruct(dims, dtype)


def factors(points, order):
    parts = split3(points)
    width = points.shape[1]
    blocks = [parts[o] for o in order]
    zero16 = jnp.zeros((16, width), F32)
    tail = jnp.zeros((DEPTH - 144 - 2 * points.shape[0], width), F32)
    return jnp.concatenate(blocks[:4] + [zero16] + blocks[4:] + [tail], axis=0)


X_ORDER = (0, 0, 1, 0, 2, 1)
Y_ORDER = (0, 1, 0, 2, 0, 1)


def prepare_body(x_hbm, y_hbm, ax0, ax1, ay0, ay1, bx, by, start_ref, out, x_ref, y_ref, sems):
    copies = [
        pltpu.make_async_copy(x_hbm, x_ref, sems.at[0]),
        pltpu.make_async_copy(y_hbm, y_ref, sems.at[1]),
    ]
    for copy in copies:
        copy.start()
    for copy in copies:
        copy.wait()
    x = x_ref[...]
    y = y_ref[...]
    xf = factors(x * (2.0 * SCALE), X_ORDER)
    yf = factors(y, Y_ORDER)
    for factor, left0, left1, right in ((xf, ax0, ax1, bx), (yf, ay0, ay1, by)):
        right[...] = factor.astype(BF16)
        turned = factor.T
        left0[...] = turned[:, :128].astype(BF16)
        left1[...] = turned[:, 128:]
    start = -SCALE * jnp.sum(y * y, axis=0, keepdims=True)
    start_ref[...] = start
    left, unused = left_factor(ay0, ay1, start)
    partial_lse(left, bx, out)


def left_factor(left0, left1, pot, adj=None):
    width = pot.shape[1]
    high, mid, low = split3(pot)
    one = jnp.ones((1, width), F32)
    rows = [high, mid, low, one, one, one, jnp.zeros_like(one)]
    rows.append(jnp.zeros_like(one) if adj is None else adj)
    rows.append(jnp.zeros((120, width), F32))
    turned = jnp.concatenate(rows, axis=0).T
    column = None
    if adj is not None:
        column = turned[:, 7:8]
        lane = lax.broadcasted_iota(jnp.int32, turned.shape, 1)
        turned = jnp.where(lane == 7, 0.0, turned)
    return jnp.concatenate([left0[...], (left1[...] + turned).astype(BF16)], axis=1), column


def right_rows(pot):
    width = pot.shape[1]
    one = jnp.ones((3, width), F32)
    high, mid, low = split3(pot)
    return jnp.concatenate([one, high, mid, low, jnp.zeros((10, width), F32)], axis=0).astype(BF16)


def right_chunk(right, rows, at, wide):
    return jnp.concatenate(
        [right[0:128, at : at + wide], rows[:, at : at + wide], right[144:DEPTH, at : at + wide]], axis=0
    )


def matmul(a, b):
    return jnp.dot(a, b, preferred_element_type=F32)


def partial_lse(left, right, out):
    width = right.shape[1]
    rows = right_rows(jnp.zeros((1, width), F32))
    wide = min(CHUNK, width)
    for at in range(0, width, wide):
        scores = matmul(left, right_chunk(right, rows, at, wide))
        top = jnp.max(scores, axis=0, keepdims=True)
        total = jnp.sum(jnp.exp(scores - top), axis=0, keepdims=True)
        out[:, at : at + wide] = top + jnp.log(total)


def join_lse(parts):
    parts = [p[...] for p in parts]
    top = functools.reduce(jnp.maximum, parts)
    return top + jnp.log(sum(jnp.exp(p - top) for p in parts))


def join_sum(parts):
    return sum(p[...] for p in parts)


def join_body(join, *refs):
    refs[-1][...] = join(refs[:-1])


def forward_body(log_mass, left0, left1, right, *refs):
    got, (pot_out, out) = refs[:-2], refs[-2:]
    pot = log_mass - join_lse(got)
    pot_out[...] = pot
    left, unused = left_factor(left0, left1, pot)
    partial_lse(left, right, out)


def weighted_sums(left, column, right, rows, out):
    width = right.shape[1]
    wide = min(CHUNK, width)
    for at in range(0, width, wide):
        scores = matmul(left, right_chunk(right, rows, at, wide))
        out[:, at : at + wide] = jnp.sum(jnp.exp(scores) * column, axis=0, keepdims=True)


def turn_body(log_mass, log_scale, left0, left1, right, pot_right, *refs):
    got, (pot_out, out) = refs[:-2], refs[-2:]
    pot = log_mass - join_lse(got)
    pot_out[...] = pot
    left, column = left_factor(left0, left1, pot, jnp.ones_like(pot))
    weighted_sums(left, column, right, right_rows(pot_right[...] + log_scale), out)


def backward_body(leading, log_scale, left0, left1, right, pot_left, pot_right, *refs):
    got, (adj_out, out) = refs[:-2], refs[-2:]
    adj = leading - join_sum(got)
    adj_out[...] = adj
    left, column = left_factor(left0, left1, pot_left[...], adj)
    weighted_sums(left, column, right, right_rows(pot_right[...] + log_scale), out)


SPREAD = 20.0
STRIP = 256


def gradient_body(dim, log_cols, log_rows, n_got, n_col, n_row, ax0, ax1, by, x_ref, y_ref, *refs):
    pots_rows = refs[:ITERS]
    pots_cols = refs[ITERS : 2 * ITERS + 1]
    adjs_rows = refs[2 * ITERS + 1 : 3 * ITERS]
    adjs_cols = refs[3 * ITERS : 4 * ITERS - 1]
    refs = refs[4 * ITERS - 1 :]
    got, refs = refs[:n_got], refs[n_got:]
    us = [p[...] for p in pots_rows]
    vs = [p[...] for p in pots_cols]
    first = (1.0 if ITERS == 1 else 0.0) - join_sum(got)
    adjs_rows = [first] + [a[...] for a in adjs_rows]
    adjs_cols = [a[...] for a in adjs_cols] + [jnp.ones(vs[0].shape, F32)]
    gradient(log_cols, log_rows, n_col, n_row, ax0, ax1, by, x_ref, y_ref, us, vs, adjs_rows, adjs_cols, refs)


def gradient(log_cols, log_rows, n_col, n_row, ax0, ax1, by, x_ref, y_ref, us, vs, adjs_rows, adjs_cols, refs):
    outs_x, outs_y = refs[:n_col], refs[n_col : n_col + n_row]
    cols_rows, x_parts, y_parts, gx, gy, left_e, left_r, right_r, all_x, all_y = refs[n_col + n_row :]
    dim, count_rows = x_ref.shape
    count_cols = y_ref.shape[1]
    shift = log_rows - log_cols

    x = x_ref[...]
    y = y_ref[...]
    one = jnp.ones((1, count_cols), F32)
    pad = jnp.zeros((31, count_cols), F32)
    y_parts[...] = jnp.concatenate(list(split3(y)) + [one, pad], axis=0).T.astype(BF16)
    one = jnp.ones((1, count_rows), F32)
    pad = jnp.zeros((31, count_rows), F32)
    x_parts[...] = jnp.concatenate(list(split3(x)) + [one, pad], axis=0).astype(BF16)
    gy[...] = jnp.zeros_like(gy)

    far_u = functools.reduce(jnp.maximum, [jnp.abs(u - us[-1]) for u in us])
    far_v = functools.reduce(jnp.maximum, [jnp.abs(v - vs[-1]) for v in vs])
    near = jnp.maximum(jnp.max(far_u), jnp.max(far_v)) < SPREAD

    def add_strip(at, total):
        upper = total.astype(BF16)
        lower = (total - upper.astype(F32)).astype(BF16)
        gx[at, :] = matmul(upper, y_parts[...]) + matmul(lower, y_parts[...])
        gy[...] += matmul(x_parts[:, at], upper) + matmul(x_parts[:, at], lower)

    @pl.when(near)
    def factored():
        alpha = [jnp.exp(u - us[-1]) for u in us]
        beta = [jnp.exp(v - vs[-1]) for v in vs]
        p_rows = alpha + [a * adj for a, adj in zip(alpha, adjs_rows)]
        q_rows = [b * adj for b, adj in zip(beta[1:], adjs_cols)] + [b * math.exp(shift) for b in beta[:-1]]
        fill = 16 - 2 * ITERS
        p_split = split3(jnp.concatenate(p_rows + [jnp.zeros((fill, count_rows), F32)], axis=0))
        q_split = split3(jnp.concatenate(q_rows + [jnp.zeros((fill, count_cols), F32)], axis=0))
        tail = [jnp.zeros((32, count_rows), F32)]
        left_r[...] = jnp.concatenate([p_split[o] for o in X_ORDER] + tail, axis=0).T.astype(BF16)
        tail = [jnp.zeros((32, count_cols), F32)]
        right_r[...] = jnp.concatenate([q_split[o] for o in Y_ORDER] + tail, axis=0).astype(BF16)
        left, unused = left_factor(ax0, ax1, us[-1] + log_cols)
        left_e[...] = left
        right = right_chunk(by, right_rows(vs[-1]), 0, count_cols)
        strip = min(STRIP, count_rows)
        for step in range(count_rows // strip):
            at = pl.ds(step * strip, strip)
            total = jnp.exp(matmul(left_e[at, :], right)) * matmul(left_r[at, :], right_r[...])
            add_strip(at, total)

    @pl.when(jnp.logical_not(near))
    def separate():
        stack = [u + log_cols for u in us] + adjs_rows
        stack.append(jnp.zeros((128 - len(stack), count_rows), F32))
        cols_rows[...] = jnp.concatenate(stack, axis=0).T
        strip = 128

        def block(step, carry):
            at = pl.ds(pl.multiple_of(step * strip, strip), strip)
            left = jnp.concatenate([ax0[at, :], ax1[at, :].astype(BF16)], axis=1)
            inner = matmul(left, by[...])
            columns = cols_rows[at, :]
            total = jnp.zeros_like(inner)
            for k in range(ITERS):
                base = inner + columns[:, k : k + 1]
                total += jnp.exp(base + vs[k + 1]) * adjs_cols[k]
                total += jnp.exp(base + (vs[k] + shift)) * columns[:, ITERS + k : ITERS + k + 1]
            add_strip(at, total)
            return carry

        lax.fori_loop(0, count_rows // strip, block, 0)

    def finish(points, sums):
        mixed = sums[0:dim] + sums[dim : 2 * dim] + sums[2 * dim : 3 * dim]
        return 2.0 * (points * sums[3 * dim : 3 * dim + 1] - mixed)

    for value, held, outs, axis in (
        (finish(x, gx[...].T), all_x, outs_x, "col"),
        (finish(y, gy[...]), all_y, outs_y, "row"),
    ):
        share = held.shape[2]
        for p in range(held.shape[0]):
            held[p] = value[:, p * share : (p + 1) * share]
        me = lax.axis_index(axis)
        for s, out in enumerate(outs):
            out[...] = held[me ^ s]


def swap(value, axis, distance):
    return lax.ppermute(value, axis, [(d, d ^ distance) for d in range(lax.axis_size(axis))])


def exchange(part, axis, join):
    size = lax.axis_size(axis)
    assert size & (size - 1) == 0
    distance = 1
    got = (part,)
    while distance < size:
        if len(got) > 1:
            (part,) = call(functools.partial(join_body, join), [shape(part.shape)], len(got))(*got)
        got = (part, swap(part, axis, distance))
        distance *= 2
    return got


def scatter(pieces, axis):
    got = [pieces[0]] + [swap(pieces[s], axis, s) for s in range(1, len(pieces))]
    return sum(got[1:], got[0])


def slot(column, lane, state):
    return jnp.where(lax.broadcasted_iota(jnp.int32, state.shape, 1) == lane, column, state)


def left_strip(left0, left1, at, pot):
    strip = left1[at, :]
    for lane, part in enumerate(split3(jnp.broadcast_to(pot, strip.shape))):
        strip = slot(part, lane, strip)
    return jnp.concatenate([left0[at, :], strip.astype(BF16)], axis=1)


def halves(value):
    return sum(value[:, p : p + 128] for p in range(0, value.shape[1], 128))


def octets(value):
    return jnp.sum(value.reshape(value.shape[0] // 8, 8, value.shape[1]), axis=0)


SWEEP = 128


def sweep(left_of, right, rows, out, held, acc, times, store, close):
    strip, wide_all = held.shape[1:]
    strips = times.shape[0]
    for s in range(strips + 1):
        at = slice(s * strip, (s + 1) * strip)
        left = left_of(at) if s < strips else None
        sums = None
        for c in range(0, wide_all, CHUNK):
            place = slice(c, c + CHUNK)
            if s < strips:
                sums = store(held.at[s % 2], matmul(left, right_chunk(right, rows, c, CHUNK)), place, sums)
            if s > 0:
                factor = times[s - 1]
                part = octets(held[(s - 1) % 2, :, place] * jnp.concatenate([factor] * (CHUNK // 128), axis=1))
                if s > 1:
                    part += acc[:, place]
                if s < strips:
                    acc[:, place] = part
                else:
                    out[:, place] = jnp.sum(part, axis=0, keepdims=True)
        if s < strips:
            times[s] = jnp.broadcast_to(close(at, sums, held.at[s % 2]), times.shape[1:])


def exponentials(weigh):
    def store(held, scores, place, sums):
        power = jnp.exp(scores)
        held[:, place] = power
        part = halves(weigh(power, place))
        return part if sums is None else sums + part

    return store


def prepare_own_body(x_hbm, y_hbm, ax0, ax1, ay0, ay1, by, state, out, x_ref, y_ref, bx, sems):
    copies = [
        pltpu.make_async_copy(x_hbm, x_ref, sems.at[0]),
        pltpu.make_async_copy(y_hbm, y_ref, sems.at[1]),
    ]
    for copy in copies:
        copy.start()
    for copy in copies:
        copy.wait()
    x = x_ref[...]
    y = y_ref[...]
    xf = factors(x * (2.0 * SCALE), X_ORDER)
    yf = factors(y, Y_ORDER)
    for factor, left0, left1, right in ((xf, ax0, ax1, bx), (yf, ay0, ay1, by)):
        right[...] = factor.astype(BF16)
        turned = factor.T
        left0[...] = turned[:, :128].astype(BF16)
        left1[...] = turned[:, 128:]
    start = -SCALE * jnp.sum(y * y, axis=0, keepdims=True)
    state[...] = jnp.concatenate([start, jnp.zeros((127, y.shape[1]), F32)], axis=0).T
    left, unused = left_factor(ay0, ay1, start)
    partial_lse(left, bx, out)
    lane = lax.broadcasted_iota(jnp.int32, ay1.shape, 1)
    ay1[...] = jnp.where((lane >= 3) & (lane < 6), 1.0, ay1[...])


def first_pot_body(log_rows, *refs):
    refs[-1][...] = -log_rows - join_lse(refs[:-1])


def opening_body(n_row, log_rows, log_cols, left0, left1, state, *refs):
    xs, us = refs[:n_row], refs[n_row : 2 * n_row]
    right, u_out, state_out, out, held, acc, times = refs[2 * n_row :]
    x = jnp.concatenate([r[...] for r in xs], axis=1)
    right[...] = factors(x * (2.0 * SCALE), X_ORDER).astype(BF16)
    u = jnp.concatenate([r[...] for r in us], axis=1)
    u_out[...] = u

    def left_of(at):
        return jnp.concatenate([left0[at, :], left1[at, :].astype(BF16)], axis=1)

    def store(held, scores, place, tops):
        held[:, place] = scores
        for p in range(0, CHUNK, 128):
            part = scores[:, p : p + 128]
            tops = part if tops is None else jnp.maximum(tops, part)
        return tops

    def close(at, tops, held):
        top = jnp.max(tops, axis=1, keepdims=True)
        sums = None
        for c in range(0, held.shape[1], CHUNK):
            place = slice(c, c + CHUNK)
            power = jnp.exp(held[:, place] - top)
            held[:, place] = power
            part = halves(power)
            sums = part if sums is None else sums + part
        column = jnp.sum(sums, axis=1, keepdims=True)
        state_out[at, :] = slot(-log_cols - (top + jnp.log(column)), 1, state[at, :])
        return math.exp(-log_cols) / column

    sweep(left_of, right, right_rows(u), out, held, acc, times, store, close)


def iteration_body(k, n_got, log_rows, log_cols, left0, left1, right, state, u_old, *refs):
    got, (u_out, state_out, out, held, acc, times) = refs[:n_got], refs[n_got:]
    u = u_old[...] - (log_rows + jnp.log(join_sum(got)))
    u_out[...] = u

    def left_of(at):
        return left_strip(left0, left1, at, state[at, k - 1 : k])

    def close(at, sums, held):
        column = jnp.sum(sums, axis=1, keepdims=True)
        old = state[at, :]
        pot = old[:, k - 1 : k] - (log_cols + jnp.log(column))
        state_out[at, :] = slot(math.exp(log_cols) * column, 8 + k, slot(pot, k, old))
        return math.exp(-log_cols) / column

    store = exponentials(lambda power, place: power)
    sweep(left_of, right, right_rows(u), out, held, acc, times, store, close)


def adjoint_body(k, n_got, log_rows, log_cols, left0, left1, right, state, u_ref, u_before, *refs):
    got, (adj_out, state_out, out, held, acc, times) = refs[:n_got], refs[n_got:]
    if k == ITERS:
        adj_out[...] = 1.0 - math.exp(log_cols) * join_sum(got)
    else:
        adj_out[...] = -join_sum(got)
    u = u_ref[...]
    shift = math.exp(log_rows - log_cols)

    def left_of(at):
        return left_strip(left0, left1, at, state[at, k : k + 1])

    def close(at, sums, held):
        column = jnp.sum(sums, axis=1, keepdims=True)
        old = state[at, :]
        sigma = old[:, 8 + k : 9 + k]
        adj = -shift * sigma * column
        state_out[at, :] = slot(adj, 16 + k - 1, old)
        return sigma * adj

    store = exponentials(lambda power, place: power * adj_out[:, place])
    sweep(left_of, right, right_rows(u + log_cols), out, held, acc, times, store, close)
    out[...] = out[...] * jnp.exp(u_before[...] - u)


def closing_body(n_got, log_cols, log_rows, n_col, n_row, ax0, ax1, by, x_ref, y_ref, state, *refs):
    count_rows, count_cols = x_ref.shape[1], y_ref.shape[1]
    us = [r[:, :count_rows] for r in refs[:ITERS]]
    adjs_rows = [r[:, :count_rows] for r in refs[ITERS : 2 * ITERS - 1]]
    refs = refs[2 * ITERS - 1 :]
    got, refs = refs[:n_got], refs[n_got:]
    first = -join_sum([r[:, :count_rows] for r in got])
    turned = state[0:count_cols, :].T
    vs = [turned[k : k + 1] for k in range(ITERS + 1)]
    adjs_cols = [turned[16 + k : 17 + k] for k in range(1, ITERS)] + [jnp.ones((1, count_cols), F32)]
    adjs_rows = [first] + adjs_rows
    gradient(log_cols, log_rows, n_col, n_row, ax0, ax1, by, x_ref, y_ref, us, vs, adjs_rows, adjs_cols, refs)


def gradient_scratch(dim, count_rows, count_cols, n_col, n_row):
    return [
        pltpu.VMEM((count_rows, 128), F32),
        pltpu.VMEM((128, count_rows), BF16),
        pltpu.VMEM((count_cols, 128), BF16),
        pltpu.VMEM((count_rows, 128), F32),
        pltpu.VMEM((128, count_cols), F32),
        pltpu.VMEM((count_rows, DEPTH), BF16),
        pltpu.VMEM((count_rows, 128), BF16),
        pltpu.VMEM((128, count_cols), BF16),
        pltpu.VMEM((n_col, dim, count_rows // n_col), F32),
        pltpu.VMEM((n_row, dim, count_cols // n_row), F32),
    ]


def repeated(x, y):
    dim, count_rows = x.shape
    count_cols = y.shape[1]
    n_row, n_col = lax.axis_size("row"), lax.axis_size("col")
    all_rows, held_cols = count_rows * n_row, count_cols
    log_rows, log_cols = math.log(all_rows), math.log(count_cols * n_col)
    row, col = (1, all_rows), (1, held_cols)

    xs = [x] + [swap(x, "row", s) for s in range(1, n_row)]
    own = (1, count_rows)
    ax0, ax1, ay0, ay1, by, state, part, x, y = pl.pallas_call(
        prepare_own_body,
        out_shape=[
            shape((count_rows, 128), BF16),
            shape((count_rows, 128)),
            shape((count_cols, 128), BF16),
            shape((count_cols, 128)),
            shape((DEPTH, count_cols), BF16),
            shape((count_cols, 128)),
            shape(own),
            shape(x.shape),
            shape(y.shape),
        ],
        in_specs=[pl.BlockSpec(memory_space=pltpu.HBM)] * 2,
        out_specs=vmem(9),
        scratch_shapes=[pltpu.VMEM((DEPTH, count_rows), BF16), pltpu.SemaphoreType.DMA((2,))],
        compiler_params=pltpu.CompilerParams(vmem_limit_bytes=VMEM_LIMIT),
    )(x, y)
    xs[0] = x
    got = exchange(part, "col", join_lse)
    (u,) = call(functools.partial(first_pot_body, log_rows), [shape(own)], len(got))(*got)
    u_blocks = [u] + [swap(u, "row", s) for s in range(1, n_row)]

    strip = min(SWEEP, held_cols)
    scratch = [
        pltpu.VMEM((2, strip, all_rows), F32),
        pltpu.VMEM((8, all_rows), F32),
        pltpu.VMEM((held_cols // strip, strip, 128), F32),
    ]
    results = [shape(row), shape((held_cols, 128)), shape(row)]
    us = []
    bx, u, state, part = call(
        functools.partial(opening_body, n_row, log_rows, log_cols),
        [shape((DEPTH, all_rows), BF16)] + results,
        3 + 2 * n_row,
        scratch,
    )(ay0, ay1, state, *xs, *u_blocks)
    us.append(u)
    for k in range(2, ITERS + 1):
        got = exchange(part, "col", join_sum)
        u, state, part = call(
            functools.partial(iteration_body, k, len(got), log_rows, log_cols), results, 5 + len(got), scratch
        )(ay0, ay1, bx, state, u, *got)
        us.append(u)
    adjs_rows = []
    for k in range(ITERS, 1, -1):
        got = exchange(part, "col", join_sum)
        adj, state, part = call(
            functools.partial(adjoint_body, k, len(got), log_rows, log_cols),
            results,
            6 + len(got),
            scratch,
        )(ay0, ay1, bx, state, us[k - 1], us[k - 2], *got)
        adjs_rows.insert(0, adj)
    got = exchange(part, "col", join_sum)
    outs = call(
        functools.partial(closing_body, len(got), log_cols, log_rows, n_col, n_row),
        [shape((dim, count_rows // n_col))] * n_col + [shape((dim, count_cols // n_row))] * n_row,
        6 + 2 * ITERS - 1 + len(got),
        gradient_scratch(dim, count_rows, count_cols, n_col, n_row),
    )(ax0, ax1, by, x, y, state, *us, *adjs_rows, *got)
    return scatter(outs[:n_col], "col").T, scatter(outs[n_col:], "row").T


REPEAT_PAIRS = 1 << 23


def on_device(x_points, y_points):
    x = x_points.T
    y = y_points.T
    n_row, n_col = lax.axis_size("row"), lax.axis_size("col")
    if ITERS > 1 and x.shape[1] * n_row * y.shape[1] <= REPEAT_PAIRS:
        return repeated(x, y)
    return shared(x, y)


def shared(x, y):
    dim, count_rows = x.shape
    count_cols = y.shape[1]
    n_row, n_col = lax.axis_size("row"), lax.axis_size("col")
    log_rows = math.log(count_rows * n_row)
    log_cols = math.log(count_cols * n_col)
    row, col = (1, count_rows), (1, count_cols)

    ax0, ax1, ay0, ay1, bx, by, start, part, x, y = pl.pallas_call(
        prepare_body,
        out_shape=[
            shape((count_rows, 128), BF16),
            shape((count_rows, 128)),
            shape((count_cols, 128), BF16),
            shape((count_cols, 128)),
            shape((DEPTH, count_rows), BF16),
            shape((DEPTH, count_cols), BF16),
            shape(col),
            shape(row),
            shape(x.shape),
            shape(y.shape),
        ],
        in_specs=[pl.BlockSpec(memory_space=pltpu.HBM)] * 2,
        out_specs=vmem(10),
        scratch_shapes=[pltpu.SemaphoreType.DMA((2,))],
        compiler_params=pltpu.CompilerParams(vmem_limit_bytes=VMEM_LIMIT),
    )(x, y)

    pots_rows, pots_cols = [], [start]
    for k in range(ITERS):
        got = exchange(part, "col", join_lse)
        pot, part = call(functools.partial(forward_body, -log_rows), [shape(row), shape(col)], 3 + len(got))(
            ax0, ax1, by, *got
        )
        pots_rows.append(pot)
        got = exchange(part, "row", join_lse)
        if k < ITERS - 1:
            pot, part = call(functools.partial(forward_body, -log_cols), [shape(col), shape(row)], 3 + len(got))(
                ay0, ay1, bx, *got
            )
            pots_cols.append(pot)
    pot, part = call(functools.partial(turn_body, -log_cols, log_cols), [shape(col), shape(row)], 4 + len(got))(
        ay0, ay1, bx, pots_rows[-1], *got
    )
    pots_cols.append(pot)

    adjs_rows, adjs_cols = [], []
    for k in reversed(range(1, ITERS)):
        leading = 1.0 if k == ITERS - 1 else 0.0
        got = exchange(part, "col", join_sum)
        adj, part = call(functools.partial(backward_body, leading, log_rows), [shape(row), shape(col)], 5 + len(got))(
            ax0, ax1, by, pots_rows[k], pots_cols[k], *got
        )
        adjs_rows.insert(0, adj)
        got = exchange(part, "row", join_sum)
        adj, part = call(functools.partial(backward_body, 0.0, log_cols), [shape(col), shape(row)], 5 + len(got))(
            ay0, ay1, bx, pots_cols[k], pots_rows[k - 1], *got
        )
        adjs_cols.insert(0, adj)
    got = exchange(part, "col", join_sum)

    share_x, share_y = count_rows // n_col, count_cols // n_row
    outs = call(
        functools.partial(gradient_body, dim, log_cols, log_rows, len(got), n_col, n_row),
        [shape((dim, share_x))] * n_col + [shape((dim, share_y))] * n_row,
        5 + 4 * ITERS - 1 + len(got),
        gradient_scratch(dim, count_rows, count_cols, n_col, n_row),
    )(ax0, ax1, by, x, y, *pots_rows, *pots_cols, *adjs_rows, *adjs_cols, *got)
    grad_x = scatter(outs[:n_col], "col")
    grad_y = scatter(outs[n_col:], "row")
    return (grad_x.T, grad_y.T)


def solution(mesh):
    in_specs = (P(("groups", "row"), None), P(("groups", "col"), None))
    out_specs = (P(("groups", "row", "col"), None), P(("groups", "col", "row"), None))
    return jax.shard_map(
        on_device, mesh=mesh, in_specs=in_specs, out_specs=out_specs, check_vma=False
    )
```

```python
import functools
import math

import jax
import jax.numpy as jnp
from jax import lax
from jax.experimental import pallas as pl
from jax.experimental.pallas import tpu as pltpu
from jax.sharding import PartitionSpec as P

ITERS = 5
EPSILON = 0.05
SCALE = 1.0 / EPSILON
DEPTH = 256
CHUNK = 256
F32 = jnp.float32
BF16 = jnp.bfloat16
VMEM_LIMIT = 32 * 1024 * 1024
SWEEP_LIMIT = 24 * 1024 * 1024


def split3(v):
    high = v.astype(BF16).astype(F32)
    rest = v - high
    mid = rest.astype(BF16).astype(F32)
    low = (rest - mid).astype(BF16).astype(F32)
    return high, mid, low


def vmem(count):
    return [pl.BlockSpec(memory_space=pltpu.VMEM)] * count


def call(body, outs, count, scratch=(), limit=VMEM_LIMIT):
    return pl.pallas_call(
        body,
        out_shape=outs,
        in_specs=vmem(count),
        out_specs=vmem(len(outs)),
        scratch_shapes=list(scratch),
        compiler_params=pltpu.CompilerParams(vmem_limit_bytes=limit),
    )


def shape(dims, dtype=F32):
    return jax.ShapeDtypeStruct(dims, dtype)


def factors(points, order):
    parts = split3(points)
    width = points.shape[1]
    blocks = [parts[o] for o in order]
    zero16 = jnp.zeros((16, width), F32)
    tail = jnp.zeros((DEPTH - 144 - 2 * points.shape[0], width), F32)
    return jnp.concatenate(blocks[:4] + [zero16] + blocks[4:] + [tail], axis=0)


X_ORDER = (0, 0, 1, 0, 2, 1)
Y_ORDER = (0, 1, 0, 2, 0, 1)


def prepare_body(x_hbm, y_hbm, ax0, ax1, ay0, ay1, bx, by, start_ref, out, x_ref, y_ref, sems):
    copies = [
        pltpu.make_async_copy(x_hbm, x_ref, sems.at[0]),
        pltpu.make_async_copy(y_hbm, y_ref, sems.at[1]),
    ]
    for copy in copies:
        copy.start()
    for copy in copies:
        copy.wait()
    x = x_ref[...]
    y = y_ref[...]
    xf = factors(x * (2.0 * SCALE), X_ORDER)
    yf = factors(y, Y_ORDER)
    for factor, left0, left1, right in ((xf, ax0, ax1, bx), (yf, ay0, ay1, by)):
        right[...] = factor.astype(BF16)
        turned = factor.T
        left0[...] = turned[:, :128].astype(BF16)
        left1[...] = turned[:, 128:]
    start = -SCALE * jnp.sum(y * y, axis=0, keepdims=True)
    start_ref[...] = start
    left, unused = left_factor(ay0, ay1, start)
    partial_lse(left, bx, out)


def left_factor(left0, left1, pot, adj=None):
    width = pot.shape[1]
    high, mid, low = split3(pot)
    one = jnp.ones((1, width), F32)
    rows = [high, mid, low, one, one, one, jnp.zeros_like(one)]
    rows.append(jnp.zeros_like(one) if adj is None else adj)
    rows.append(jnp.zeros((120, width), F32))
    turned = jnp.concatenate(rows, axis=0).T
    column = None
    if adj is not None:
        column = turned[:, 7:8]
        lane = lax.broadcasted_iota(jnp.int32, turned.shape, 1)
        turned = jnp.where(lane == 7, 0.0, turned)
    return jnp.concatenate([left0[...], (left1[...] + turned).astype(BF16)], axis=1), column


def right_rows(pot):
    width = pot.shape[1]
    one = jnp.ones((3, width), F32)
    high, mid, low = split3(pot)
    return jnp.concatenate([one, high, mid, low, jnp.zeros((10, width), F32)], axis=0).astype(BF16)


def right_chunk(right, rows, at, wide):
    return jnp.concatenate(
        [right[0:128, at : at + wide], rows[:, at : at + wide], right[144:DEPTH, at : at + wide]], axis=0
    )


def matmul(a, b):
    return jnp.dot(a, b, preferred_element_type=F32)


def partial_lse(left, right, out):
    width = right.shape[1]
    rows = right_rows(jnp.zeros((1, width), F32))
    wide = min(CHUNK, width)
    for at in range(0, width, wide):
        scores = matmul(left, right_chunk(right, rows, at, wide))
        top = jnp.max(scores, axis=0, keepdims=True)
        total = jnp.sum(jnp.exp(scores - top), axis=0, keepdims=True)
        out[:, at : at + wide] = top + jnp.log(total)


def join_lse(parts):
    parts = [p[...] for p in parts]
    top = functools.reduce(jnp.maximum, parts)
    return top + jnp.log(sum(jnp.exp(p - top) for p in parts))


def join_sum(parts):
    return sum(p[...] for p in parts)


def join_body(join, *refs):
    refs[-1][...] = join(refs[:-1])


def forward_body(log_mass, left0, left1, right, *refs):
    got, (pot_out, out) = refs[:-2], refs[-2:]
    pot = log_mass - join_lse(got)
    pot_out[...] = pot
    left, unused = left_factor(left0, left1, pot)
    partial_lse(left, right, out)


def weighted_sums(left, column, right, rows, out):
    width = right.shape[1]
    wide = min(CHUNK, width)
    for at in range(0, width, wide):
        scores = matmul(left, right_chunk(right, rows, at, wide))
        out[:, at : at + wide] = jnp.sum(jnp.exp(scores) * column, axis=0, keepdims=True)


def turn_body(log_mass, log_scale, left0, left1, right, pot_right, *refs):
    got, (pot_out, out) = refs[:-2], refs[-2:]
    pot = log_mass - join_lse(got)
    pot_out[...] = pot
    left, column = left_factor(left0, left1, pot, jnp.ones_like(pot))
    weighted_sums(left, column, right, right_rows(pot_right[...] + log_scale), out)


def backward_body(leading, log_scale, left0, left1, right, pot_left, pot_right, *refs):
    got, (adj_out, out) = refs[:-2], refs[-2:]
    adj = leading - join_sum(got)
    adj_out[...] = adj
    left, column = left_factor(left0, left1, pot_left[...], adj)
    weighted_sums(left, column, right, right_rows(pot_right[...] + log_scale), out)


SPREAD = 20.0
STRIP = 256


def gradient_body(dim, log_cols, log_rows, n_got, n_col, n_row, ax0, ax1, by, x_ref, y_ref, *refs):
    pots_rows = refs[:ITERS]
    pots_cols = refs[ITERS : 2 * ITERS + 1]
    adjs_rows = refs[2 * ITERS + 1 : 3 * ITERS]
    adjs_cols = refs[3 * ITERS : 4 * ITERS - 1]
    refs = refs[4 * ITERS - 1 :]
    got, refs = refs[:n_got], refs[n_got:]
    us = [p[...] for p in pots_rows]
    vs = [p[...] for p in pots_cols]
    first = (1.0 if ITERS == 1 else 0.0) - join_sum(got)
    adjs_rows = [first] + [a[...] for a in adjs_rows]
    adjs_cols = [a[...] for a in adjs_cols] + [jnp.ones(vs[0].shape, F32)]
    gradient(log_cols, log_rows, n_col, n_row, ax0, ax1, by, x_ref, y_ref, us, vs, adjs_rows, adjs_cols, refs)


def gradient(log_cols, log_rows, n_col, n_row, ax0, ax1, by, x_ref, y_ref, us, vs, adjs_rows, adjs_cols, refs):
    outs_x, outs_y = refs[:n_col], refs[n_col : n_col + n_row]
    cols_rows, x_parts, y_parts, gx, gy, left_e, left_r, right_r, all_x, all_y = refs[n_col + n_row :]
    dim, count_rows = x_ref.shape
    count_cols = y_ref.shape[1]
    shift = log_rows - log_cols

    x = x_ref[...]
    y = y_ref[...]
    one = jnp.ones((1, count_cols), F32)
    pad = jnp.zeros((31, count_cols), F32)
    y_parts[...] = jnp.concatenate(list(split3(y)) + [one, pad], axis=0).T.astype(BF16)
    one = jnp.ones((1, count_rows), F32)
    pad = jnp.zeros((31, count_rows), F32)
    x_parts[...] = jnp.concatenate(list(split3(x)) + [one, pad], axis=0).astype(BF16)
    gy[...] = jnp.zeros_like(gy)

    far_u = functools.reduce(jnp.maximum, [jnp.abs(u - us[-1]) for u in us])
    far_v = functools.reduce(jnp.maximum, [jnp.abs(v - vs[-1]) for v in vs])
    near = jnp.maximum(jnp.max(far_u), jnp.max(far_v)) < SPREAD

    def add_strip(at, total):
        upper = total.astype(BF16)
        lower = (total - upper.astype(F32)).astype(BF16)
        gx[at, :] = matmul(upper, y_parts[...]) + matmul(lower, y_parts[...])
        gy[...] += matmul(x_parts[:, at], upper) + matmul(x_parts[:, at], lower)

    @pl.when(near)
    def factored():
        alpha = [jnp.exp(u - us[-1]) for u in us]
        beta = [jnp.exp(v - vs[-1]) for v in vs]
        p_rows = alpha + [a * adj for a, adj in zip(alpha, adjs_rows)]
        q_rows = [b * adj for b, adj in zip(beta[1:], adjs_cols)] + [b * math.exp(shift) for b in beta[:-1]]
        fill = 16 - 2 * ITERS
        p_split = split3(jnp.concatenate(p_rows + [jnp.zeros((fill, count_rows), F32)], axis=0))
        q_split = split3(jnp.concatenate(q_rows + [jnp.zeros((fill, count_cols), F32)], axis=0))
        tail = [jnp.zeros((32, count_rows), F32)]
        left_r[...] = jnp.concatenate([p_split[o] for o in X_ORDER] + tail, axis=0).T.astype(BF16)
        tail = [jnp.zeros((32, count_cols), F32)]
        right_r[...] = jnp.concatenate([q_split[o] for o in Y_ORDER] + tail, axis=0).astype(BF16)
        left, unused = left_factor(ax0, ax1, us[-1] + log_cols)
        left_e[...] = left
        right = right_chunk(by, right_rows(vs[-1]), 0, count_cols)
        strip = min(STRIP, count_rows)
        for step in range(count_rows // strip):
            at = pl.ds(step * strip, strip)
            total = jnp.exp(matmul(left_e[at, :], right)) * matmul(left_r[at, :], right_r[...])
            add_strip(at, total)

    @pl.when(jnp.logical_not(near))
    def separate():
        stack = [u + log_cols for u in us] + adjs_rows
        stack.append(jnp.zeros((128 - len(stack), count_rows), F32))
        cols_rows[...] = jnp.concatenate(stack, axis=0).T
        strip = 128

        def block(step, carry):
            at = pl.ds(pl.multiple_of(step * strip, strip), strip)
            left = jnp.concatenate([ax0[at, :], ax1[at, :].astype(BF16)], axis=1)
            inner = matmul(left, by[...])
            columns = cols_rows[at, :]
            total = jnp.zeros_like(inner)
            for k in range(ITERS):
                base = inner + columns[:, k : k + 1]
                total += jnp.exp(base + vs[k + 1]) * adjs_cols[k]
                total += jnp.exp(base + (vs[k] + shift)) * columns[:, ITERS + k : ITERS + k + 1]
            add_strip(at, total)
            return carry

        lax.fori_loop(0, count_rows // strip, block, 0)

    def finish(points, sums):
        mixed = sums[0:dim] + sums[dim : 2 * dim] + sums[2 * dim : 3 * dim]
        return 2.0 * (points * sums[3 * dim : 3 * dim + 1] - mixed)

    for value, held, outs, axis in (
        (finish(x, gx[...].T), all_x, outs_x, "col"),
        (finish(y, gy[...]), all_y, outs_y, "row"),
    ):
        share = held.shape[2]
        for p in range(held.shape[0]):
            held[p] = value[:, p * share : (p + 1) * share]
        me = lax.axis_index(axis)
        for s, out in enumerate(outs):
            out[...] = held[me ^ s]


def swap(value, axis, distance):
    return lax.ppermute(value, axis, [(d, d ^ distance) for d in range(lax.axis_size(axis))])


def exchange(part, axis, join):
    size = lax.axis_size(axis)
    assert size & (size - 1) == 0
    if size == 4:
        return (part,) + tuple(swap(part, axis, d) for d in (2, 3, 1))
    distance = 1
    got = (part,)
    while distance < size:
        if len(got) > 1:
            (part,) = call(functools.partial(join_body, join), [shape(part.shape)], len(got))(*got)
        got = (part, swap(part, axis, distance))
        distance *= 2
    return got


def scatter(pieces, axis):
    got = [pieces[0]] + [swap(pieces[s], axis, s) for s in range(1, len(pieces))]
    return sum(got[1:], got[0])


def slot(column, lane, state):
    return jnp.where(lax.broadcasted_iota(jnp.int32, state.shape, 1) == lane, column, state)


def left_strip(left0, left1, at, pot):
    strip = left1[at, :]
    for lane, part in enumerate(split3(jnp.broadcast_to(pot, strip.shape))):
        strip = slot(part, lane, strip)
    return jnp.concatenate([left0[at, :], strip.astype(BF16)], axis=1)


def halves(value):
    return sum(value[:, p : p + 128] for p in range(0, value.shape[1], 128))


def octets(value):
    return jnp.sum(value.reshape(value.shape[0] // 8, 8, value.shape[1]), axis=0)


SWEEP = 256


def sweep(left_of, right, rows, out, held_of, acc, times, store, close):
    strips, strip = times.shape[:2]
    wide_all = right.shape[1]
    for s in range(strips + 1):
        at = slice(s * strip, (s + 1) * strip)
        left = left_of(at) if s < strips else None
        sums = None
        for c in range(0, wide_all, CHUNK):
            place = slice(c, c + CHUNK)
            if s < strips:
                sums = store(held_of(s), matmul(left, right_chunk(right, rows, c, CHUNK)), place, sums)
            if s > 0:
                factor = times[s - 1]
                part = octets(held_of(s - 1)[:, place] * jnp.concatenate([factor] * (CHUNK // 128), axis=1))
                if s > 1:
                    part += acc[:, place]
                if s < strips:
                    acc[:, place] = part
                else:
                    out[:, place] = jnp.sum(part, axis=0, keepdims=True)
        if s < strips:
            times[s] = jnp.broadcast_to(close(at, sums, held_of(s)), times.shape[1:])


def exponentials(weigh):
    def store(held, scores, place, sums):
        power = jnp.exp(scores)
        held[:, place] = power
        part = halves(weigh(power, place))
        return part if sums is None else sums + part

    return store


def prepare_own_body(x_hbm, y_hbm, ax0, ax1, ay0, ay1, by, state, out, x_ref, y_ref, bx, sems):
    copies = [
        pltpu.make_async_copy(x_hbm, x_ref, sems.at[0]),
        pltpu.make_async_copy(y_hbm, y_ref, sems.at[1]),
    ]
    for copy in copies:
        copy.start()
    for copy in copies:
        copy.wait()
    x = x_ref[...]
    y = y_ref[...]
    xf = factors(x * (2.0 * SCALE), X_ORDER)
    yf = factors(y, Y_ORDER)
    for factor, left0, left1, right in ((xf, ax0, ax1, bx), (yf, ay0, ay1, by)):
        right[...] = factor.astype(BF16)
        turned = factor.T
        left0[...] = turned[:, :128].astype(BF16)
        left1[...] = turned[:, 128:]
    start = -SCALE * jnp.sum(y * y, axis=0, keepdims=True)
    state[...] = jnp.concatenate([start, jnp.zeros((127, y.shape[1]), F32)], axis=0).T
    left, unused = left_factor(ay0, ay1, start)
    partial_lse(left, bx, out)
    lane = lax.broadcasted_iota(jnp.int32, ay1.shape, 1)
    ay1[...] = jnp.where((lane >= 3) & (lane < 6), 1.0, ay1[...])


def first_pot_body(log_rows, *refs):
    refs[-1][...] = -log_rows - join_lse(refs[:-1])


def opening_body(n_row, log_rows, log_cols, left0, left1, state, *refs):
    xs, us = refs[:n_row], refs[n_row : 2 * n_row]
    right, kept, u_out, state_out, out, acc, times = refs[2 * n_row :]
    strip = times.shape[1]
    x = jnp.concatenate([r[...] for r in xs], axis=1)
    right[...] = factors(x * (2.0 * SCALE), X_ORDER).astype(BF16)
    u = jnp.concatenate([r[...] for r in us], axis=1)
    u_out[...] = u

    def left_of(at):
        return jnp.concatenate([left0[at, :], left1[at, :].astype(BF16)], axis=1)

    def store(held, scores, place, tops):
        held[:, place] = scores
        for p in range(0, CHUNK, 128):
            part = scores[:, p : p + 128]
            tops = part if tops is None else jnp.maximum(tops, part)
        return tops

    def close(at, tops, held):
        top = jnp.max(tops, axis=1, keepdims=True)
        sums = None
        for c in range(0, held.shape[1], CHUNK):
            place = slice(c, c + CHUNK)
            power = jnp.exp(held[:, place] - top)
            held[:, place] = power
            part = halves(power)
            sums = part if sums is None else sums + part
        column = jnp.sum(sums, axis=1, keepdims=True)
        pot = -log_cols - (top + jnp.log(column))
        state_out[at, :] = slot(pot, 1, slot(-top, BASE, state[at, :]))
        return math.exp(-log_cols) / column

    def held_of(s):
        return kept.at[s * strip : (s + 1) * strip]

    sweep(left_of, right, right_rows(u), out, held_of, acc, times, store, close)


BASE = 6
NEAR = 25.0


def scaled(kept, row, column_of, out, acc, hold):
    count, total = kept.shape
    block = min(128, count)

    def across(index, carry):
        at = pl.ds(pl.multiple_of(index * block, block), block)
        sums = None
        for c in range(0, total, 128):
            part = kept[at, c : c + 128] * row[:, c : c + 128]
            sums = part if sums is None else sums + part
        hold[at, :] = sums
        return carry

    lax.fori_loop(0, count // block, across, 0)
    hold[...] = jnp.broadcast_to(column_of(jnp.sum(hold[...], axis=1, keepdims=True)), hold.shape)
    acc[...] = jnp.zeros_like(acc)

    def down(index, carry):
        at = pl.ds(pl.multiple_of(index * block, block), block)
        factor = hold[at, :]
        for c in range(0, total, 128):
            acc[:, c : c + 128] += octets(kept[at, c : c + 128] * factor)
        return carry

    lax.fori_loop(0, count // block, down, 0)
    out[...] = jnp.sum(acc[...], axis=0, keepdims=True)


def iteration_body(k, n_got, log_rows, log_cols, left0, left1, right, kept, state, u_first, u_old, *refs):
    got, (u_out, state_out, out, held, acc, times, hold, row) = refs[:n_got], refs[n_got:]
    u = u_old[...] - (log_rows + jnp.log(join_sum(got)))
    u_out[...] = u
    apart = u - u_first[...]
    near = jnp.max(jnp.abs(apart)) < NEAR

    @pl.when(near)
    def scale():
        row[...] = jnp.exp(apart)

        def column_of(sums):
            old = state[...]
            state_out[...] = slot(old[:, BASE : BASE + 1] - (log_cols + jnp.log(sums)), k, old)
            return math.exp(-log_cols) / sums

        scaled(kept, row, column_of, out, acc, hold)
        out[...] = out[...] * row[...]

    @pl.when(jnp.logical_not(near))
    def renew():
        def left_of(at):
            return left_strip(left0, left1, at, state[at, k - 1 : k])

        def close(at, sums, held):
            column = jnp.sum(sums, axis=1, keepdims=True)
            old = state[at, :]
            state_out[at, :] = slot(old[:, k - 1 : k] - (log_cols + jnp.log(column)), k, old)
            return math.exp(-log_cols) / column

        store = exponentials(lambda power, place: power)
        sweep(left_of, right, right_rows(u), out, lambda s: held.at[s % 2], acc, times, store, close)


def adjoint_body(k, n_got, log_rows, log_cols, left0, left1, right, kept, state, u_first, u_ref, u_before, *refs):
    got, (adj_out, state_out, out, held, acc, times, hold, row) = refs[:n_got], refs[n_got:]
    if k == ITERS:
        adj_out[...] = 1.0 - math.exp(log_cols) * join_sum(got)
    else:
        adj_out[...] = -join_sum(got)
    u, before = u_ref[...], u_before[...]
    shift = math.exp(log_rows - log_cols)
    mass = math.exp(log_cols)
    apart, apart_before = u - u_first[...], before - u_first[...]
    near = jnp.max(jnp.maximum(jnp.abs(apart), jnp.abs(apart_before))) < NEAR

    @pl.when(near)
    def scale():
        row[...] = jnp.exp(apart) * adj_out[...]

        def column_of(sums):
            old = state[...]
            beta = mass * jnp.exp(old[:, k - 1 : k] - old[:, BASE : BASE + 1])
            adj = -shift * beta * sums
            state_out[...] = slot(adj, 16 + k - 1, old)
            return beta * adj

        scaled(kept, row, column_of, out, acc, hold)
        out[...] = out[...] * jnp.exp(apart_before)

    @pl.when(jnp.logical_not(near))
    def renew():
        def left_of(at):
            return left_strip(left0, left1, at, state[at, k : k + 1])

        def close(at, sums, held):
            column = jnp.sum(sums, axis=1, keepdims=True)
            old = state[at, :]
            sigma = jnp.exp(old[:, k - 1 : k] - old[:, k : k + 1])
            adj = -shift * sigma * column
            state_out[at, :] = slot(adj, 16 + k - 1, old)
            return sigma * adj

        store = exponentials(lambda power, place: power * adj_out[:, place])
        rows = right_rows(u + log_cols)
        sweep(left_of, right, rows, out, lambda s: held.at[s % 2], acc, times, store, close)
        out[...] = out[...] * jnp.exp(before - u)


def closing_body(n_got, log_cols, log_rows, n_col, n_row, ax0, ax1, by, x_ref, y_ref, state, *refs):
    count_rows, count_cols = x_ref.shape[1], y_ref.shape[1]
    us = [r[:, :count_rows] for r in refs[:ITERS]]
    adjs_rows = [r[:, :count_rows] for r in refs[ITERS : 2 * ITERS - 1]]
    refs = refs[2 * ITERS - 1 :]
    got, refs = refs[:n_got], refs[n_got:]
    first = -join_sum([r[:, :count_rows] for r in got])
    turned = state[0:count_cols, :].T
    vs = [turned[k : k + 1] for k in range(ITERS + 1)]
    adjs_cols = [turned[16 + k : 17 + k] for k in range(1, ITERS)] + [jnp.ones((1, count_cols), F32)]
    adjs_rows = [first] + adjs_rows
    gradient(log_cols, log_rows, n_col, n_row, ax0, ax1, by, x_ref, y_ref, us, vs, adjs_rows, adjs_cols, refs)


def gradient_scratch(dim, count_rows, count_cols, n_col, n_row):
    return [
        pltpu.VMEM((count_rows, 128), F32),
        pltpu.VMEM((128, count_rows), BF16),
        pltpu.VMEM((count_cols, 128), BF16),
        pltpu.VMEM((count_rows, 128), F32),
        pltpu.VMEM((128, count_cols), F32),
        pltpu.VMEM((count_rows, DEPTH), BF16),
        pltpu.VMEM((count_rows, 128), BF16),
        pltpu.VMEM((128, count_cols), BF16),
        pltpu.VMEM((n_col, dim, count_rows // n_col), F32),
        pltpu.VMEM((n_row, dim, count_cols // n_row), F32),
    ]


def repeated(x, y):
    dim, count_rows = x.shape
    count_cols = y.shape[1]
    n_row, n_col = lax.axis_size("row"), lax.axis_size("col")
    all_rows, held_cols = count_rows * n_row, count_cols
    log_rows, log_cols = math.log(all_rows), math.log(count_cols * n_col)
    row, col = (1, all_rows), (1, held_cols)

    xs = [x] + [swap(x, "row", s) for s in range(1, n_row)]
    own = (1, count_rows)
    ax0, ax1, ay0, ay1, by, state, part, x, y = pl.pallas_call(
        prepare_own_body,
        out_shape=[
            shape((count_rows, 128), BF16),
            shape((count_rows, 128)),
            shape((count_cols, 128), BF16),
            shape((count_cols, 128)),
            shape((DEPTH, count_cols), BF16),
            shape((count_cols, 128)),
            shape(own),
            shape(x.shape),
            shape(y.shape),
        ],
        in_specs=[pl.BlockSpec(memory_space=pltpu.HBM)] * 2,
        out_specs=vmem(9),
        scratch_shapes=[pltpu.VMEM((DEPTH, count_rows), BF16), pltpu.SemaphoreType.DMA((2,))],
        compiler_params=pltpu.CompilerParams(vmem_limit_bytes=VMEM_LIMIT),
    )(x, y)
    xs[0] = x
    got = exchange(part, "col", join_lse)
    (u,) = call(functools.partial(first_pot_body, log_rows), [shape(own)], len(got))(*got)
    u_blocks = [u] + [swap(u, "row", s) for s in range(1, n_row)]

    strip = min(SWEEP, held_cols)
    sums = [pltpu.VMEM((8, all_rows), F32), pltpu.VMEM((held_cols // strip, strip, 128), F32)]
    scratch = [pltpu.VMEM((2, strip, all_rows), F32)] + sums
    scratch += [pltpu.VMEM((held_cols, 128), F32), pltpu.VMEM(row, F32)]
    results = [shape(row), shape((held_cols, 128)), shape(row)]
    us = []
    bx, kept, u, state, part = call(
        functools.partial(opening_body, n_row, log_rows, log_cols),
        [shape((DEPTH, all_rows), BF16), shape((held_cols, all_rows))] + results,
        3 + 2 * n_row,
        sums,
        SWEEP_LIMIT,
    )(ay0, ay1, state, *xs, *u_blocks)
    us.append(u)
    for k in range(2, ITERS + 1):
        got = exchange(part, "col", join_sum)
        u, state, part = call(
            functools.partial(iteration_body, k, len(got), log_rows, log_cols),
            results,
            7 + len(got),
            scratch,
            SWEEP_LIMIT,
        )(ay0, ay1, bx, kept, state, us[0], u, *got)
        us.append(u)
    adjs_rows = []
    for k in range(ITERS, 1, -1):
        got = exchange(part, "col", join_sum)
        adj, state, part = call(
            functools.partial(adjoint_body, k, len(got), log_rows, log_cols),
            results,
            8 + len(got),
            scratch,
            SWEEP_LIMIT,
        )(ay0, ay1, bx, kept, state, us[0], us[k - 1], us[k - 2], *got)
        adjs_rows.insert(0, adj)
    got = exchange(part, "col", join_sum)
    outs = call(
        functools.partial(closing_body, len(got), log_cols, log_rows, n_col, n_row),
        [shape((dim, count_rows // n_col))] * n_col + [shape((dim, count_cols // n_row))] * n_row,
        6 + 2 * ITERS - 1 + len(got),
        gradient_scratch(dim, count_rows, count_cols, n_col, n_row),
    )(ax0, ax1, by, x, y, state, *us, *adjs_rows, *got)
    return scatter(outs[:n_col], "col").T, scatter(outs[n_col:], "row").T


REPEAT_PAIRS = 1 << 23


def on_device(x_points, y_points):
    x = x_points.T
    y = y_points.T
    n_row, n_col = lax.axis_size("row"), lax.axis_size("col")
    if ITERS > 1 and x.shape[1] * n_row * y.shape[1] <= REPEAT_PAIRS:
        return repeated(x, y)
    return shared(x, y)


def shared(x, y):
    dim, count_rows = x.shape
    count_cols = y.shape[1]
    n_row, n_col = lax.axis_size("row"), lax.axis_size("col")
    log_rows = math.log(count_rows * n_row)
    log_cols = math.log(count_cols * n_col)
    row, col = (1, count_rows), (1, count_cols)

    ax0, ax1, ay0, ay1, bx, by, start, part, x, y = pl.pallas_call(
        prepare_body,
        out_shape=[
            shape((count_rows, 128), BF16),
            shape((count_rows, 128)),
            shape((count_cols, 128), BF16),
            shape((count_cols, 128)),
            shape((DEPTH, count_rows), BF16),
            shape((DEPTH, count_cols), BF16),
            shape(col),
            shape(row),
            shape(x.shape),
            shape(y.shape),
        ],
        in_specs=[pl.BlockSpec(memory_space=pltpu.HBM)] * 2,
        out_specs=vmem(10),
        scratch_shapes=[pltpu.SemaphoreType.DMA((2,))],
        compiler_params=pltpu.CompilerParams(vmem_limit_bytes=VMEM_LIMIT),
    )(x, y)

    pots_rows, pots_cols = [], [start]
    for k in range(ITERS):
        got = exchange(part, "col", join_lse)
        pot, part = call(functools.partial(forward_body, -log_rows), [shape(row), shape(col)], 3 + len(got))(
            ax0, ax1, by, *got
        )
        pots_rows.append(pot)
        got = exchange(part, "row", join_lse)
        if k < ITERS - 1:
            pot, part = call(functools.partial(forward_body, -log_cols), [shape(col), shape(row)], 3 + len(got))(
                ay0, ay1, bx, *got
            )
            pots_cols.append(pot)
    pot, part = call(functools.partial(turn_body, -log_cols, log_cols), [shape(col), shape(row)], 4 + len(got))(
        ay0, ay1, bx, pots_rows[-1], *got
    )
    pots_cols.append(pot)

    adjs_rows, adjs_cols = [], []
    for k in reversed(range(1, ITERS)):
        leading = 1.0 if k == ITERS - 1 else 0.0
        got = exchange(part, "col", join_sum)
        adj, part = call(functools.partial(backward_body, leading, log_rows), [shape(row), shape(col)], 5 + len(got))(
            ax0, ax1, by, pots_rows[k], pots_cols[k], *got
        )
        adjs_rows.insert(0, adj)
        got = exchange(part, "row", join_sum)
        adj, part = call(functools.partial(backward_body, 0.0, log_cols), [shape(col), shape(row)], 5 + len(got))(
            ay0, ay1, bx, pots_cols[k], pots_rows[k - 1], *got
        )
        adjs_cols.insert(0, adj)
    got = exchange(part, "col", join_sum)

    share_x, share_y = count_rows // n_col, count_cols // n_row
    outs = call(
        functools.partial(gradient_body, dim, log_cols, log_rows, len(got), n_col, n_row),
        [shape((dim, share_x))] * n_col + [shape((dim, share_y))] * n_row,
        5 + 4 * ITERS - 1 + len(got),
        gradient_scratch(dim, count_rows, count_cols, n_col, n_row),
    )(ax0, ax1, by, x, y, *pots_rows, *pots_cols, *adjs_rows, *adjs_cols, *got)
    grad_x = scatter(outs[:n_col], "col")
    grad_y = scatter(outs[n_col:], "row")
    return (grad_x.T, grad_y.T)


def solution(mesh):
    in_specs = (P(("groups", "row"), None), P(("groups", "col"), None))
    out_specs = (P(("groups", "row", "col"), None), P(("groups", "col", "row"), None))
    return jax.shard_map(
        on_device, mesh=mesh, in_specs=in_specs, out_specs=out_specs, check_vma=False
    )
```

```python
import functools
import math

import jax
import jax.numpy as jnp
from jax import lax
from jax.experimental import pallas as pl
from jax.experimental.pallas import tpu as pltpu
from jax.sharding import PartitionSpec as P

ITERS = 5
EPSILON = 0.05
SCALE = 1.0 / EPSILON
DEPTH = 256
CHUNK = 256
F32 = jnp.float32
BF16 = jnp.bfloat16
VMEM_LIMIT = 32 * 1024 * 1024
SWEEP_LIMIT = 24 * 1024 * 1024


def split3(v):
    high = v.astype(BF16).astype(F32)
    rest = v - high
    mid = rest.astype(BF16).astype(F32)
    low = (rest - mid).astype(BF16).astype(F32)
    return high, mid, low


def vmem(count):
    return [pl.BlockSpec(memory_space=pltpu.VMEM)] * count


def call(body, outs, count, scratch=(), limit=VMEM_LIMIT, cost=None):
    return pl.pallas_call(
        body,
        out_shape=outs,
        in_specs=vmem(count),
        out_specs=vmem(len(outs)),
        scratch_shapes=list(scratch),
        compiler_params=pltpu.CompilerParams(vmem_limit_bytes=limit),
        cost_estimate=cost,
    )


def shape(dims, dtype=F32):
    return jax.ShapeDtypeStruct(dims, dtype)


def factors(points, order):
    parts = split3(points)
    width = points.shape[1]
    blocks = [parts[o] for o in order]
    zero16 = jnp.zeros((16, width), F32)
    tail = jnp.zeros((DEPTH - 144 - 2 * points.shape[0], width), F32)
    return jnp.concatenate(blocks[:4] + [zero16] + blocks[4:] + [tail], axis=0)


X_ORDER = (0, 0, 1, 0, 2, 1)
Y_ORDER = (0, 1, 0, 2, 0, 1)


def prepare_body(x_hbm, y_hbm, ax0, ax1, ay0, ay1, bx, by, start_ref, out, x_ref, y_ref, sems):
    copies = [
        pltpu.make_async_copy(x_hbm, x_ref, sems.at[0]),
        pltpu.make_async_copy(y_hbm, y_ref, sems.at[1]),
    ]
    for copy in copies:
        copy.start()
    for copy in copies:
        copy.wait()
    x = x_ref[...]
    y = y_ref[...]
    xf = factors(x * (2.0 * SCALE), X_ORDER)
    yf = factors(y, Y_ORDER)
    for factor, left0, left1, right in ((xf, ax0, ax1, bx), (yf, ay0, ay1, by)):
        right[...] = factor.astype(BF16)
        turned = factor.T
        left0[...] = turned[:, :128].astype(BF16)
        left1[...] = turned[:, 128:]
    start = -SCALE * jnp.sum(y * y, axis=0, keepdims=True)
    start_ref[...] = start
    left, unused = left_factor(ay0, ay1, start)
    partial_lse(left, bx, out)


def left_factor(left0, left1, pot, adj=None):
    width = pot.shape[1]
    high, mid, low = split3(pot)
    one = jnp.ones((1, width), F32)
    rows = [high, mid, low, one, one, one, jnp.zeros_like(one)]
    rows.append(jnp.zeros_like(one) if adj is None else adj)
    rows.append(jnp.zeros((120, width), F32))
    turned = jnp.concatenate(rows, axis=0).T
    column = None
    if adj is not None:
        column = turned[:, 7:8]
        lane = lax.broadcasted_iota(jnp.int32, turned.shape, 1)
        turned = jnp.where(lane == 7, 0.0, turned)
    return jnp.concatenate([left0[...], (left1[...] + turned).astype(BF16)], axis=1), column


def right_rows(pot):
    width = pot.shape[1]
    one = jnp.ones((3, width), F32)
    high, mid, low = split3(pot)
    return jnp.concatenate([one, high, mid, low, jnp.zeros((10, width), F32)], axis=0).astype(BF16)


def right_chunk(right, rows, at, wide):
    return jnp.concatenate(
        [right[0:128, at : at + wide], rows[:, at : at + wide], right[144:DEPTH, at : at + wide]], axis=0
    )


def matmul(a, b):
    return jnp.dot(a, b, preferred_element_type=F32)


def partial_lse(left, right, out):
    width = right.shape[1]
    rows = right_rows(jnp.zeros((1, width), F32))
    wide = min(CHUNK, width)
    for at in range(0, width, wide):
        scores = matmul(left, right_chunk(right, rows, at, wide))
        top = jnp.max(scores, axis=0, keepdims=True)
        total = jnp.sum(jnp.exp(scores - top), axis=0, keepdims=True)
        out[:, at : at + wide] = top + jnp.log(total)


def join_lse(parts):
    parts = [p[...] for p in parts]
    top = functools.reduce(jnp.maximum, parts)
    return top + jnp.log(sum(jnp.exp(p - top) for p in parts))


def join_sum(parts):
    return sum(p[...] for p in parts)


def join_body(join, *refs):
    refs[-1][...] = join(refs[:-1])


def forward_body(log_mass, left0, left1, right, *refs):
    got, (pot_out, out) = refs[:-2], refs[-2:]
    pot = log_mass - join_lse(got)
    pot_out[...] = pot
    left, unused = left_factor(left0, left1, pot)
    partial_lse(left, right, out)


def weighted_sums(left, column, right, rows, out):
    width = right.shape[1]
    wide = min(CHUNK, width)
    for at in range(0, width, wide):
        scores = matmul(left, right_chunk(right, rows, at, wide))
        out[:, at : at + wide] = jnp.sum(jnp.exp(scores) * column, axis=0, keepdims=True)


def turn_body(log_mass, log_scale, left0, left1, right, pot_right, *refs):
    got, (pot_out, out) = refs[:-2], refs[-2:]
    pot = log_mass - join_lse(got)
    pot_out[...] = pot
    left, column = left_factor(left0, left1, pot, jnp.ones_like(pot))
    weighted_sums(left, column, right, right_rows(pot_right[...] + log_scale), out)


def backward_body(leading, log_scale, left0, left1, right, pot_left, pot_right, *refs):
    got, (adj_out, out) = refs[:-2], refs[-2:]
    adj = leading - join_sum(got)
    adj_out[...] = adj
    left, column = left_factor(left0, left1, pot_left[...], adj)
    weighted_sums(left, column, right, right_rows(pot_right[...] + log_scale), out)


SPREAD = 20.0
STRIP = 256


def gradient_body(dim, log_cols, log_rows, n_got, n_col, n_row, ax0, ax1, by, x_ref, y_ref, *refs):
    pots_rows = refs[:ITERS]
    pots_cols = refs[ITERS : 2 * ITERS + 1]
    adjs_rows = refs[2 * ITERS + 1 : 3 * ITERS]
    adjs_cols = refs[3 * ITERS : 4 * ITERS - 1]
    refs = refs[4 * ITERS - 1 :]
    got, refs = refs[:n_got], refs[n_got:]
    us = [p[...] for p in pots_rows]
    vs = [p[...] for p in pots_cols]
    first = (1.0 if ITERS == 1 else 0.0) - join_sum(got)
    adjs_rows = [first] + [a[...] for a in adjs_rows]
    adjs_cols = [a[...] for a in adjs_cols] + [jnp.ones(vs[0].shape, F32)]
    gradient(log_cols, log_rows, n_col, n_row, ax0, ax1, by, x_ref, y_ref, us, vs, adjs_rows, adjs_cols, refs)


def gradient(log_cols, log_rows, n_col, n_row, ax0, ax1, by, x_ref, y_ref, us, vs, adjs_rows, adjs_cols, refs):
    outs_x, outs_y = refs[:n_col], refs[n_col : n_col + n_row]
    cols_rows, x_parts, y_parts, gx, gy, left_e, left_r, right_r, all_x, all_y = refs[n_col + n_row :]
    dim, count_rows = x_ref.shape
    count_cols = y_ref.shape[1]
    shift = log_rows - log_cols

    x = x_ref[...]
    y = y_ref[...]
    one = jnp.ones((1, count_cols), F32)
    pad = jnp.zeros((31, count_cols), F32)
    y_parts[...] = jnp.concatenate(list(split3(y)) + [one, pad], axis=0).T.astype(BF16)
    one = jnp.ones((1, count_rows), F32)
    pad = jnp.zeros((31, count_rows), F32)
    x_parts[...] = jnp.concatenate(list(split3(x)) + [one, pad], axis=0).astype(BF16)
    gy[...] = jnp.zeros_like(gy)

    far_u = functools.reduce(jnp.maximum, [jnp.abs(u - us[-1]) for u in us])
    far_v = functools.reduce(jnp.maximum, [jnp.abs(v - vs[-1]) for v in vs])
    near = jnp.maximum(jnp.max(far_u), jnp.max(far_v)) < SPREAD

    def add_strip(at, total):
        upper = total.astype(BF16)
        lower = (total - upper.astype(F32)).astype(BF16)
        gx[at, :] = matmul(upper, y_parts[...]) + matmul(lower, y_parts[...])
        gy[...] += matmul(x_parts[:, at], upper) + matmul(x_parts[:, at], lower)

    @pl.when(near)
    def factored():
        alpha = [jnp.exp(u - us[-1]) for u in us]
        beta = [jnp.exp(v - vs[-1]) for v in vs]
        p_rows = alpha + [a * adj for a, adj in zip(alpha, adjs_rows)]
        q_rows = [b * adj for b, adj in zip(beta[1:], adjs_cols)] + [b * math.exp(shift) for b in beta[:-1]]
        fill = 16 - 2 * ITERS
        p_split = split3(jnp.concatenate(p_rows + [jnp.zeros((fill, count_rows), F32)], axis=0))
        q_split = split3(jnp.concatenate(q_rows + [jnp.zeros((fill, count_cols), F32)], axis=0))
        tail = [jnp.zeros((32, count_rows), F32)]
        left_r[...] = jnp.concatenate([p_split[o] for o in X_ORDER] + tail, axis=0).T.astype(BF16)
        tail = [jnp.zeros((32, count_cols), F32)]
        right_r[...] = jnp.concatenate([q_split[o] for o in Y_ORDER] + tail, axis=0).astype(BF16)
        left, unused = left_factor(ax0, ax1, us[-1] + log_cols)
        left_e[...] = left
        right = right_chunk(by, right_rows(vs[-1]), 0, count_cols)
        strip = min(STRIP, count_rows)
        for step in range(count_rows // strip):
            at = pl.ds(step * strip, strip)
            total = jnp.exp(matmul(left_e[at, :], right)) * matmul(left_r[at, :], right_r[...])
            add_strip(at, total)

    @pl.when(jnp.logical_not(near))
    def separate():
        stack = [u + log_cols for u in us] + adjs_rows
        stack.append(jnp.zeros((128 - len(stack), count_rows), F32))
        cols_rows[...] = jnp.concatenate(stack, axis=0).T
        strip = 128

        def block(step, carry):
            at = pl.ds(pl.multiple_of(step * strip, strip), strip)
            left = jnp.concatenate([ax0[at, :], ax1[at, :].astype(BF16)], axis=1)
            inner = matmul(left, by[...])
            columns = cols_rows[at, :]
            total = jnp.zeros_like(inner)
            for k in range(ITERS):
                base = inner + columns[:, k : k + 1]
                total += jnp.exp(base + vs[k + 1]) * adjs_cols[k]
                total += jnp.exp(base + (vs[k] + shift)) * columns[:, ITERS + k : ITERS + k + 1]
            add_strip(at, total)
            return carry

        lax.fori_loop(0, count_rows // strip, block, 0)

    def finish(points, sums):
        mixed = sums[0:dim] + sums[dim : 2 * dim] + sums[2 * dim : 3 * dim]
        return 2.0 * (points * sums[3 * dim : 3 * dim + 1] - mixed)

    for value, held, outs, axis in (
        (finish(x, gx[...].T), all_x, outs_x, "col"),
        (finish(y, gy[...]), all_y, outs_y, "row"),
    ):
        share = held.shape[2]
        for p in range(held.shape[0]):
            held[p] = value[:, p * share : (p + 1) * share]
        me = lax.axis_index(axis)
        for s, out in enumerate(outs):
            out[...] = held[me ^ s]


def swap(value, axis, distance):
    return lax.ppermute(value, axis, [(d, d ^ distance) for d in range(lax.axis_size(axis))])


def exchange(part, axis, join):
    size = lax.axis_size(axis)
    assert size & (size - 1) == 0
    if size == 4:
        return (part,) + tuple(swap(part, axis, d) for d in (2, 3, 1))
    distance = 1
    got = (part,)
    while distance < size:
        if len(got) > 1:
            (part,) = call(functools.partial(join_body, join), [shape(part.shape)], len(got))(*got)
        got = (part, swap(part, axis, distance))
        distance *= 2
    return got


def scatter(pieces, axis):
    got = [pieces[0]] + [swap(pieces[s], axis, s) for s in range(1, len(pieces))]
    return sum(got[1:], got[0])


def slot(column, lane, state):
    return jnp.where(lax.broadcasted_iota(jnp.int32, state.shape, 1) == lane, column, state)


def left_strip(left0, left1, at, pot):
    strip = left1[at, :]
    for lane, part in enumerate(split3(jnp.broadcast_to(pot, strip.shape))):
        strip = slot(part, lane, strip)
    return jnp.concatenate([left0[at, :], strip.astype(BF16)], axis=1)


def halves(value):
    return sum(value[:, p : p + 128] for p in range(0, value.shape[1], 128))


def octets(value):
    return jnp.sum(value.reshape(value.shape[0] // 8, 8, value.shape[1]), axis=0)


SWEEP = 256


def sweep(left_of, right, rows, out, held_of, acc, times, store, close):
    strips, strip = times.shape[:2]
    wide_all = right.shape[1]
    for s in range(strips + 1):
        at = slice(s * strip, (s + 1) * strip)
        left = left_of(at) if s < strips else None
        sums = None
        for c in range(0, wide_all, CHUNK):
            place = slice(c, c + CHUNK)
            if s < strips:
                sums = store(held_of(s), matmul(left, right_chunk(right, rows, c, CHUNK)), place, sums)
            if s > 0:
                factor = times[s - 1]
                part = octets(held_of(s - 1)[:, place] * jnp.concatenate([factor] * (CHUNK // 128), axis=1))
                if s > 1:
                    part += acc[:, place]
                if s < strips:
                    acc[:, place] = part
                else:
                    out[:, place] = jnp.sum(part, axis=0, keepdims=True)
        if s < strips:
            times[s] = jnp.broadcast_to(close(at, sums, held_of(s)), times.shape[1:])


def exponentials(weigh):
    def store(held, scores, place, sums):
        power = jnp.exp(scores)
        held[:, place] = power
        part = halves(weigh(power, place))
        return part if sums is None else sums + part

    return store


def prepare_own_body(x_hbm, y_hbm, ax0, ax1, ay0, ay1, by, state, out, x_ref, y_ref, bx, sems):
    copies = [
        pltpu.make_async_copy(x_hbm, x_ref, sems.at[0]),
        pltpu.make_async_copy(y_hbm, y_ref, sems.at[1]),
    ]
    for copy in copies:
        copy.start()
    for copy in copies:
        copy.wait()
    x = x_ref[...]
    y = y_ref[...]
    xf = factors(x * (2.0 * SCALE), X_ORDER)
    yf = factors(y, Y_ORDER)
    for factor, left0, left1, right in ((xf, ax0, ax1, bx), (yf, ay0, ay1, by)):
        right[...] = factor.astype(BF16)
        turned = factor.T
        left0[...] = turned[:, :128].astype(BF16)
        left1[...] = turned[:, 128:]
    start = -SCALE * jnp.sum(y * y, axis=0, keepdims=True)
    state[...] = jnp.concatenate([start, jnp.zeros((127, y.shape[1]), F32)], axis=0).T
    left, unused = left_factor(ay0, ay1, start)
    partial_lse(left, bx, out)
    lane = lax.broadcasted_iota(jnp.int32, ay1.shape, 1)
    ay1[...] = jnp.where((lane >= 3) & (lane < 6), 1.0, ay1[...])


def first_pot_body(log_rows, *refs):
    refs[-1][...] = -log_rows - join_lse(refs[:-1])


def opening_body(n_row, log_rows, log_cols, left0, left1, state, *refs):
    xs, us = refs[:n_row], refs[n_row : 2 * n_row]
    right, kept, u_out, state_out, out, acc, times = refs[2 * n_row :]
    strip = times.shape[1]
    x = jnp.concatenate([r[...] for r in xs], axis=1)
    right[...] = factors(x * (2.0 * SCALE), X_ORDER).astype(BF16)
    u = jnp.concatenate([r[...] for r in us], axis=1)
    u_out[...] = u

    def left_of(at):
        return jnp.concatenate([left0[at, :], left1[at, :].astype(BF16)], axis=1)

    def store(held, scores, place, tops):
        held[:, place] = scores
        for p in range(0, CHUNK, 128):
            part = scores[:, p : p + 128]
            tops = part if tops is None else jnp.maximum(tops, part)
        return tops

    def close(at, tops, held):
        top = jnp.max(tops, axis=1, keepdims=True)
        sums = None
        for c in range(0, held.shape[1], CHUNK):
            place = slice(c, c + CHUNK)
            power = jnp.exp(held[:, place] - top)
            held[:, place] = power
            part = halves(power)
            sums = part if sums is None else sums + part
        column = jnp.sum(sums, axis=1, keepdims=True)
        pot = -log_cols - (top + jnp.log(column))
        state_out[at, :] = slot(pot, 1, slot(-top, BASE, state[at, :]))
        return math.exp(-log_cols) / column

    def held_of(s):
        return kept.at[s * strip : (s + 1) * strip]

    sweep(left_of, right, right_rows(u), out, held_of, acc, times, store, close)


BASE = 6
NEAR = 25.0


def scaled(kept, row, column_of, out, hold):
    count, total = kept.shape
    block = min(128, count)

    for at in [slice(b, b + block) for b in range(0, count, block)]:
        sums = None
        for c in range(0, total, 128):
            part = kept[at, c : c + 128] * row[:, c : c + 128]
            sums = part if sums is None else sums + part
        hold[at, :] = sums
    hold[...] = jnp.broadcast_to(column_of(jnp.sum(hold[...], axis=1, keepdims=True)), hold.shape)
    wide = min(1024, total)
    for start in range(0, total, wide):
        places = [slice(c, c + 128) for c in range(start, start + wide, 128)]
        sums = [None] * len(places)
        for at in [slice(b, b + block) for b in range(0, count, block)]:
            factor = hold[at, :]
            for p, place in enumerate(places):
                part = octets(kept[at, place] * factor)
                sums[p] = part if sums[p] is None else sums[p] + part
        for p, place in enumerate(places):
            out[:, place] = jnp.sum(sums[p], axis=0, keepdims=True)


def iteration_body(k, n_got, log_rows, log_cols, left0, left1, right, kept, state, u_first, u_old, *refs):
    got, (u_out, state_out, out, held, acc, times, hold, row) = refs[:n_got], refs[n_got:]
    u = u_old[...] - (log_rows + jnp.log(join_sum(got)))
    u_out[...] = u
    apart = u - u_first[...]
    near = jnp.max(jnp.abs(apart)) < NEAR

    @pl.when(near)
    def scale():
        row[...] = jnp.exp(apart)

        def column_of(sums):
            old = state[...]
            state_out[...] = slot(old[:, BASE : BASE + 1] - (log_cols + jnp.log(sums)), k, old)
            return math.exp(-log_cols) / sums

        scaled(kept, row, column_of, out, hold)
        out[...] = out[...] * row[...]

    @pl.when(jnp.logical_not(near))
    def renew():
        def left_of(at):
            return left_strip(left0, left1, at, state[at, k - 1 : k])

        def close(at, sums, held):
            column = jnp.sum(sums, axis=1, keepdims=True)
            old = state[at, :]
            state_out[at, :] = slot(old[:, k - 1 : k] - (log_cols + jnp.log(column)), k, old)
            return math.exp(-log_cols) / column

        store = exponentials(lambda power, place: power)
        sweep(left_of, right, right_rows(u), out, lambda s: held.at[s % 2], acc, times, store, close)


def adjoint_body(k, n_got, log_rows, log_cols, left0, left1, right, kept, state, u_first, u_ref, u_before, *refs):
    got, (adj_out, state_out, out, held, acc, times, hold, row) = refs[:n_got], refs[n_got:]
    if k == ITERS:
        adj_out[...] = 1.0 - math.exp(log_cols) * join_sum(got)
    else:
        adj_out[...] = -join_sum(got)
    u, before = u_ref[...], u_before[...]
    shift = math.exp(log_rows - log_cols)
    mass = math.exp(log_cols)
    apart, apart_before = u - u_first[...], before - u_first[...]
    near = jnp.max(jnp.maximum(jnp.abs(apart), jnp.abs(apart_before))) < NEAR

    @pl.when(near)
    def scale():
        row[...] = jnp.exp(apart) * adj_out[...]

        def column_of(sums):
            old = state[...]
            beta = mass * jnp.exp(old[:, k - 1 : k] - old[:, BASE : BASE + 1])
            adj = -shift * beta * sums
            state_out[...] = slot(adj, 16 + k - 1, old)
            return beta * adj

        scaled(kept, row, column_of, out, hold)
        out[...] = out[...] * jnp.exp(apart_before)

    @pl.when(jnp.logical_not(near))
    def renew():
        def left_of(at):
            return left_strip(left0, left1, at, state[at, k : k + 1])

        def close(at, sums, held):
            column = jnp.sum(sums, axis=1, keepdims=True)
            old = state[at, :]
            sigma = jnp.exp(old[:, k - 1 : k] - old[:, k : k + 1])
            adj = -shift * sigma * column
            state_out[at, :] = slot(adj, 16 + k - 1, old)
            return sigma * adj

        store = exponentials(lambda power, place: power * adj_out[:, place])
        rows = right_rows(u + log_cols)
        sweep(left_of, right, rows, out, lambda s: held.at[s % 2], acc, times, store, close)
        out[...] = out[...] * jnp.exp(before - u)


def finish(points, sums):
    dim = points.shape[0]
    mixed = sums[0:dim] + sums[dim : 2 * dim] + sums[2 * dim : 3 * dim]
    return 2.0 * (points * sums[3 * dim : 3 * dim + 1] - mixed)


def with_total(points):
    width = points.shape[1]
    one = jnp.ones((1, width), F32)
    pad = jnp.zeros((128 - 3 * points.shape[0] - 1, width), F32)
    return jnp.concatenate(list(split3(points)) + [one, pad], axis=0).astype(BF16)


def all_weights(log_rows, log_cols, left0, left1, right, kept, state, us, adjs, at, take):
    turned = state[at, :].T
    v = [turned[k : k + 1] for k in range(ITERS + 1)]
    adjs_cols = [turned[16 + k : 17 + k] for k in range(1, ITERS)] + [jnp.ones_like(v[0])]
    shift = math.exp(log_rows - log_cols)
    apart = [u - us[0] for u in us]
    near = jnp.max(functools.reduce(jnp.maximum, [jnp.abs(a) for a in apart])) < NEAR
    total = us[0].shape[1]

    @pl.when(near)
    def scale():
        alpha = [jnp.exp(a) for a in apart]
        beta = [math.exp(log_cols) * jnp.exp(pot - turned[BASE : BASE + 1]) for pot in v]
        p_rows = alpha + [a * adj for a, adj in zip(alpha, adjs)]
        q_rows = [b * adj for b, adj in zip(beta[1:], adjs_cols)] + [shift * b for b in beta[:-1]]

        def stacked(rows, order):
            zero = jnp.zeros((16 - len(rows), rows[0].shape[1]), F32)
            parts = split3(jnp.concatenate(rows + [zero], axis=0))
            tail = jnp.zeros((32, rows[0].shape[1]), F32)
            return jnp.concatenate([parts[o] for o in order] + [tail], axis=0)

        p_right = stacked(p_rows, X_ORDER).astype(BF16)
        q_left = stacked(q_rows, Y_ORDER).T.astype(BF16)
        for c in range(0, total, CHUNK):
            place = slice(c, c + CHUNK)
            take(kept[at, place] * matmul(q_left, p_right[:, place]), place)

    @pl.when(jnp.logical_not(near))
    def separate():
        lefts = [left_strip(left0, left1, at, state[at, k : k + 1]) for k in range(ITERS + 1)]
        for c in range(0, total, CHUNK):
            place = slice(c, c + CHUNK)
            weights = 0.0
            for k in range(ITERS):
                adj_col = 1.0 if k == ITERS - 1 else state[at, 17 + k : 18 + k]
                full = right_chunk(right, right_rows(us[k] + log_cols), c, CHUNK)
                weights += jnp.exp(matmul(lefts[k + 1], full)) * adj_col
                weights += jnp.exp(matmul(lefts[k], full)) * (shift * adjs[k][:, place])
            take(weights, place)


def halved(weights):
    upper = weights.astype(BF16)
    return upper, (weights - upper.astype(F32)).astype(BF16)


def row_grad_body(n_got, log_rows, log_cols, left0, left1, right, kept, state, x_ref, y_ref, *refs):
    count = x_ref.shape[1]
    us = [r[:, :count] for r in refs[:ITERS]]
    adjs = [r[:, :count] for r in refs[ITERS : 2 * ITERS - 1]]
    refs = refs[2 * ITERS - 1 :]
    got, outs, (sums, pieces) = refs[:n_got], refs[n_got:-2], refs[-2:]
    adjs = [-join_sum([r[:, :count] for r in got])] + adjs
    y_parts = with_total(y_ref[...])

    def take(weights, place):
        upper, lower = halved(weights)
        sums[:, place] = matmul(y_parts, upper) + matmul(y_parts, lower)

    at = pl.ds(0, left0.shape[0])
    all_weights(log_rows, log_cols, left0, left1, right, kept, state, us, adjs, at, take)
    value = finish(x_ref[...], sums[...])
    share = count // len(outs)
    for p in range(len(outs)):
        pieces[p] = value[:, p * share : (p + 1) * share]
    me = lax.axis_index("col")
    for s, out in enumerate(outs):
        out[...] = pieces[me ^ s]


def col_grad_body(n_got, n_row, log_rows, log_cols, left0, left1, right, kept, state, y_ref, *refs):
    xs, refs = refs[:n_row], refs[n_row:]
    us = [r[...] for r in refs[:ITERS]]
    adjs = [r[...] for r in refs[ITERS : 2 * ITERS - 1]]
    refs = refs[2 * ITERS - 1 :]
    got, (out, sums) = refs[:n_got], refs[n_got:]
    adjs = [-join_sum(got)] + adjs
    x_parts = with_total(jnp.concatenate([r[...] for r in xs], axis=1))
    share = out.shape[1]
    start = pl.multiple_of(lax.axis_index("row") * share, share)
    sums[...] = jnp.zeros_like(sums)

    def across(weights, place):
        return lax.dot_general(
            weights, x_parts[:, place], (((1,), (1,)), ((), ())), preferred_element_type=F32
        )

    def take(weights, place):
        upper, lower = halved(weights)
        sums[...] += across(upper, place) + across(lower, place)

    at = pl.ds(start, share)
    all_weights(log_rows, log_cols, left0, left1, right, kept, state, us, adjs, at, take)
    out[...] = finish(y_ref[:, at], sums[...].T)


def gradient_scratch(dim, count_rows, count_cols, n_col, n_row):
    return [
        pltpu.VMEM((count_rows, 128), F32),
        pltpu.VMEM((128, count_rows), BF16),
        pltpu.VMEM((count_cols, 128), BF16),
        pltpu.VMEM((count_rows, 128), F32),
        pltpu.VMEM((128, count_cols), F32),
        pltpu.VMEM((count_rows, DEPTH), BF16),
        pltpu.VMEM((count_rows, 128), BF16),
        pltpu.VMEM((128, count_cols), BF16),
        pltpu.VMEM((n_col, dim, count_rows // n_col), F32),
        pltpu.VMEM((n_row, dim, count_cols // n_row), F32),
    ]


def repeated(x, y):
    dim, count_rows = x.shape
    count_cols = y.shape[1]
    n_row, n_col = lax.axis_size("row"), lax.axis_size("col")
    all_rows, held_cols = count_rows * n_row, count_cols
    log_rows, log_cols = math.log(all_rows), math.log(count_cols * n_col)
    row, col = (1, all_rows), (1, held_cols)

    xs = [x] + [swap(x, "row", s) for s in range(1, n_row)]
    own = (1, count_rows)
    ax0, ax1, ay0, ay1, by, state, part, x, y = pl.pallas_call(
        prepare_own_body,
        out_shape=[
            shape((count_rows, 128), BF16),
            shape((count_rows, 128)),
            shape((count_cols, 128), BF16),
            shape((count_cols, 128)),
            shape((DEPTH, count_cols), BF16),
            shape((count_cols, 128)),
            shape(own),
            shape(x.shape),
            shape(y.shape),
        ],
        in_specs=[pl.BlockSpec(memory_space=pltpu.HBM)] * 2,
        out_specs=vmem(9),
        scratch_shapes=[pltpu.VMEM((DEPTH, count_rows), BF16), pltpu.SemaphoreType.DMA((2,))],
        compiler_params=pltpu.CompilerParams(vmem_limit_bytes=VMEM_LIMIT),
    )(x, y)
    xs[0] = x
    got = exchange(part, "col", join_lse)
    (u,) = call(functools.partial(first_pot_body, log_rows), [shape(own)], len(got))(*got)
    u_blocks = [u] + [swap(u, "row", s) for s in range(1, n_row)]

    strip = min(SWEEP, held_cols)
    sums = [pltpu.VMEM((8, all_rows), F32), pltpu.VMEM((held_cols // strip, strip, 128), F32)]
    scratch = [pltpu.VMEM((2, strip, all_rows), F32)] + sums
    scratch += [pltpu.VMEM((held_cols, 128), F32), pltpu.VMEM(row, F32)]
    results = [shape(row), shape((held_cols, 128)), shape(row)]
    us = []
    bx, kept, u, state, part = call(
        functools.partial(opening_body, n_row, log_rows, log_cols),
        [shape((DEPTH, all_rows), BF16), shape((held_cols, all_rows))] + results,
        3 + 2 * n_row,
        sums,
        SWEEP_LIMIT,
    )(ay0, ay1, state, *xs, *u_blocks)
    us.append(u)
    for k in range(2, ITERS + 1):
        got = exchange(part, "col", join_sum)
        u, state, part = call(
            functools.partial(iteration_body, k, len(got), log_rows, log_cols),
            results,
            7 + len(got),
            scratch,
            SWEEP_LIMIT,
        )(ay0, ay1, bx, kept, state, us[0], u, *got)
        us.append(u)
    adjs_rows = []
    for k in range(ITERS, 1, -1):
        got = exchange(part, "col", join_sum)
        adj, state, part = call(
            functools.partial(adjoint_body, k, len(got), log_rows, log_cols),
            results,
            8 + len(got),
            scratch,
            SWEEP_LIMIT,
        )(ay0, ay1, bx, kept, state, us[0], us[k - 1], us[k - 2], *got)
        adjs_rows.insert(0, adj)
    got = exchange(part, "col", join_sum)
    share_x, share_y = count_rows // n_col, count_cols // n_row
    outs_x = call(
        functools.partial(row_grad_body, len(got), log_rows, log_cols),
        [shape((dim, share_x))] * n_col,
        7 + 2 * ITERS - 1 + len(got),
        [pltpu.VMEM((128, count_rows), F32), pltpu.VMEM((n_col, dim, share_x), F32)],
        SWEEP_LIMIT,
    )(ay0, ay1, bx, kept, state, x, y, *us, *adjs_rows, *got)
    (grad_y,) = call(
        functools.partial(col_grad_body, len(got), n_row, log_rows, log_cols),
        [shape((dim, share_y))],
        6 + n_row + 2 * ITERS - 1 + len(got),
        [pltpu.VMEM((share_y, 128), F32)],
        SWEEP_LIMIT,
        pl.CostEstimate(flops=1 << 31, bytes_accessed=1 << 23, transcendentals=0),
    )(ay0, ay1, bx, kept, state, y, *xs, *us, *adjs_rows, *got)
    return scatter(outs_x, "col").T, grad_y.T


REPEAT_PAIRS = 1 << 23


def on_device(x_points, y_points):
    x = x_points.T
    y = y_points.T
    n_row, n_col = lax.axis_size("row"), lax.axis_size("col")
    if ITERS > 1 and x.shape[1] * n_row * y.shape[1] <= REPEAT_PAIRS:
        return repeated(x, y)
    return shared(x, y)


def shared(x, y):
    dim, count_rows = x.shape
    count_cols = y.shape[1]
    n_row, n_col = lax.axis_size("row"), lax.axis_size("col")
    log_rows = math.log(count_rows * n_row)
    log_cols = math.log(count_cols * n_col)
    row, col = (1, count_rows), (1, count_cols)

    ax0, ax1, ay0, ay1, bx, by, start, part, x, y = pl.pallas_call(
        prepare_body,
        out_shape=[
            shape((count_rows, 128), BF16),
            shape((count_rows, 128)),
            shape((count_cols, 128), BF16),
            shape((count_cols, 128)),
            shape((DEPTH, count_rows), BF16),
            shape((DEPTH, count_cols), BF16),
            shape(col),
            shape(row),
            shape(x.shape),
            shape(y.shape),
        ],
        in_specs=[pl.BlockSpec(memory_space=pltpu.HBM)] * 2,
        out_specs=vmem(10),
        scratch_shapes=[pltpu.SemaphoreType.DMA((2,))],
        compiler_params=pltpu.CompilerParams(vmem_limit_bytes=VMEM_LIMIT),
    )(x, y)

    pots_rows, pots_cols = [], [start]
    for k in range(ITERS):
        got = exchange(part, "col", join_lse)
        pot, part = call(functools.partial(forward_body, -log_rows), [shape(row), shape(col)], 3 + len(got))(
            ax0, ax1, by, *got
        )
        pots_rows.append(pot)
        got = exchange(part, "row", join_lse)
        if k < ITERS - 1:
            pot, part = call(functools.partial(forward_body, -log_cols), [shape(col), shape(row)], 3 + len(got))(
                ay0, ay1, bx, *got
            )
            pots_cols.append(pot)
    pot, part = call(functools.partial(turn_body, -log_cols, log_cols), [shape(col), shape(row)], 4 + len(got))(
        ay0, ay1, bx, pots_rows[-1], *got
    )
    pots_cols.append(pot)

    adjs_rows, adjs_cols = [], []
    for k in reversed(range(1, ITERS)):
        leading = 1.0 if k == ITERS - 1 else 0.0
        got = exchange(part, "col", join_sum)
        adj, part = call(functools.partial(backward_body, leading, log_rows), [shape(row), shape(col)], 5 + len(got))(
            ax0, ax1, by, pots_rows[k], pots_cols[k], *got
        )
        adjs_rows.insert(0, adj)
        got = exchange(part, "row", join_sum)
        adj, part = call(functools.partial(backward_body, 0.0, log_cols), [shape(col), shape(row)], 5 + len(got))(
            ay0, ay1, bx, pots_cols[k], pots_rows[k - 1], *got
        )
        adjs_cols.insert(0, adj)
    got = exchange(part, "col", join_sum)

    share_x, share_y = count_rows // n_col, count_cols // n_row
    outs = call(
        functools.partial(gradient_body, dim, log_cols, log_rows, len(got), n_col, n_row),
        [shape((dim, share_x))] * n_col + [shape((dim, share_y))] * n_row,
        5 + 4 * ITERS - 1 + len(got),
        gradient_scratch(dim, count_rows, count_cols, n_col, n_row),
    )(ax0, ax1, by, x, y, *pots_rows, *pots_cols, *adjs_rows, *adjs_cols, *got)
    grad_x = scatter(outs[:n_col], "col")
    grad_y = scatter(outs[n_col:], "row")
    return (grad_x.T, grad_y.T)


def solution(mesh):
    in_specs = (P(("groups", "row"), None), P(("groups", "col"), None))
    out_specs = (P(("groups", "row", "col"), None), P(("groups", "col", "row"), None))
    return jax.shard_map(
        on_device, mesh=mesh, in_specs=in_specs, out_specs=out_specs, check_vma=False
    )
```

```python
import functools
import math

import jax
import jax.numpy as jnp
from jax import lax
from jax.experimental import pallas as pl
from jax.experimental.pallas import tpu as pltpu
from jax.sharding import PartitionSpec as P

ITERS = 5
EPSILON = 0.05
SCALE = 1.0 / EPSILON
DEPTH = 256
CHUNK = 256
F32 = jnp.float32
BF16 = jnp.bfloat16
VMEM_LIMIT = 32 * 1024 * 1024
SWEEP_LIMIT = 24 * 1024 * 1024


def split3(v):
    high = v.astype(BF16).astype(F32)
    rest = v - high
    mid = rest.astype(BF16).astype(F32)
    low = (rest - mid).astype(BF16).astype(F32)
    return high, mid, low


def vmem(count):
    return [pl.BlockSpec(memory_space=pltpu.VMEM)] * count


def call(body, outs, count, scratch=(), limit=VMEM_LIMIT, cost=None):
    return pl.pallas_call(
        body,
        out_shape=outs,
        in_specs=vmem(count),
        out_specs=vmem(len(outs)),
        scratch_shapes=list(scratch),
        compiler_params=pltpu.CompilerParams(vmem_limit_bytes=limit),
        cost_estimate=cost,
    )


def shape(dims, dtype=F32):
    return jax.ShapeDtypeStruct(dims, dtype)


def factors(points, order):
    parts = split3(points)
    width = points.shape[1]
    blocks = [parts[o] for o in order]
    zero16 = jnp.zeros((16, width), F32)
    tail = jnp.zeros((DEPTH - 144 - 2 * points.shape[0], width), F32)
    return jnp.concatenate(blocks[:4] + [zero16] + blocks[4:] + [tail], axis=0)


X_ORDER = (0, 0, 1, 0, 2, 1)
Y_ORDER = (0, 1, 0, 2, 0, 1)


def prepare_body(x_hbm, y_hbm, ax0, ax1, ay0, ay1, bx, by, start_ref, out, x_ref, y_ref, sems):
    copies = [
        pltpu.make_async_copy(x_hbm, x_ref, sems.at[0]),
        pltpu.make_async_copy(y_hbm, y_ref, sems.at[1]),
    ]
    for copy in copies:
        copy.start()
    for copy in copies:
        copy.wait()
    x = x_ref[...]
    y = y_ref[...]
    xf = factors(x * (2.0 * SCALE), X_ORDER)
    yf = factors(y, Y_ORDER)
    for factor, left0, left1, right in ((xf, ax0, ax1, bx), (yf, ay0, ay1, by)):
        right[...] = factor.astype(BF16)
        turned = factor.T
        left0[...] = turned[:, :128].astype(BF16)
        left1[...] = turned[:, 128:]
    start = -SCALE * jnp.sum(y * y, axis=0, keepdims=True)
    start_ref[...] = start
    left, unused = left_factor(ay0, ay1, start)
    partial_lse(left, bx, out)


def left_factor(left0, left1, pot, adj=None):
    width = pot.shape[1]
    high, mid, low = split3(pot)
    one = jnp.ones((1, width), F32)
    rows = [high, mid, low, one, one, one, jnp.zeros_like(one)]
    rows.append(jnp.zeros_like(one) if adj is None else adj)
    rows.append(jnp.zeros((120, width), F32))
    turned = jnp.concatenate(rows, axis=0).T
    column = None
    if adj is not None:
        column = turned[:, 7:8]
        lane = lax.broadcasted_iota(jnp.int32, turned.shape, 1)
        turned = jnp.where(lane == 7, 0.0, turned)
    return jnp.concatenate([left0[...], (left1[...] + turned).astype(BF16)], axis=1), column


def right_rows(pot):
    width = pot.shape[1]
    one = jnp.ones((3, width), F32)
    high, mid, low = split3(pot)
    return jnp.concatenate([one, high, mid, low, jnp.zeros((10, width), F32)], axis=0).astype(BF16)


def right_chunk(right, rows, at, wide):
    return jnp.concatenate(
        [right[0:128, at : at + wide], rows[:, at : at + wide], right[144:DEPTH, at : at + wide]], axis=0
    )


def matmul(a, b):
    return jnp.dot(a, b, preferred_element_type=F32)


def partial_lse(left, right, out):
    width = right.shape[1]
    rows = right_rows(jnp.zeros((1, width), F32))
    wide = min(CHUNK, width)
    for at in range(0, width, wide):
        scores = matmul(left, right_chunk(right, rows, at, wide))
        top = jnp.max(scores, axis=0, keepdims=True)
        total = jnp.sum(jnp.exp(scores - top), axis=0, keepdims=True)
        out[:, at : at + wide] = top + jnp.log(total)


def join_lse(parts):
    parts = [p[...] for p in parts]
    top = functools.reduce(jnp.maximum, parts)
    return top + jnp.log(sum(jnp.exp(p - top) for p in parts))


def join_sum(parts):
    return sum(p[...] for p in parts)


def join_body(join, *refs):
    refs[-1][...] = join(refs[:-1])


def forward_body(log_mass, left0, left1, right, *refs):
    got, (pot_out, out) = refs[:-2], refs[-2:]
    pot = log_mass - join_lse(got)
    pot_out[...] = pot
    left, unused = left_factor(left0, left1, pot)
    partial_lse(left, right, out)


def weighted_sums(left, column, right, rows, out):
    width = right.shape[1]
    wide = min(CHUNK, width)
    for at in range(0, width, wide):
        scores = matmul(left, right_chunk(right, rows, at, wide))
        out[:, at : at + wide] = jnp.sum(jnp.exp(scores) * column, axis=0, keepdims=True)


def turn_body(log_mass, log_scale, left0, left1, right, pot_right, *refs):
    got, (pot_out, out) = refs[:-2], refs[-2:]
    pot = log_mass - join_lse(got)
    pot_out[...] = pot
    left, column = left_factor(left0, left1, pot, jnp.ones_like(pot))
    weighted_sums(left, column, right, right_rows(pot_right[...] + log_scale), out)


def backward_body(leading, log_scale, left0, left1, right, pot_left, pot_right, *refs):
    got, (adj_out, out) = refs[:-2], refs[-2:]
    adj = leading - join_sum(got)
    adj_out[...] = adj
    left, column = left_factor(left0, left1, pot_left[...], adj)
    weighted_sums(left, column, right, right_rows(pot_right[...] + log_scale), out)


SPREAD = 20.0
STRIP = 256


def gradient_body(dim, log_cols, log_rows, n_got, n_col, n_row, ax0, ax1, by, x_ref, y_ref, *refs):
    pots_rows = refs[:ITERS]
    pots_cols = refs[ITERS : 2 * ITERS + 1]
    adjs_rows = refs[2 * ITERS + 1 : 3 * ITERS]
    adjs_cols = refs[3 * ITERS : 4 * ITERS - 1]
    refs = refs[4 * ITERS - 1 :]
    got, refs = refs[:n_got], refs[n_got:]
    us = [p[...] for p in pots_rows]
    vs = [p[...] for p in pots_cols]
    first = (1.0 if ITERS == 1 else 0.0) - join_sum(got)
    adjs_rows = [first] + [a[...] for a in adjs_rows]
    adjs_cols = [a[...] for a in adjs_cols] + [jnp.ones(vs[0].shape, F32)]
    gradient(log_cols, log_rows, n_col, n_row, ax0, ax1, by, x_ref, y_ref, us, vs, adjs_rows, adjs_cols, refs)


def gradient(log_cols, log_rows, n_col, n_row, ax0, ax1, by, x_ref, y_ref, us, vs, adjs_rows, adjs_cols, refs):
    outs_x, outs_y = refs[:n_col], refs[n_col : n_col + n_row]
    cols_rows, x_parts, y_parts, gx, gy, left_e, left_r, right_r, all_x, all_y = refs[n_col + n_row :]
    dim, count_rows = x_ref.shape
    count_cols = y_ref.shape[1]
    shift = log_rows - log_cols

    x = x_ref[...]
    y = y_ref[...]
    one = jnp.ones((1, count_cols), F32)
    pad = jnp.zeros((31, count_cols), F32)
    y_parts[...] = jnp.concatenate(list(split3(y)) + [one, pad], axis=0).T.astype(BF16)
    one = jnp.ones((1, count_rows), F32)
    pad = jnp.zeros((31, count_rows), F32)
    x_parts[...] = jnp.concatenate(list(split3(x)) + [one, pad], axis=0).astype(BF16)
    gy[...] = jnp.zeros_like(gy)

    far_u = functools.reduce(jnp.maximum, [jnp.abs(u - us[-1]) for u in us])
    far_v = functools.reduce(jnp.maximum, [jnp.abs(v - vs[-1]) for v in vs])
    near = jnp.maximum(jnp.max(far_u), jnp.max(far_v)) < SPREAD

    def add_strip(at, total):
        upper = total.astype(BF16)
        lower = (total - upper.astype(F32)).astype(BF16)
        gx[at, :] = matmul(upper, y_parts[...]) + matmul(lower, y_parts[...])
        gy[...] += matmul(x_parts[:, at], upper) + matmul(x_parts[:, at], lower)

    @pl.when(near)
    def factored():
        alpha = [jnp.exp(u - us[-1]) for u in us]
        beta = [jnp.exp(v - vs[-1]) for v in vs]
        p_rows = alpha + [a * adj for a, adj in zip(alpha, adjs_rows)]
        q_rows = [b * adj for b, adj in zip(beta[1:], adjs_cols)] + [b * math.exp(shift) for b in beta[:-1]]
        fill = 16 - 2 * ITERS
        p_split = split3(jnp.concatenate(p_rows + [jnp.zeros((fill, count_rows), F32)], axis=0))
        q_split = split3(jnp.concatenate(q_rows + [jnp.zeros((fill, count_cols), F32)], axis=0))
        tail = [jnp.zeros((32, count_rows), F32)]
        left_r[...] = jnp.concatenate([p_split[o] for o in X_ORDER] + tail, axis=0).T.astype(BF16)
        tail = [jnp.zeros((32, count_cols), F32)]
        right_r[...] = jnp.concatenate([q_split[o] for o in Y_ORDER] + tail, axis=0).astype(BF16)
        left, unused = left_factor(ax0, ax1, us[-1] + log_cols)
        left_e[...] = left
        right = right_chunk(by, right_rows(vs[-1]), 0, count_cols)
        strip = min(STRIP, count_rows)
        for step in range(count_rows // strip):
            at = pl.ds(step * strip, strip)
            total = jnp.exp(matmul(left_e[at, :], right)) * matmul(left_r[at, :], right_r[...])
            add_strip(at, total)

    @pl.when(jnp.logical_not(near))
    def separate():
        stack = [u + log_cols for u in us] + adjs_rows
        stack.append(jnp.zeros((128 - len(stack), count_rows), F32))
        cols_rows[...] = jnp.concatenate(stack, axis=0).T
        strip = 128

        def block(step, carry):
            at = pl.ds(pl.multiple_of(step * strip, strip), strip)
            left = jnp.concatenate([ax0[at, :], ax1[at, :].astype(BF16)], axis=1)
            inner = matmul(left, by[...])
            columns = cols_rows[at, :]
            total = jnp.zeros_like(inner)
            for k in range(ITERS):
                base = inner + columns[:, k : k + 1]
                total += jnp.exp(base + vs[k + 1]) * adjs_cols[k]
                total += jnp.exp(base + (vs[k] + shift)) * columns[:, ITERS + k : ITERS + k + 1]
            add_strip(at, total)
            return carry

        lax.fori_loop(0, count_rows // strip, block, 0)

    def finish(points, sums):
        mixed = sums[0:dim] + sums[dim : 2 * dim] + sums[2 * dim : 3 * dim]
        return 2.0 * (points * sums[3 * dim : 3 * dim + 1] - mixed)

    for value, held, outs, axis in (
        (finish(x, gx[...].T), all_x, outs_x, "col"),
        (finish(y, gy[...]), all_y, outs_y, "row"),
    ):
        share = held.shape[2]
        for p in range(held.shape[0]):
            held[p] = value[:, p * share : (p + 1) * share]
        me = lax.axis_index(axis)
        for s, out in enumerate(outs):
            out[...] = held[me ^ s]


def swap(value, axis, distance):
    return lax.ppermute(value, axis, [(d, d ^ distance) for d in range(lax.axis_size(axis))])


def exchange(part, axis, join):
    size = lax.axis_size(axis)
    assert size & (size - 1) == 0
    if size == 4:
        return (part,) + tuple(swap(part, axis, d) for d in (2, 3, 1))
    distance = 1
    got = (part,)
    while distance < size:
        if len(got) > 1:
            (part,) = call(functools.partial(join_body, join), [shape(part.shape)], len(got))(*got)
        got = (part, swap(part, axis, distance))
        distance *= 2
    return got


def scatter(pieces, axis):
    got = [pieces[0]] + [swap(pieces[s], axis, s) for s in range(1, len(pieces))]
    return sum(got[1:], got[0])


def slot(column, lane, state):
    return jnp.where(lax.broadcasted_iota(jnp.int32, state.shape, 1) == lane, column, state)


def left_strip(left0, left1, at, pot):
    strip = left1[at, :]
    for lane, part in enumerate(split3(jnp.broadcast_to(pot, strip.shape))):
        strip = slot(part, lane, strip)
    return jnp.concatenate([left0[at, :], strip.astype(BF16)], axis=1)


def halves(value):
    return sum(value[:, p : p + 128] for p in range(0, value.shape[1], 128))


def octets(value):
    return jnp.sum(value.reshape(value.shape[0] // 8, 8, value.shape[1]), axis=0)


SWEEP = 256


def sweep(left_of, right, rows, out, held_of, acc, times, store, close):
    strips, strip = times.shape[:2]
    wide_all = right.shape[1]
    for s in range(strips + 1):
        at = slice(s * strip, (s + 1) * strip)
        left = left_of(at) if s < strips else None
        sums = None
        for c in range(0, wide_all, CHUNK):
            place = slice(c, c + CHUNK)
            if s < strips:
                sums = store(held_of(s), matmul(left, right_chunk(right, rows, c, CHUNK)), place, sums)
            if s > 0:
                factor = times[s - 1]
                part = octets(held_of(s - 1)[:, place] * jnp.concatenate([factor] * (CHUNK // 128), axis=1))
                if s > 1:
                    part += acc[:, place]
                if s < strips:
                    acc[:, place] = part
                else:
                    out[:, place] = jnp.sum(part, axis=0, keepdims=True)
        if s < strips:
            times[s] = jnp.broadcast_to(close(at, sums, held_of(s)), times.shape[1:])


def exponentials(weigh):
    def store(held, scores, place, sums):
        power = jnp.exp(scores)
        held[:, place] = power
        part = halves(weigh(power, place))
        return part if sums is None else sums + part

    return store


def prepare_own_body(x_hbm, y_hbm, ax0, ax1, ay0, ay1, by, state, out, x_ref, y_ref, bx, sems):
    copies = [
        pltpu.make_async_copy(x_hbm, x_ref, sems.at[0]),
        pltpu.make_async_copy(y_hbm, y_ref, sems.at[1]),
    ]
    for copy in copies:
        copy.start()
    for copy in copies:
        copy.wait()
    x = x_ref[...]
    y = y_ref[...]
    xf = factors(x * (2.0 * SCALE), X_ORDER)
    yf = factors(y, Y_ORDER)
    for factor, left0, left1, right in ((xf, ax0, ax1, bx), (yf, ay0, ay1, by)):
        right[...] = factor.astype(BF16)
        turned = factor.T
        left0[...] = turned[:, :128].astype(BF16)
        left1[...] = turned[:, 128:]
    start = -SCALE * jnp.sum(y * y, axis=0, keepdims=True)
    state[...] = jnp.concatenate([start, jnp.zeros((127, y.shape[1]), F32)], axis=0).T
    left, unused = left_factor(ay0, ay1, start)
    partial_lse(left, bx, out)
    lane = lax.broadcasted_iota(jnp.int32, ay1.shape, 1)
    ay1[...] = jnp.where((lane >= 3) & (lane < 6), 1.0, ay1[...])


def first_pot_body(log_rows, *refs):
    refs[-1][...] = -log_rows - join_lse(refs[:-1])


def opening_body(n_row, log_rows, log_cols, left0, left1, state, *refs):
    xs, us = refs[:n_row], refs[n_row : 2 * n_row]
    right, kept, u_out, state_out, out, acc, times = refs[2 * n_row :]
    strip = times.shape[1]
    x = jnp.concatenate([r[...] for r in xs], axis=1)
    right[...] = factors(x * (2.0 * SCALE), X_ORDER).astype(BF16)
    u = jnp.concatenate([r[...] for r in us], axis=1)
    u_out[...] = u

    def left_of(at):
        return jnp.concatenate([left0[at, :], left1[at, :].astype(BF16)], axis=1)

    def store(held, scores, place, tops):
        held[:, place] = scores
        for p in range(0, CHUNK, 128):
            part = scores[:, p : p + 128]
            tops = part if tops is None else jnp.maximum(tops, part)
        return tops

    def close(at, tops, held):
        top = jnp.max(tops, axis=1, keepdims=True)
        sums = None
        for c in range(0, held.shape[1], CHUNK):
            place = slice(c, c + CHUNK)
            power = jnp.exp(held[:, place] - top)
            held[:, place] = power
            part = halves(power)
            sums = part if sums is None else sums + part
        column = jnp.sum(sums, axis=1, keepdims=True)
        pot = -log_cols - (top + jnp.log(column))
        state_out[at, :] = slot(pot, 1, slot(-top, BASE, state[at, :]))
        return math.exp(-log_cols) / column

    def held_of(s):
        return kept.at[s * strip : (s + 1) * strip]

    sweep(left_of, right, right_rows(u), out, held_of, acc, times, store, close)


BASE = 6
NEAR = 25.0


def scaled(kept, row, column_of, out, acc, hold):
    count, total = kept.shape
    block = min(128, count)

    def across(index, carry):
        at = pl.ds(pl.multiple_of(index * block, block), block)
        sums = None
        for c in range(0, total, 128):
            part = kept[at, c : c + 128] * row[:, c : c + 128]
            sums = part if sums is None else sums + part
        hold[at, :] = sums
        return carry

    lax.fori_loop(0, count // block, across, 0)
    hold[...] = jnp.broadcast_to(column_of(jnp.sum(hold[...], axis=1, keepdims=True)), hold.shape)
    acc[...] = jnp.zeros_like(acc)

    def down(index, carry):
        at = pl.ds(pl.multiple_of(index * block, block), block)
        factor = hold[at, :]
        for c in range(0, total, 128):
            acc[:, c : c + 128] += octets(kept[at, c : c + 128] * factor)
        return carry

    lax.fori_loop(0, count // block, down, 0)
    out[...] = jnp.sum(acc[...], axis=0, keepdims=True)


def iteration_body(k, n_got, log_rows, log_cols, left0, left1, right, kept, state, u_first, u_old, *refs):
    got, (u_out, state_out, out, held, acc, times, hold, row) = refs[:n_got], refs[n_got:]
    u = u_old[...] - (log_rows + jnp.log(join_sum(got)))
    u_out[...] = u
    apart = u - u_first[...]
    near = jnp.max(jnp.abs(apart)) < NEAR

    @pl.when(near)
    def scale():
        row[...] = jnp.exp(apart)

        def column_of(sums):
            old = state[...]
            state_out[...] = slot(old[:, BASE : BASE + 1] - (log_cols + jnp.log(sums)), k, old)
            return math.exp(-log_cols) / sums

        scaled(kept, row, column_of, out, acc, hold)
        out[...] = out[...] * row[...]

    @pl.when(jnp.logical_not(near))
    def renew():
        def left_of(at):
            return left_strip(left0, left1, at, state[at, k - 1 : k])

        def close(at, sums, held):
            column = jnp.sum(sums, axis=1, keepdims=True)
            old = state[at, :]
            state_out[at, :] = slot(old[:, k - 1 : k] - (log_cols + jnp.log(column)), k, old)
            return math.exp(-log_cols) / column

        store = exponentials(lambda power, place: power)
        sweep(left_of, right, right_rows(u), out, lambda s: held.at[s % 2], acc, times, store, close)


def adjoint_body(k, n_got, log_rows, log_cols, left0, left1, right, kept, state, u_first, u_ref, u_before, *refs):
    got, (adj_out, state_out, out, held, acc, times, hold, row) = refs[:n_got], refs[n_got:]
    if k == ITERS:
        adj_out[...] = 1.0 - math.exp(log_cols) * join_sum(got)
    else:
        adj_out[...] = -join_sum(got)
    u, before = u_ref[...], u_before[...]
    shift = math.exp(log_rows - log_cols)
    mass = math.exp(log_cols)
    apart, apart_before = u - u_first[...], before - u_first[...]
    near = jnp.max(jnp.maximum(jnp.abs(apart), jnp.abs(apart_before))) < NEAR

    @pl.when(near)
    def scale():
        row[...] = jnp.exp(apart) * adj_out[...]

        def column_of(sums):
            old = state[...]
            beta = mass * jnp.exp(old[:, k - 1 : k] - old[:, BASE : BASE + 1])
            adj = -shift * beta * sums
            state_out[...] = slot(adj, 16 + k - 1, old)
            return beta * adj

        scaled(kept, row, column_of, out, acc, hold)
        out[...] = out[...] * jnp.exp(apart_before)

    @pl.when(jnp.logical_not(near))
    def renew():
        def left_of(at):
            return left_strip(left0, left1, at, state[at, k : k + 1])

        def close(at, sums, held):
            column = jnp.sum(sums, axis=1, keepdims=True)
            old = state[at, :]
            sigma = jnp.exp(old[:, k - 1 : k] - old[:, k : k + 1])
            adj = -shift * sigma * column
            state_out[at, :] = slot(adj, 16 + k - 1, old)
            return sigma * adj

        store = exponentials(lambda power, place: power * adj_out[:, place])
        rows = right_rows(u + log_cols)
        sweep(left_of, right, rows, out, lambda s: held.at[s % 2], acc, times, store, close)
        out[...] = out[...] * jnp.exp(before - u)


def finish(points, sums):
    dim = points.shape[0]
    mixed = sums[0:dim] + sums[dim : 2 * dim] + sums[2 * dim : 3 * dim]
    return 2.0 * (points * sums[3 * dim : 3 * dim + 1] - mixed)


def with_total(points):
    width = points.shape[1]
    one = jnp.ones((1, width), F32)
    pad = jnp.zeros((128 - 3 * points.shape[0] - 1, width), F32)
    return jnp.concatenate(list(split3(points)) + [one, pad], axis=0).astype(BF16)


def all_weights(log_rows, log_cols, left0, left1, right, kept, state, us, adjs, at, take):
    turned = state[at, :].T
    v = [turned[k : k + 1] for k in range(ITERS + 1)]
    adjs_cols = [turned[16 + k : 17 + k] for k in range(1, ITERS)] + [jnp.ones_like(v[0])]
    shift = math.exp(log_rows - log_cols)
    apart = [u - us[0] for u in us]
    near = jnp.max(functools.reduce(jnp.maximum, [jnp.abs(a) for a in apart])) < NEAR
    total = us[0].shape[1]

    @pl.when(near)
    def scale():
        alpha = [jnp.exp(a) for a in apart]
        beta = [math.exp(log_cols) * jnp.exp(pot - turned[BASE : BASE + 1]) for pot in v]
        p_rows = alpha + [a * adj for a, adj in zip(alpha, adjs)]
        q_rows = [b * adj for b, adj in zip(beta[1:], adjs_cols)] + [shift * b for b in beta[:-1]]

        def stacked(rows, order):
            zero = jnp.zeros((16 - len(rows), rows[0].shape[1]), F32)
            parts = split3(jnp.concatenate(rows + [zero], axis=0))
            tail = jnp.zeros((32, rows[0].shape[1]), F32)
            return jnp.concatenate([parts[o] for o in order] + [tail], axis=0)

        p_right = stacked(p_rows, X_ORDER).astype(BF16)
        q_left = stacked(q_rows, Y_ORDER).T.astype(BF16)
        for c in range(0, total, CHUNK):
            place = slice(c, c + CHUNK)
            take(kept[at, place] * matmul(q_left, p_right[:, place]), place)

    @pl.when(jnp.logical_not(near))
    def separate():
        lefts = [left_strip(left0, left1, at, state[at, k : k + 1]) for k in range(ITERS + 1)]
        for c in range(0, total, CHUNK):
            place = slice(c, c + CHUNK)
            weights = 0.0
            for k in range(ITERS):
                adj_col = 1.0 if k == ITERS - 1 else state[at, 17 + k : 18 + k]
                full = right_chunk(right, right_rows(us[k] + log_cols), c, CHUNK)
                weights += jnp.exp(matmul(lefts[k + 1], full)) * adj_col
                weights += jnp.exp(matmul(lefts[k], full)) * (shift * adjs[k][:, place])
            take(weights, place)


def halved(weights):
    upper = weights.astype(BF16)
    return upper, (weights - upper.astype(F32)).astype(BF16)


def row_grad_body(n_got, log_rows, log_cols, left0, left1, right, kept, state, x_ref, y_ref, *refs):
    count = x_ref.shape[1]
    us = [r[:, :count] for r in refs[:ITERS]]
    adjs = [r[:, :count] for r in refs[ITERS : 2 * ITERS - 1]]
    refs = refs[2 * ITERS - 1 :]
    got, outs, (sums, pieces) = refs[:n_got], refs[n_got:-2], refs[-2:]
    adjs = [-join_sum([r[:, :count] for r in got])] + adjs
    y_parts = with_total(y_ref[...])

    def take(weights, place):
        upper, lower = halved(weights)
        sums[:, place] = matmul(y_parts, upper) + matmul(y_parts, lower)

    at = pl.ds(0, left0.shape[0])
    all_weights(log_rows, log_cols, left0, left1, right, kept, state, us, adjs, at, take)
    value = finish(x_ref[...], sums[...])
    share = count // len(outs)
    for p in range(len(outs)):
        pieces[p] = value[:, p * share : (p + 1) * share]
    me = lax.axis_index("col")
    for s, out in enumerate(outs):
        out[...] = pieces[me ^ s]


def col_grad_body(n_got, n_row, log_rows, log_cols, left0, left1, right, kept, state, y_ref, *refs):
    xs, refs = refs[:n_row], refs[n_row:]
    us = [r[...] for r in refs[:ITERS]]
    adjs = [r[...] for r in refs[ITERS : 2 * ITERS - 1]]
    refs = refs[2 * ITERS - 1 :]
    got, (out, sums) = refs[:n_got], refs[n_got:]
    adjs = [-join_sum(got)] + adjs
    x_parts = with_total(jnp.concatenate([r[...] for r in xs], axis=1))
    share = out.shape[1]
    start = pl.multiple_of(lax.axis_index("row") * share, share)
    sums[...] = jnp.zeros_like(sums)

    def across(weights, place):
        return lax.dot_general(
            weights, x_parts[:, place], (((1,), (1,)), ((), ())), preferred_element_type=F32
        )

    def take(weights, place):
        upper, lower = halved(weights)
        sums[...] += across(upper, place) + across(lower, place)

    at = pl.ds(start, share)
    all_weights(log_rows, log_cols, left0, left1, right, kept, state, us, adjs, at, take)
    out[...] = finish(y_ref[:, at], sums[...].T)


def gradient_scratch(dim, count_rows, count_cols, n_col, n_row):
    return [
        pltpu.VMEM((count_rows, 128), F32),
        pltpu.VMEM((128, count_rows), BF16),
        pltpu.VMEM((count_cols, 128), BF16),
        pltpu.VMEM((count_rows, 128), F32),
        pltpu.VMEM((128, count_cols), F32),
        pltpu.VMEM((count_rows, DEPTH), BF16),
        pltpu.VMEM((count_rows, 128), BF16),
        pltpu.VMEM((128, count_cols), BF16),
        pltpu.VMEM((n_col, dim, count_rows // n_col), F32),
        pltpu.VMEM((n_row, dim, count_cols // n_row), F32),
    ]


def repeated(x, y):
    dim, count_rows = x.shape
    count_cols = y.shape[1]
    n_row, n_col = lax.axis_size("row"), lax.axis_size("col")
    all_rows, held_cols = count_rows * n_row, count_cols
    log_rows, log_cols = math.log(all_rows), math.log(count_cols * n_col)
    row, col = (1, all_rows), (1, held_cols)

    own = (1, count_rows)
    ax0, ax1, ay0, ay1, by, state, part, x, y = pl.pallas_call(
        prepare_own_body,
        out_shape=[
            shape((count_rows, 128), BF16),
            shape((count_rows, 128)),
            shape((count_cols, 128), BF16),
            shape((count_cols, 128)),
            shape((DEPTH, count_cols), BF16),
            shape((count_cols, 128)),
            shape(own),
            shape(x.shape),
            shape(y.shape),
        ],
        in_specs=[pl.BlockSpec(memory_space=pltpu.HBM)] * 2,
        out_specs=vmem(9),
        scratch_shapes=[pltpu.VMEM((DEPTH, count_rows), BF16), pltpu.SemaphoreType.DMA((2,))],
        compiler_params=pltpu.CompilerParams(vmem_limit_bytes=VMEM_LIMIT),
    )(x, y)
    xs = [x] + [swap(x, "row", s) for s in range(1, n_row)]
    got = exchange(part, "col", join_lse)
    (u,) = call(functools.partial(first_pot_body, log_rows), [shape(own)], len(got))(*got)
    u_blocks = [u] + [swap(u, "row", s) for s in range(1, n_row)]

    strip = min(SWEEP, held_cols)
    sums = [pltpu.VMEM((8, all_rows), F32), pltpu.VMEM((held_cols // strip, strip, 128), F32)]
    scratch = [pltpu.VMEM((2, strip, all_rows), F32)] + sums
    scratch += [pltpu.VMEM((held_cols, 128), F32), pltpu.VMEM(row, F32)]
    results = [shape(row), shape((held_cols, 128)), shape(row)]
    us = []
    bx, kept, u, state, part = call(
        functools.partial(opening_body, n_row, log_rows, log_cols),
        [shape((DEPTH, all_rows), BF16), shape((held_cols, all_rows))] + results,
        3 + 2 * n_row,
        sums,
        SWEEP_LIMIT,
    )(ay0, ay1, state, *xs, *u_blocks)
    us.append(u)
    for k in range(2, ITERS + 1):
        got = exchange(part, "col", join_sum)
        u, state, part = call(
            functools.partial(iteration_body, k, len(got), log_rows, log_cols),
            results,
            7 + len(got),
            scratch,
            SWEEP_LIMIT,
        )(ay0, ay1, bx, kept, state, us[0], u, *got)
        us.append(u)
    adjs_rows = []
    for k in range(ITERS, 1, -1):
        got = exchange(part, "col", join_sum)
        adj, state, part = call(
            functools.partial(adjoint_body, k, len(got), log_rows, log_cols),
            results,
            8 + len(got),
            scratch,
            SWEEP_LIMIT,
        )(ay0, ay1, bx, kept, state, us[0], us[k - 1], us[k - 2], *got)
        adjs_rows.insert(0, adj)
    got = exchange(part, "col", join_sum)
    share_x, share_y = count_rows // n_col, count_cols // n_row
    outs_x = call(
        functools.partial(row_grad_body, len(got), log_rows, log_cols),
        [shape((dim, share_x))] * n_col,
        7 + 2 * ITERS - 1 + len(got),
        [pltpu.VMEM((128, count_rows), F32), pltpu.VMEM((n_col, dim, share_x), F32)],
        SWEEP_LIMIT,
    )(ay0, ay1, bx, kept, state, x, y, *us, *adjs_rows, *got)
    (grad_y,) = call(
        functools.partial(col_grad_body, len(got), n_row, log_rows, log_cols),
        [shape((dim, share_y))],
        6 + n_row + 2 * ITERS - 1 + len(got),
        [pltpu.VMEM((share_y, 128), F32)],
        SWEEP_LIMIT,
        pl.CostEstimate(flops=1 << 31, bytes_accessed=1 << 23, transcendentals=0),
    )(ay0, ay1, bx, kept, state, y, *xs, *us, *adjs_rows, *got)
    return scatter(outs_x, "col").T, grad_y.T


REPEAT_PAIRS = 1 << 23


def on_device(x_points, y_points):
    x = x_points.T
    y = y_points.T
    n_row, n_col = lax.axis_size("row"), lax.axis_size("col")
    if ITERS > 1 and x.shape[1] * n_row * y.shape[1] <= REPEAT_PAIRS:
        return repeated(x, y)
    return shared(x, y)


def shared(x, y):
    dim, count_rows = x.shape
    count_cols = y.shape[1]
    n_row, n_col = lax.axis_size("row"), lax.axis_size("col")
    log_rows = math.log(count_rows * n_row)
    log_cols = math.log(count_cols * n_col)
    row, col = (1, count_rows), (1, count_cols)

    ax0, ax1, ay0, ay1, bx, by, start, part, x, y = pl.pallas_call(
        prepare_body,
        out_shape=[
            shape((count_rows, 128), BF16),
            shape((count_rows, 128)),
            shape((count_cols, 128), BF16),
            shape((count_cols, 128)),
            shape((DEPTH, count_rows), BF16),
            shape((DEPTH, count_cols), BF16),
            shape(col),
            shape(row),
            shape(x.shape),
            shape(y.shape),
        ],
        in_specs=[pl.BlockSpec(memory_space=pltpu.HBM)] * 2,
        out_specs=vmem(10),
        scratch_shapes=[pltpu.SemaphoreType.DMA((2,))],
        compiler_params=pltpu.CompilerParams(vmem_limit_bytes=VMEM_LIMIT),
    )(x, y)

    pots_rows, pots_cols = [], [start]
    for k in range(ITERS):
        got = exchange(part, "col", join_lse)
        pot, part = call(functools.partial(forward_body, -log_rows), [shape(row), shape(col)], 3 + len(got))(
            ax0, ax1, by, *got
        )
        pots_rows.append(pot)
        got = exchange(part, "row", join_lse)
        if k < ITERS - 1:
            pot, part = call(functools.partial(forward_body, -log_cols), [shape(col), shape(row)], 3 + len(got))(
                ay0, ay1, bx, *got
            )
            pots_cols.append(pot)
    pot, part = call(functools.partial(turn_body, -log_cols, log_cols), [shape(col), shape(row)], 4 + len(got))(
        ay0, ay1, bx, pots_rows[-1], *got
    )
    pots_cols.append(pot)

    adjs_rows, adjs_cols = [], []
    for k in reversed(range(1, ITERS)):
        leading = 1.0 if k == ITERS - 1 else 0.0
        got = exchange(part, "col", join_sum)
        adj, part = call(functools.partial(backward_body, leading, log_rows), [shape(row), shape(col)], 5 + len(got))(
            ax0, ax1, by, pots_rows[k], pots_cols[k], *got
        )
        adjs_rows.insert(0, adj)
        got = exchange(part, "row", join_sum)
        adj, part = call(functools.partial(backward_body, 0.0, log_cols), [shape(col), shape(row)], 5 + len(got))(
            ay0, ay1, bx, pots_cols[k], pots_rows[k - 1], *got
        )
        adjs_cols.insert(0, adj)
    got = exchange(part, "col", join_sum)

    share_x, share_y = count_rows // n_col, count_cols // n_row
    outs = call(
        functools.partial(gradient_body, dim, log_cols, log_rows, len(got), n_col, n_row),
        [shape((dim, share_x))] * n_col + [shape((dim, share_y))] * n_row,
        5 + 4 * ITERS - 1 + len(got),
        gradient_scratch(dim, count_rows, count_cols, n_col, n_row),
    )(ax0, ax1, by, x, y, *pots_rows, *pots_cols, *adjs_rows, *adjs_cols, *got)
    grad_x = scatter(outs[:n_col], "col")
    grad_y = scatter(outs[n_col:], "row")
    return (grad_x.T, grad_y.T)


def solution(mesh):
    in_specs = (P(("groups", "row"), None), P(("groups", "col"), None))
    out_specs = (P(("groups", "row", "col"), None), P(("groups", "col", "row"), None))
    return jax.shard_map(
        on_device, mesh=mesh, in_specs=in_specs, out_specs=out_specs, check_vma=False
    )
```

```python
import functools
import math

import jax
import jax.numpy as jnp
from jax import lax
from jax.experimental import pallas as pl
from jax.experimental.pallas import tpu as pltpu
from jax.sharding import PartitionSpec as P

ITERS = 5
EPSILON = 0.05
SCALE = 1.0 / EPSILON
DEPTH = 256
CHUNK = 256
F32 = jnp.float32
BF16 = jnp.bfloat16
VMEM_LIMIT = 32 * 1024 * 1024
SWEEP_LIMIT = 24 * 1024 * 1024


def split3(v):
    high = v.astype(BF16).astype(F32)
    rest = v - high
    mid = rest.astype(BF16).astype(F32)
    low = (rest - mid).astype(BF16).astype(F32)
    return high, mid, low


def vmem(count):
    return [pl.BlockSpec(memory_space=pltpu.VMEM)] * count


def call(body, outs, count, scratch=(), limit=VMEM_LIMIT, cost=None):
    return pl.pallas_call(
        body,
        out_shape=outs,
        in_specs=vmem(count),
        out_specs=vmem(len(outs)),
        scratch_shapes=list(scratch),
        compiler_params=pltpu.CompilerParams(vmem_limit_bytes=limit),
        cost_estimate=cost,
    )


def shape(dims, dtype=F32):
    return jax.ShapeDtypeStruct(dims, dtype)


def factors(points, order):
    parts = split3(points)
    width = points.shape[1]
    blocks = [parts[o] for o in order]
    zero16 = jnp.zeros((16, width), F32)
    tail = jnp.zeros((DEPTH - 144 - 2 * points.shape[0], width), F32)
    return jnp.concatenate(blocks[:4] + [zero16] + blocks[4:] + [tail], axis=0)


X_ORDER = (0, 0, 1, 0, 2, 1)
Y_ORDER = (0, 1, 0, 2, 0, 1)


def prepare_body(x_hbm, y_hbm, ax0, ax1, ay0, ay1, bx, by, start_ref, out, x_ref, y_ref, sems):
    copies = [
        pltpu.make_async_copy(x_hbm, x_ref, sems.at[0]),
        pltpu.make_async_copy(y_hbm, y_ref, sems.at[1]),
    ]
    for copy in copies:
        copy.start()
    for copy in copies:
        copy.wait()
    x = x_ref[...]
    y = y_ref[...]
    xf = factors(x * (2.0 * SCALE), X_ORDER)
    yf = factors(y, Y_ORDER)
    for factor, left0, left1, right in ((xf, ax0, ax1, bx), (yf, ay0, ay1, by)):
        right[...] = factor.astype(BF16)
        turned = factor.T
        left0[...] = turned[:, :128].astype(BF16)
        left1[...] = turned[:, 128:]
    start = -SCALE * jnp.sum(y * y, axis=0, keepdims=True)
    start_ref[...] = start
    left, unused = left_factor(ay0, ay1, start)
    partial_lse(left, bx, out)


def left_factor(left0, left1, pot, adj=None):
    width = pot.shape[1]
    high, mid, low = split3(pot)
    one = jnp.ones((1, width), F32)
    rows = [high, mid, low, one, one, one, jnp.zeros_like(one)]
    rows.append(jnp.zeros_like(one) if adj is None else adj)
    rows.append(jnp.zeros((120, width), F32))
    turned = jnp.concatenate(rows, axis=0).T
    column = None
    if adj is not None:
        column = turned[:, 7:8]
        lane = lax.broadcasted_iota(jnp.int32, turned.shape, 1)
        turned = jnp.where(lane == 7, 0.0, turned)
    return jnp.concatenate([left0[...], (left1[...] + turned).astype(BF16)], axis=1), column


def right_rows(pot):
    width = pot.shape[1]
    one = jnp.ones((3, width), F32)
    high, mid, low = split3(pot)
    return jnp.concatenate([one, high, mid, low, jnp.zeros((10, width), F32)], axis=0).astype(BF16)


def right_chunk(right, rows, at, wide):
    return jnp.concatenate(
        [right[0:128, at : at + wide], rows[:, at : at + wide], right[144:DEPTH, at : at + wide]], axis=0
    )


def matmul(a, b):
    return jnp.dot(a, b, preferred_element_type=F32)


def partial_lse(left, right, out):
    width = right.shape[1]
    rows = right_rows(jnp.zeros((1, width), F32))
    wide = min(CHUNK, width)
    for at in range(0, width, wide):
        scores = matmul(left, right_chunk(right, rows, at, wide))
        top = jnp.max(scores, axis=0, keepdims=True)
        total = jnp.sum(jnp.exp(scores - top), axis=0, keepdims=True)
        out[:, at : at + wide] = top + jnp.log(total)


def join_lse(parts):
    parts = [p[...] for p in parts]
    top = functools.reduce(jnp.maximum, parts)
    return top + jnp.log(sum(jnp.exp(p - top) for p in parts))


def join_sum(parts):
    return sum(p[...] for p in parts)


def join_body(join, *refs):
    refs[-1][...] = join(refs[:-1])


def forward_body(log_mass, left0, left1, right, *refs):
    got, (pot_out, out) = refs[:-2], refs[-2:]
    pot = log_mass - join_lse(got)
    pot_out[...] = pot
    left, unused = left_factor(left0, left1, pot)
    partial_lse(left, right, out)


def weighted_sums(left, column, right, rows, out):
    width = right.shape[1]
    wide = min(CHUNK, width)
    for at in range(0, width, wide):
        scores = matmul(left, right_chunk(right, rows, at, wide))
        out[:, at : at + wide] = jnp.sum(jnp.exp(scores) * column, axis=0, keepdims=True)


def turn_body(log_mass, log_scale, left0, left1, right, pot_right, *refs):
    got, (pot_out, out) = refs[:-2], refs[-2:]
    pot = log_mass - join_lse(got)
    pot_out[...] = pot
    left, column = left_factor(left0, left1, pot, jnp.ones_like(pot))
    weighted_sums(left, column, right, right_rows(pot_right[...] + log_scale), out)


def backward_body(leading, log_scale, left0, left1, right, pot_left, pot_right, *refs):
    got, (adj_out, out) = refs[:-2], refs[-2:]
    adj = leading - join_sum(got)
    adj_out[...] = adj
    left, column = left_factor(left0, left1, pot_left[...], adj)
    weighted_sums(left, column, right, right_rows(pot_right[...] + log_scale), out)


SPREAD = 20.0
STRIP = 256


def gradient_body(dim, log_cols, log_rows, n_got, n_col, n_row, ax0, ax1, by, x_ref, y_ref, *refs):
    pots_rows = refs[:ITERS]
    pots_cols = refs[ITERS : 2 * ITERS + 1]
    adjs_rows = refs[2 * ITERS + 1 : 3 * ITERS]
    adjs_cols = refs[3 * ITERS : 4 * ITERS - 1]
    refs = refs[4 * ITERS - 1 :]
    got, refs = refs[:n_got], refs[n_got:]
    us = [p[...] for p in pots_rows]
    vs = [p[...] for p in pots_cols]
    first = (1.0 if ITERS == 1 else 0.0) - join_sum(got)
    adjs_rows = [first] + [a[...] for a in adjs_rows]
    adjs_cols = [a[...] for a in adjs_cols] + [jnp.ones(vs[0].shape, F32)]
    gradient(log_cols, log_rows, n_col, n_row, ax0, ax1, by, x_ref, y_ref, us, vs, adjs_rows, adjs_cols, refs)


def gradient(log_cols, log_rows, n_col, n_row, ax0, ax1, by, x_ref, y_ref, us, vs, adjs_rows, adjs_cols, refs):
    outs_x, outs_y = refs[:n_col], refs[n_col : n_col + n_row]
    cols_rows, x_parts, y_parts, gx, gy, left_e, left_r, right_r, all_x, all_y = refs[n_col + n_row :]
    dim, count_rows = x_ref.shape
    count_cols = y_ref.shape[1]
    shift = log_rows - log_cols

    x = x_ref[...]
    y = y_ref[...]
    one = jnp.ones((1, count_cols), F32)
    pad = jnp.zeros((31, count_cols), F32)
    y_parts[...] = jnp.concatenate(list(split3(y)) + [one, pad], axis=0).T.astype(BF16)
    one = jnp.ones((1, count_rows), F32)
    pad = jnp.zeros((31, count_rows), F32)
    x_parts[...] = jnp.concatenate(list(split3(x)) + [one, pad], axis=0).astype(BF16)
    gy[...] = jnp.zeros_like(gy)

    far_u = functools.reduce(jnp.maximum, [jnp.abs(u - us[-1]) for u in us])
    far_v = functools.reduce(jnp.maximum, [jnp.abs(v - vs[-1]) for v in vs])
    near = jnp.maximum(jnp.max(far_u), jnp.max(far_v)) < SPREAD

    def add_strip(at, total):
        upper = total.astype(BF16)
        lower = (total - upper.astype(F32)).astype(BF16)
        gx[at, :] = matmul(upper, y_parts[...]) + matmul(lower, y_parts[...])
        gy[...] += matmul(x_parts[:, at], upper) + matmul(x_parts[:, at], lower)

    @pl.when(near)
    def factored():
        alpha = [jnp.exp(u - us[-1]) for u in us]
        beta = [jnp.exp(v - vs[-1]) for v in vs]
        p_rows = alpha + [a * adj for a, adj in zip(alpha, adjs_rows)]
        q_rows = [b * adj for b, adj in zip(beta[1:], adjs_cols)] + [b * math.exp(shift) for b in beta[:-1]]
        fill = 16 - 2 * ITERS
        p_split = split3(jnp.concatenate(p_rows + [jnp.zeros((fill, count_rows), F32)], axis=0))
        q_split = split3(jnp.concatenate(q_rows + [jnp.zeros((fill, count_cols), F32)], axis=0))
        tail = [jnp.zeros((32, count_rows), F32)]
        left_r[...] = jnp.concatenate([p_split[o] for o in X_ORDER] + tail, axis=0).T.astype(BF16)
        tail = [jnp.zeros((32, count_cols), F32)]
        right_r[...] = jnp.concatenate([q_split[o] for o in Y_ORDER] + tail, axis=0).astype(BF16)
        left, unused = left_factor(ax0, ax1, us[-1] + log_cols)
        left_e[...] = left
        right = right_chunk(by, right_rows(vs[-1]), 0, count_cols)
        strip = min(STRIP, count_rows)
        for step in range(count_rows // strip):
            at = pl.ds(step * strip, strip)
            total = jnp.exp(matmul(left_e[at, :], right)) * matmul(left_r[at, :], right_r[...])
            add_strip(at, total)

    @pl.when(jnp.logical_not(near))
    def separate():
        stack = [u + log_cols for u in us] + adjs_rows
        stack.append(jnp.zeros((128 - len(stack), count_rows), F32))
        cols_rows[...] = jnp.concatenate(stack, axis=0).T
        strip = 128

        def block(step, carry):
            at = pl.ds(pl.multiple_of(step * strip, strip), strip)
            left = jnp.concatenate([ax0[at, :], ax1[at, :].astype(BF16)], axis=1)
            inner = matmul(left, by[...])
            columns = cols_rows[at, :]
            total = jnp.zeros_like(inner)
            for k in range(ITERS):
                base = inner + columns[:, k : k + 1]
                total += jnp.exp(base + vs[k + 1]) * adjs_cols[k]
                total += jnp.exp(base + (vs[k] + shift)) * columns[:, ITERS + k : ITERS + k + 1]
            add_strip(at, total)
            return carry

        lax.fori_loop(0, count_rows // strip, block, 0)

    def finish(points, sums):
        mixed = sums[0:dim] + sums[dim : 2 * dim] + sums[2 * dim : 3 * dim]
        return 2.0 * (points * sums[3 * dim : 3 * dim + 1] - mixed)

    for value, held, outs, axis in (
        (finish(x, gx[...].T), all_x, outs_x, "col"),
        (finish(y, gy[...]), all_y, outs_y, "row"),
    ):
        share = held.shape[2]
        for p in range(held.shape[0]):
            held[p] = value[:, p * share : (p + 1) * share]
        me = lax.axis_index(axis)
        for s, out in enumerate(outs):
            out[...] = held[me ^ s]


def swap(value, axis, distance):
    return lax.ppermute(value, axis, [(d, d ^ distance) for d in range(lax.axis_size(axis))])


def exchange(part, axis, join):
    size = lax.axis_size(axis)
    assert size & (size - 1) == 0
    if size == 4:
        return (part,) + tuple(swap(part, axis, d) for d in (2, 3, 1))
    distance = 1
    got = (part,)
    while distance < size:
        if len(got) > 1:
            (part,) = call(functools.partial(join_body, join), [shape(part.shape)], len(got))(*got)
        got = (part, swap(part, axis, distance))
        distance *= 2
    return got


def scatter(pieces, axis):
    got = [pieces[0]] + [swap(pieces[s], axis, s) for s in range(1, len(pieces))]
    return sum(got[1:], got[0])


def slot(column, lane, state):
    return jnp.where(lax.broadcasted_iota(jnp.int32, state.shape, 1) == lane, column, state)


def left_strip(left0, left1, at, pot):
    strip = left1[at, :]
    for lane, part in enumerate(split3(jnp.broadcast_to(pot, strip.shape))):
        strip = slot(part, lane, strip)
    return jnp.concatenate([left0[at, :], strip.astype(BF16)], axis=1)


def halves(value):
    return sum(value[:, p : p + 128] for p in range(0, value.shape[1], 128))


def octets(value):
    return jnp.sum(value.reshape(value.shape[0] // 8, 8, value.shape[1]), axis=0)


SWEEP = 256


def sweep(left_of, right, rows, out, held_of, acc, times, store, close):
    strips, strip = times.shape[:2]
    wide_all = right.shape[1]
    for s in range(strips + 1):
        at = slice(s * strip, (s + 1) * strip)
        left = left_of(at) if s < strips else None
        sums = None
        for c in range(0, wide_all, CHUNK):
            place = slice(c, c + CHUNK)
            if s < strips:
                sums = store(held_of(s), matmul(left, right_chunk(right, rows, c, CHUNK)), place, sums)
            if s > 0:
                factor = times[s - 1]
                part = octets(held_of(s - 1)[:, place] * jnp.concatenate([factor] * (CHUNK // 128), axis=1))
                if s > 1:
                    part += acc[:, place]
                if s < strips:
                    acc[:, place] = part
                else:
                    out[:, place] = jnp.sum(part, axis=0, keepdims=True)
        if s < strips:
            times[s] = jnp.broadcast_to(close(at, sums, held_of(s)), times.shape[1:])


def exponentials(weigh):
    def store(held, scores, place, sums):
        power = jnp.exp(scores)
        held[:, place] = power
        part = halves(weigh(power, place))
        return part if sums is None else sums + part

    return store


def prepare_own_body(x_hbm, y_hbm, ax0, ax1, ay0, ay1, by, state, out, x_ref, y_ref, bx, sems):
    copies = [
        pltpu.make_async_copy(x_hbm, x_ref, sems.at[0]),
        pltpu.make_async_copy(y_hbm, y_ref, sems.at[1]),
    ]
    for copy in copies:
        copy.start()
    for copy in copies:
        copy.wait()
    x = x_ref[...]
    y = y_ref[...]
    xf = factors(x * (2.0 * SCALE), X_ORDER)
    yf = factors(y, Y_ORDER)
    for factor, left0, left1, right in ((xf, ax0, ax1, bx), (yf, ay0, ay1, by)):
        right[...] = factor.astype(BF16)
        turned = factor.T
        left0[...] = turned[:, :128].astype(BF16)
        left1[...] = turned[:, 128:]
    start = -SCALE * jnp.sum(y * y, axis=0, keepdims=True)
    state[...] = jnp.concatenate([start, jnp.zeros((127, y.shape[1]), F32)], axis=0).T
    left, unused = left_factor(ay0, ay1, start)
    partial_lse(left, bx, out)
    lane = lax.broadcasted_iota(jnp.int32, ay1.shape, 1)
    ay1[...] = jnp.where((lane >= 3) & (lane < 6), 1.0, ay1[...])


def first_pot_body(log_rows, *refs):
    refs[-1][...] = -log_rows - join_lse(refs[:-1])


def opening_body(n_row, log_rows, log_cols, left0, left1, state, *refs):
    xs, us = refs[:n_row], refs[n_row : 2 * n_row]
    right, kept, u_out, state_out, out, acc, times = refs[2 * n_row :]
    strip = times.shape[1]
    x = jnp.concatenate([r[...] for r in xs], axis=1)
    right[...] = factors(x * (2.0 * SCALE), X_ORDER).astype(BF16)
    u = jnp.concatenate([r[...] for r in us], axis=1)
    u_out[...] = u

    def left_of(at):
        return jnp.concatenate([left0[at, :], left1[at, :].astype(BF16)], axis=1)

    def store(held, scores, place, tops):
        held[:, place] = scores
        for p in range(0, CHUNK, 128):
            part = scores[:, p : p + 128]
            tops = part if tops is None else jnp.maximum(tops, part)
        return tops

    def close(at, tops, held):
        top = jnp.max(tops, axis=1, keepdims=True)
        sums = None
        for c in range(0, held.shape[1], CHUNK):
            place = slice(c, c + CHUNK)
            power = jnp.exp(held[:, place] - top)
            held[:, place] = power
            part = halves(power)
            sums = part if sums is None else sums + part
        column = jnp.sum(sums, axis=1, keepdims=True)
        pot = -log_cols - (top + jnp.log(column))
        state_out[at, :] = slot(pot, 1, slot(-top, BASE, state[at, :]))
        return math.exp(-log_cols) / column

    def held_of(s):
        return kept.at[s * strip : (s + 1) * strip]

    sweep(left_of, right, right_rows(u), out, held_of, acc, times, store, close)


BASE = 6
NEAR = 25.0


def scaled(kept, row, column_of, out, acc, hold):
    count, total = kept.shape
    block = min(256, count)

    def across(index, carry):
        at = pl.ds(pl.multiple_of(index * block, block), block)
        sums = None
        for c in range(0, total, 128):
            part = kept[at, c : c + 128] * row[:, c : c + 128]
            sums = part if sums is None else sums + part
        hold[at, :] = sums
        return carry

    lax.fori_loop(0, count // block, across, 0)
    hold[...] = jnp.broadcast_to(column_of(jnp.sum(hold[...], axis=1, keepdims=True)), hold.shape)
    acc[...] = jnp.zeros_like(acc)

    def down(index, carry):
        at = pl.ds(pl.multiple_of(index * block, block), block)
        factor = hold[at, :]
        for c in range(0, total, 128):
            acc[:, c : c + 128] += octets(kept[at, c : c + 128] * factor)
        return carry

    lax.fori_loop(0, count // block, down, 0)
    out[...] = jnp.sum(acc[...], axis=0, keepdims=True)


def iteration_body(k, n_got, log_rows, log_cols, left0, left1, right, kept, state, u_first, u_old, *refs):
    got, (u_out, state_out, out, held, acc, times, hold, row) = refs[:n_got], refs[n_got:]
    u = u_old[...] - (log_rows + jnp.log(join_sum(got)))
    u_out[...] = u
    apart = u - u_first[...]
    near = jnp.max(jnp.abs(apart)) < NEAR

    @pl.when(near)
    def scale():
        row[...] = jnp.exp(apart)

        def column_of(sums):
            old = state[...]
            state_out[...] = slot(old[:, BASE : BASE + 1] - (log_cols + jnp.log(sums)), k, old)
            return math.exp(-log_cols) / sums

        scaled(kept, row, column_of, out, acc, hold)
        out[...] = out[...] * row[...]

    @pl.when(jnp.logical_not(near))
    def renew():
        def left_of(at):
            return left_strip(left0, left1, at, state[at, k - 1 : k])

        def close(at, sums, held):
            column = jnp.sum(sums, axis=1, keepdims=True)
            old = state[at, :]
            state_out[at, :] = slot(old[:, k - 1 : k] - (log_cols + jnp.log(column)), k, old)
            return math.exp(-log_cols) / column

        store = exponentials(lambda power, place: power)
        sweep(left_of, right, right_rows(u), out, lambda s: held.at[s % 2], acc, times, store, close)


def adjoint_body(k, n_got, log_rows, log_cols, left0, left1, right, kept, state, u_first, u_ref, u_before, *refs):
    got, (adj_out, state_out, out, held, acc, times, hold, row) = refs[:n_got], refs[n_got:]
    if k == ITERS:
        adj_out[...] = 1.0 - math.exp(log_cols) * join_sum(got)
    else:
        adj_out[...] = -join_sum(got)
    u, before = u_ref[...], u_before[...]
    shift = math.exp(log_rows - log_cols)
    mass = math.exp(log_cols)
    apart, apart_before = u - u_first[...], before - u_first[...]
    near = jnp.max(jnp.maximum(jnp.abs(apart), jnp.abs(apart_before))) < NEAR

    @pl.when(near)
    def scale():
        row[...] = jnp.exp(apart) * adj_out[...]

        def column_of(sums):
            old = state[...]
            beta = mass * jnp.exp(old[:, k - 1 : k] - old[:, BASE : BASE + 1])
            adj = -shift * beta * sums
            state_out[...] = slot(adj, 16 + k - 1, old)
            return beta * adj

        scaled(kept, row, column_of, out, acc, hold)
        out[...] = out[...] * jnp.exp(apart_before)

    @pl.when(jnp.logical_not(near))
    def renew():
        def left_of(at):
            return left_strip(left0, left1, at, state[at, k : k + 1])

        def close(at, sums, held):
            column = jnp.sum(sums, axis=1, keepdims=True)
            old = state[at, :]
            sigma = jnp.exp(old[:, k - 1 : k] - old[:, k : k + 1])
            adj = -shift * sigma * column
            state_out[at, :] = slot(adj, 16 + k - 1, old)
            return sigma * adj

        store = exponentials(lambda power, place: power * adj_out[:, place])
        rows = right_rows(u + log_cols)
        sweep(left_of, right, rows, out, lambda s: held.at[s % 2], acc, times, store, close)
        out[...] = out[...] * jnp.exp(before - u)


def finish(points, sums):
    dim = points.shape[0]
    mixed = sums[0:dim] + sums[dim : 2 * dim] + sums[2 * dim : 3 * dim]
    return 2.0 * (points * sums[3 * dim : 3 * dim + 1] - mixed)


def with_total(points):
    width = points.shape[1]
    one = jnp.ones((1, width), F32)
    pad = jnp.zeros((128 - 3 * points.shape[0] - 1, width), F32)
    return jnp.concatenate(list(split3(points)) + [one, pad], axis=0).astype(BF16)


def all_weights(log_rows, log_cols, left0, left1, right, kept, state, us, adjs, at, wide, take):
    turned = state[at, :].T
    v = [turned[k : k + 1] for k in range(ITERS + 1)]
    adjs_cols = [turned[16 + k : 17 + k] for k in range(1, ITERS)] + [jnp.ones_like(v[0])]
    shift = math.exp(log_rows - log_cols)
    apart = [u - us[0] for u in us]
    near = jnp.max(functools.reduce(jnp.maximum, [jnp.abs(a) for a in apart])) < NEAR
    total = us[0].shape[1]

    @pl.when(near)
    def scale():
        alpha = [jnp.exp(a) for a in apart]
        beta = [math.exp(log_cols) * jnp.exp(pot - turned[BASE : BASE + 1]) for pot in v]
        p_rows = alpha + [a * adj for a, adj in zip(alpha, adjs)]
        q_rows = [b * adj for b, adj in zip(beta[1:], adjs_cols)] + [shift * b for b in beta[:-1]]

        def stacked(rows, order):
            zero = jnp.zeros((16 - len(rows), rows[0].shape[1]), F32)
            parts = split3(jnp.concatenate(rows + [zero], axis=0))
            tail = jnp.zeros((32, rows[0].shape[1]), F32)
            return jnp.concatenate([parts[o] for o in order] + [tail], axis=0)

        p_right = stacked(p_rows, X_ORDER).astype(BF16)
        q_left = stacked(q_rows, Y_ORDER).T.astype(BF16)
        for c in range(0, total, wide):
            place = slice(c, c + wide)
            take(kept[at, place] * matmul(q_left, p_right[:, place]), place)

    @pl.when(jnp.logical_not(near))
    def separate():
        lefts = [left_strip(left0, left1, at, state[at, k : k + 1]) for k in range(ITERS + 1)]
        for c in range(0, total, wide):
            place = slice(c, c + wide)
            weights = 0.0
            for k in range(ITERS):
                adj_col = 1.0 if k == ITERS - 1 else state[at, 17 + k : 18 + k]
                full = right_chunk(right, right_rows(us[k] + log_cols), c, wide)
                weights += jnp.exp(matmul(lefts[k + 1], full)) * adj_col
                weights += jnp.exp(matmul(lefts[k], full)) * (shift * adjs[k][:, place])
            take(weights, place)


def halved(weights):
    upper = weights.astype(BF16)
    return upper, (weights - upper.astype(F32)).astype(BF16)


def row_grad_body(n_got, log_rows, log_cols, left0, left1, right, kept, state, x_ref, y_ref, *refs):
    count = x_ref.shape[1]
    us = [r[:, :count] for r in refs[:ITERS]]
    adjs = [r[:, :count] for r in refs[ITERS : 2 * ITERS - 1]]
    refs = refs[2 * ITERS - 1 :]
    got, outs, (sums, pieces) = refs[:n_got], refs[n_got:-2], refs[-2:]
    adjs = [-join_sum([r[:, :count] for r in got])] + adjs
    y_parts = with_total(y_ref[...])

    def take(weights, place):
        upper, lower = halved(weights)
        sums[:, place] = matmul(y_parts, upper) + matmul(y_parts, lower)

    at = pl.ds(0, left0.shape[0])
    all_weights(log_rows, log_cols, left0, left1, right, kept, state, us, adjs, at, CHUNK, take)
    value = finish(x_ref[...], sums[...])
    share = count // len(outs)
    for p in range(len(outs)):
        pieces[p] = value[:, p * share : (p + 1) * share]
    me = lax.axis_index("col")
    for s, out in enumerate(outs):
        out[...] = pieces[me ^ s]


def col_grad_body(n_got, n_row, log_rows, log_cols, left0, left1, right, kept, state, y_ref, *refs):
    xs, refs = refs[:n_row], refs[n_row:]
    us = [r[...] for r in refs[:ITERS]]
    adjs = [r[...] for r in refs[ITERS : 2 * ITERS - 1]]
    refs = refs[2 * ITERS - 1 :]
    got, (out, sums) = refs[:n_got], refs[n_got:]
    adjs = [-join_sum(got)] + adjs
    x_parts = with_total(jnp.concatenate([r[...] for r in xs], axis=1))
    share = out.shape[1]
    start = pl.multiple_of(lax.axis_index("row") * share, share)
    sums[...] = jnp.zeros_like(sums)

    def across(weights, place):
        return lax.dot_general(
            weights, x_parts[:, place], (((1,), (1,)), ((), ())), preferred_element_type=F32
        )

    def take(weights, place):
        upper, lower = halved(weights)
        sums[...] += across(upper, place) + across(lower, place)

    at = pl.ds(start, share)
    all_weights(log_rows, log_cols, left0, left1, right, kept, state, us, adjs, at, 4 * CHUNK, take)
    out[...] = finish(y_ref[:, at], sums[...].T)


def gradient_scratch(dim, count_rows, count_cols, n_col, n_row):
    return [
        pltpu.VMEM((count_rows, 128), F32),
        pltpu.VMEM((128, count_rows), BF16),
        pltpu.VMEM((count_cols, 128), BF16),
        pltpu.VMEM((count_rows, 128), F32),
        pltpu.VMEM((128, count_cols), F32),
        pltpu.VMEM((count_rows, DEPTH), BF16),
        pltpu.VMEM((count_rows, 128), BF16),
        pltpu.VMEM((128, count_cols), BF16),
        pltpu.VMEM((n_col, dim, count_rows // n_col), F32),
        pltpu.VMEM((n_row, dim, count_cols // n_row), F32),
    ]


def repeated(x, y):
    dim, count_rows = x.shape
    count_cols = y.shape[1]
    n_row, n_col = lax.axis_size("row"), lax.axis_size("col")
    all_rows, held_cols = count_rows * n_row, count_cols
    log_rows, log_cols = math.log(all_rows), math.log(count_cols * n_col)
    row, col = (1, all_rows), (1, held_cols)

    own = (1, count_rows)
    ax0, ax1, ay0, ay1, by, state, part, x, y = pl.pallas_call(
        prepare_own_body,
        out_shape=[
            shape((count_rows, 128), BF16),
            shape((count_rows, 128)),
            shape((count_cols, 128), BF16),
            shape((count_cols, 128)),
            shape((DEPTH, count_cols), BF16),
            shape((count_cols, 128)),
            shape(own),
            shape(x.shape),
            shape(y.shape),
        ],
        in_specs=[pl.BlockSpec(memory_space=pltpu.HBM)] * 2,
        out_specs=vmem(9),
        scratch_shapes=[pltpu.VMEM((DEPTH, count_rows), BF16), pltpu.SemaphoreType.DMA((2,))],
        compiler_params=pltpu.CompilerParams(vmem_limit_bytes=VMEM_LIMIT),
    )(x, y)
    xs = [x] + [swap(x, "row", s) for s in range(1, n_row)]
    got = exchange(part, "col", join_lse)
    (u,) = call(functools.partial(first_pot_body, log_rows), [shape(own)], len(got))(*got)
    u_blocks = [u] + [swap(u, "row", s) for s in range(1, n_row)]

    strip = min(SWEEP, held_cols)
    sums = [pltpu.VMEM((8, all_rows), F32), pltpu.VMEM((held_cols // strip, strip, 128), F32)]
    scratch = [pltpu.VMEM((2, strip, all_rows), F32)] + sums
    scratch += [pltpu.VMEM((held_cols, 128), F32), pltpu.VMEM(row, F32)]
    results = [shape(row), shape((held_cols, 128)), shape(row)]
    us = []
    bx, kept, u, state, part = call(
        functools.partial(opening_body, n_row, log_rows, log_cols),
        [shape((DEPTH, all_rows), BF16), shape((held_cols, all_rows))] + results,
        3 + 2 * n_row,
        sums,
        SWEEP_LIMIT,
    )(ay0, ay1, state, *xs, *u_blocks)
    us.append(u)
    for k in range(2, ITERS + 1):
        got = exchange(part, "col", join_sum)
        u, state, part = call(
            functools.partial(iteration_body, k, len(got), log_rows, log_cols),
            results,
            7 + len(got),
            scratch,
            SWEEP_LIMIT,
        )(ay0, ay1, bx, kept, state, us[0], u, *got)
        us.append(u)
    adjs_rows = []
    for k in range(ITERS, 1, -1):
        got = exchange(part, "col", join_sum)
        adj, state, part = call(
            functools.partial(adjoint_body, k, len(got), log_rows, log_cols),
            results,
            8 + len(got),
            scratch,
            SWEEP_LIMIT,
        )(ay0, ay1, bx, kept, state, us[0], us[k - 1], us[k - 2], *got)
        adjs_rows.insert(0, adj)
    got = exchange(part, "col", join_sum)
    share_x, share_y = count_rows // n_col, count_cols // n_row
    outs_x = call(
        functools.partial(row_grad_body, len(got), log_rows, log_cols),
        [shape((dim, share_x))] * n_col,
        7 + 2 * ITERS - 1 + len(got),
        [pltpu.VMEM((128, count_rows), F32), pltpu.VMEM((n_col, dim, share_x), F32)],
        SWEEP_LIMIT,
    )(ay0, ay1, bx, kept, state, x, y, *us, *adjs_rows, *got)
    (grad_y,) = call(
        functools.partial(col_grad_body, len(got), n_row, log_rows, log_cols),
        [shape((dim, share_y))],
        6 + n_row + 2 * ITERS - 1 + len(got),
        [pltpu.VMEM((share_y, 128), F32)],
        SWEEP_LIMIT,
        pl.CostEstimate(flops=1 << 31, bytes_accessed=1 << 23, transcendentals=0),
    )(ay0, ay1, bx, kept, state, y, *xs, *us, *adjs_rows, *got)
    return scatter(outs_x, "col").T, grad_y.T


REPEAT_PAIRS = 1 << 23


def on_device(x_points, y_points):
    x = x_points.T
    y = y_points.T
    n_row, n_col = lax.axis_size("row"), lax.axis_size("col")
    if ITERS > 1 and x.shape[1] * n_row * y.shape[1] <= REPEAT_PAIRS:
        return repeated(x, y)
    return shared(x, y)


def shared(x, y):
    dim, count_rows = x.shape
    count_cols = y.shape[1]
    n_row, n_col = lax.axis_size("row"), lax.axis_size("col")
    log_rows = math.log(count_rows * n_row)
    log_cols = math.log(count_cols * n_col)
    row, col = (1, count_rows), (1, count_cols)

    ax0, ax1, ay0, ay1, bx, by, start, part, x, y = pl.pallas_call(
        prepare_body,
        out_shape=[
            shape((count_rows, 128), BF16),
            shape((count_rows, 128)),
            shape((count_cols, 128), BF16),
            shape((count_cols, 128)),
            shape((DEPTH, count_rows), BF16),
            shape((DEPTH, count_cols), BF16),
            shape(col),
            shape(row),
            shape(x.shape),
            shape(y.shape),
        ],
        in_specs=[pl.BlockSpec(memory_space=pltpu.HBM)] * 2,
        out_specs=vmem(10),
        scratch_shapes=[pltpu.SemaphoreType.DMA((2,))],
        compiler_params=pltpu.CompilerParams(vmem_limit_bytes=VMEM_LIMIT),
    )(x, y)

    pots_rows, pots_cols = [], [start]
    for k in range(ITERS):
        got = exchange(part, "col", join_lse)
        pot, part = call(functools.partial(forward_body, -log_rows), [shape(row), shape(col)], 3 + len(got))(
            ax0, ax1, by, *got
        )
        pots_rows.append(pot)
        got = exchange(part, "row", join_lse)
        if k < ITERS - 1:
            pot, part = call(functools.partial(forward_body, -log_cols), [shape(col), shape(row)], 3 + len(got))(
                ay0, ay1, bx, *got
            )
            pots_cols.append(pot)
    pot, part = call(functools.partial(turn_body, -log_cols, log_cols), [shape(col), shape(row)], 4 + len(got))(
        ay0, ay1, bx, pots_rows[-1], *got
    )
    pots_cols.append(pot)

    adjs_rows, adjs_cols = [], []
    for k in reversed(range(1, ITERS)):
        leading = 1.0 if k == ITERS - 1 else 0.0
        got = exchange(part, "col", join_sum)
        adj, part = call(functools.partial(backward_body, leading, log_rows), [shape(row), shape(col)], 5 + len(got))(
            ax0, ax1, by, pots_rows[k], pots_cols[k], *got
        )
        adjs_rows.insert(0, adj)
        got = exchange(part, "row", join_sum)
        adj, part = call(functools.partial(backward_body, 0.0, log_cols), [shape(col), shape(row)], 5 + len(got))(
            ay0, ay1, bx, pots_cols[k], pots_rows[k - 1], *got
        )
        adjs_cols.insert(0, adj)
    got = exchange(part, "col", join_sum)

    share_x, share_y = count_rows // n_col, count_cols // n_row
    outs = call(
        functools.partial(gradient_body, dim, log_cols, log_rows, len(got), n_col, n_row),
        [shape((dim, share_x))] * n_col + [shape((dim, share_y))] * n_row,
        5 + 4 * ITERS - 1 + len(got),
        gradient_scratch(dim, count_rows, count_cols, n_col, n_row),
    )(ax0, ax1, by, x, y, *pots_rows, *pots_cols, *adjs_rows, *adjs_cols, *got)
    grad_x = scatter(outs[:n_col], "col")
    grad_y = scatter(outs[n_col:], "row")
    return (grad_x.T, grad_y.T)


def solution(mesh):
    in_specs = (P(("groups", "row"), None), P(("groups", "col"), None))
    out_specs = (P(("groups", "row", "col"), None), P(("groups", "col", "row"), None))
    return jax.shard_map(
        on_device, mesh=mesh, in_specs=in_specs, out_specs=out_specs, check_vma=False
    )
```

```python
import functools
import math

import jax
import jax.numpy as jnp
from jax import lax
from jax.experimental import pallas as pl
from jax.experimental.pallas import tpu as pltpu
from jax.sharding import PartitionSpec as P

ITERS = 5
EPSILON = 0.05
SCALE = 1.0 / EPSILON
DEPTH = 256
CHUNK = 256
F32 = jnp.float32
BF16 = jnp.bfloat16
VMEM_LIMIT = 32 * 1024 * 1024
SWEEP_LIMIT = 24 * 1024 * 1024


def split3(v):
    high = v.astype(BF16).astype(F32)
    rest = v - high
    mid = rest.astype(BF16).astype(F32)
    low = (rest - mid).astype(BF16).astype(F32)
    return high, mid, low


def vmem(count):
    return [pl.BlockSpec(memory_space=pltpu.VMEM)] * count


def call(body, outs, count, scratch=(), limit=VMEM_LIMIT, cost=None):
    return pl.pallas_call(
        body,
        out_shape=outs,
        in_specs=vmem(count),
        out_specs=vmem(len(outs)),
        scratch_shapes=list(scratch),
        compiler_params=pltpu.CompilerParams(vmem_limit_bytes=limit),
        cost_estimate=cost,
    )


def shape(dims, dtype=F32):
    return jax.ShapeDtypeStruct(dims, dtype)


def factors(points, order):
    parts = split3(points)
    width = points.shape[1]
    blocks = [parts[o] for o in order]
    zero16 = jnp.zeros((16, width), F32)
    tail = jnp.zeros((DEPTH - 144 - 2 * points.shape[0], width), F32)
    return jnp.concatenate(blocks[:4] + [zero16] + blocks[4:] + [tail], axis=0)


X_ORDER = (0, 0, 1, 0, 2, 1)
Y_ORDER = (0, 1, 0, 2, 0, 1)


def prepare_body(x_hbm, y_hbm, ax0, ax1, ay0, ay1, bx, by, start_ref, out, x_ref, y_ref, sems):
    copies = [
        pltpu.make_async_copy(x_hbm, x_ref, sems.at[0]),
        pltpu.make_async_copy(y_hbm, y_ref, sems.at[1]),
    ]
    for copy in copies:
        copy.start()
    for copy in copies:
        copy.wait()
    x = x_ref[...]
    y = y_ref[...]
    xf = factors(x * (2.0 * SCALE), X_ORDER)
    yf = factors(y, Y_ORDER)
    for factor, left0, left1, right in ((xf, ax0, ax1, bx), (yf, ay0, ay1, by)):
        right[...] = factor.astype(BF16)
        turned = factor.T
        left0[...] = turned[:, :128].astype(BF16)
        left1[...] = turned[:, 128:]
    start = -SCALE * jnp.sum(y * y, axis=0, keepdims=True)
    start_ref[...] = start
    left, unused = left_factor(ay0, ay1, start)
    partial_lse(left, bx, out)


def left_factor(left0, left1, pot, adj=None):
    width = pot.shape[1]
    high, mid, low = split3(pot)
    one = jnp.ones((1, width), F32)
    rows = [high, mid, low, one, one, one, jnp.zeros_like(one)]
    rows.append(jnp.zeros_like(one) if adj is None else adj)
    rows.append(jnp.zeros((120, width), F32))
    turned = jnp.concatenate(rows, axis=0).T
    column = None
    if adj is not None:
        column = turned[:, 7:8]
        lane = lax.broadcasted_iota(jnp.int32, turned.shape, 1)
        turned = jnp.where(lane == 7, 0.0, turned)
    return jnp.concatenate([left0[...], (left1[...] + turned).astype(BF16)], axis=1), column


def right_rows(pot):
    width = pot.shape[1]
    one = jnp.ones((3, width), F32)
    high, mid, low = split3(pot)
    return jnp.concatenate([one, high, mid, low, jnp.zeros((10, width), F32)], axis=0).astype(BF16)


def right_chunk(right, rows, at, wide):
    return jnp.concatenate(
        [right[0:128, at : at + wide], rows[:, at : at + wide], right[144:DEPTH, at : at + wide]], axis=0
    )


def matmul(a, b):
    return jnp.dot(a, b, preferred_element_type=F32)


def partial_lse(left, right, out):
    width = right.shape[1]
    rows = right_rows(jnp.zeros((1, width), F32))
    wide = min(CHUNK, width)
    for at in range(0, width, wide):
        scores = matmul(left, right_chunk(right, rows, at, wide))
        top = jnp.max(scores, axis=0, keepdims=True)
        total = jnp.sum(jnp.exp(scores - top), axis=0, keepdims=True)
        out[:, at : at + wide] = top + jnp.log(total)


def join_lse(parts):
    parts = [p[...] for p in parts]
    top = functools.reduce(jnp.maximum, parts)
    return top + jnp.log(sum(jnp.exp(p - top) for p in parts))


def join_sum(parts):
    return sum(p[...] for p in parts)


def join_body(join, *refs):
    refs[-1][...] = join(refs[:-1])


def forward_body(log_mass, left0, left1, right, *refs):
    got, (pot_out, out) = refs[:-2], refs[-2:]
    pot = log_mass - join_lse(got)
    pot_out[...] = pot
    left, unused = left_factor(left0, left1, pot)
    partial_lse(left, right, out)


def weighted_sums(left, column, right, rows, out):
    width = right.shape[1]
    wide = min(CHUNK, width)
    for at in range(0, width, wide):
        scores = matmul(left, right_chunk(right, rows, at, wide))
        out[:, at : at + wide] = jnp.sum(jnp.exp(scores) * column, axis=0, keepdims=True)


def turn_body(log_mass, log_scale, left0, left1, right, pot_right, *refs):
    got, (pot_out, out) = refs[:-2], refs[-2:]
    pot = log_mass - join_lse(got)
    pot_out[...] = pot
    left, column = left_factor(left0, left1, pot, jnp.ones_like(pot))
    weighted_sums(left, column, right, right_rows(pot_right[...] + log_scale), out)


def backward_body(leading, log_scale, left0, left1, right, pot_left, pot_right, *refs):
    got, (adj_out, out) = refs[:-2], refs[-2:]
    adj = leading - join_sum(got)
    adj_out[...] = adj
    left, column = left_factor(left0, left1, pot_left[...], adj)
    weighted_sums(left, column, right, right_rows(pot_right[...] + log_scale), out)


SPREAD = 20.0
STRIP = 256


def gradient_body(dim, log_cols, log_rows, n_got, n_col, n_row, ax0, ax1, by, x_ref, y_ref, *refs):
    pots_rows = refs[:ITERS]
    pots_cols = refs[ITERS : 2 * ITERS + 1]
    adjs_rows = refs[2 * ITERS + 1 : 3 * ITERS]
    adjs_cols = refs[3 * ITERS : 4 * ITERS - 1]
    refs = refs[4 * ITERS - 1 :]
    got, refs = refs[:n_got], refs[n_got:]
    us = [p[...] for p in pots_rows]
    vs = [p[...] for p in pots_cols]
    first = (1.0 if ITERS == 1 else 0.0) - join_sum(got)
    adjs_rows = [first] + [a[...] for a in adjs_rows]
    adjs_cols = [a[...] for a in adjs_cols] + [jnp.ones(vs[0].shape, F32)]
    gradient(log_cols, log_rows, n_col, n_row, ax0, ax1, by, x_ref, y_ref, us, vs, adjs_rows, adjs_cols, refs)


def gradient(log_cols, log_rows, n_col, n_row, ax0, ax1, by, x_ref, y_ref, us, vs, adjs_rows, adjs_cols, refs):
    outs_x, outs_y = refs[:n_col], refs[n_col : n_col + n_row]
    cols_rows, x_parts, y_parts, gx, gy, left_e, left_r, right_r, all_x, all_y = refs[n_col + n_row :]
    dim, count_rows = x_ref.shape
    count_cols = y_ref.shape[1]
    shift = log_rows - log_cols

    x = x_ref[...]
    y = y_ref[...]
    one = jnp.ones((1, count_cols), F32)
    pad = jnp.zeros((31, count_cols), F32)
    y_parts[...] = jnp.concatenate(list(split3(y)) + [one, pad], axis=0).T.astype(BF16)
    one = jnp.ones((1, count_rows), F32)
    pad = jnp.zeros((31, count_rows), F32)
    x_parts[...] = jnp.concatenate(list(split3(x)) + [one, pad], axis=0).astype(BF16)
    gy[...] = jnp.zeros_like(gy)

    far_u = functools.reduce(jnp.maximum, [jnp.abs(u - us[-1]) for u in us])
    far_v = functools.reduce(jnp.maximum, [jnp.abs(v - vs[-1]) for v in vs])
    near = jnp.maximum(jnp.max(far_u), jnp.max(far_v)) < SPREAD

    def add_strip(at, total):
        upper = total.astype(BF16)
        lower = (total - upper.astype(F32)).astype(BF16)
        gx[at, :] = matmul(upper, y_parts[...]) + matmul(lower, y_parts[...])
        gy[...] += matmul(x_parts[:, at], upper) + matmul(x_parts[:, at], lower)

    @pl.when(near)
    def factored():
        alpha = [jnp.exp(u - us[-1]) for u in us]
        beta = [jnp.exp(v - vs[-1]) for v in vs]
        p_rows = alpha + [a * adj for a, adj in zip(alpha, adjs_rows)]
        q_rows = [b * adj for b, adj in zip(beta[1:], adjs_cols)] + [b * math.exp(shift) for b in beta[:-1]]
        fill = 16 - 2 * ITERS
        p_split = split3(jnp.concatenate(p_rows + [jnp.zeros((fill, count_rows), F32)], axis=0))
        q_split = split3(jnp.concatenate(q_rows + [jnp.zeros((fill, count_cols), F32)], axis=0))
        tail = [jnp.zeros((32, count_rows), F32)]
        left_r[...] = jnp.concatenate([p_split[o] for o in X_ORDER] + tail, axis=0).T.astype(BF16)
        tail = [jnp.zeros((32, count_cols), F32)]
        right_r[...] = jnp.concatenate([q_split[o] for o in Y_ORDER] + tail, axis=0).astype(BF16)
        left, unused = left_factor(ax0, ax1, us[-1] + log_cols)
        left_e[...] = left
        right = right_chunk(by, right_rows(vs[-1]), 0, count_cols)
        strip = min(STRIP, count_rows)
        for step in range(count_rows // strip):
            at = pl.ds(step * strip, strip)
            total = jnp.exp(matmul(left_e[at, :], right)) * matmul(left_r[at, :], right_r[...])
            add_strip(at, total)

    @pl.when(jnp.logical_not(near))
    def separate():
        stack = [u + log_cols for u in us] + adjs_rows
        stack.append(jnp.zeros((128 - len(stack), count_rows), F32))
        cols_rows[...] = jnp.concatenate(stack, axis=0).T
        strip = 128

        def block(step, carry):
            at = pl.ds(pl.multiple_of(step * strip, strip), strip)
            left = jnp.concatenate([ax0[at, :], ax1[at, :].astype(BF16)], axis=1)
            inner = matmul(left, by[...])
            columns = cols_rows[at, :]
            total = jnp.zeros_like(inner)
            for k in range(ITERS):
                base = inner + columns[:, k : k + 1]
                total += jnp.exp(base + vs[k + 1]) * adjs_cols[k]
                total += jnp.exp(base + (vs[k] + shift)) * columns[:, ITERS + k : ITERS + k + 1]
            add_strip(at, total)
            return carry

        lax.fori_loop(0, count_rows // strip, block, 0)

    def finish(points, sums):
        mixed = sums[0:dim] + sums[dim : 2 * dim] + sums[2 * dim : 3 * dim]
        return 2.0 * (points * sums[3 * dim : 3 * dim + 1] - mixed)

    for value, held, outs, axis in (
        (finish(x, gx[...].T), all_x, outs_x, "col"),
        (finish(y, gy[...]), all_y, outs_y, "row"),
    ):
        share = held.shape[2]
        for p in range(held.shape[0]):
            held[p] = value[:, p * share : (p + 1) * share]
        me = lax.axis_index(axis)
        for s, out in enumerate(outs):
            out[...] = held[me ^ s]


def swap(value, axis, distance):
    return lax.ppermute(value, axis, [(d, d ^ distance) for d in range(lax.axis_size(axis))])


def exchange(part, axis, join):
    size = lax.axis_size(axis)
    assert size & (size - 1) == 0
    if size == 4:
        return (part,) + tuple(swap(part, axis, d) for d in (2, 3, 1))
    distance = 1
    got = (part,)
    while distance < size:
        if len(got) > 1:
            (part,) = call(functools.partial(join_body, join), [shape(part.shape)], len(got))(*got)
        got = (part, swap(part, axis, distance))
        distance *= 2
    return got


def scatter(pieces, axis):
    got = [pieces[0]] + [swap(pieces[s], axis, s) for s in range(1, len(pieces))]
    return sum(got[1:], got[0])


def slot(column, lane, state):
    return jnp.where(lax.broadcasted_iota(jnp.int32, state.shape, 1) == lane, column, state)


def left_strip(left0, left1, at, pot):
    strip = left1[at, :]
    for lane, part in enumerate(split3(jnp.broadcast_to(pot, strip.shape))):
        strip = slot(part, lane, strip)
    return jnp.concatenate([left0[at, :], strip.astype(BF16)], axis=1)


def halves(value):
    return sum(value[:, p : p + 128] for p in range(0, value.shape[1], 128))


def octets(value):
    return jnp.sum(value.reshape(value.shape[0] // 8, 8, value.shape[1]), axis=0)


SWEEP = 256


def sweep(left_of, right, rows, out, held_of, acc, times, store, close):
    strips, strip = times.shape[:2]
    wide_all = right.shape[1]
    for s in range(strips + 1):
        at = slice(s * strip, (s + 1) * strip)
        left = left_of(at) if s < strips else None
        sums = None
        for c in range(0, wide_all, CHUNK):
            place = slice(c, c + CHUNK)
            if s < strips:
                sums = store(held_of(s), matmul(left, right_chunk(right, rows, c, CHUNK)), place, sums)
            if s > 0:
                factor = times[s - 1]
                part = octets(held_of(s - 1)[:, place] * jnp.concatenate([factor] * (CHUNK // 128), axis=1))
                if s > 1:
                    part += acc[:, place]
                if s < strips:
                    acc[:, place] = part
                else:
                    out[:, place] = jnp.sum(part, axis=0, keepdims=True)
        if s < strips:
            times[s] = jnp.broadcast_to(close(at, sums, held_of(s)), times.shape[1:])


def exponentials(weigh):
    def store(held, scores, place, sums):
        power = jnp.exp(scores)
        held[:, place] = power
        part = halves(weigh(power, place))
        return part if sums is None else sums + part

    return store


def prepare_own_body(x_hbm, y_hbm, ax0, ax1, ay0, ay1, by, state, out, x_ref, y_ref, bx, sems):
    copies = [
        pltpu.make_async_copy(x_hbm, x_ref, sems.at[0]),
        pltpu.make_async_copy(y_hbm, y_ref, sems.at[1]),
    ]
    for copy in copies:
        copy.start()
    for copy in copies:
        copy.wait()
    x = x_ref[...]
    y = y_ref[...]
    xf = factors(x * (2.0 * SCALE), X_ORDER)
    yf = factors(y, Y_ORDER)
    for factor, left0, left1, right in ((xf, ax0, ax1, bx), (yf, ay0, ay1, by)):
        right[...] = factor.astype(BF16)
        turned = factor.T
        left0[...] = turned[:, :128].astype(BF16)
        left1[...] = turned[:, 128:]
    start = -SCALE * jnp.sum(y * y, axis=0, keepdims=True)
    state[...] = jnp.concatenate([start, jnp.zeros((127, y.shape[1]), F32)], axis=0).T
    left, unused = left_factor(ay0, ay1, start)
    partial_lse(left, bx, out)
    lane = lax.broadcasted_iota(jnp.int32, ay1.shape, 1)
    ay1[...] = jnp.where((lane >= 3) & (lane < 6), 1.0, ay1[...])


def first_pot_body(log_rows, *refs):
    refs[-1][...] = -log_rows - join_lse(refs[:-1])


def opening_body(n_row, log_rows, log_cols, left0, left1, state, *refs):
    xs, us = refs[:n_row], refs[n_row : 2 * n_row]
    right, kept, u_out, state_out, out, acc, times = refs[2 * n_row :]
    strip = times.shape[1]
    x = jnp.concatenate([r[...] for r in xs], axis=1)
    right[...] = factors(x * (2.0 * SCALE), X_ORDER).astype(BF16)
    u = jnp.concatenate([r[...] for r in us], axis=1)
    u_out[...] = u

    def left_of(at):
        return jnp.concatenate([left0[at, :], left1[at, :].astype(BF16)], axis=1)

    def store(held, scores, place, tops):
        held[:, place] = scores
        for p in range(0, CHUNK, 128):
            part = scores[:, p : p + 128]
            tops = part if tops is None else jnp.maximum(tops, part)
        return tops

    def close(at, tops, held):
        top = jnp.max(tops, axis=1, keepdims=True)
        sums = None
        for c in range(0, held.shape[1], CHUNK):
            place = slice(c, c + CHUNK)
            power = jnp.exp(held[:, place] - top)
            held[:, place] = power
            part = halves(power)
            sums = part if sums is None else sums + part
        column = jnp.sum(sums, axis=1, keepdims=True)
        pot = -log_cols - (top + jnp.log(column))
        state_out[at, :] = slot(pot, 1, slot(-top, BASE, state[at, :]))
        return math.exp(-log_cols) / column

    def held_of(s):
        return kept.at[s * strip : (s + 1) * strip]

    sweep(left_of, right, right_rows(u), out, held_of, acc, times, store, close)


BASE = 6
NEAR = 25.0


def scaled(kept, row, column_of, out, acc, hold):
    count, total = kept.shape
    block = min(256, count)

    def across(index, carry):
        at = pl.ds(pl.multiple_of(index * block, block), block)
        sums = None
        for c in range(0, total, 128):
            part = kept[at, c : c + 128] * row[:, c : c + 128]
            sums = part if sums is None else sums + part
        hold[at, :] = sums
        return carry

    lax.fori_loop(0, count // block, across, 0)
    hold[...] = jnp.broadcast_to(column_of(jnp.sum(hold[...], axis=1, keepdims=True)), hold.shape)
    acc[...] = jnp.zeros_like(acc)

    def down(index, carry):
        at = pl.ds(pl.multiple_of(index * block, block), block)
        factor = hold[at, :]
        for c in range(0, total, 128):
            acc[:, c : c + 128] += octets(kept[at, c : c + 128] * factor)
        return carry

    lax.fori_loop(0, count // block, down, 0)
    out[...] = jnp.sum(acc[...], axis=0, keepdims=True)


def iteration_body(k, n_got, log_rows, log_cols, left0, left1, right, kept, state, u_first, u_old, *refs):
    got, (u_out, state_out, out, held, acc, times, hold, row) = refs[:n_got], refs[n_got:]
    u = u_old[...] - (log_rows + jnp.log(join_sum(got)))
    u_out[...] = u
    apart = u - u_first[...]
    near = jnp.max(jnp.abs(apart)) < NEAR

    @pl.when(near)
    def scale():
        row[...] = jnp.exp(apart)

        def column_of(sums):
            old = state[...]
            state_out[...] = slot(old[:, BASE : BASE + 1] - (log_cols + jnp.log(sums)), k, old)
            return math.exp(-log_cols) / sums

        scaled(kept, row, column_of, out, acc, hold)
        out[...] = out[...] * row[...]

    @pl.when(jnp.logical_not(near))
    def renew():
        def left_of(at):
            return left_strip(left0, left1, at, state[at, k - 1 : k])

        def close(at, sums, held):
            column = jnp.sum(sums, axis=1, keepdims=True)
            old = state[at, :]
            state_out[at, :] = slot(old[:, k - 1 : k] - (log_cols + jnp.log(column)), k, old)
            return math.exp(-log_cols) / column

        store = exponentials(lambda power, place: power)
        sweep(left_of, right, right_rows(u), out, lambda s: held.at[s % 2], acc, times, store, close)


def adjoint_body(k, n_got, log_rows, log_cols, left0, left1, right, kept, state, u_first, u_ref, u_before, *refs):
    got, (adj_out, state_out, out, held, acc, times, hold, row) = refs[:n_got], refs[n_got:]
    if k == ITERS:
        adj_out[...] = 1.0 - math.exp(log_cols) * join_sum(got)
    else:
        adj_out[...] = -join_sum(got)
    u, before = u_ref[...], u_before[...]
    shift = math.exp(log_rows - log_cols)
    mass = math.exp(log_cols)
    apart, apart_before = u - u_first[...], before - u_first[...]
    near = jnp.max(jnp.maximum(jnp.abs(apart), jnp.abs(apart_before))) < NEAR

    @pl.when(near)
    def scale():
        row[...] = jnp.exp(apart) * adj_out[...]

        def column_of(sums):
            old = state[...]
            beta = mass * jnp.exp(old[:, k - 1 : k] - old[:, BASE : BASE + 1])
            adj = -shift * beta * sums
            state_out[...] = slot(adj, 16 + k - 1, old)
            return beta * adj

        scaled(kept, row, column_of, out, acc, hold)
        out[...] = out[...] * jnp.exp(apart_before)

    @pl.when(jnp.logical_not(near))
    def renew():
        def left_of(at):
            return left_strip(left0, left1, at, state[at, k : k + 1])

        def close(at, sums, held):
            column = jnp.sum(sums, axis=1, keepdims=True)
            old = state[at, :]
            sigma = jnp.exp(old[:, k - 1 : k] - old[:, k : k + 1])
            adj = -shift * sigma * column
            state_out[at, :] = slot(adj, 16 + k - 1, old)
            return sigma * adj

        store = exponentials(lambda power, place: power * adj_out[:, place])
        rows = right_rows(u + log_cols)
        sweep(left_of, right, rows, out, lambda s: held.at[s % 2], acc, times, store, close)
        out[...] = out[...] * jnp.exp(before - u)


def finish(points, sums):
    dim = points.shape[0]
    mixed = sums[0:dim] + sums[dim : 2 * dim] + sums[2 * dim : 3 * dim]
    return 2.0 * (points * sums[3 * dim : 3 * dim + 1] - mixed)


def with_total(points):
    width = points.shape[1]
    one = jnp.ones((1, width), F32)
    pad = jnp.zeros((128 - 3 * points.shape[0] - 1, width), F32)
    return jnp.concatenate(list(split3(points)) + [one, pad], axis=0).astype(BF16)


def all_weights(log_rows, log_cols, left0, left1, right, kept, state, us, adjs, at, wide, take):
    turned = state[at, :].T
    v = [turned[k : k + 1] for k in range(ITERS + 1)]
    adjs_cols = [turned[16 + k : 17 + k] for k in range(1, ITERS)] + [jnp.ones_like(v[0])]
    shift = math.exp(log_rows - log_cols)
    apart = [u - us[0] for u in us]
    near = jnp.max(functools.reduce(jnp.maximum, [jnp.abs(a) for a in apart])) < NEAR
    total = us[0].shape[1]

    @pl.when(near)
    def scale():
        alpha = [jnp.exp(a) for a in apart]
        beta = [math.exp(log_cols) * jnp.exp(pot - turned[BASE : BASE + 1]) for pot in v]
        p_rows = alpha + [a * adj for a, adj in zip(alpha, adjs)]
        q_rows = [b * adj for b, adj in zip(beta[1:], adjs_cols)] + [shift * b for b in beta[:-1]]

        def stacked(rows, order):
            zero = jnp.zeros((16 - len(rows), rows[0].shape[1]), F32)
            parts = split3(jnp.concatenate(rows + [zero], axis=0))
            tail = jnp.zeros((32, rows[0].shape[1]), F32)
            return jnp.concatenate([parts[o] for o in order] + [tail], axis=0)

        p_right = stacked(p_rows, X_ORDER).astype(BF16)
        q_left = stacked(q_rows, Y_ORDER).T.astype(BF16)
        for c in range(0, total, wide):
            place = slice(c, c + wide)
            take(kept[at, place] * matmul(q_left, p_right[:, place]), place)

    @pl.when(jnp.logical_not(near))
    def separate():
        lefts = [left_strip(left0, left1, at, state[at, k : k + 1]) for k in range(ITERS + 1)]
        for c in range(0, total, wide):
            place = slice(c, c + wide)
            weights = 0.0
            for k in range(ITERS):
                adj_col = 1.0 if k == ITERS - 1 else state[at, 17 + k : 18 + k]
                full = right_chunk(right, right_rows(us[k] + log_cols), c, wide)
                weights += jnp.exp(matmul(lefts[k + 1], full)) * adj_col
                weights += jnp.exp(matmul(lefts[k], full)) * (shift * adjs[k][:, place])
            take(weights, place)


def halved(weights):
    upper = weights.astype(BF16)
    return upper, (weights - upper.astype(F32)).astype(BF16)


def row_grad_body(n_got, log_rows, log_cols, left0, left1, right, kept, state, x_ref, y_ref, *refs):
    count = x_ref.shape[1]
    us = [r[:, :count] for r in refs[:ITERS]]
    adjs = [r[:, :count] for r in refs[ITERS : 2 * ITERS - 1]]
    refs = refs[2 * ITERS - 1 :]
    got, outs, (sums, pieces) = refs[:n_got], refs[n_got:-2], refs[-2:]
    adjs = [-join_sum([r[:, :count] for r in got])] + adjs
    y_parts = with_total(y_ref[...])

    def take(weights, place):
        upper, lower = halved(weights)
        sums[:, place] = matmul(y_parts, upper) + matmul(y_parts, lower)

    at = pl.ds(0, left0.shape[0])
    all_weights(log_rows, log_cols, left0, left1, right, kept, state, us, adjs, at, CHUNK, take)
    value = finish(x_ref[...], sums[...])
    share = count // len(outs)
    for p in range(len(outs)):
        pieces[p] = value[:, p * share : (p + 1) * share]
    me = lax.axis_index("col")
    for s, out in enumerate(outs):
        out[...] = pieces[me ^ s]


def turned_body(*refs):
    refs[-1][...] = with_total(jnp.concatenate([r[...] for r in refs[:-1]], axis=1)).astype(F32).T.astype(BF16)


def col_grad_body(n_got, log_rows, log_cols, left0, left1, right, kept, state, y_ref, x_turned, *refs):
    us = [r[...] for r in refs[:ITERS]]
    adjs = [r[...] for r in refs[ITERS : 2 * ITERS - 1]]
    refs = refs[2 * ITERS - 1 :]
    got, (out, sums) = refs[:n_got], refs[n_got:]
    adjs = [-join_sum(got)] + adjs
    share = out.shape[1]
    start = pl.multiple_of(lax.axis_index("row") * share, share)
    sums[...] = jnp.zeros_like(sums)

    def take(weights, place):
        upper, lower = halved(weights)
        sums[...] += matmul(upper, x_turned[place, :]) + matmul(lower, x_turned[place, :])

    at = pl.ds(start, share)
    all_weights(log_rows, log_cols, left0, left1, right, kept, state, us, adjs, at, CHUNK, take)
    out[...] = finish(y_ref[:, at], sums[...].T)


def gradient_scratch(dim, count_rows, count_cols, n_col, n_row):
    return [
        pltpu.VMEM((count_rows, 128), F32),
        pltpu.VMEM((128, count_rows), BF16),
        pltpu.VMEM((count_cols, 128), BF16),
        pltpu.VMEM((count_rows, 128), F32),
        pltpu.VMEM((128, count_cols), F32),
        pltpu.VMEM((count_rows, DEPTH), BF16),
        pltpu.VMEM((count_rows, 128), BF16),
        pltpu.VMEM((128, count_cols), BF16),
        pltpu.VMEM((n_col, dim, count_rows // n_col), F32),
        pltpu.VMEM((n_row, dim, count_cols // n_row), F32),
    ]


def repeated(x, y):
    dim, count_rows = x.shape
    count_cols = y.shape[1]
    n_row, n_col = lax.axis_size("row"), lax.axis_size("col")
    all_rows, held_cols = count_rows * n_row, count_cols
    log_rows, log_cols = math.log(all_rows), math.log(count_cols * n_col)
    row, col = (1, all_rows), (1, held_cols)

    own = (1, count_rows)
    ax0, ax1, ay0, ay1, by, state, part, x, y = pl.pallas_call(
        prepare_own_body,
        out_shape=[
            shape((count_rows, 128), BF16),
            shape((count_rows, 128)),
            shape((count_cols, 128), BF16),
            shape((count_cols, 128)),
            shape((DEPTH, count_cols), BF16),
            shape((count_cols, 128)),
            shape(own),
            shape(x.shape),
            shape(y.shape),
        ],
        in_specs=[pl.BlockSpec(memory_space=pltpu.HBM)] * 2,
        out_specs=vmem(9),
        scratch_shapes=[pltpu.VMEM((DEPTH, count_rows), BF16), pltpu.SemaphoreType.DMA((2,))],
        compiler_params=pltpu.CompilerParams(vmem_limit_bytes=VMEM_LIMIT),
    )(x, y)
    xs = [x] + [swap(x, "row", s) for s in range(1, n_row)]
    got = exchange(part, "col", join_lse)
    (u,) = call(functools.partial(first_pot_body, log_rows), [shape(own)], len(got))(*got)
    u_blocks = [u] + [swap(u, "row", s) for s in range(1, n_row)]

    strip = min(SWEEP, held_cols)
    sums = [pltpu.VMEM((8, all_rows), F32), pltpu.VMEM((held_cols // strip, strip, 128), F32)]
    scratch = [pltpu.VMEM((2, strip, all_rows), F32)] + sums
    scratch += [pltpu.VMEM((held_cols, 128), F32), pltpu.VMEM(row, F32)]
    results = [shape(row), shape((held_cols, 128)), shape(row)]
    us = []
    bx, kept, u, state, part = call(
        functools.partial(opening_body, n_row, log_rows, log_cols),
        [shape((DEPTH, all_rows), BF16), shape((held_cols, all_rows))] + results,
        3 + 2 * n_row,
        sums,
        SWEEP_LIMIT,
    )(ay0, ay1, state, *xs, *u_blocks)
    us.append(u)
    for k in range(2, ITERS + 1):
        got = exchange(part, "col", join_sum)
        u, state, part = call(
            functools.partial(iteration_body, k, len(got), log_rows, log_cols),
            results,
            7 + len(got),
            scratch,
            SWEEP_LIMIT,
        )(ay0, ay1, bx, kept, state, us[0], u, *got)
        us.append(u)
    adjs_rows = []
    for k in range(ITERS, 1, -1):
        got = exchange(part, "col", join_sum)
        adj, state, part = call(
            functools.partial(adjoint_body, k, len(got), log_rows, log_cols),
            results,
            8 + len(got),
            scratch,
            SWEEP_LIMIT,
        )(ay0, ay1, bx, kept, state, us[0], us[k - 1], us[k - 2], *got)
        adjs_rows.insert(0, adj)
    got = exchange(part, "col", join_sum)
    (x_turned,) = call(turned_body, [shape((all_rows, 128), BF16)], n_row)(*xs)
    share_x, share_y = count_rows // n_col, count_cols // n_row
    outs_x = call(
        functools.partial(row_grad_body, len(got), log_rows, log_cols),
        [shape((dim, share_x))] * n_col,
        7 + 2 * ITERS - 1 + len(got),
        [pltpu.VMEM((128, count_rows), F32), pltpu.VMEM((n_col, dim, share_x), F32)],
        SWEEP_LIMIT,
    )(ay0, ay1, bx, kept, state, x, y, *us, *adjs_rows, *got)
    (grad_y,) = call(
        functools.partial(col_grad_body, len(got), log_rows, log_cols),
        [shape((dim, share_y))],
        7 + 2 * ITERS - 1 + len(got),
        [pltpu.VMEM((share_y, 128), F32)],
        SWEEP_LIMIT,
        pl.CostEstimate(flops=1 << 31, bytes_accessed=1 << 23, transcendentals=0),
    )(ay0, ay1, bx, kept, state, y, x_turned, *us, *adjs_rows, *got)
    return scatter(outs_x, "col").T, grad_y.T


REPEAT_PAIRS = 1 << 23


def on_device(x_points, y_points):
    x = x_points.T
    y = y_points.T
    n_row, n_col = lax.axis_size("row"), lax.axis_size("col")
    if ITERS > 1 and x.shape[1] * n_row * y.shape[1] <= REPEAT_PAIRS:
        return repeated(x, y)
    return shared(x, y)


def shared(x, y):
    dim, count_rows = x.shape
    count_cols = y.shape[1]
    n_row, n_col = lax.axis_size("row"), lax.axis_size("col")
    log_rows = math.log(count_rows * n_row)
    log_cols = math.log(count_cols * n_col)
    row, col = (1, count_rows), (1, count_cols)

    ax0, ax1, ay0, ay1, bx, by, start, part, x, y = pl.pallas_call(
        prepare_body,
        out_shape=[
            shape((count_rows, 128), BF16),
            shape((count_rows, 128)),
            shape((count_cols, 128), BF16),
            shape((count_cols, 128)),
            shape((DEPTH, count_rows), BF16),
            shape((DEPTH, count_cols), BF16),
            shape(col),
            shape(row),
            shape(x.shape),
            shape(y.shape),
        ],
        in_specs=[pl.BlockSpec(memory_space=pltpu.HBM)] * 2,
        out_specs=vmem(10),
        scratch_shapes=[pltpu.SemaphoreType.DMA((2,))],
        compiler_params=pltpu.CompilerParams(vmem_limit_bytes=VMEM_LIMIT),
    )(x, y)

    pots_rows, pots_cols = [], [start]
    for k in range(ITERS):
        got = exchange(part, "col", join_lse)
        pot, part = call(functools.partial(forward_body, -log_rows), [shape(row), shape(col)], 3 + len(got))(
            ax0, ax1, by, *got
        )
        pots_rows.append(pot)
        got = exchange(part, "row", join_lse)
        if k < ITERS - 1:
            pot, part = call(functools.partial(forward_body, -log_cols), [shape(col), shape(row)], 3 + len(got))(
                ay0, ay1, bx, *got
            )
            pots_cols.append(pot)
    pot, part = call(functools.partial(turn_body, -log_cols, log_cols), [shape(col), shape(row)], 4 + len(got))(
        ay0, ay1, bx, pots_rows[-1], *got
    )
    pots_cols.append(pot)

    adjs_rows, adjs_cols = [], []
    for k in reversed(range(1, ITERS)):
        leading = 1.0 if k == ITERS - 1 else 0.0
        got = exchange(part, "col", join_sum)
        adj, part = call(functools.partial(backward_body, leading, log_rows), [shape(row), shape(col)], 5 + len(got))(
            ax0, ax1, by, pots_rows[k], pots_cols[k], *got
        )
        adjs_rows.insert(0, adj)
        got = exchange(part, "row", join_sum)
        adj, part = call(functools.partial(backward_body, 0.0, log_cols), [shape(col), shape(row)], 5 + len(got))(
            ay0, ay1, bx, pots_cols[k], pots_rows[k - 1], *got
        )
        adjs_cols.insert(0, adj)
    got = exchange(part, "col", join_sum)

    share_x, share_y = count_rows // n_col, count_cols // n_row
    outs = call(
        functools.partial(gradient_body, dim, log_cols, log_rows, len(got), n_col, n_row),
        [shape((dim, share_x))] * n_col + [shape((dim, share_y))] * n_row,
        5 + 4 * ITERS - 1 + len(got),
        gradient_scratch(dim, count_rows, count_cols, n_col, n_row),
    )(ax0, ax1, by, x, y, *pots_rows, *pots_cols, *adjs_rows, *adjs_cols, *got)
    grad_x = scatter(outs[:n_col], "col")
    grad_y = scatter(outs[n_col:], "row")
    return (grad_x.T, grad_y.T)


def solution(mesh):
    in_specs = (P(("groups", "row"), None), P(("groups", "col"), None))
    out_specs = (P(("groups", "row", "col"), None), P(("groups", "col", "row"), None))
    return jax.shard_map(
        on_device, mesh=mesh, in_specs=in_specs, out_specs=out_specs, check_vma=False
    )
```

```python
import functools
import math

import jax
import jax.numpy as jnp
from jax import lax
from jax.experimental import pallas as pl
from jax.experimental.pallas import tpu as pltpu
from jax.sharding import PartitionSpec as P

ITERS = 5
EPSILON = 0.05
SCALE = 1.0 / EPSILON
DEPTH = 256
CHUNK = 256
F32 = jnp.float32
BF16 = jnp.bfloat16
VMEM_LIMIT = 32 * 1024 * 1024
SWEEP_LIMIT = 24 * 1024 * 1024


def split3(v):
    high = v.astype(BF16).astype(F32)
    rest = v - high
    mid = rest.astype(BF16).astype(F32)
    low = (rest - mid).astype(BF16).astype(F32)
    return high, mid, low


def vmem(count):
    return [pl.BlockSpec(memory_space=pltpu.VMEM)] * count


def call(body, outs, count, scratch=(), limit=VMEM_LIMIT, cost=None):
    return pl.pallas_call(
        body,
        out_shape=outs,
        in_specs=vmem(count),
        out_specs=vmem(len(outs)),
        scratch_shapes=list(scratch),
        compiler_params=pltpu.CompilerParams(vmem_limit_bytes=limit),
        cost_estimate=cost,
    )


def shape(dims, dtype=F32):
    return jax.ShapeDtypeStruct(dims, dtype)


def factors(points, order):
    parts = split3(points)
    width = points.shape[1]
    blocks = [parts[o] for o in order]
    zero16 = jnp.zeros((16, width), F32)
    tail = jnp.zeros((DEPTH - 144 - 2 * points.shape[0], width), F32)
    return jnp.concatenate(blocks[:4] + [zero16] + blocks[4:] + [tail], axis=0)


X_ORDER = (0, 0, 1, 0, 2, 1)
Y_ORDER = (0, 1, 0, 2, 0, 1)


def prepare_body(x_hbm, y_hbm, ax0, ax1, ay0, ay1, bx, by, start_ref, out, x_ref, y_ref, sems):
    copies = [
        pltpu.make_async_copy(x_hbm, x_ref, sems.at[0]),
        pltpu.make_async_copy(y_hbm, y_ref, sems.at[1]),
    ]
    for copy in copies:
        copy.start()
    for copy in copies:
        copy.wait()
    x = x_ref[...]
    y = y_ref[...]
    xf = factors(x * (2.0 * SCALE), X_ORDER)
    yf = factors(y, Y_ORDER)
    for factor, left0, left1, right in ((xf, ax0, ax1, bx), (yf, ay0, ay1, by)):
        right[...] = factor.astype(BF16)
        turned = factor.T
        left0[...] = turned[:, :128].astype(BF16)
        left1[...] = turned[:, 128:]
    start = -SCALE * jnp.sum(y * y, axis=0, keepdims=True)
    start_ref[...] = start
    left, unused = left_factor(ay0, ay1, start)
    partial_lse(left, bx, out)


def left_factor(left0, left1, pot, adj=None):
    width = pot.shape[1]
    high, mid, low = split3(pot)
    one = jnp.ones((1, width), F32)
    rows = [high, mid, low, one, one, one, jnp.zeros_like(one)]
    rows.append(jnp.zeros_like(one) if adj is None else adj)
    rows.append(jnp.zeros((120, width), F32))
    turned = jnp.concatenate(rows, axis=0).T
    column = None
    if adj is not None:
        column = turned[:, 7:8]
        lane = lax.broadcasted_iota(jnp.int32, turned.shape, 1)
        turned = jnp.where(lane == 7, 0.0, turned)
    return jnp.concatenate([left0[...], (left1[...] + turned).astype(BF16)], axis=1), column


def right_rows(pot):
    width = pot.shape[1]
    one = jnp.ones((3, width), F32)
    high, mid, low = split3(pot)
    return jnp.concatenate([one, high, mid, low, jnp.zeros((10, width), F32)], axis=0).astype(BF16)


def right_chunk(right, rows, at, wide):
    return jnp.concatenate(
        [right[0:128, at : at + wide], rows[:, at : at + wide], right[144:DEPTH, at : at + wide]], axis=0
    )


def matmul(a, b):
    return jnp.dot(a, b, preferred_element_type=F32)


def partial_lse(left, right, out):
    width = right.shape[1]
    rows = right_rows(jnp.zeros((1, width), F32))
    wide = min(CHUNK, width)
    for at in range(0, width, wide):
        scores = matmul(left, right_chunk(right, rows, at, wide))
        top = jnp.max(scores, axis=0, keepdims=True)
        total = jnp.sum(jnp.exp(scores - top), axis=0, keepdims=True)
        out[:, at : at + wide] = top + jnp.log(total)


def join_lse(parts):
    parts = [p[...] for p in parts]
    top = functools.reduce(jnp.maximum, parts)
    return top + jnp.log(sum(jnp.exp(p - top) for p in parts))


def join_sum(parts):
    return sum(p[...] for p in parts)


def join_body(join, *refs):
    refs[-1][...] = join(refs[:-1])


def forward_body(log_mass, left0, left1, right, *refs):
    got, (pot_out, out) = refs[:-2], refs[-2:]
    pot = log_mass - join_lse(got)
    pot_out[...] = pot
    left, unused = left_factor(left0, left1, pot)
    partial_lse(left, right, out)


def weighted_sums(left, column, right, rows, out):
    width = right.shape[1]
    wide = min(CHUNK, width)
    for at in range(0, width, wide):
        scores = matmul(left, right_chunk(right, rows, at, wide))
        out[:, at : at + wide] = jnp.sum(jnp.exp(scores) * column, axis=0, keepdims=True)


def turn_body(log_mass, log_scale, left0, left1, right, pot_right, *refs):
    got, (pot_out, out) = refs[:-2], refs[-2:]
    pot = log_mass - join_lse(got)
    pot_out[...] = pot
    left, column = left_factor(left0, left1, pot, jnp.ones_like(pot))
    weighted_sums(left, column, right, right_rows(pot_right[...] + log_scale), out)


def backward_body(leading, log_scale, left0, left1, right, pot_left, pot_right, *refs):
    got, (adj_out, out) = refs[:-2], refs[-2:]
    adj = leading - join_sum(got)
    adj_out[...] = adj
    left, column = left_factor(left0, left1, pot_left[...], adj)
    weighted_sums(left, column, right, right_rows(pot_right[...] + log_scale), out)


SPREAD = 20.0
STRIP = 256


def gradient_body(dim, log_cols, log_rows, n_got, n_col, n_row, ax0, ax1, by, x_ref, y_ref, *refs):
    pots_rows = refs[:ITERS]
    pots_cols = refs[ITERS : 2 * ITERS + 1]
    adjs_rows = refs[2 * ITERS + 1 : 3 * ITERS]
    adjs_cols = refs[3 * ITERS : 4 * ITERS - 1]
    refs = refs[4 * ITERS - 1 :]
    got, refs = refs[:n_got], refs[n_got:]
    us = [p[...] for p in pots_rows]
    vs = [p[...] for p in pots_cols]
    first = (1.0 if ITERS == 1 else 0.0) - join_sum(got)
    adjs_rows = [first] + [a[...] for a in adjs_rows]
    adjs_cols = [a[...] for a in adjs_cols] + [jnp.ones(vs[0].shape, F32)]
    gradient(log_cols, log_rows, n_col, n_row, ax0, ax1, by, x_ref, y_ref, us, vs, adjs_rows, adjs_cols, refs)


def gradient(log_cols, log_rows, n_col, n_row, ax0, ax1, by, x_ref, y_ref, us, vs, adjs_rows, adjs_cols, refs):
    outs_x, outs_y = refs[:n_col], refs[n_col : n_col + n_row]
    cols_rows, x_parts, y_parts, gx, gy, left_e, left_r, right_r, all_x, all_y = refs[n_col + n_row :]
    dim, count_rows = x_ref.shape
    count_cols = y_ref.shape[1]
    shift = log_rows - log_cols

    x = x_ref[...]
    y = y_ref[...]
    one = jnp.ones((1, count_cols), F32)
    pad = jnp.zeros((31, count_cols), F32)
    y_parts[...] = jnp.concatenate(list(split3(y)) + [one, pad], axis=0).T.astype(BF16)
    one = jnp.ones((1, count_rows), F32)
    pad = jnp.zeros((31, count_rows), F32)
    x_parts[...] = jnp.concatenate(list(split3(x)) + [one, pad], axis=0).astype(BF16)
    gy[...] = jnp.zeros_like(gy)

    far_u = functools.reduce(jnp.maximum, [jnp.abs(u - us[-1]) for u in us])
    far_v = functools.reduce(jnp.maximum, [jnp.abs(v - vs[-1]) for v in vs])
    near = jnp.maximum(jnp.max(far_u), jnp.max(far_v)) < SPREAD

    def add_strip(at, total):
        upper = total.astype(BF16)
        lower = (total - upper.astype(F32)).astype(BF16)
        gx[at, :] = matmul(upper, y_parts[...]) + matmul(lower, y_parts[...])
        gy[...] += matmul(x_parts[:, at], upper) + matmul(x_parts[:, at], lower)

    @pl.when(near)
    def factored():
        alpha = [jnp.exp(u - us[-1]) for u in us]
        beta = [jnp.exp(v - vs[-1]) for v in vs]
        p_rows = alpha + [a * adj for a, adj in zip(alpha, adjs_rows)]
        q_rows = [b * adj for b, adj in zip(beta[1:], adjs_cols)] + [b * math.exp(shift) for b in beta[:-1]]
        fill = 16 - 2 * ITERS
        p_split = split3(jnp.concatenate(p_rows + [jnp.zeros((fill, count_rows), F32)], axis=0))
        q_split = split3(jnp.concatenate(q_rows + [jnp.zeros((fill, count_cols), F32)], axis=0))
        tail = [jnp.zeros((32, count_rows), F32)]
        left_r[...] = jnp.concatenate([p_split[o] for o in X_ORDER] + tail, axis=0).T.astype(BF16)
        tail = [jnp.zeros((32, count_cols), F32)]
        right_r[...] = jnp.concatenate([q_split[o] for o in Y_ORDER] + tail, axis=0).astype(BF16)
        left, unused = left_factor(ax0, ax1, us[-1] + log_cols)
        left_e[...] = left
        right = right_chunk(by, right_rows(vs[-1]), 0, count_cols)
        strip = min(STRIP, count_rows)
        for step in range(count_rows // strip):
            at = pl.ds(step * strip, strip)
            total = jnp.exp(matmul(left_e[at, :], right)) * matmul(left_r[at, :], right_r[...])
            add_strip(at, total)

    @pl.when(jnp.logical_not(near))
    def separate():
        stack = [u + log_cols for u in us] + adjs_rows
        stack.append(jnp.zeros((128 - len(stack), count_rows), F32))
        cols_rows[...] = jnp.concatenate(stack, axis=0).T
        strip = 128

        def block(step, carry):
            at = pl.ds(pl.multiple_of(step * strip, strip), strip)
            left = jnp.concatenate([ax0[at, :], ax1[at, :].astype(BF16)], axis=1)
            inner = matmul(left, by[...])
            columns = cols_rows[at, :]
            total = jnp.zeros_like(inner)
            for k in range(ITERS):
                base = inner + columns[:, k : k + 1]
                total += jnp.exp(base + vs[k + 1]) * adjs_cols[k]
                total += jnp.exp(base + (vs[k] + shift)) * columns[:, ITERS + k : ITERS + k + 1]
            add_strip(at, total)
            return carry

        lax.fori_loop(0, count_rows // strip, block, 0)

    def finish(points, sums):
        mixed = sums[0:dim] + sums[dim : 2 * dim] + sums[2 * dim : 3 * dim]
        return 2.0 * (points * sums[3 * dim : 3 * dim + 1] - mixed)

    for value, held, outs, axis in (
        (finish(x, gx[...].T), all_x, outs_x, "col"),
        (finish(y, gy[...]), all_y, outs_y, "row"),
    ):
        share = held.shape[2]
        for p in range(held.shape[0]):
            held[p] = value[:, p * share : (p + 1) * share]
        me = lax.axis_index(axis)
        for s, out in enumerate(outs):
            out[...] = held[me ^ s]


def swap(value, axis, distance):
    return lax.ppermute(value, axis, [(d, d ^ distance) for d in range(lax.axis_size(axis))])


def exchange(part, axis, join):
    size = lax.axis_size(axis)
    assert size & (size - 1) == 0
    if size == 4:
        return (part,) + tuple(swap(part, axis, d) for d in (2, 3, 1))
    distance = 1
    got = (part,)
    while distance < size:
        if len(got) > 1:
            (part,) = call(functools.partial(join_body, join), [shape(part.shape)], len(got))(*got)
        got = (part, swap(part, axis, distance))
        distance *= 2
    return got


def scatter(pieces, axis):
    got = [pieces[0]] + [swap(pieces[s], axis, s) for s in range(1, len(pieces))]
    return sum(got[1:], got[0])


def slot(column, lane, state):
    return jnp.where(lax.broadcasted_iota(jnp.int32, state.shape, 1) == lane, column, state)


def left_strip(left0, left1, at, pot):
    strip = left1[at, :]
    for lane, part in enumerate(split3(jnp.broadcast_to(pot, strip.shape))):
        strip = slot(part, lane, strip)
    return jnp.concatenate([left0[at, :], strip.astype(BF16)], axis=1)


def halves(value):
    return sum(value[:, p : p + 128] for p in range(0, value.shape[1], 128))


def octets(value):
    return jnp.sum(value.reshape(value.shape[0] // 8, 8, value.shape[1]), axis=0)


SWEEP = 256


def sweep(left_of, right, rows, out, held_of, acc, times, store, close):
    strips, strip = times.shape[:2]
    wide_all = right.shape[1]
    for s in range(strips + 1):
        at = slice(s * strip, (s + 1) * strip)
        left = left_of(at) if s < strips else None
        sums = None
        for c in range(0, wide_all, CHUNK):
            place = slice(c, c + CHUNK)
            if s < strips:
                sums = store(held_of(s), matmul(left, right_chunk(right, rows, c, CHUNK)), place, sums)
            if s > 0:
                factor = times[s - 1]
                part = octets(held_of(s - 1)[:, place] * jnp.concatenate([factor] * (CHUNK // 128), axis=1))
                if s > 1:
                    part += acc[:, place]
                if s < strips:
                    acc[:, place] = part
                else:
                    out[:, place] = jnp.sum(part, axis=0, keepdims=True)
        if s < strips:
            times[s] = jnp.broadcast_to(close(at, sums, held_of(s)), times.shape[1:])


def exponentials(weigh):
    def store(held, scores, place, sums):
        power = jnp.exp(scores)
        held[:, place] = power
        part = halves(weigh(power, place))
        return part if sums is None else sums + part

    return store


def prepare_own_body(x_hbm, y_hbm, ax0, ax1, ay0, ay1, by, state, out, x_ref, y_ref, bx, sems):
    copies = [
        pltpu.make_async_copy(x_hbm, x_ref, sems.at[0]),
        pltpu.make_async_copy(y_hbm, y_ref, sems.at[1]),
    ]
    for copy in copies:
        copy.start()
    for copy in copies:
        copy.wait()
    x = x_ref[...]
    y = y_ref[...]
    xf = factors(x * (2.0 * SCALE), X_ORDER)
    yf = factors(y, Y_ORDER)
    for factor, left0, left1, right in ((xf, ax0, ax1, bx), (yf, ay0, ay1, by)):
        right[...] = factor.astype(BF16)
        turned = factor.T
        left0[...] = turned[:, :128].astype(BF16)
        left1[...] = turned[:, 128:]
    start = -SCALE * jnp.sum(y * y, axis=0, keepdims=True)
    state[...] = jnp.concatenate([start, jnp.zeros((127, y.shape[1]), F32)], axis=0).T
    left, unused = left_factor(ay0, ay1, start)
    partial_lse(left, bx, out)
    lane = lax.broadcasted_iota(jnp.int32, ay1.shape, 1)
    ay1[...] = jnp.where((lane >= 3) & (lane < 6), 1.0, ay1[...])


def first_pot_body(log_rows, *refs):
    refs[-1][...] = -log_rows - join_lse(refs[:-1])


def opening_body(n_row, log_rows, log_cols, left0, left1, state, *refs):
    xs, us = refs[:n_row], refs[n_row : 2 * n_row]
    right, kept, u_out, state_out, out, acc, times = refs[2 * n_row :]
    strip = times.shape[1]
    x = jnp.concatenate([r[...] for r in xs], axis=1)
    right[...] = factors(x * (2.0 * SCALE), X_ORDER).astype(BF16)
    u = jnp.concatenate([r[...] for r in us], axis=1)
    u_out[...] = u

    def left_of(at):
        return jnp.concatenate([left0[at, :], left1[at, :].astype(BF16)], axis=1)

    def store(held, scores, place, tops):
        held[:, place] = scores
        for p in range(0, CHUNK, 128):
            part = scores[:, p : p + 128]
            tops = part if tops is None else jnp.maximum(tops, part)
        return tops

    def close(at, tops, held):
        top = jnp.max(tops, axis=1, keepdims=True)
        sums = None
        for c in range(0, held.shape[1], CHUNK):
            place = slice(c, c + CHUNK)
            power = jnp.exp(held[:, place] - top)
            held[:, place] = power
            part = halves(power)
            sums = part if sums is None else sums + part
        column = jnp.sum(sums, axis=1, keepdims=True)
        pot = -log_cols - (top + jnp.log(column))
        state_out[at, :] = slot(pot, 1, slot(-top, BASE, state[at, :]))
        return math.exp(-log_cols) / column

    def held_of(s):
        return kept.at[s * strip : (s + 1) * strip]

    sweep(left_of, right, right_rows(u), out, held_of, acc, times, store, close)


BASE = 6
NEAR = 25.0


def scaled(kept, row, column_of, out, acc, hold):
    count, total = kept.shape
    block = min(256, count)

    def across(index, carry):
        at = pl.ds(pl.multiple_of(index * block, block), block)
        sums = None
        for c in range(0, total, 128):
            part = kept[at, c : c + 128] * row[:, c : c + 128]
            sums = part if sums is None else sums + part
        hold[at, :] = sums
        return carry

    lax.fori_loop(0, count // block, across, 0)
    hold[...] = jnp.broadcast_to(column_of(jnp.sum(hold[...], axis=1, keepdims=True)), hold.shape)
    acc[...] = jnp.zeros_like(acc)

    def down(index, carry):
        at = pl.ds(pl.multiple_of(index * block, block), block)
        factor = hold[at, :]
        for c in range(0, total, 128):
            acc[:, c : c + 128] += octets(kept[at, c : c + 128] * factor)
        return carry

    lax.fori_loop(0, count // block, down, 0)
    out[...] = jnp.sum(acc[...], axis=0, keepdims=True)


def iteration_body(k, n_got, log_rows, log_cols, left0, left1, right, kept, state, u_first, u_old, *refs):
    got, (u_out, state_out, out, held, acc, times, hold, row) = refs[:n_got], refs[n_got:]
    u = u_old[...] - (log_rows + jnp.log(join_sum(got)))
    u_out[...] = u
    apart = u - u_first[...]
    near = jnp.max(jnp.abs(apart)) < NEAR

    @pl.when(near)
    def scale():
        row[...] = jnp.exp(apart)

        def column_of(sums):
            old = state[...]
            state_out[...] = slot(old[:, BASE : BASE + 1] - (log_cols + jnp.log(sums)), k, old)
            return math.exp(-log_cols) / sums

        scaled(kept, row, column_of, out, acc, hold)
        out[...] = out[...] * row[...]

    @pl.when(jnp.logical_not(near))
    def renew():
        def left_of(at):
            return left_strip(left0, left1, at, state[at, k - 1 : k])

        def close(at, sums, held):
            column = jnp.sum(sums, axis=1, keepdims=True)
            old = state[at, :]
            state_out[at, :] = slot(old[:, k - 1 : k] - (log_cols + jnp.log(column)), k, old)
            return math.exp(-log_cols) / column

        store = exponentials(lambda power, place: power)
        sweep(left_of, right, right_rows(u), out, lambda s: held.at[s % 2], acc, times, store, close)


def adjoint_body(k, n_got, log_rows, log_cols, left0, left1, right, kept, state, u_first, u_ref, u_before, *refs):
    got, (adj_out, state_out, out, held, acc, times, hold, row) = refs[:n_got], refs[n_got:]
    if k == ITERS:
        adj_out[...] = 1.0 - math.exp(log_cols) * join_sum(got)
    else:
        adj_out[...] = -join_sum(got)
    u, before = u_ref[...], u_before[...]
    shift = math.exp(log_rows - log_cols)
    mass = math.exp(log_cols)
    apart, apart_before = u - u_first[...], before - u_first[...]
    near = jnp.max(jnp.maximum(jnp.abs(apart), jnp.abs(apart_before))) < NEAR

    @pl.when(near)
    def scale():
        row[...] = jnp.exp(apart) * adj_out[...]

        def column_of(sums):
            old = state[...]
            beta = mass * jnp.exp(old[:, k - 1 : k] - old[:, BASE : BASE + 1])
            adj = -shift * beta * sums
            state_out[...] = slot(adj, 16 + k - 1, old)
            return beta * adj

        scaled(kept, row, column_of, out, acc, hold)
        out[...] = out[...] * jnp.exp(apart_before)

    @pl.when(jnp.logical_not(near))
    def renew():
        def left_of(at):
            return left_strip(left0, left1, at, state[at, k : k + 1])

        def close(at, sums, held):
            column = jnp.sum(sums, axis=1, keepdims=True)
            old = state[at, :]
            sigma = jnp.exp(old[:, k - 1 : k] - old[:, k : k + 1])
            adj = -shift * sigma * column
            state_out[at, :] = slot(adj, 16 + k - 1, old)
            return sigma * adj

        store = exponentials(lambda power, place: power * adj_out[:, place])
        rows = right_rows(u + log_cols)
        sweep(left_of, right, rows, out, lambda s: held.at[s % 2], acc, times, store, close)
        out[...] = out[...] * jnp.exp(before - u)


def finish(points, sums):
    dim = points.shape[0]
    mixed = sums[0:dim] + sums[dim : 2 * dim] + sums[2 * dim : 3 * dim]
    return 2.0 * (points * sums[3 * dim : 3 * dim + 1] - mixed)


def with_total(points):
    width = points.shape[1]
    one = jnp.ones((1, width), F32)
    pad = jnp.zeros((128 - 3 * points.shape[0] - 1, width), F32)
    return jnp.concatenate(list(split3(points)) + [one, pad], axis=0).astype(BF16)


def all_weights(log_rows, log_cols, left0, left1, right, kept, state, us, adjs, at, p_right, looped, take):
    turned = state[at, :].T
    v = [turned[k : k + 1] for k in range(ITERS + 1)]
    adjs_cols = [turned[16 + k : 17 + k] for k in range(1, ITERS)] + [jnp.ones_like(v[0])]
    shift = math.exp(log_rows - log_cols)
    apart = [u - us[0] for u in us]
    near = jnp.max(functools.reduce(jnp.maximum, [jnp.abs(a) for a in apart])) < NEAR
    total = us[0].shape[1]
    us_at, adjs_at = looped if looped else (lambda k, place: us[k][:, place], lambda k, place: adjs[k][:, place])

    def each(body):
        if not looped:
            for c in range(0, total, CHUNK):
                body(slice(c, c + CHUNK))
            return

        def step(index, carry):
            body(pl.ds(pl.multiple_of(index * CHUNK, CHUNK), CHUNK))
            return carry

        lax.fori_loop(0, total // CHUNK, step, 0)


    @pl.when(near)
    def scale():
        alpha = [jnp.exp(a) for a in apart]
        beta = [math.exp(log_cols) * jnp.exp(pot - turned[BASE : BASE + 1]) for pot in v]
        p_rows = alpha + [a * adj for a, adj in zip(alpha, adjs)]
        q_rows = [b * adj for b, adj in zip(beta[1:], adjs_cols)] + [shift * b for b in beta[:-1]]

        def stacked(rows, order):
            zero = jnp.zeros((16 - len(rows), rows[0].shape[1]), F32)
            parts = split3(jnp.concatenate(rows + [zero], axis=0))
            tail = jnp.zeros((32, rows[0].shape[1]), F32)
            return jnp.concatenate([parts[o] for o in order] + [tail], axis=0)

        p_right[...] = stacked(p_rows, X_ORDER).astype(BF16)
        q_left = stacked(q_rows, Y_ORDER).T.astype(BF16)

        def body(place):
            take(kept[at, place] * matmul(q_left, p_right[:, place]), place)

        each(body)

    @pl.when(jnp.logical_not(near))
    def separate():
        lefts = [left_strip(left0, left1, at, state[at, k : k + 1]) for k in range(ITERS + 1)]

        def body(place):
            weights = 0.0
            for k in range(ITERS):
                adj_col = 1.0 if k == ITERS - 1 else state[at, 17 + k : 18 + k]
                rows = right_rows(us_at(k, place) + log_cols)
                full = jnp.concatenate([right[0:128, place], rows, right[144:DEPTH, place]], axis=0)
                weights += jnp.exp(matmul(lefts[k + 1], full)) * adj_col
                weights += jnp.exp(matmul(lefts[k], full)) * (shift * adjs_at(k, place))
            take(weights, place)

        each(body)


def halved(weights):
    upper = weights.astype(BF16)
    return upper, (weights - upper.astype(F32)).astype(BF16)


def row_grad_body(n_got, log_rows, log_cols, left0, left1, right, kept, state, x_ref, y_ref, *refs):
    count = x_ref.shape[1]
    us = [r[:, :count] for r in refs[:ITERS]]
    adjs = [r[:, :count] for r in refs[ITERS : 2 * ITERS - 1]]
    refs = refs[2 * ITERS - 1 :]
    got, outs, (sums, pieces, p_right) = refs[:n_got], refs[n_got:-3], refs[-3:]
    adjs = [-join_sum([r[:, :count] for r in got])] + adjs
    y_parts = with_total(y_ref[...])

    def take(weights, place):
        upper, lower = halved(weights)
        sums[:, place] = matmul(y_parts, upper) + matmul(y_parts, lower)

    at = pl.ds(0, left0.shape[0])
    all_weights(log_rows, log_cols, left0, left1, right, kept, state, us, adjs, at, p_right, None, take)
    value = finish(x_ref[...], sums[...])
    share = count // len(outs)
    for p in range(len(outs)):
        pieces[p] = value[:, p * share : (p + 1) * share]
    me = lax.axis_index("col")
    for s, out in enumerate(outs):
        out[...] = pieces[me ^ s]


def turned_body(*refs):
    refs[-1][...] = with_total(jnp.concatenate([r[...] for r in refs[:-1]], axis=1)).astype(F32).T.astype(BF16)


def col_grad_body(n_got, log_rows, log_cols, left0, left1, right, kept, state, y_ref, x_turned, *refs):
    u_refs, adj_refs = refs[:ITERS], refs[ITERS : 2 * ITERS - 1]
    us = [r[...] for r in u_refs]
    adjs = [r[...] for r in adj_refs]
    refs = refs[2 * ITERS - 1 :]
    got, (out, sums, p_right) = refs[:n_got], refs[n_got:]
    adjs = [-join_sum(got)] + adjs
    share = out.shape[1]
    start = pl.multiple_of(lax.axis_index("row") * share, share)
    sums[...] = jnp.zeros_like(sums)

    def take(weights, place):
        upper, lower = halved(weights)
        sums[...] += matmul(upper, x_turned[place, :]) + matmul(lower, x_turned[place, :])

    def us_at(k, place):
        return u_refs[k][:, place]

    def adjs_at(k, place):
        return adj_refs[k - 1][:, place] if k else -sum(r[:, place] for r in got)

    at = pl.ds(start, share)
    all_weights(log_rows, log_cols, left0, left1, right, kept, state, us, adjs, at, p_right, (us_at, adjs_at), take)
    out[...] = finish(y_ref[:, at], sums[...].T)


def gradient_scratch(dim, count_rows, count_cols, n_col, n_row):
    return [
        pltpu.VMEM((count_rows, 128), F32),
        pltpu.VMEM((128, count_rows), BF16),
        pltpu.VMEM((count_cols, 128), BF16),
        pltpu.VMEM((count_rows, 128), F32),
        pltpu.VMEM((128, count_cols), F32),
        pltpu.VMEM((count_rows, DEPTH), BF16),
        pltpu.VMEM((count_rows, 128), BF16),
        pltpu.VMEM((128, count_cols), BF16),
        pltpu.VMEM((n_col, dim, count_rows // n_col), F32),
        pltpu.VMEM((n_row, dim, count_cols // n_row), F32),
    ]


def repeated(x, y):
    dim, count_rows = x.shape
    count_cols = y.shape[1]
    n_row, n_col = lax.axis_size("row"), lax.axis_size("col")
    all_rows, held_cols = count_rows * n_row, count_cols
    log_rows, log_cols = math.log(all_rows), math.log(count_cols * n_col)
    row, col = (1, all_rows), (1, held_cols)

    own = (1, count_rows)
    ax0, ax1, ay0, ay1, by, state, part, x, y = pl.pallas_call(
        prepare_own_body,
        out_shape=[
            shape((count_rows, 128), BF16),
            shape((count_rows, 128)),
            shape((count_cols, 128), BF16),
            shape((count_cols, 128)),
            shape((DEPTH, count_cols), BF16),
            shape((count_cols, 128)),
            shape(own),
            shape(x.shape),
            shape(y.shape),
        ],
        in_specs=[pl.BlockSpec(memory_space=pltpu.HBM)] * 2,
        out_specs=vmem(9),
        scratch_shapes=[pltpu.VMEM((DEPTH, count_rows), BF16), pltpu.SemaphoreType.DMA((2,))],
        compiler_params=pltpu.CompilerParams(vmem_limit_bytes=VMEM_LIMIT),
    )(x, y)
    xs = [x] + [swap(x, "row", s) for s in range(1, n_row)]
    got = exchange(part, "col", join_lse)
    (u,) = call(functools.partial(first_pot_body, log_rows), [shape(own)], len(got))(*got)
    u_blocks = [u] + [swap(u, "row", s) for s in range(1, n_row)]

    strip = min(SWEEP, held_cols)
    sums = [pltpu.VMEM((8, all_rows), F32), pltpu.VMEM((held_cols // strip, strip, 128), F32)]
    scratch = [pltpu.VMEM((2, strip, all_rows), F32)] + sums
    scratch += [pltpu.VMEM((held_cols, 128), F32), pltpu.VMEM(row, F32)]
    results = [shape(row), shape((held_cols, 128)), shape(row)]
    us = []
    bx, kept, u, state, part = call(
        functools.partial(opening_body, n_row, log_rows, log_cols),
        [shape((DEPTH, all_rows), BF16), shape((held_cols, all_rows))] + results,
        3 + 2 * n_row,
        sums,
        SWEEP_LIMIT,
    )(ay0, ay1, state, *xs, *u_blocks)
    us.append(u)
    for k in range(2, ITERS + 1):
        got = exchange(part, "col", join_sum)
        u, state, part = call(
            functools.partial(iteration_body, k, len(got), log_rows, log_cols),
            results,
            7 + len(got),
            scratch,
            SWEEP_LIMIT,
        )(ay0, ay1, bx, kept, state, us[0], u, *got)
        us.append(u)
    adjs_rows = []
    for k in range(ITERS, 1, -1):
        got = exchange(part, "col", join_sum)
        adj, state, part = call(
            functools.partial(adjoint_body, k, len(got), log_rows, log_cols),
            results,
            8 + len(got),
            scratch,
            SWEEP_LIMIT,
        )(ay0, ay1, bx, kept, state, us[0], us[k - 1], us[k - 2], *got)
        adjs_rows.insert(0, adj)
    got = exchange(part, "col", join_sum)
    (x_turned,) = call(turned_body, [shape((all_rows, 128), BF16)], n_row)(*xs)
    share_x, share_y = count_rows // n_col, count_cols // n_row
    outs_x = call(
        functools.partial(row_grad_body, len(got), log_rows, log_cols),
        [shape((dim, share_x))] * n_col,
        7 + 2 * ITERS - 1 + len(got),
        [
            pltpu.VMEM((128, count_rows), F32),
            pltpu.VMEM((n_col, dim, share_x), F32),
            pltpu.VMEM((128, count_rows), BF16),
        ],
        SWEEP_LIMIT,
    )(ay0, ay1, bx, kept, state, x, y, *us, *adjs_rows, *got)
    (grad_y,) = call(
        functools.partial(col_grad_body, len(got), log_rows, log_cols),
        [shape((dim, share_y))],
        7 + 2 * ITERS - 1 + len(got),
        [pltpu.VMEM((share_y, 128), F32), pltpu.VMEM((128, all_rows), BF16)],
        SWEEP_LIMIT,
        pl.CostEstimate(flops=1 << 31, bytes_accessed=1 << 23, transcendentals=0),
    )(ay0, ay1, bx, kept, state, y, x_turned, *us, *adjs_rows, *got)
    return scatter(outs_x, "col").T, grad_y.T


REPEAT_PAIRS = 1 << 23


def on_device(x_points, y_points):
    x = x_points.T
    y = y_points.T
    n_row, n_col = lax.axis_size("row"), lax.axis_size("col")
    if ITERS > 1 and x.shape[1] * n_row * y.shape[1] <= REPEAT_PAIRS:
        return repeated(x, y)
    return shared(x, y)


def shared(x, y):
    dim, count_rows = x.shape
    count_cols = y.shape[1]
    n_row, n_col = lax.axis_size("row"), lax.axis_size("col")
    log_rows = math.log(count_rows * n_row)
    log_cols = math.log(count_cols * n_col)
    row, col = (1, count_rows), (1, count_cols)

    ax0, ax1, ay0, ay1, bx, by, start, part, x, y = pl.pallas_call(
        prepare_body,
        out_shape=[
            shape((count_rows, 128), BF16),
            shape((count_rows, 128)),
            shape((count_cols, 128), BF16),
            shape((count_cols, 128)),
            shape((DEPTH, count_rows), BF16),
            shape((DEPTH, count_cols), BF16),
            shape(col),
            shape(row),
            shape(x.shape),
            shape(y.shape),
        ],
        in_specs=[pl.BlockSpec(memory_space=pltpu.HBM)] * 2,
        out_specs=vmem(10),
        scratch_shapes=[pltpu.SemaphoreType.DMA((2,))],
        compiler_params=pltpu.CompilerParams(vmem_limit_bytes=VMEM_LIMIT),
    )(x, y)

    pots_rows, pots_cols = [], [start]
    for k in range(ITERS):
        got = exchange(part, "col", join_lse)
        pot, part = call(functools.partial(forward_body, -log_rows), [shape(row), shape(col)], 3 + len(got))(
            ax0, ax1, by, *got
        )
        pots_rows.append(pot)
        got = exchange(part, "row", join_lse)
        if k < ITERS - 1:
            pot, part = call(functools.partial(forward_body, -log_cols), [shape(col), shape(row)], 3 + len(got))(
                ay0, ay1, bx, *got
            )
            pots_cols.append(pot)
    pot, part = call(functools.partial(turn_body, -log_cols, log_cols), [shape(col), shape(row)], 4 + len(got))(
        ay0, ay1, bx, pots_rows[-1], *got
    )
    pots_cols.append(pot)

    adjs_rows, adjs_cols = [], []
    for k in reversed(range(1, ITERS)):
        leading = 1.0 if k == ITERS - 1 else 0.0
        got = exchange(part, "col", join_sum)
        adj, part = call(functools.partial(backward_body, leading, log_rows), [shape(row), shape(col)], 5 + len(got))(
            ax0, ax1, by, pots_rows[k], pots_cols[k], *got
        )
        adjs_rows.insert(0, adj)
        got = exchange(part, "row", join_sum)
        adj, part = call(functools.partial(backward_body, 0.0, log_cols), [shape(col), shape(row)], 5 + len(got))(
            ay0, ay1, bx, pots_cols[k], pots_rows[k - 1], *got
        )
        adjs_cols.insert(0, adj)
    got = exchange(part, "col", join_sum)

    share_x, share_y = count_rows // n_col, count_cols // n_row
    outs = call(
        functools.partial(gradient_body, dim, log_cols, log_rows, len(got), n_col, n_row),
        [shape((dim, share_x))] * n_col + [shape((dim, share_y))] * n_row,
        5 + 4 * ITERS - 1 + len(got),
        gradient_scratch(dim, count_rows, count_cols, n_col, n_row),
    )(ax0, ax1, by, x, y, *pots_rows, *pots_cols, *adjs_rows, *adjs_cols, *got)
    grad_x = scatter(outs[:n_col], "col")
    grad_y = scatter(outs[n_col:], "row")
    return (grad_x.T, grad_y.T)


def solution(mesh):
    in_specs = (P(("groups", "row"), None), P(("groups", "col"), None))
    out_specs = (P(("groups", "row", "col"), None), P(("groups", "col", "row"), None))
    return jax.shard_map(
        on_device, mesh=mesh, in_specs=in_specs, out_specs=out_specs, check_vma=False
    )
```

```python
import functools
import math

import jax
import jax.numpy as jnp
from jax import lax
from jax.experimental import pallas as pl
from jax.experimental.pallas import tpu as pltpu
from jax.sharding import PartitionSpec as P

ITERS = 5
EPSILON = 0.05
SCALE = 1.0 / EPSILON
DEPTH = 256
CHUNK = 256
F32 = jnp.float32
BF16 = jnp.bfloat16
VMEM_LIMIT = 32 * 1024 * 1024
SWEEP_LIMIT = 24 * 1024 * 1024


def split3(v):
    high = v.astype(BF16).astype(F32)
    rest = v - high
    mid = rest.astype(BF16).astype(F32)
    low = (rest - mid).astype(BF16).astype(F32)
    return high, mid, low


def vmem(count):
    return [pl.BlockSpec(memory_space=pltpu.VMEM)] * count


def call(body, outs, count, scratch=(), limit=VMEM_LIMIT, cost=None):
    return pl.pallas_call(
        body,
        out_shape=outs,
        in_specs=vmem(count),
        out_specs=vmem(len(outs)),
        scratch_shapes=list(scratch),
        compiler_params=pltpu.CompilerParams(vmem_limit_bytes=limit),
        cost_estimate=cost,
    )


def shape(dims, dtype=F32):
    return jax.ShapeDtypeStruct(dims, dtype)


def factors(points, order):
    parts = split3(points)
    width = points.shape[1]
    blocks = [parts[o] for o in order]
    zero16 = jnp.zeros((16, width), F32)
    tail = jnp.zeros((DEPTH - 144 - 2 * points.shape[0], width), F32)
    return jnp.concatenate(blocks[:4] + [zero16] + blocks[4:] + [tail], axis=0)


X_ORDER = (0, 0, 1, 0, 2, 1)
Y_ORDER = (0, 1, 0, 2, 0, 1)


def prepare_body(x_hbm, y_hbm, ax0, ax1, ay0, ay1, bx, by, start_ref, out, x_ref, y_ref, sems):
    copies = [
        pltpu.make_async_copy(x_hbm, x_ref, sems.at[0]),
        pltpu.make_async_copy(y_hbm, y_ref, sems.at[1]),
    ]
    for copy in copies:
        copy.start()
    for copy in copies:
        copy.wait()
    x = x_ref[...]
    y = y_ref[...]
    xf = factors(x * (2.0 * SCALE), X_ORDER)
    yf = factors(y, Y_ORDER)
    for factor, left0, left1, right in ((xf, ax0, ax1, bx), (yf, ay0, ay1, by)):
        right[...] = factor.astype(BF16)
        turned = factor.T
        left0[...] = turned[:, :128].astype(BF16)
        left1[...] = turned[:, 128:]
    start = -SCALE * jnp.sum(y * y, axis=0, keepdims=True)
    start_ref[...] = start
    left, unused = left_factor(ay0, ay1, start)
    partial_lse(left, bx, out)


def left_factor(left0, left1, pot, adj=None):
    width = pot.shape[1]
    high, mid, low = split3(pot)
    one = jnp.ones((1, width), F32)
    rows = [high, mid, low, one, one, one, jnp.zeros_like(one)]
    rows.append(jnp.zeros_like(one) if adj is None else adj)
    rows.append(jnp.zeros((120, width), F32))
    turned = jnp.concatenate(rows, axis=0).T
    column = None
    if adj is not None:
        column = turned[:, 7:8]
        lane = lax.broadcasted_iota(jnp.int32, turned.shape, 1)
        turned = jnp.where(lane == 7, 0.0, turned)
    return jnp.concatenate([left0[...], (left1[...] + turned).astype(BF16)], axis=1), column


def right_rows(pot):
    width = pot.shape[1]
    one = jnp.ones((3, width), F32)
    high, mid, low = split3(pot)
    return jnp.concatenate([one, high, mid, low, jnp.zeros((10, width), F32)], axis=0).astype(BF16)


def right_chunk(right, rows, at, wide):
    return jnp.concatenate(
        [right[0:128, at : at + wide], rows[:, at : at + wide], right[144:DEPTH, at : at + wide]], axis=0
    )


def matmul(a, b):
    return jnp.dot(a, b, preferred_element_type=F32)


def partial_lse(left, right, out):
    width = right.shape[1]
    rows = right_rows(jnp.zeros((1, width), F32))
    wide = min(CHUNK, width)
    for at in range(0, width, wide):
        scores = matmul(left, right_chunk(right, rows, at, wide))
        top = jnp.max(scores, axis=0, keepdims=True)
        total = jnp.sum(jnp.exp(scores - top), axis=0, keepdims=True)
        out[:, at : at + wide] = top + jnp.log(total)


def join_lse(parts):
    parts = [p[...] for p in parts]
    top = functools.reduce(jnp.maximum, parts)
    return top + jnp.log(sum(jnp.exp(p - top) for p in parts))


def join_sum(parts):
    return sum(p[...] for p in parts)


def join_body(join, *refs):
    refs[-1][...] = join(refs[:-1])


def forward_body(log_mass, left0, left1, right, *refs):
    got, (pot_out, out) = refs[:-2], refs[-2:]
    pot = log_mass - join_lse(got)
    pot_out[...] = pot
    left, unused = left_factor(left0, left1, pot)
    partial_lse(left, right, out)


def weighted_sums(left, column, right, rows, out):
    width = right.shape[1]
    wide = min(CHUNK, width)
    for at in range(0, width, wide):
        scores = matmul(left, right_chunk(right, rows, at, wide))
        out[:, at : at + wide] = jnp.sum(jnp.exp(scores) * column, axis=0, keepdims=True)


def turn_body(log_mass, log_scale, left0, left1, right, pot_right, *refs):
    got, (pot_out, out) = refs[:-2], refs[-2:]
    pot = log_mass - join_lse(got)
    pot_out[...] = pot
    left, column = left_factor(left0, left1, pot, jnp.ones_like(pot))
    weighted_sums(left, column, right, right_rows(pot_right[...] + log_scale), out)


def backward_body(leading, log_scale, left0, left1, right, pot_left, pot_right, *refs):
    got, (adj_out, out) = refs[:-2], refs[-2:]
    adj = leading - join_sum(got)
    adj_out[...] = adj
    left, column = left_factor(left0, left1, pot_left[...], adj)
    weighted_sums(left, column, right, right_rows(pot_right[...] + log_scale), out)


SPREAD = 20.0
STRIP = 256


def gradient_body(dim, log_cols, log_rows, n_got, n_col, n_row, ax0, ax1, by, x_ref, y_ref, *refs):
    pots_rows = refs[:ITERS]
    pots_cols = refs[ITERS : 2 * ITERS + 1]
    adjs_rows = refs[2 * ITERS + 1 : 3 * ITERS]
    adjs_cols = refs[3 * ITERS : 4 * ITERS - 1]
    refs = refs[4 * ITERS - 1 :]
    got, refs = refs[:n_got], refs[n_got:]
    us = [p[...] for p in pots_rows]
    vs = [p[...] for p in pots_cols]
    first = (1.0 if ITERS == 1 else 0.0) - join_sum(got)
    adjs_rows = [first] + [a[...] for a in adjs_rows]
    adjs_cols = [a[...] for a in adjs_cols] + [jnp.ones(vs[0].shape, F32)]
    gradient(log_cols, log_rows, n_col, n_row, ax0, ax1, by, x_ref, y_ref, us, vs, adjs_rows, adjs_cols, refs)


def gradient(log_cols, log_rows, n_col, n_row, ax0, ax1, by, x_ref, y_ref, us, vs, adjs_rows, adjs_cols, refs):
    outs_x, outs_y = refs[:n_col], refs[n_col : n_col + n_row]
    cols_rows, x_parts, y_parts, gx, gy, left_e, left_r, right_r, all_x, all_y = refs[n_col + n_row :]
    dim, count_rows = x_ref.shape
    count_cols = y_ref.shape[1]
    shift = log_rows - log_cols

    x = x_ref[...]
    y = y_ref[...]
    one = jnp.ones((1, count_cols), F32)
    pad = jnp.zeros((31, count_cols), F32)
    y_parts[...] = jnp.concatenate(list(split3(y)) + [one, pad], axis=0).T.astype(BF16)
    one = jnp.ones((1, count_rows), F32)
    pad = jnp.zeros((31, count_rows), F32)
    x_parts[...] = jnp.concatenate(list(split3(x)) + [one, pad], axis=0).astype(BF16)
    gy[...] = jnp.zeros_like(gy)

    far_u = functools.reduce(jnp.maximum, [jnp.abs(u - us[-1]) for u in us])
    far_v = functools.reduce(jnp.maximum, [jnp.abs(v - vs[-1]) for v in vs])
    near = jnp.maximum(jnp.max(far_u), jnp.max(far_v)) < SPREAD

    def add_strip(at, total):
        upper = total.astype(BF16)
        lower = (total - upper.astype(F32)).astype(BF16)
        gx[at, :] = matmul(upper, y_parts[...]) + matmul(lower, y_parts[...])
        gy[...] += matmul(x_parts[:, at], upper) + matmul(x_parts[:, at], lower)

    @pl.when(near)
    def factored():
        alpha = [jnp.exp(u - us[-1]) for u in us]
        beta = [jnp.exp(v - vs[-1]) for v in vs]
        p_rows = alpha + [a * adj for a, adj in zip(alpha, adjs_rows)]
        q_rows = [b * adj for b, adj in zip(beta[1:], adjs_cols)] + [b * math.exp(shift) for b in beta[:-1]]
        fill = 16 - 2 * ITERS
        p_split = split3(jnp.concatenate(p_rows + [jnp.zeros((fill, count_rows), F32)], axis=0))
        q_split = split3(jnp.concatenate(q_rows + [jnp.zeros((fill, count_cols), F32)], axis=0))
        tail = [jnp.zeros((32, count_rows), F32)]
        left_r[...] = jnp.concatenate([p_split[o] for o in X_ORDER] + tail, axis=0).T.astype(BF16)
        tail = [jnp.zeros((32, count_cols), F32)]
        right_r[...] = jnp.concatenate([q_split[o] for o in Y_ORDER] + tail, axis=0).astype(BF16)
        left, unused = left_factor(ax0, ax1, us[-1] + log_cols)
        left_e[...] = left
        right = right_chunk(by, right_rows(vs[-1]), 0, count_cols)
        strip = min(STRIP, count_rows)
        for step in range(count_rows // strip):
            at = pl.ds(step * strip, strip)
            total = jnp.exp(matmul(left_e[at, :], right)) * matmul(left_r[at, :], right_r[...])
            add_strip(at, total)

    @pl.when(jnp.logical_not(near))
    def separate():
        stack = [u + log_cols for u in us] + adjs_rows
        stack.append(jnp.zeros((128 - len(stack), count_rows), F32))
        cols_rows[...] = jnp.concatenate(stack, axis=0).T
        strip = 128

        def block(step, carry):
            at = pl.ds(pl.multiple_of(step * strip, strip), strip)
            left = jnp.concatenate([ax0[at, :], ax1[at, :].astype(BF16)], axis=1)
            inner = matmul(left, by[...])
            columns = cols_rows[at, :]
            total = jnp.zeros_like(inner)
            for k in range(ITERS):
                base = inner + columns[:, k : k + 1]
                total += jnp.exp(base + vs[k + 1]) * adjs_cols[k]
                total += jnp.exp(base + (vs[k] + shift)) * columns[:, ITERS + k : ITERS + k + 1]
            add_strip(at, total)
            return carry

        lax.fori_loop(0, count_rows // strip, block, 0)

    def finish(points, sums):
        mixed = sums[0:dim] + sums[dim : 2 * dim] + sums[2 * dim : 3 * dim]
        return 2.0 * (points * sums[3 * dim : 3 * dim + 1] - mixed)

    for value, held, outs, axis in (
        (finish(x, gx[...].T), all_x, outs_x, "col"),
        (finish(y, gy[...]), all_y, outs_y, "row"),
    ):
        share = held.shape[2]
        for p in range(held.shape[0]):
            held[p] = value[:, p * share : (p + 1) * share]
        me = lax.axis_index(axis)
        for s, out in enumerate(outs):
            out[...] = held[me ^ s]


def swap(value, axis, distance):
    return lax.ppermute(value, axis, [(d, d ^ distance) for d in range(lax.axis_size(axis))])


def exchange(part, axis, join):
    size = lax.axis_size(axis)
    assert size & (size - 1) == 0
    if size == 4:
        return (part,) + tuple(swap(part, axis, d) for d in (2, 3, 1))
    distance = 1
    got = (part,)
    while distance < size:
        if len(got) > 1:
            (part,) = call(functools.partial(join_body, join), [shape(part.shape)], len(got))(*got)
        got = (part, swap(part, axis, distance))
        distance *= 2
    return got


def scatter(pieces, axis):
    got = [pieces[0]] + [swap(pieces[s], axis, s) for s in range(1, len(pieces))]
    return sum(got[1:], got[0])


def slot(column, lane, state):
    return jnp.where(lax.broadcasted_iota(jnp.int32, state.shape, 1) == lane, column, state)


def left_strip(left0, left1, at, pot):
    strip = left1[at, :]
    for lane, part in enumerate(split3(jnp.broadcast_to(pot, strip.shape))):
        strip = slot(part, lane, strip)
    return jnp.concatenate([left0[at, :], strip.astype(BF16)], axis=1)


def halves(value):
    return sum(value[:, p : p + 128] for p in range(0, value.shape[1], 128))


def octets(value):
    return jnp.sum(value.reshape(value.shape[0] // 8, 8, value.shape[1]), axis=0)


SWEEP = 256


def sweep(left_of, right, rows, out, held_of, acc, times, store, close):
    strips, strip = times.shape[:2]
    wide_all = right.shape[1]
    for s in range(strips + 1):
        at = slice(s * strip, (s + 1) * strip)
        left = left_of(at) if s < strips else None
        sums = None
        for c in range(0, wide_all, CHUNK):
            place = slice(c, c + CHUNK)
            if s < strips:
                sums = store(held_of(s), matmul(left, right_chunk(right, rows, c, CHUNK)), place, sums)
            if s > 0:
                factor = times[s - 1]
                part = octets(held_of(s - 1)[:, place] * jnp.concatenate([factor] * (CHUNK // 128), axis=1))
                if s > 1:
                    part += acc[:, place]
                if s < strips:
                    acc[:, place] = part
                else:
                    out[:, place] = jnp.sum(part, axis=0, keepdims=True)
        if s < strips:
            times[s] = jnp.broadcast_to(close(at, sums, held_of(s)), times.shape[1:])


def exponentials(weigh):
    def store(held, scores, place, sums):
        power = jnp.exp(scores)
        held[:, place] = power
        part = halves(weigh(power, place))
        return part if sums is None else sums + part

    return store


def prepare_own_body(x_hbm, y_hbm, ax0, ax1, ay0, ay1, by, state, out, x_ref, y_ref, bx, sems):
    copies = [
        pltpu.make_async_copy(x_hbm, x_ref, sems.at[0]),
        pltpu.make_async_copy(y_hbm, y_ref, sems.at[1]),
    ]
    for copy in copies:
        copy.start()
    for copy in copies:
        copy.wait()
    x = x_ref[...]
    y = y_ref[...]
    xf = factors(x * (2.0 * SCALE), X_ORDER)
    yf = factors(y, Y_ORDER)
    for factor, left0, left1, right in ((xf, ax0, ax1, bx), (yf, ay0, ay1, by)):
        right[...] = factor.astype(BF16)
        turned = factor.T
        left0[...] = turned[:, :128].astype(BF16)
        left1[...] = turned[:, 128:]
    start = -SCALE * jnp.sum(y * y, axis=0, keepdims=True)
    state[...] = jnp.concatenate([start, jnp.zeros((127, y.shape[1]), F32)], axis=0).T
    left, unused = left_factor(ay0, ay1, start)
    partial_lse(left, bx, out)
    lane = lax.broadcasted_iota(jnp.int32, ay1.shape, 1)
    ay1[...] = jnp.where((lane >= 3) & (lane < 6), 1.0, ay1[...])


def first_pot_body(log_rows, *refs):
    refs[-1][...] = -log_rows - join_lse(refs[:-1])


def opening_body(n_row, log_rows, log_cols, left0, left1, state, *refs):
    xs, us = refs[:n_row], refs[n_row : 2 * n_row]
    right, kept, u_out, state_out, out, acc, times = refs[2 * n_row :]
    strip = times.shape[1]
    x = jnp.concatenate([r[...] for r in xs], axis=1)
    right[...] = factors(x * (2.0 * SCALE), X_ORDER).astype(BF16)
    u = jnp.concatenate([r[...] for r in us], axis=1)
    u_out[...] = u

    def left_of(at):
        return jnp.concatenate([left0[at, :], left1[at, :].astype(BF16)], axis=1)

    def store(held, scores, place, tops):
        held[:, place] = scores
        for p in range(0, CHUNK, 128):
            part = scores[:, p : p + 128]
            tops = part if tops is None else jnp.maximum(tops, part)
        return tops

    def close(at, tops, held):
        top = jnp.max(tops, axis=1, keepdims=True)
        sums = None
        for c in range(0, held.shape[1], CHUNK):
            place = slice(c, c + CHUNK)
            power = jnp.exp(held[:, place] - top)
            held[:, place] = power
            part = halves(power)
            sums = part if sums is None else sums + part
        column = jnp.sum(sums, axis=1, keepdims=True)
        pot = -log_cols - (top + jnp.log(column))
        state_out[at, :] = slot(pot, 1, slot(-top, BASE, state[at, :]))
        return math.exp(-log_cols) / column

    def held_of(s):
        return kept.at[s * strip : (s + 1) * strip]

    sweep(left_of, right, right_rows(u), out, held_of, acc, times, store, close)


BASE = 6
NEAR = 25.0


def scaled(kept, row, column_of, out, acc, hold):
    count, total = kept.shape
    block = min(256, count)

    def across(index, carry):
        at = pl.ds(pl.multiple_of(index * block, block), block)
        sums = None
        for c in range(0, total, 128):
            part = kept[at, c : c + 128] * row[:, c : c + 128]
            sums = part if sums is None else sums + part
        hold[at, :] = sums
        return carry

    lax.fori_loop(0, count // block, across, 0)
    hold[...] = jnp.broadcast_to(column_of(jnp.sum(hold[...], axis=1, keepdims=True)), hold.shape)
    acc[...] = jnp.zeros_like(acc)

    def down(index, carry):
        at = pl.ds(pl.multiple_of(index * block, block), block)
        factor = hold[at, :]
        for c in range(0, total, 128):
            acc[:, c : c + 128] += octets(kept[at, c : c + 128] * factor)
        return carry

    lax.fori_loop(0, count // block, down, 0)
    out[...] = jnp.sum(acc[...], axis=0, keepdims=True)


def iteration_body(k, n_got, log_rows, log_cols, left0, left1, right, kept, state, u_first, u_old, *refs):
    got, (u_out, state_out, out, held, acc, times, hold, row) = refs[:n_got], refs[n_got:]
    u = u_old[...] - (log_rows + jnp.log(join_sum(got)))
    u_out[...] = u
    apart = u - u_first[...]
    near = jnp.max(jnp.abs(apart)) < NEAR

    @pl.when(near)
    def scale():
        row[...] = jnp.exp(apart)

        def column_of(sums):
            old = state[...]
            state_out[...] = slot(old[:, BASE : BASE + 1] - (log_cols + jnp.log(sums)), k, old)
            return math.exp(-log_cols) / sums

        scaled(kept, row, column_of, out, acc, hold)
        out[...] = out[...] * row[...]

    @pl.when(jnp.logical_not(near))
    def renew():
        def left_of(at):
            return left_strip(left0, left1, at, state[at, k - 1 : k])

        def close(at, sums, held):
            column = jnp.sum(sums, axis=1, keepdims=True)
            old = state[at, :]
            state_out[at, :] = slot(old[:, k - 1 : k] - (log_cols + jnp.log(column)), k, old)
            return math.exp(-log_cols) / column

        store = exponentials(lambda power, place: power)
        sweep(left_of, right, right_rows(u), out, lambda s: held.at[s % 2], acc, times, store, close)


def adjoint_body(k, n_got, log_rows, log_cols, left0, left1, right, kept, state, u_first, u_ref, u_before, *refs):
    got, (adj_out, state_out, out, held, acc, times, hold, row) = refs[:n_got], refs[n_got:]
    if k == ITERS:
        adj_out[...] = 1.0 - math.exp(log_cols) * join_sum(got)
    else:
        adj_out[...] = -join_sum(got)
    u, before = u_ref[...], u_before[...]
    shift = math.exp(log_rows - log_cols)
    mass = math.exp(log_cols)
    apart, apart_before = u - u_first[...], before - u_first[...]
    near = jnp.max(jnp.maximum(jnp.abs(apart), jnp.abs(apart_before))) < NEAR

    @pl.when(near)
    def scale():
        row[...] = jnp.exp(apart) * adj_out[...]

        def column_of(sums):
            old = state[...]
            beta = mass * jnp.exp(old[:, k - 1 : k] - old[:, BASE : BASE + 1])
            adj = -shift * beta * sums
            state_out[...] = slot(adj, 16 + k - 1, old)
            return beta * adj

        scaled(kept, row, column_of, out, acc, hold)
        out[...] = out[...] * jnp.exp(apart_before)

    @pl.when(jnp.logical_not(near))
    def renew():
        def left_of(at):
            return left_strip(left0, left1, at, state[at, k : k + 1])

        def close(at, sums, held):
            column = jnp.sum(sums, axis=1, keepdims=True)
            old = state[at, :]
            sigma = jnp.exp(old[:, k - 1 : k] - old[:, k : k + 1])
            adj = -shift * sigma * column
            state_out[at, :] = slot(adj, 16 + k - 1, old)
            return sigma * adj

        store = exponentials(lambda power, place: power * adj_out[:, place])
        rows = right_rows(u + log_cols)
        sweep(left_of, right, rows, out, lambda s: held.at[s % 2], acc, times, store, close)
        out[...] = out[...] * jnp.exp(before - u)


def finish(points, sums):
    dim = points.shape[0]
    mixed = sums[0:dim] + sums[dim : 2 * dim] + sums[2 * dim : 3 * dim]
    return 2.0 * (points * sums[3 * dim : 3 * dim + 1] - mixed)


def with_total(points):
    width = points.shape[1]
    one = jnp.ones((1, width), F32)
    pad = jnp.zeros((128 - 3 * points.shape[0] - 1, width), F32)
    return jnp.concatenate(list(split3(points)) + [one, pad], axis=0).astype(BF16)


def all_weights(log_rows, log_cols, left0, left1, right, kept, state, us, adjs, at, p_right, looped, take):
    turned = state[at, :].T
    v = [turned[k : k + 1] for k in range(ITERS + 1)]
    adjs_cols = [turned[16 + k : 17 + k] for k in range(1, ITERS)] + [jnp.ones_like(v[0])]
    shift = math.exp(log_rows - log_cols)
    apart = [u - us[0] for u in us]
    near = jnp.max(functools.reduce(jnp.maximum, [jnp.abs(a) for a in apart])) < NEAR
    total = us[0].shape[1]
    us_at, adjs_at = looped if looped else (lambda k, place: us[k][:, place], lambda k, place: adjs[k][:, place])

    def each(body):
        if not looped:
            for c in range(0, total, CHUNK):
                body(slice(c, c + CHUNK))
            return

        def step(index, carry):
            body(pl.ds(pl.multiple_of(index * CHUNK, CHUNK), CHUNK))
            return carry

        lax.fori_loop(0, total // CHUNK, step, 0)


    @pl.when(near)
    def scale():
        alpha = [jnp.exp(a) for a in apart]
        beta = [math.exp(log_cols) * jnp.exp(pot - turned[BASE : BASE + 1]) for pot in v]
        p_rows = alpha + [a * adj for a, adj in zip(alpha, adjs)]
        q_rows = [b * adj for b, adj in zip(beta[1:], adjs_cols)] + [shift * b for b in beta[:-1]]

        def stacked(rows, order):
            zero = jnp.zeros((16 - len(rows), rows[0].shape[1]), F32)
            parts = split3(jnp.concatenate(rows + [zero], axis=0))
            tail = jnp.zeros((32, rows[0].shape[1]), F32)
            return jnp.concatenate([parts[o] for o in order] + [tail], axis=0)

        p_right[...] = stacked(p_rows, X_ORDER).astype(BF16)
        q_left = stacked(q_rows, Y_ORDER).T.astype(BF16)

        def body(place):
            take(kept[at, place] * matmul(q_left, p_right[:, place]), place)

        each(body)

    @pl.when(jnp.logical_not(near))
    def separate():
        lefts = [left_strip(left0, left1, at, state[at, k : k + 1]) for k in range(ITERS + 1)]

        def body(place):
            weights = 0.0
            for k in range(ITERS):
                adj_col = 1.0 if k == ITERS - 1 else state[at, 17 + k : 18 + k]
                rows = right_rows(us_at(k, place) + log_cols)
                full = jnp.concatenate([right[0:128, place], rows, right[144:DEPTH, place]], axis=0)
                weights += jnp.exp(matmul(lefts[k + 1], full)) * adj_col
                weights += jnp.exp(matmul(lefts[k], full)) * (shift * adjs_at(k, place))
            take(weights, place)

        each(body)


def halved(weights):
    upper = weights.astype(BF16)
    return upper, (weights - upper.astype(F32)).astype(BF16)


def row_grad_body(n_got, log_rows, log_cols, left0, left1, right, kept, state, x_ref, y_ref, *refs):
    count = x_ref.shape[1]
    u_refs, adj_refs = refs[:ITERS], refs[ITERS : 2 * ITERS - 1]
    us = [r[:, :count] for r in u_refs]
    adjs = [r[:, :count] for r in refs[ITERS : 2 * ITERS - 1]]
    refs = refs[2 * ITERS - 1 :]
    got, outs, (sums, pieces, p_right) = refs[:n_got], refs[n_got:-3], refs[-3:]
    adjs = [-join_sum([r[:, :count] for r in got])] + adjs
    y_parts = with_total(y_ref[...])

    def take(weights, place):
        upper, lower = halved(weights)
        sums[:, place] = matmul(y_parts, upper) + matmul(y_parts, lower)

    def us_at(k, place):
        return u_refs[k][:, place]

    def adjs_at(k, place):
        return adj_refs[k - 1][:, place] if k else -sum(r[:, place] for r in got)

    at = pl.ds(0, left0.shape[0])
    all_weights(log_rows, log_cols, left0, left1, right, kept, state, us, adjs, at, p_right, (us_at, adjs_at), take)
    value = finish(x_ref[...], sums[...])
    share = count // len(outs)
    for p in range(len(outs)):
        pieces[p] = value[:, p * share : (p + 1) * share]
    me = lax.axis_index("col")
    for s, out in enumerate(outs):
        out[...] = pieces[me ^ s]


def turned_body(*refs):
    refs[-1][...] = with_total(jnp.concatenate([r[...] for r in refs[:-1]], axis=1)).astype(F32).T.astype(BF16)


def col_grad_body(n_got, log_rows, log_cols, left0, left1, right, kept, state, y_ref, x_turned, *refs):
    u_refs, adj_refs = refs[:ITERS], refs[ITERS : 2 * ITERS - 1]
    us = [r[...] for r in u_refs]
    adjs = [r[...] for r in adj_refs]
    refs = refs[2 * ITERS - 1 :]
    got, (out, sums, p_right) = refs[:n_got], refs[n_got:]
    adjs = [-join_sum(got)] + adjs
    share = out.shape[1]
    start = pl.multiple_of(lax.axis_index("row") * share, share)
    sums[...] = jnp.zeros_like(sums)

    def take(weights, place):
        upper, lower = halved(weights)
        sums[...] += matmul(upper, x_turned[place, :]) + matmul(lower, x_turned[place, :])

    def us_at(k, place):
        return u_refs[k][:, place]

    def adjs_at(k, place):
        return adj_refs[k - 1][:, place] if k else -sum(r[:, place] for r in got)

    at = pl.ds(start, share)
    all_weights(log_rows, log_cols, left0, left1, right, kept, state, us, adjs, at, p_right, (us_at, adjs_at), take)
    out[...] = finish(y_ref[:, at], sums[...].T)


def gradient_scratch(dim, count_rows, count_cols, n_col, n_row):
    return [
        pltpu.VMEM((count_rows, 128), F32),
        pltpu.VMEM((128, count_rows), BF16),
        pltpu.VMEM((count_cols, 128), BF16),
        pltpu.VMEM((count_rows, 128), F32),
        pltpu.VMEM((128, count_cols), F32),
        pltpu.VMEM((count_rows, DEPTH), BF16),
        pltpu.VMEM((count_rows, 128), BF16),
        pltpu.VMEM((128, count_cols), BF16),
        pltpu.VMEM((n_col, dim, count_rows // n_col), F32),
        pltpu.VMEM((n_row, dim, count_cols // n_row), F32),
    ]


def repeated(x, y):
    dim, count_rows = x.shape
    count_cols = y.shape[1]
    n_row, n_col = lax.axis_size("row"), lax.axis_size("col")
    all_rows, held_cols = count_rows * n_row, count_cols
    log_rows, log_cols = math.log(all_rows), math.log(count_cols * n_col)
    row, col = (1, all_rows), (1, held_cols)

    own = (1, count_rows)
    ax0, ax1, ay0, ay1, by, state, part, x, y = pl.pallas_call(
        prepare_own_body,
        out_shape=[
            shape((count_rows, 128), BF16),
            shape((count_rows, 128)),
            shape((count_cols, 128), BF16),
            shape((count_cols, 128)),
            shape((DEPTH, count_cols), BF16),
            shape((count_cols, 128)),
            shape(own),
            shape(x.shape),
            shape(y.shape),
        ],
        in_specs=[pl.BlockSpec(memory_space=pltpu.HBM)] * 2,
        out_specs=vmem(9),
        scratch_shapes=[pltpu.VMEM((DEPTH, count_rows), BF16), pltpu.SemaphoreType.DMA((2,))],
        compiler_params=pltpu.CompilerParams(vmem_limit_bytes=VMEM_LIMIT),
    )(x, y)
    xs = [x] + [swap(x, "row", s) for s in range(1, n_row)]
    got = exchange(part, "col", join_lse)
    (u,) = call(functools.partial(first_pot_body, log_rows), [shape(own)], len(got))(*got)
    u_blocks = [u] + [swap(u, "row", s) for s in range(1, n_row)]

    strip = min(SWEEP, held_cols)
    sums = [pltpu.VMEM((8, all_rows), F32), pltpu.VMEM((held_cols // strip, strip, 128), F32)]
    scratch = [pltpu.VMEM((2, strip, all_rows), F32)] + sums
    scratch += [pltpu.VMEM((held_cols, 128), F32), pltpu.VMEM(row, F32)]
    results = [shape(row), shape((held_cols, 128)), shape(row)]
    us = []
    bx, kept, u, state, part = call(
        functools.partial(opening_body, n_row, log_rows, log_cols),
        [shape((DEPTH, all_rows), BF16), shape((held_cols, all_rows))] + results,
        3 + 2 * n_row,
        sums,
        SWEEP_LIMIT,
    )(ay0, ay1, state, *xs, *u_blocks)
    us.append(u)
    for k in range(2, ITERS + 1):
        got = exchange(part, "col", join_sum)
        u, state, part = call(
            functools.partial(iteration_body, k, len(got), log_rows, log_cols),
            results,
            7 + len(got),
            scratch,
            SWEEP_LIMIT,
        )(ay0, ay1, bx, kept, state, us[0], u, *got)
        us.append(u)
    adjs_rows = []
    for k in range(ITERS, 1, -1):
        got = exchange(part, "col", join_sum)
        adj, state, part = call(
            functools.partial(adjoint_body, k, len(got), log_rows, log_cols),
            results,
            8 + len(got),
            scratch,
            SWEEP_LIMIT,
        )(ay0, ay1, bx, kept, state, us[0], us[k - 1], us[k - 2], *got)
        adjs_rows.insert(0, adj)
    got = exchange(part, "col", join_sum)
    (x_turned,) = call(turned_body, [shape((all_rows, 128), BF16)], n_row)(*xs)
    share_x, share_y = count_rows // n_col, count_cols // n_row
    outs_x = call(
        functools.partial(row_grad_body, len(got), log_rows, log_cols),
        [shape((dim, share_x))] * n_col,
        7 + 2 * ITERS - 1 + len(got),
        [
            pltpu.VMEM((128, count_rows), F32),
            pltpu.VMEM((n_col, dim, share_x), F32),
            pltpu.VMEM((128, count_rows), BF16),
        ],
        SWEEP_LIMIT,
    )(ay0, ay1, bx, kept, state, x, y, *us, *adjs_rows, *got)
    (grad_y,) = call(
        functools.partial(col_grad_body, len(got), log_rows, log_cols),
        [shape((dim, share_y))],
        7 + 2 * ITERS - 1 + len(got),
        [pltpu.VMEM((share_y, 128), F32), pltpu.VMEM((128, all_rows), BF16)],
        SWEEP_LIMIT,
        pl.CostEstimate(flops=1 << 31, bytes_accessed=1 << 23, transcendentals=0),
    )(ay0, ay1, bx, kept, state, y, x_turned, *us, *adjs_rows, *got)
    return scatter(outs_x, "col").T, grad_y.T


REPEAT_PAIRS = 1 << 23


def on_device(x_points, y_points):
    x = x_points.T
    y = y_points.T
    n_row, n_col = lax.axis_size("row"), lax.axis_size("col")
    if ITERS > 1 and x.shape[1] * n_row * y.shape[1] <= REPEAT_PAIRS:
        return repeated(x, y)
    return shared(x, y)


def shared(x, y):
    dim, count_rows = x.shape
    count_cols = y.shape[1]
    n_row, n_col = lax.axis_size("row"), lax.axis_size("col")
    log_rows = math.log(count_rows * n_row)
    log_cols = math.log(count_cols * n_col)
    row, col = (1, count_rows), (1, count_cols)

    ax0, ax1, ay0, ay1, bx, by, start, part, x, y = pl.pallas_call(
        prepare_body,
        out_shape=[
            shape((count_rows, 128), BF16),
            shape((count_rows, 128)),
            shape((count_cols, 128), BF16),
            shape((count_cols, 128)),
            shape((DEPTH, count_rows), BF16),
            shape((DEPTH, count_cols), BF16),
            shape(col),
            shape(row),
            shape(x.shape),
            shape(y.shape),
        ],
        in_specs=[pl.BlockSpec(memory_space=pltpu.HBM)] * 2,
        out_specs=vmem(10),
        scratch_shapes=[pltpu.SemaphoreType.DMA((2,))],
        compiler_params=pltpu.CompilerParams(vmem_limit_bytes=VMEM_LIMIT),
    )(x, y)

    pots_rows, pots_cols = [], [start]
    for k in range(ITERS):
        got = exchange(part, "col", join_lse)
        pot, part = call(functools.partial(forward_body, -log_rows), [shape(row), shape(col)], 3 + len(got))(
            ax0, ax1, by, *got
        )
        pots_rows.append(pot)
        got = exchange(part, "row", join_lse)
        if k < ITERS - 1:
            pot, part = call(functools.partial(forward_body, -log_cols), [shape(col), shape(row)], 3 + len(got))(
                ay0, ay1, bx, *got
            )
            pots_cols.append(pot)
    pot, part = call(functools.partial(turn_body, -log_cols, log_cols), [shape(col), shape(row)], 4 + len(got))(
        ay0, ay1, bx, pots_rows[-1], *got
    )
    pots_cols.append(pot)

    adjs_rows, adjs_cols = [], []
    for k in reversed(range(1, ITERS)):
        leading = 1.0 if k == ITERS - 1 else 0.0
        got = exchange(part, "col", join_sum)
        adj, part = call(functools.partial(backward_body, leading, log_rows), [shape(row), shape(col)], 5 + len(got))(
            ax0, ax1, by, pots_rows[k], pots_cols[k], *got
        )
        adjs_rows.insert(0, adj)
        got = exchange(part, "row", join_sum)
        adj, part = call(functools.partial(backward_body, 0.0, log_cols), [shape(col), shape(row)], 5 + len(got))(
            ay0, ay1, bx, pots_cols[k], pots_rows[k - 1], *got
        )
        adjs_cols.insert(0, adj)
    got = exchange(part, "col", join_sum)

    share_x, share_y = count_rows // n_col, count_cols // n_row
    outs = call(
        functools.partial(gradient_body, dim, log_cols, log_rows, len(got), n_col, n_row),
        [shape((dim, share_x))] * n_col + [shape((dim, share_y))] * n_row,
        5 + 4 * ITERS - 1 + len(got),
        gradient_scratch(dim, count_rows, count_cols, n_col, n_row),
    )(ax0, ax1, by, x, y, *pots_rows, *pots_cols, *adjs_rows, *adjs_cols, *got)
    grad_x = scatter(outs[:n_col], "col")
    grad_y = scatter(outs[n_col:], "row")
    return (grad_x.T, grad_y.T)


def solution(mesh):
    in_specs = (P(("groups", "row"), None), P(("groups", "col"), None))
    out_specs = (P(("groups", "row", "col"), None), P(("groups", "col", "row"), None))
    return jax.shard_map(
        on_device, mesh=mesh, in_specs=in_specs, out_specs=out_specs, check_vma=False
    )
```
